32 devices in a mesh: fsdp: 32 (over z, y, x, core).
Axes of the slice: x: 2, y: 2, z: 4, core: 2. Of those that a mesh axis runs over, the one named last changes fastest.
Arguments:
- tokens: bfloat16 [32768, 256], P('fsdp'), may hold values from -6 to 6
- params: bfloat16 [6176, 128], P('fsdp'), as said below
- segment_ids: int32 [32768], P('fsdp'), may hold values from 0 to 15, as said below
- cotangent: bfloat16 [32768, 256], P('fsdp'), may hold values from -6 to 6
Outputs:
- outputs: bfloat16 [32768, 256], P('fsdp')
- input_grad: float32 [32768, 256], P('fsdp')
- param_grad: float32 [6176, 128], P('fsdp')
The draws below stay inside these ranges and needn't reach their ends.
Inputs may be any that keep to these rules, and one draw needn't show every extreme that they name: `segment_ids`: within each sequence of 128 positions the ids start at 0 and never fall; a new document may begin only at positions that are multiples of 8. `params`: entries after the first 789504 are padding and are not used.
All inputs are finite; a program needn't handle non-finite values.
Results may differ from the reference program's by a relative error of at most 0.0081.
Values may be sent and summed in bfloat16 or wider, within the bound.
No kernel may reach another device: no remote copies, remote signals or barrier semaphores. Data moves between devices by JAX's collectives and lax.ppermute only.
A program may use at most 64 MiB of HBM per device.

```python
import math
import jax
import jax.numpy as jnp
from jax import lax

D = 256
HEADS = 4
HEAD_DIM = 64
FF = 1024
SEQ = 128
TOKENS = 32768
PCOUNT = 789504
PROWS = 6176


def draw_params(key, part):
    key = jax.random.fold_in(key, 11)
    total = PROWS * 128
    base = jax.random.normal(key, (total,), jnp.float32)
    layout = [(3 * D * D, D ** (-0.5), 0.0), (D * D, 2.0 * D ** (-0.5), 0.0), (D * FF, D ** (-0.5), 0.0), (FF * D, FF ** (-0.5), 0.0), (D, 0.1, 1.0), (D, 0.2, 0.0), (D, 0.2, 0.0), (D, 0.2, 0.0), (D, 0.2, 0.0), (D, 0.1, 1.0), (D, 0.2, 0.0), (FF, 0.2, 0.0), (D, 0.2, 0.0), (total - PCOUNT, 0.02, 0.0)]
    scales = jnp.concatenate([jnp.full((length,), factor, jnp.float32) for length, factor, center in layout])
    centers = jnp.concatenate([jnp.full((length,), center, jnp.float32) for length, factor, center in layout])
    return (base * scales + centers).reshape(PROWS, 128).astype(jnp.bfloat16)


def draw_segment_ids(key, part):
    key = jax.random.fold_in(key, 23)
    start_key, row_key = jax.random.split(key)
    sequences = TOKENS // SEQ
    blocks = SEQ // 8
    starts = (jax.random.randint(start_key, (sequences, blocks), 0, 10) < 3).astype(jnp.int32)
    chosen = jax.random.randint(row_key, (), 0, sequences)
    row_index = jnp.arange(sequences)[:, None]
    starts = jnp.where(row_index == chosen, 1, starts)
    column = jnp.arange(blocks)[None, :]
    starts = jnp.where(column == 0, 0, starts)
    numbers = jnp.cumsum(starts, axis=1).astype(jnp.int32)
    return jnp.repeat(numbers, 8, axis=1).reshape(TOKENS).astype(jnp.int32)


def shard_levels(key, dims, shards, low, largest):
    level, own = 1.0, jax.random.fold_in(key, 6)
    for position, parts in shards:
        heights = jnp.exp(jax.random.uniform(jax.random.fold_in(own, position), (parts,), jnp.float32, low / len(shards), largest / len(shards)))
        level = level * jnp.repeat(heights, dims[position] // parts).reshape([-1 if axis == position else 1 for axis in range(len(dims))])
    return level


def scatter_about(rng, shape, deviation, reach, cuts=(), kind=jnp.bfloat16):
    factor_of = shard_levels(rng, shape, cuts, -0.22, 0.18) if cuts else 1.0
    drawn = jax.random.normal(rng, shape, jnp.float32) * deviation * factor_of
    return jnp.minimum(jnp.maximum(drawn, -reach), reach).astype(kind)


def setup_inputs(seed: int = 0) -> dict:
    seeds = jax.random.split(jax.random.key(seed), 5)
    tokens = scatter_about(seeds[0], (TOKENS, D), 1.0, 6.0, ((0, 32),))
    params = draw_params(jax.random.fold_in(seeds[4], 71), 0)
    segment_ids = draw_segment_ids(jax.random.fold_in(seeds[4], 71), 0)
    cotangent = scatter_about(seeds[3], (TOKENS, D), 1.0, 6.0, ((0, 32),))
    return {"tokens": tokens, "params": params, "segment_ids": segment_ids, "cotangent": cotangent}


EPSILON = 1e-05
HIGH = lax.Precision.HIGHEST

@jax.custom_vjp
def low(v):
    return lax.optimization_barrier(v.astype(jnp.bfloat16)).astype(jnp.float32)

@jax.custom_vjp
def low_back(v):
    return v

def low_keep(v):
    return (low(v), None)

def low_pass(kept, grad):
    return (grad,)

def back_keep(v):
    return (v, None)

def back_low(kept, grad):
    return (low(grad),)
low.defvjp(low_keep, low_pass)
low_back.defvjp(back_keep, back_low)

def layer_norm(values, gain, shift):
    center = values - lax.optimization_barrier(jnp.mean(values, axis=-1, keepdims=True))
    spread = lax.optimization_barrier(jnp.mean(center * center, axis=-1, keepdims=True))
    return center * lax.rsqrt(spread + EPSILON) * gain + shift

def piece_shapes():
    return [(D, 3 * D), (D, D), (D, FF), (FF, D), (D,), (D,), (D,), (D,), (D,), (D,), (D,), (FF,), (D,)]

def split_params(flat):
    pieces = []
    offset = 0
    for piece_shape in piece_shapes():
        length = math.prod(piece_shape)
        pieces.append(flat[offset:offset + length].reshape(piece_shape))
        offset += length
    return pieces

def forward(inputs, pieces, segments):
    w_qkv, w_out, w_up, w_down, gain_one, shift_one, bias_query, bias_value, bias_out, gain_two, shift_two, bias_up, bias_down = pieces
    count = inputs.shape[0]
    normed = low(layer_norm(inputs, gain_one, shift_one))
    bias_all = jnp.concatenate([bias_query, jnp.zeros_like(bias_query), bias_value])
    project = low_back(low(jnp.einsum('gtd,de->gte', normed, w_qkv, precision=HIGH) + bias_all))
    project = project.reshape(count, SEQ, 3, HEADS, HEAD_DIM)
    query_rows = project[:, :, 0]
    key_rows = project[:, :, 1]
    value_rows = project[:, :, 2]
    scores = low_back(jnp.einsum('gqhd,gkhd->ghqk', query_rows, key_rows, precision=HIGH) * HEAD_DIM ** (-0.5))
    positions = jnp.arange(SEQ)
    causal = positions[None, :] <= positions[:, None]
    allowed = causal[None] & (segments[:, :, None] == segments[:, None, :])
    scores = jnp.where(allowed[:, None], scores, -1e+30)
    weights = low(jax.nn.softmax(scores, axis=-1))
    attended = jnp.einsum('ghqk,gkhd->gqhd', weights, value_rows, precision=HIGH).reshape(count, SEQ, D)
    attended = low_back(low(attended))
    branch_one = low_back(jnp.einsum('gtd,de->gte', attended, w_out, precision=HIGH) + bias_out)
    middle = inputs + branch_one
    normed_two = low(layer_norm(middle, gain_two, shift_two))
    hidden_pre = low_back(jnp.einsum('gtd,df->gtf', normed_two, w_up, precision=HIGH) + bias_up)
    activated = low(jax.nn.gelu(hidden_pre, approximate=True))
    branch_two = low_back(jnp.einsum('gtf,fd->gtd', activated, w_down, precision=HIGH) + bias_down)
    return middle + branch_two

def reference(tokens, params, segment_ids, cotangent):
    flat = params.astype(jnp.float32).reshape(-1)
    pieces = tuple(split_params(flat))
    total_seqs = TOKENS // SEQ
    group = math.gcd(total_seqs, max(1, 4096 // SEQ))
    rounds = total_seqs // group
    inputs = tokens.astype(jnp.float32).reshape(rounds, group, SEQ, D)
    segments = segment_ids.reshape(rounds, group, SEQ)
    cot_all = cotangent.astype(jnp.float32).reshape(rounds, group, SEQ, D)

    def one_group(totals, batch):
        inputs_group, segment_group, cot_group = batch
        result, pullback = jax.vjp(lambda values, weights_in: forward(values, weights_in, segment_group), inputs_group, pieces)
        grad_in, grad_pieces = pullback(cot_group)
        totals = tuple((summed + added for summed, added in zip(totals, grad_pieces)))
        return (totals, (result.astype(jnp.bfloat16), grad_in))
    zeros = tuple((jnp.zeros_like(piece) for piece in pieces))
    totals, (result, grad_in) = lax.scan(one_group, zeros, (inputs, segments, cot_all))
    flat_grad = jnp.concatenate([piece.reshape(-1) for piece in totals])
    padding = jnp.zeros((PROWS * 128 - flat_grad.shape[0],), flat_grad.dtype)
    param_grad = jnp.concatenate([flat_grad, padding]).reshape(PROWS, 128)
    return (result.reshape(TOKENS, D), grad_in.reshape(TOKENS, D), param_grad)
```

```python
import functools

import jax
import jax.numpy as jnp
from jax import lax
from jax.experimental import pallas as pl
from jax.experimental.pallas import tpu as pltpu
from jax.sharding import PartitionSpec as P

D = 256
HEADS = 4
HEAD_DIM = 64
FF = 1024
SEQ = 128
LANES = 128
BLOCK = 2 * SEQ
EPSILON = 1e-05
SCALE = HEAD_DIM ** (-0.5)
VMEM_BYTES = 48 * 1024 * 1024

ROW_QKV = 0
ROW_OUT = 1536
ROW_UP = 2048
ROW_DOWN = 4096
ROW_SMALL = 6144
ROW_END = 6168
GAIN_ONE, SHIFT_ONE, BIAS_QUERY, BIAS_VALUE, BIAS_OUT = 0, 2, 4, 6, 8
GAIN_TWO, SHIFT_TWO, BIAS_UP, BIAS_DOWN = 10, 12, 14, 22
SMALL_ROWS = 24

F32 = jnp.float32
BF16 = jnp.bfloat16


def dot(left, right):
    return jnp.dot(left, right, preferred_element_type=F32)


def dot_nt(left, right):
    return lax.dot_general(left, right, (((1,), (1,)), ((), ())), preferred_element_type=F32)


def dot_tn(left, right):
    return lax.dot_general(left, right, (((0,), (0,)), ((), ())), preferred_element_type=F32)


def small_vector(small, row, count):
    return jnp.concatenate([small[row + i : row + i + 1, :] for i in range(count)], axis=1)


def fold_rows(values):
    rows, columns = values.shape
    return jnp.sum(values.reshape(rows // 8, 8, columns), axis=0)


def normalize(values):
    center = values - jnp.mean(values, axis=-1, keepdims=True)
    rate = lax.rsqrt(jnp.mean(center * center, axis=-1, keepdims=True) + EPSILON)
    return center * rate, rate


def normalize_back(grad, gain, normed, rate):
    scaled = grad * gain
    return rate * (
        scaled
        - jnp.mean(scaled, axis=-1, keepdims=True)
        - normed * jnp.mean(scaled * normed, axis=-1, keepdims=True)
    )


def head_masks():
    lane = lax.broadcasted_iota(jnp.int32, (1, D), 1)
    return [(lane // HEAD_DIM == h).astype(F32).astype(BF16) for h in range(HEADS)]


def spread_heads(rows):
    return jnp.concatenate([rows * mask for mask in head_masks()], axis=0)


def matrix_from_flat(flat, start, rows, columns, out):
    per_row = columns // LANES
    for j in range(per_row):
        out[:, j * LANES : (j + 1) * LANES] = flat[
            pl.ds(start + j, rows, stride=per_row), :
        ].astype(BF16)


def matrix_to_flat(matrix, rows, columns, flat, start):
    per_row = columns // LANES
    for j in range(per_row):
        flat[pl.ds(start + j, rows, stride=per_row), :] = matrix[:, j * LANES : (j + 1) * LANES]


def attend_kernel(n_bufs, ids, seg, tok, *refs):
    bufs = refs[:n_bufs]
    (project_out, weights_out, attended_out, w_qkv, w_out, w_up, w_down, small, flat) = refs[n_bufs:]

    @pl.when(pl.program_id(0) == 0)
    def _():
        slot = 0
        for buf in bufs:
            count, rows, _ = buf.shape

            def place(i, carry, buf=buf, slot=slot, rows=rows):
                flat[pl.ds(ids[slot + i] * rows, rows), :] = buf[i].astype(F32)
                return carry

            lax.fori_loop(0, count, place, 0)
            slot += count
        matrix_from_flat(flat, ROW_QKV, D, 3 * D, w_qkv)
        matrix_from_flat(flat, ROW_OUT, D, D, w_out)
        matrix_from_flat(flat, ROW_UP, D, FF, w_up)
        matrix_from_flat(flat, ROW_DOWN, FF, D, w_down)
        small[...] = flat[ROW_SMALL:ROW_END, :]

    normed, _ = normalize(tok[...].astype(F32))
    normed_low = (
        normed * small_vector(small, GAIN_ONE, 2) + small_vector(small, SHIFT_ONE, 2)
    ).astype(BF16)
    bias = jnp.concatenate(
        [
            small_vector(small, BIAS_QUERY, 2),
            jnp.zeros((1, D), F32),
            small_vector(small, BIAS_VALUE, 2),
        ],
        axis=1,
    )
    project = (dot(normed_low, w_qkv[...]) + bias).astype(BF16)
    project_out[...] = project
    causal = lax.broadcasted_iota(jnp.int32, (SEQ, SEQ), 1) <= lax.broadcasted_iota(
        jnp.int32, (SEQ, SEQ), 0
    )
    for s in range(BLOCK // SEQ):
        rows = slice(s * SEQ, (s + 1) * SEQ)
        across = jnp.broadcast_to(seg[s].astype(F32), (SEQ, SEQ))
        allowed = causal & (across == across.T)
        query = project[rows, :D]
        key = spread_heads(project[rows, D : 2 * D])
        value = spread_heads(project[rows, 2 * D :])
        scores = dot_nt(query, key) * SCALE
        low = []
        for h in range(HEADS):
            columns = slice(h * SEQ, (h + 1) * SEQ)
            mine = jnp.where(allowed, scores[:, columns], -1e30)
            grown = jnp.exp(mine - jnp.max(mine, axis=-1, keepdims=True))
            weights = grown * (1.0 / jnp.sum(grown, axis=-1, keepdims=True))
            weights_out[rows, columns] = weights
            low.append(weights.astype(BF16))
        attended_out[rows, :] = dot(jnp.concatenate(low, axis=1), value).astype(BF16)


def feed_kernel(
    tok, attended, cot, w_out, w_up, w_down, small,
    result_out, grad_middle_out, grad_attended_out, flat_out, small_out,
    acc_out, acc_up, acc_down, acc_small,
):
    step = pl.program_id(0)

    @pl.when(step == 0)
    def _():
        acc_out[...] = jnp.zeros_like(acc_out)
        acc_up[...] = jnp.zeros_like(acc_up)
        acc_down[...] = jnp.zeros_like(acc_down)
        acc_small[...] = jnp.zeros_like(acc_small)

    gain = small_vector(small, GAIN_TWO, 2)
    middle = tok[...].astype(F32) + dot(attended[...], w_out[...]) + small_vector(small, BIAS_OUT, 2)
    normed, rate = normalize(middle)
    normed_low = (normed * gain + small_vector(small, SHIFT_TWO, 2)).astype(BF16)
    hidden = dot(normed_low, w_up[...]) + small_vector(small, BIAS_UP, 8)
    square = hidden * hidden
    slope = 0.7978845608028654
    bent = jnp.tanh(hidden * (slope + (slope * 0.044715) * square))
    half = 0.5 + 0.5 * bent
    activated = (hidden * half).astype(BF16)
    derivative = half + hidden * (0.5 - 0.5 * bent * bent) * (
        slope + (3 * slope * 0.044715) * square
    )
    result = middle + dot(activated, w_down[...]) + small_vector(small, BIAS_DOWN, 2)
    result_out[...] = result.astype(BF16)
    cotangent = cot[...]
    grad_result = cotangent.astype(F32)
    acc_down[...] += dot_tn(activated, cotangent)
    grad_hidden = (dot_nt(cotangent, w_down[...]) * derivative).astype(BF16)
    acc_up[...] += dot_tn(normed_low, grad_hidden)
    grad_normed = dot_nt(grad_hidden, w_up[...])
    grad_middle = grad_result + normalize_back(grad_normed, gain, normed, rate)
    grad_middle_out[...] = grad_middle
    grad_middle_low = grad_middle.astype(BF16)
    acc_out[...] += dot_tn(attended[...], grad_middle_low)
    grad_attended_out[...] = dot_nt(grad_middle_low, w_out[...]).astype(BF16)
    acc_small[:, 0:D] += fold_rows(grad_middle_low.astype(F32))
    acc_small[:, D : 2 * D] += fold_rows(grad_normed * normed)
    acc_small[:, 2 * D : 3 * D] += fold_rows(grad_normed)
    acc_small[:, 3 * D : 3 * D + FF] += fold_rows(grad_hidden.astype(F32))
    acc_small[:, 3 * D + FF :] += fold_rows(grad_result)

    @pl.when(step == pl.num_programs(0) - 1)
    def _():
        matrix_to_flat(acc_out, D, D, flat_out, ROW_OUT - ROW_OUT)
        matrix_to_flat(acc_up, D, FF, flat_out, ROW_UP - ROW_OUT)
        matrix_to_flat(acc_down, FF, D, flat_out, ROW_DOWN - ROW_OUT)
        sums = jnp.sum(acc_small[...], axis=0, keepdims=True)
        for i in range(SMALL_ROWS - BIAS_OUT):
            small_out[i : i + 1, :] = sums[:, i * LANES : (i + 1) * LANES]


def attend_back_kernel(
    n_bufs, ids, tok, project, weights, grad_attended, grad_middle, w_qkv, small, flat_in, small_in,
    input_grad_out, *refs,
):
    bufs = refs[:n_bufs]
    acc_qkv, acc_small, flat, grad_project = refs[n_bufs:]
    step = pl.program_id(0)

    @pl.when(step == 0)
    def _():
        acc_qkv[...] = jnp.zeros_like(acc_qkv)
        acc_small[...] = jnp.zeros_like(acc_small)

    masks = head_masks()
    for s in range(BLOCK // SEQ):
        rows = slice(s * SEQ, (s + 1) * SEQ)
        query = spread_heads(project[rows, :D])
        key = spread_heads(project[rows, D : 2 * D])
        value = spread_heads(project[rows, 2 * D :])
        grad_rows = grad_attended[rows, :]
        grad_weights = dot_nt(grad_rows, value)
        scores_low, scores_turned, weights_turned = [], [], []
        for h in range(HEADS):
            columns = slice(h * SEQ, (h + 1) * SEQ)
            mine = weights[rows, columns]
            product = mine * grad_weights[:, columns]
            grad_scores = product - mine * jnp.sum(product, axis=-1, keepdims=True)
            scores_low.append(grad_scores.astype(BF16))
            scores_turned.append(grad_scores.T.astype(BF16))
            weights_turned.append(mine.T.astype(BF16))
        grad_query = dot(jnp.concatenate(scores_low, axis=1), key) * SCALE
        grad_key = dot(jnp.concatenate(scores_turned, axis=1), query) * SCALE
        grad_value = dot(jnp.concatenate(weights_turned, axis=1), spread_heads(grad_rows))
        grad_project[rows, :D] = grad_query.astype(BF16)
        grad_project[rows, D : 2 * D] = grad_key.astype(BF16)
        grad_project[rows, 2 * D :] = grad_value.astype(BF16)

    gain = small_vector(small, GAIN_ONE, 2)
    normed, rate = normalize(tok[...].astype(F32))
    normed_low = (normed * gain + small_vector(small, SHIFT_ONE, 2)).astype(BF16)
    acc_qkv[...] += dot_tn(normed_low, grad_project[...])
    grad_normed = dot_nt(grad_project[...], w_qkv[...])
    input_grad_out[...] = grad_middle[...] + normalize_back(grad_normed, gain, normed, rate)
    acc_small[:, 0:D] += fold_rows(grad_normed * normed)
    acc_small[:, D : 2 * D] += fold_rows(grad_normed)
    acc_small[:, 2 * D : 3 * D] += fold_rows(grad_project[:, :D].astype(F32))
    acc_small[:, 3 * D :] += fold_rows(grad_project[:, 2 * D :].astype(F32))

    @pl.when(step == pl.num_programs(0) - 1)
    def _():
        matrix_to_flat(acc_qkv, D, 3 * D, flat, ROW_QKV)
        flat[ROW_OUT:ROW_SMALL, :] = flat_in[...]
        sums = jnp.sum(acc_small[...], axis=0, keepdims=True)
        for i in range(BIAS_OUT):
            flat[ROW_SMALL + i : ROW_SMALL + i + 1, :] = sums[:, i * LANES : (i + 1) * LANES]
        flat[ROW_SMALL + BIAS_OUT : ROW_END, :] = small_in[...]
        if flat.shape[0] > ROW_END:
            flat[ROW_END:, :] = jnp.zeros((flat.shape[0] - ROW_END, LANES), F32)
        slot = 0
        for buf in bufs:
            count, rows, _ = buf.shape

            def place(i, carry, buf=buf, slot=slot, rows=rows):
                buf[i] = flat[pl.ds(ids[slot + i] * rows, rows), :].astype(buf.dtype)
                return carry

            lax.fori_loop(0, count, place, 0)
            slot += count


def rows_spec(columns):
    return pl.BlockSpec((BLOCK, columns), lambda i: (i, 0))


def whole_spec(shape):
    return pl.BlockSpec(shape, lambda i: (0,) * len(shape))


SMEM_SPEC = pl.BlockSpec(memory_space=pltpu.SMEM)
PARAMS = pltpu.CompilerParams(
    dimension_semantics=("arbitrary",), vmem_limit_bytes=VMEM_BYTES
)


def attend(ids, segments, tokens, bufs):
    rows = tokens.shape[0]
    total = sum(buf.shape[0] * buf.shape[1] for buf in bufs)
    fixed = [(D, 3 * D), (D, D), (D, FF), (FF, D)]
    outs = [((rows, 3 * D), BF16), ((rows, HEADS * SEQ), F32), ((rows, D), BF16)]
    return pl.pallas_call(
        functools.partial(attend_kernel, len(bufs)),
        grid=(rows // BLOCK,),
        in_specs=[
            SMEM_SPEC,
            pl.BlockSpec((BLOCK // SEQ, 1, SEQ), lambda i: (i, 0, 0)),
            rows_spec(D),
        ]
        + [whole_spec(buf.shape) for buf in bufs],
        out_specs=[rows_spec(shape[1]) for shape, _ in outs]
        + [whole_spec(shape) for shape in fixed]
        + [whole_spec((SMALL_ROWS, LANES))],
        out_shape=[jax.ShapeDtypeStruct(shape, kind) for shape, kind in outs]
        + [jax.ShapeDtypeStruct(shape, BF16) for shape in fixed]
        + [jax.ShapeDtypeStruct((SMALL_ROWS, LANES), F32)],
        scratch_shapes=[pltpu.VMEM((total, LANES), F32)],
        compiler_params=PARAMS,
        name="attend",
    )(ids, segments, tokens, *bufs)


def feed(tokens, attended, cotangent, w_out, w_up, w_down, small):
    rows = tokens.shape[0]
    flat_rows = ROW_SMALL - ROW_OUT
    small_rows = SMALL_ROWS - BIAS_OUT
    return pl.pallas_call(
        feed_kernel,
        grid=(rows // BLOCK,),
        in_specs=[rows_spec(D)] * 3
        + [whole_spec(item.shape) for item in (w_out, w_up, w_down, small)],
        out_specs=[rows_spec(D)] * 3
        + [whole_spec((flat_rows, LANES)), whole_spec((small_rows, LANES))],
        out_shape=[
            jax.ShapeDtypeStruct((rows, D), BF16),
            jax.ShapeDtypeStruct((rows, D), F32),
            jax.ShapeDtypeStruct((rows, D), BF16),
            jax.ShapeDtypeStruct((flat_rows, LANES), F32),
            jax.ShapeDtypeStruct((small_rows, LANES), F32),
        ],
        scratch_shapes=[
            pltpu.VMEM((D, D), F32),
            pltpu.VMEM((D, FF), F32),
            pltpu.VMEM((FF, D), F32),
            pltpu.VMEM((8, small_rows * LANES), F32),
        ],
        compiler_params=PARAMS,
        name="feed",
    )(tokens, attended, cotangent, w_out, w_up, w_down, small)


def attend_back(ids, tokens, project, weights, grad_attended, grad_middle, w_qkv, small, flat, few, bufs):
    rows = tokens.shape[0]
    total = sum(shape[0] * shape[1] for shape, _ in bufs)
    return pl.pallas_call(
        functools.partial(attend_back_kernel, len(bufs)),
        grid=(rows // BLOCK,),
        in_specs=[SMEM_SPEC]
        + [rows_spec(item.shape[1]) for item in (tokens, project, weights, grad_attended, grad_middle)]
        + [whole_spec(item.shape) for item in (w_qkv, small, flat, few)],
        out_specs=[rows_spec(D)] + [whole_spec(shape) for shape, _ in bufs],
        out_shape=[jax.ShapeDtypeStruct((rows, D), F32)]
        + [jax.ShapeDtypeStruct(shape, kind) for shape, kind in bufs],
        scratch_shapes=[
            pltpu.VMEM((D, 3 * D), F32),
            pltpu.VMEM((8, BIAS_OUT * LANES), F32),
            pltpu.VMEM((total, LANES), F32),
            pltpu.VMEM((BLOCK, 3 * D), BF16),
        ],
        compiler_params=PARAMS,
        name="attend_back",
    )(ids, tokens, project, weights, grad_attended, grad_middle, w_qkv, small, flat, few)


def block(tokens, segment_ids, cotangent, share_ids, shares, grad_ids, grad_bufs):
    segments = segment_ids.reshape(-1, 1, SEQ)
    project, weights, attended, w_qkv, w_out, w_up, w_down, small = attend(
        share_ids, segments, tokens, shares
    )
    outputs, grad_middle, grad_attended, flat, few = feed(
        tokens, attended, cotangent, w_out, w_up, w_down, small
    )
    input_grad, *grads = attend_back(
        grad_ids, tokens, project, weights, grad_attended, grad_middle, w_qkv, small, flat, few, grad_bufs
    )
    return outputs, input_grad, grads


def local_any(n, tokens, params, segment_ids, cotangent):
    rows = params.shape[0]
    gathered = lax.all_gather(params, "fsdp", axis=0)
    ids = jnp.arange(n, dtype=jnp.int32)
    outputs, input_grad, (grads,) = block(
        tokens, segment_ids, cotangent, ids, [gathered], ids, [((n, rows, LANES), F32)]
    )
    param_grad = lax.psum_scatter(
        grads.reshape(n * rows, LANES), "fsdp", scatter_dimension=0, tiled=True
    )
    return outputs, input_grad, param_grad


Z, PLANE = 4, 4


def index_of(z, plane, core):
    return (z * PLANE + plane) * 2 + core


def move(values, step_z, step_plane, step_core):
    pairs = [
        (index_of(z, p, c), index_of((z + step_z) % Z, p ^ step_plane, c ^ step_core))
        for z in range(Z)
        for p in range(PLANE)
        for c in range(2)
    ]
    return lax.ppermute(values, "fsdp", pairs)


def local_slice(tokens, params, segment_ids, cotangent):
    me = lax.axis_index("fsdp").astype(jnp.int32)
    z, plane, core = me // (2 * PLANE), (me // 2) % PLANE, me % 2

    column = jnp.stack([params] + [move(params, d, 0, 0) for d in range(1, Z)])
    same = [column] + [move(column, 0, d, 0) for d in range(1, PLANE)]
    shares = same + [move(item, 0, 0, 1) for item in same]
    share_ids = jnp.stack(
        [
            index_of((z - dz) % Z, plane ^ dp, core ^ dc)
            for dc in range(2)
            for dp in range(PLANE)
            for dz in range(Z)
        ]
    )
    grad_ids = jnp.stack(
        [
            index_of((z + dz) % Z, plane ^ dp, core ^ dc)
            for dc in range(2)
            for dp in range(PLANE)
            for dz in range(Z)
        ]
    )
    shape = (PLANE * Z,) + params.shape
    outputs, input_grad, (kept, sent) = block(
        tokens, segment_ids, cotangent, share_ids, shares, grad_ids, [(shape, F32), (shape, BF16)]
    )

    totals = kept + move(sent, 0, 0, 1).astype(F32)
    totals = totals.reshape((PLANE, Z) + params.shape)
    column = totals[0]
    for d in range(1, PLANE):
        column = column + move(totals[d].astype(BF16), 0, d, 0).astype(F32)
    param_grad = column[0]
    for d in range(1, Z):
        param_grad = param_grad + move(column[d].astype(BF16), d, 0, 0).astype(F32)
    return outputs, input_grad, param_grad


def solution(mesh):
    n = mesh.shape["fsdp"]
    local = local_slice if n == 2 * PLANE * Z else functools.partial(local_any, n)
    in_specs = (P("fsdp", None), P("fsdp", None), P("fsdp"), P("fsdp", None))
    out_specs = (P("fsdp", None), P("fsdp", None), P("fsdp", None))
    return jax.shard_map(local, mesh=mesh, in_specs=in_specs, out_specs=out_specs, check_vma=False)
```

```python
import functools

import jax
import jax.numpy as jnp
from jax import lax
from jax.experimental import pallas as pl
from jax.experimental.pallas import tpu as pltpu
from jax.sharding import PartitionSpec as P

D = 256
HEADS = 4
HEAD_DIM = 64
FF = 1024
SEQ = 128
LANES = 128
BLOCK = 2 * SEQ
EPSILON = 1e-05
SCALE = HEAD_DIM ** (-0.5)
VMEM_BYTES = 48 * 1024 * 1024

ROW_QKV = 0
ROW_OUT = 1536
ROW_UP = 2048
ROW_DOWN = 4096
ROW_SMALL = 6144
ROW_END = 6168
ROW_TOTAL = 6176
GAIN_ONE, SHIFT_ONE, BIAS_QUERY, BIAS_VALUE, BIAS_OUT = 0, 2, 4, 6, 8
GAIN_TWO, SHIFT_TWO, BIAS_UP, BIAS_DOWN = 10, 12, 14, 22
SMALL_ROWS = 32
LATE_SMALL = 8

SHARE = 193
Z, PLANE = 4, 4
FIRST_ROWS = 2 * PLANE * SHARE
HEAD_ROWS = FIRST_ROWS - ROW_OUT
SMALL_IN_SHARE = ROW_SMALL - (2 * PLANE * Z - 1) * SHARE
SIDE = 208

F32 = jnp.float32
BF16 = jnp.bfloat16


def dot(left, right):
    return jnp.dot(left, right, preferred_element_type=F32)


def dot_nt(left, right):
    return lax.dot_general(left, right, (((1,), (1,)), ((), ())), preferred_element_type=F32)


def dot_tn(left, right):
    return lax.dot_general(left, right, (((0,), (0,)), ((), ())), preferred_element_type=F32)


def small_vector(small, row, count):
    return jnp.concatenate([small[row + i : row + i + 1, :] for i in range(count)], axis=1)


def fold_rows(values):
    rows, columns = values.shape
    return jnp.sum(values.reshape(rows // 8, 8, columns), axis=0)


def normalize(values):
    center = values - jnp.mean(values, axis=-1, keepdims=True)
    rate = lax.rsqrt(jnp.mean(center * center, axis=-1, keepdims=True) + EPSILON)
    return center * rate, rate


def normalize_back(grad, gain, normed, rate):
    scaled = grad * gain
    return rate * (
        scaled
        - jnp.mean(scaled, axis=-1, keepdims=True)
        - normed * jnp.mean(scaled * normed, axis=-1, keepdims=True)
    )


def head_masks():
    lane = lax.broadcasted_iota(jnp.int32, (1, D), 1)
    return [(lane // HEAD_DIM == h).astype(F32).astype(BF16) for h in range(HEADS)]


def spread_heads(rows):
    return jnp.concatenate([rows * mask for mask in head_masks()], axis=0)


def matrix_from_flat(flat, start, rows, columns, out):
    per_row = columns // LANES
    for j in range(per_row):
        out[:, j * LANES : (j + 1) * LANES] = flat[
            pl.ds(start + j, rows, stride=per_row), :
        ].astype(BF16)


def matrix_to_flat(matrix, rows, columns, flat, start):
    per_row = columns // LANES
    for j in range(per_row):
        flat[pl.ds(start + j, rows, stride=per_row), :] = matrix[:, j * LANES : (j + 1) * LANES]


def place_shares(bufs, ids, flat, base):
    for slot, buf in enumerate(bufs):
        for z in range(Z - 1):
            share = ids[slot] + (z + 1) * 2 * PLANE
            flat[pl.ds(share * SHARE - base, SHARE), :] = buf[z].astype(F32)


def sort_kernel(ids, *refs):
    received, (first, rest, stage, wide) = refs[:Z], refs[Z:]
    for d in range(Z):
        stage[lax.rem(ids[0] + Z - d, Z)] = received[d][...]
    rest[...] = stage[1:]
    wide[:SHARE, :] = stage[0].astype(F32)
    wide[SHARE:SIDE, :] = jnp.zeros((SIDE - SHARE, LANES), F32)
    last = stage[Z - 1].astype(F32)
    wide[SIDE:, :] = last[SMALL_IN_SHARE:, :]
    first[...] = wide[...].astype(BF16)


def attend_kernel(
    ids, seg, tok, *refs,
):
    bufs = refs[: 2 * PLANE]
    project_out, weights_out, attended_out, w_qkv, small, first_out, flat = refs[2 * PLANE :]

    @pl.when(pl.program_id(0) == 0)
    def _():
        for slot, buf in enumerate(bufs):
            wide = buf[...].astype(F32)
            flat[pl.ds(ids[slot] * SHARE, SHARE), :] = wide[:SHARE, :]

            @pl.when(ids[slot] == 2 * PLANE - 1)
            def _():
                small[...] = wide[SIDE:, :]

        matrix_from_flat(flat, ROW_QKV, D, 3 * D, w_qkv)
        first_out[...] = flat[ROW_OUT:FIRST_ROWS, :]

    normed, _ = normalize(tok[...].astype(F32))
    normed_low = (
        normed * small_vector(small, GAIN_ONE, 2) + small_vector(small, SHIFT_ONE, 2)
    ).astype(BF16)
    bias = jnp.concatenate(
        [
            small_vector(small, BIAS_QUERY, 2),
            jnp.zeros((1, D), F32),
            small_vector(small, BIAS_VALUE, 2),
        ],
        axis=1,
    )
    project = (dot(normed_low, w_qkv[...]) + bias).astype(BF16)
    project_out[...] = project
    causal = lax.broadcasted_iota(jnp.int32, (SEQ, SEQ), 1) <= lax.broadcasted_iota(
        jnp.int32, (SEQ, SEQ), 0
    )
    for s in range(BLOCK // SEQ):
        rows = slice(s * SEQ, (s + 1) * SEQ)
        across = jnp.broadcast_to(seg[s].astype(F32), (SEQ, SEQ))
        allowed = causal & (across == across.T)
        query = project[rows, :D]
        key = spread_heads(project[rows, D : 2 * D])
        value = spread_heads(project[rows, 2 * D :])
        scores = dot_nt(query, key) * SCALE
        low = []
        for h in range(HEADS):
            columns = slice(h * SEQ, (h + 1) * SEQ)
            mine = jnp.where(allowed, scores[:, columns], -1e30)
            grown = jnp.exp(mine - jnp.max(mine, axis=-1, keepdims=True))
            weights = grown * (1.0 / jnp.sum(grown, axis=-1, keepdims=True))
            weights_out[rows, columns] = weights
            low.append(weights.astype(BF16))
        attended_out[rows, :] = dot(jnp.concatenate(low, axis=1), value).astype(BF16)


def feed_kernel(
    ids, tok, attended, cot, small, first_in, *refs,
):
    bufs = refs[: 2 * PLANE]
    (
        result_out, grad_middle_out, grad_attended_out, keep_out, send_out, first_out,
        w_out, w_up, w_down, acc_out, acc_up, acc_down, acc_small, flat,
    ) = refs[2 * PLANE :]
    step = pl.program_id(0)

    @pl.when(step == 0)
    def _():
        flat[:HEAD_ROWS, :] = first_in[...]
        place_shares(bufs, ids, flat, ROW_OUT)
        matrix_from_flat(flat, 0, D, D, w_out)
        matrix_from_flat(flat, ROW_UP - ROW_OUT, D, FF, w_up)
        matrix_from_flat(flat, ROW_DOWN - ROW_OUT, FF, D, w_down)
        acc_out[...] = jnp.zeros_like(acc_out)
        acc_up[...] = jnp.zeros_like(acc_up)
        acc_down[...] = jnp.zeros_like(acc_down)
        acc_small[...] = jnp.zeros_like(acc_small)

    gain = small_vector(small, GAIN_TWO, 2)
    middle = tok[...].astype(F32) + dot(attended[...], w_out[...]) + small_vector(small, BIAS_OUT, 2)
    normed, rate = normalize(middle)
    normed_low = (normed * gain + small_vector(small, SHIFT_TWO, 2)).astype(BF16)
    hidden = dot(normed_low, w_up[...]) + small_vector(small, BIAS_UP, 8)
    square = hidden * hidden
    slope = 0.7978845608028654
    bent = jnp.tanh(hidden * (slope + (slope * 0.044715) * square))
    half = 0.5 + 0.5 * bent
    activated = (hidden * half).astype(BF16)
    derivative = half + hidden * (0.5 - 0.5 * bent * bent) * (
        slope + (3 * slope * 0.044715) * square
    )
    result = middle + dot(activated, w_down[...]) + small_vector(small, BIAS_DOWN, 2)
    result_out[...] = result.astype(BF16)
    cotangent = cot[...]
    grad_result = cotangent.astype(F32)
    acc_down[...] += dot_tn(activated, cotangent)
    grad_hidden = (dot_nt(cotangent, w_down[...]) * derivative).astype(BF16)
    acc_up[...] += dot_tn(normed_low, grad_hidden)
    grad_normed = dot_nt(grad_hidden, w_up[...])
    grad_middle = grad_result + normalize_back(grad_normed, gain, normed, rate)
    grad_middle_out[...] = grad_middle
    grad_middle_low = grad_middle.astype(BF16)
    acc_out[...] += dot_tn(attended[...], grad_middle_low)
    grad_attended_out[...] = dot_nt(grad_middle_low, w_out[...]).astype(BF16)
    acc_small[:, 0:D] += fold_rows(grad_middle_low.astype(F32))
    acc_small[:, D : 2 * D] += fold_rows(grad_normed * normed)
    acc_small[:, 2 * D : 3 * D] += fold_rows(grad_normed)
    acc_small[:, 3 * D : 3 * D + FF] += fold_rows(grad_hidden.astype(F32))
    acc_small[:, 3 * D + FF :] += fold_rows(grad_result)

    @pl.when(step == pl.num_programs(0) - 1)
    def _():
        matrix_to_flat(acc_out, D, D, flat, 0)
        matrix_to_flat(acc_up, D, FF, flat, ROW_UP - ROW_OUT)
        matrix_to_flat(acc_down, FF, D, flat, ROW_DOWN - ROW_OUT)
        sums = jnp.sum(acc_small[...], axis=0, keepdims=True)
        base = ROW_SMALL - ROW_OUT
        flat[base : base + LATE_SMALL, :] = jnp.zeros((LATE_SMALL, LANES), F32)
        for i in range(sums.shape[1] // LANES):
            row = base + LATE_SMALL + i
            flat[row : row + 1, :] = sums[:, i * LANES : (i + 1) * LANES]
        flat[ROW_END - ROW_OUT :, :] = jnp.zeros((ROW_TOTAL - ROW_END, LANES), F32)
        first_out[...] = flat[:HEAD_ROWS, :]
        for target, out in enumerate((keep_out, send_out)):
            for p in range(PLANE):
                for z in range(Z - 1):
                    share = ids[target * PLANE + p] + (z + 1) * 2 * PLANE
                    rows = flat[pl.ds(share * SHARE - ROW_OUT, SHARE), :]
                    out[p, z] = rows.astype(out.dtype)


def attend_back_kernel(project, weights, grad_attended, grad_project):
    for s in range(BLOCK // SEQ):
        rows = slice(s * SEQ, (s + 1) * SEQ)
        query = spread_heads(project[rows, :D])
        key = spread_heads(project[rows, D : 2 * D])
        value = spread_heads(project[rows, 2 * D :])
        grad_rows = grad_attended[rows, :]
        grad_weights = dot_nt(grad_rows, value)
        scores_low, scores_turned, weights_turned = [], [], []
        for h in range(HEADS):
            columns = slice(h * SEQ, (h + 1) * SEQ)
            mine = weights[rows, columns]
            product = mine * grad_weights[:, columns]
            grad_scores = product - mine * jnp.sum(product, axis=-1, keepdims=True)
            scores_low.append(grad_scores.astype(BF16))
            scores_turned.append(grad_scores.T.astype(BF16))
            weights_turned.append(mine.T.astype(BF16))
        grad_query = dot(jnp.concatenate(scores_low, axis=1), key) * SCALE
        grad_key = dot(jnp.concatenate(scores_turned, axis=1), query) * SCALE
        grad_value = dot(jnp.concatenate(weights_turned, axis=1), spread_heads(grad_rows))
        grad_project[rows, :D] = grad_query.astype(BF16)
        grad_project[rows, D : 2 * D] = grad_key.astype(BF16)
        grad_project[rows, 2 * D :] = grad_value.astype(BF16)

def project_back_kernel(
    ids, tok, grad_project, grad_middle, w_qkv, small, first_in,
    input_grad_out, keep_out, send_out, acc_qkv, acc_small, flat,
):
    step = pl.program_id(0)

    @pl.when(step == 0)
    def _():
        acc_qkv[...] = jnp.zeros_like(acc_qkv)
        acc_small[...] = jnp.zeros_like(acc_small)

    gain = small_vector(small, GAIN_ONE, 2)
    normed, rate = normalize(tok[...].astype(F32))
    normed_low = (normed * gain + small_vector(small, SHIFT_ONE, 2)).astype(BF16)
    acc_qkv[...] += dot_tn(normed_low, grad_project[...])
    grad_normed = dot_nt(grad_project[...], w_qkv[...])
    input_grad_out[...] = grad_middle[...] + normalize_back(grad_normed, gain, normed, rate)
    acc_small[:, 0:D] += fold_rows(grad_normed * normed)
    acc_small[:, D : 2 * D] += fold_rows(grad_normed)
    acc_small[:, 2 * D : 3 * D] += fold_rows(grad_project[:, :D].astype(F32))
    acc_small[:, 3 * D :] += fold_rows(grad_project[:, 2 * D :].astype(F32))

    @pl.when(step == pl.num_programs(0) - 1)
    def _():
        matrix_to_flat(acc_qkv, D, 3 * D, flat, ROW_QKV)
        flat[ROW_OUT:, :] = first_in[...]
        sums = jnp.sum(acc_small[...], axis=0, keepdims=True)
        side = jnp.concatenate(
            [sums[:, i * LANES : (i + 1) * LANES] for i in range(LATE_SMALL)]
            + [jnp.zeros((16 - LATE_SMALL, LANES), F32)],
            axis=0,
        )
        for target, out in enumerate((keep_out, send_out)):
            for p in range(PLANE):
                share = ids[target * PLANE + p]
                rows = flat[pl.ds(share * SHARE, SHARE), :]
                padded = jnp.concatenate([rows, jnp.zeros((SIDE - SHARE, LANES), F32)], axis=0)
                mine = jnp.where(share == 2 * PLANE - 1, side, 0.0)
                out[p] = jnp.concatenate([padded, mine], axis=0).astype(out.dtype)


def add_core_kernel(kept, received, keep_out, *sends):
    keep_out[...] = kept[0] + received[0].astype(F32)
    for p, out in enumerate(sends):
        out[...] = (kept[p + 1] + received[p + 1].astype(F32)).astype(BF16)


def add_plane_kernel(ids, first_kept, rest_kept, *refs):
    firsts, rests = refs[: PLANE - 1], refs[PLANE - 1 : 2 * (PLANE - 1)]
    keep_out, *sends, first, column = refs[2 * (PLANE - 1) :]
    first[...] = first_kept[...] + sum(item[...].astype(F32) for item in firsts)
    column[0] = first[:SHARE, :]
    column[1:] = rest_kept[...] + sum(item[...].astype(F32) for item in rests)
    end = SMALL_IN_SHARE + LATE_SMALL
    column[Z - 1, SMALL_IN_SHARE:end, :] += first[SIDE : SIDE + LATE_SMALL, :]
    keep_out[...] = column[ids[0]]
    for d, out in enumerate(sends):
        out[...] = column[lax.rem(ids[0] + d + 1, Z)].astype(BF16)


def rows_spec(columns):
    return pl.BlockSpec((BLOCK, columns), lambda i: (i, 0))


def whole_spec(item):
    return pl.BlockSpec(item.shape, lambda i: (0,) * len(item.shape))


def like(*shape, kind=F32):
    return jax.ShapeDtypeStruct(shape, kind)


SMEM_SPEC = pl.BlockSpec(memory_space=pltpu.SMEM)
PARAMS = pltpu.CompilerParams(
    dimension_semantics=("arbitrary",), vmem_limit_bytes=VMEM_BYTES
)


def cost(us):
    return pl.CostEstimate(flops=int(us * 1e9), bytes_accessed=1 << 20, transcendentals=0)


def small_call(kernel, name, ids, inputs, outs, scratch=()):
    with_ids = ids is not None
    return pl.pallas_call(
        kernel,
        in_specs=[SMEM_SPEC] * with_ids + [pl.BlockSpec(memory_space=pltpu.VMEM)] * len(inputs),
        out_specs=[pl.BlockSpec(memory_space=pltpu.VMEM)] * len(outs),
        out_shape=list(outs),
        scratch_shapes=list(scratch),
        compiler_params=pltpu.CompilerParams(vmem_limit_bytes=VMEM_BYTES),
        cost_estimate=cost(1),
        name=name,
    )(*([ids] if with_ids else []), *inputs)


def attend(ids, segments, tokens, bufs):
    rows = tokens.shape[0]
    blocked = [like(rows, 3 * D, kind=BF16), like(rows, HEADS * SEQ), like(rows, D, kind=BF16)]
    fixed = [like(D, 3 * D, kind=BF16), like(SMALL_ROWS, LANES), like(HEAD_ROWS, LANES)]
    return pl.pallas_call(
        attend_kernel,
        grid=(rows // BLOCK,),
        in_specs=[
            SMEM_SPEC,
            pl.BlockSpec((BLOCK // SEQ, 1, SEQ), lambda i: (i, 0, 0)),
            rows_spec(D),
        ]
        + [whole_spec(buf) for buf in bufs],
        out_specs=[rows_spec(item.shape[1]) for item in blocked] + [whole_spec(item) for item in fixed],
        out_shape=blocked + fixed,
        scratch_shapes=[pltpu.VMEM((FIRST_ROWS, LANES), F32)],
        compiler_params=PARAMS,
        cost_estimate=cost(7),
        name="attend",
    )(ids, segments, tokens, *bufs)


def feed(ids, tokens, attended, cotangent, small, first, bufs, send_kind):
    rows = tokens.shape[0]
    small_rows = ROW_END - ROW_SMALL - LATE_SMALL
    blocked = [like(rows, D, kind=BF16), like(rows, D), like(rows, D, kind=BF16)]
    fixed = [
        like(PLANE, Z - 1, SHARE, LANES),
        like(PLANE, Z - 1, SHARE, LANES, kind=send_kind),
        like(HEAD_ROWS, LANES),
    ]
    return pl.pallas_call(
        feed_kernel,
        grid=(rows // BLOCK,),
        in_specs=[SMEM_SPEC] + [rows_spec(D)] * 3 + [whole_spec(item) for item in (small, first, *bufs)],
        out_specs=[rows_spec(D)] * 3 + [whole_spec(item) for item in fixed],
        out_shape=blocked + fixed,
        scratch_shapes=[
            pltpu.VMEM((D, D), BF16),
            pltpu.VMEM((D, FF), BF16),
            pltpu.VMEM((FF, D), BF16),
            pltpu.VMEM((D, D), F32),
            pltpu.VMEM((D, FF), F32),
            pltpu.VMEM((FF, D), F32),
            pltpu.VMEM((8, small_rows * LANES), F32),
            pltpu.VMEM((ROW_TOTAL - ROW_OUT, LANES), F32),
        ],
        compiler_params=PARAMS,
        cost_estimate=cost(10),
        name="feed",
    )(ids, tokens, attended, cotangent, small, first, *bufs)


def attend_back(project, weights, grad_attended):
    return pl.pallas_call(
        attend_back_kernel,
        grid=(project.shape[0] // BLOCK,),
        in_specs=[rows_spec(item.shape[1]) for item in (project, weights, grad_attended)],
        out_specs=rows_spec(3 * D),
        out_shape=like(*project.shape, kind=BF16),
        compiler_params=PARAMS,
        cost_estimate=cost(6),
        name="attend_back",
    )(project, weights, grad_attended)


def project_back(ids, tokens, grad_project, grad_middle, w_qkv, small, first, send_kind):
    rows = tokens.shape[0]
    fixed = [
        like(PLANE, SIDE + 16, LANES),
        like(PLANE, SIDE + 16, LANES, kind=send_kind),
    ]
    return pl.pallas_call(
        project_back_kernel,
        grid=(rows // BLOCK,),
        in_specs=[SMEM_SPEC]
        + [rows_spec(item.shape[1]) for item in (tokens, grad_project, grad_middle)]
        + [whole_spec(item) for item in (w_qkv, small, first)],
        out_specs=[rows_spec(D)] + [whole_spec(item) for item in fixed],
        out_shape=[like(rows, D)] + fixed,
        scratch_shapes=[
            pltpu.VMEM((D, 3 * D), F32),
            pltpu.VMEM((8, LATE_SMALL * LANES), F32),
            pltpu.VMEM((FIRST_ROWS, LANES), F32),
        ],
        compiler_params=PARAMS,
        cost_estimate=cost(6),
        name="project_back",
    )(ids, tokens, grad_project, grad_middle, w_qkv, small, first)


def local_any(n, tokens, params, segment_ids, cotangent):
    total = n * params.shape[0]
    gathered = lax.all_gather(params, "fsdp", axis=0).reshape(total, LANES)
    shares = gathered[:ROW_TOTAL].reshape(Z, 2 * PLANE, SHARE, LANES)
    order = [p * 2 + c for c in range(2) for p in range(PLANE)]
    side = jnp.concatenate(
        [jnp.zeros((SIDE - SHARE, LANES), BF16), gathered[ROW_SMALL:ROW_TOTAL]], axis=0
    )
    firsts = [jnp.concatenate([shares[0, k], side], axis=0) for k in order]
    rests = [shares[1:, k] for k in order]
    ids = jnp.array(order, jnp.int32)
    segments = segment_ids.reshape(-1, 1, SEQ)
    project, weights, attended, w_qkv, small, first = attend(ids, segments, tokens, firsts)
    outputs, grad_middle, grad_attended, rest_keep, rest_send, first_grad = feed(
        ids, tokens, attended, cotangent, small, first, rests, F32
    )
    grad_project = attend_back(project, weights, grad_attended)
    input_grad, keep, send = project_back(
        ids, tokens, grad_project, grad_middle, w_qkv, small, first_grad, F32
    )
    first = jnp.stack([keep, send], axis=1)
    rest = jnp.stack([rest_keep, rest_send], axis=1).transpose(2, 0, 1, 3, 4)
    flat = jnp.concatenate(
        [
            first[:, :, :SHARE].reshape(-1, LANES),
            rest.reshape(-1, LANES),
            jnp.zeros((total - ROW_TOTAL, LANES), F32),
        ],
        axis=0,
    )
    flat = flat.at[ROW_SMALL : ROW_SMALL + LATE_SMALL].add(
        first[PLANE - 1, 1, SIDE : SIDE + LATE_SMALL]
    )
    param_grad = lax.psum_scatter(flat, "fsdp", scatter_dimension=0, tiled=True)
    return outputs, input_grad, param_grad


def index_of(z, plane, core):
    return (z * PLANE + plane) * 2 + core


def move(values, step_z, step_plane, step_core):
    pairs = [
        (index_of(z, p, c), index_of((z + step_z) % Z, p ^ step_plane, c ^ step_core))
        for z in range(Z)
        for p in range(PLANE)
        for c in range(2)
    ]
    return lax.ppermute(values, "fsdp", pairs)


def spread(values):
    same = [values] + [move(values, 0, d, 0) for d in range(1, PLANE)]
    return same + [move(item, 0, 0, 1) for item in same]


def add_core(keep, send):
    item = keep.shape[1:]
    return small_call(
        add_core_kernel, "add_core", None, [keep, move(send, 0, 0, 1)],
        [like(*item)] + [like(*item, kind=BF16)] * (PLANE - 1),
    )


def add_plane(where, first, rest):
    arrived = [move(item, 0, d + 1, 0) for items in (first, rest) for d, item in enumerate(items[1:])]
    return small_call(
        add_plane_kernel, "add_plane", where, [first[0], rest[0]] + arrived,
        [like(SHARE, LANES)] + [like(SHARE, LANES, kind=BF16)] * (Z - 1),
        [pltpu.VMEM((SIDE + 16, LANES), F32), pltpu.VMEM((Z, SHARE, LANES), F32)],
    )


def local_slice(tokens, params, segment_ids, cotangent):
    me = lax.axis_index("fsdp").astype(jnp.int32)
    z, plane, core = me // (2 * PLANE), (me // 2) % PLANE, me % 2
    where = z.reshape(1)
    ids = jnp.stack([(plane ^ dp) * 2 + (core ^ dc) for dc in range(2) for dp in range(PLANE)])
    segments = segment_ids.reshape(-1, 1, SEQ)

    column = [params] + [move(params, d, 0, 0) for d in range(1, Z)]
    first, rest = small_call(
        sort_kernel, "sort_shares", where, column,
        [like(SIDE + SMALL_ROWS, LANES, kind=BF16), like(Z - 1, SHARE, LANES, kind=BF16)],
        [pltpu.VMEM((Z, SHARE, LANES), BF16), pltpu.VMEM((SIDE + SMALL_ROWS, LANES), F32)],
    )
    project, weights, attended, w_qkv, small, first = attend(ids, segments, tokens, spread(first))
    outputs, grad_middle, grad_attended, rest_keep, rest_send, first_grad = feed(
        ids, tokens, attended, cotangent, small, first, spread(rest), BF16
    )

    rest_sums = add_core(rest_keep, rest_send)
    grad_project = attend_back(project, weights, grad_attended)
    input_grad, keep, send = project_back(
        ids, tokens, grad_project, grad_middle, w_qkv, small, first_grad, BF16
    )
    first_sums = add_core(keep, send)
    param_grad, *sends = add_plane(where, first_sums, rest_sums)
    for d, item in enumerate(sends):
        param_grad = param_grad + move(item, d + 1, 0, 0).astype(F32)
    return outputs, input_grad, param_grad


def solution(mesh):
    n = mesh.shape["fsdp"]
    local = local_slice if n == 2 * PLANE * Z else functools.partial(local_any, n)
    in_specs = (P("fsdp", None), P("fsdp", None), P("fsdp"), P("fsdp", None))
    out_specs = (P("fsdp", None), P("fsdp", None), P("fsdp", None))
    return jax.shard_map(local, mesh=mesh, in_specs=in_specs, out_specs=out_specs, check_vma=False)
```

```python
import functools

import jax
import jax.numpy as jnp
from jax import lax
from jax.experimental import pallas as pl
from jax.experimental.pallas import tpu as pltpu
from jax.sharding import PartitionSpec as P

D = 256
HEADS = 4
HEAD_DIM = 64
FF = 1024
SEQ = 128
LANES = 128
BLOCK = 2 * SEQ
EPSILON = 1e-05
SCALE = HEAD_DIM ** (-0.5)
VMEM_BYTES = 48 * 1024 * 1024

ROW_QKV = 0
ROW_OUT = 1536
ROW_UP = 2048
ROW_DOWN = 4096
ROW_SMALL = 6144
ROW_END = 6168
ROW_TOTAL = 6176
GAIN_ONE, SHIFT_ONE, BIAS_QUERY, BIAS_VALUE, BIAS_OUT = 0, 2, 4, 6, 8
GAIN_TWO, SHIFT_TWO, BIAS_UP, BIAS_DOWN = 10, 12, 14, 22
SMALL_ROWS = 32
LATE_SMALL = 8

SHARE = 193
Z, PLANE = 4, 4
FIRST_ROWS = 2 * PLANE * SHARE
HEAD_ROWS = FIRST_ROWS - ROW_OUT
SMALL_IN_SHARE = ROW_SMALL - (2 * PLANE * Z - 1) * SHARE
SIDE = 208

F32 = jnp.float32
BF16 = jnp.bfloat16


def dot(left, right):
    return jnp.dot(left, right, preferred_element_type=F32)


def dot_nt(left, right):
    return lax.dot_general(left, right, (((1,), (1,)), ((), ())), preferred_element_type=F32)


def dot_tn(left, right):
    return lax.dot_general(left, right, (((0,), (0,)), ((), ())), preferred_element_type=F32)


def small_vector(small, row, count):
    return jnp.concatenate([small[row + i : row + i + 1, :] for i in range(count)], axis=1)


def fold_rows(values):
    rows, columns = values.shape
    return jnp.sum(values.reshape(rows // 8, 8, columns), axis=0)


def normalize(values):
    center = values - jnp.mean(values, axis=-1, keepdims=True)
    rate = lax.rsqrt(jnp.mean(center * center, axis=-1, keepdims=True) + EPSILON)
    return center * rate, rate


def normalize_back(grad, gain, normed, rate):
    scaled = grad * gain
    return rate * (
        scaled
        - jnp.mean(scaled, axis=-1, keepdims=True)
        - normed * jnp.mean(scaled * normed, axis=-1, keepdims=True)
    )


def head_masks():
    lane = lax.broadcasted_iota(jnp.int32, (1, D), 1)
    return [(lane // HEAD_DIM == h).astype(F32).astype(BF16) for h in range(HEADS)]


def spread_heads(rows):
    return jnp.concatenate([rows * mask for mask in head_masks()], axis=0)


def matrix_from_flat(flat, start, rows, columns, out):
    per_row = columns // LANES
    for j in range(per_row):
        out[:, j * LANES : (j + 1) * LANES] = flat[
            pl.ds(start + j, rows, stride=per_row), :
        ].astype(BF16)


def matrix_to_flat(matrix, rows, columns, flat, start):
    per_row = columns // LANES
    for j in range(per_row):
        flat[pl.ds(start + j, rows, stride=per_row), :] = matrix[:, j * LANES : (j + 1) * LANES]


def place_shares(bufs, ids, flat, base):
    for slot, buf in enumerate(bufs):
        for z in range(Z - 1):
            share = ids[slot] + (z + 1) * 2 * PLANE
            flat[pl.ds(share * SHARE - base, SHARE), :] = buf[z].astype(F32)


def sort_kernel(column, first, rest, wide):
    wide[:SHARE, :] = column[0].astype(F32)
    wide[SHARE:SIDE, :] = jnp.zeros((SIDE - SHARE, LANES), F32)
    last = column[Z - 1].astype(F32)
    wide[SIDE:, :] = last[SMALL_IN_SHARE:, :]
    for p in range(PLANE):
        first[p] = wide[...].astype(BF16)
        rest[p * (Z - 1) : (p + 1) * (Z - 1)] = column[1:]


def attend_kernel(
    ids, seg, tok, *refs,
):
    bufs = [ref.at[p] for ref in refs[:2] for p in range(PLANE)]
    project_out, weights_out, attended_out, w_qkv, small, first_out, flat = refs[2:]

    @pl.when(pl.program_id(0) == 0)
    def _():
        for slot, buf in enumerate(bufs):
            wide = buf[...].astype(F32)
            flat[pl.ds(ids[slot] * SHARE, SHARE), :] = wide[:SHARE, :]

            @pl.when(ids[slot] == 2 * PLANE - 1)
            def _():
                small[...] = wide[SIDE:, :]

        matrix_from_flat(flat, ROW_QKV, D, 3 * D, w_qkv)
        first_out[...] = flat[ROW_OUT:FIRST_ROWS, :]

    normed, _ = normalize(tok[...].astype(F32))
    normed_low = (
        normed * small_vector(small, GAIN_ONE, 2) + small_vector(small, SHIFT_ONE, 2)
    ).astype(BF16)
    bias = jnp.concatenate(
        [
            small_vector(small, BIAS_QUERY, 2),
            jnp.zeros((1, D), F32),
            small_vector(small, BIAS_VALUE, 2),
        ],
        axis=1,
    )
    project = (dot(normed_low, w_qkv[...]) + bias).astype(BF16)
    project_out[...] = project
    causal = lax.broadcasted_iota(jnp.int32, (SEQ, SEQ), 1) <= lax.broadcasted_iota(
        jnp.int32, (SEQ, SEQ), 0
    )
    for s in range(BLOCK // SEQ):
        rows = slice(s * SEQ, (s + 1) * SEQ)
        across = jnp.broadcast_to(seg[s].astype(F32), (SEQ, SEQ))
        allowed = causal & (across == across.T)
        query = project[rows, :D]
        key = spread_heads(project[rows, D : 2 * D])
        value = spread_heads(project[rows, 2 * D :])
        scores = dot_nt(query, key) * SCALE
        low = []
        for h in range(HEADS):
            columns = slice(h * SEQ, (h + 1) * SEQ)
            mine = jnp.where(allowed, scores[:, columns], -1e30)
            grown = jnp.exp(mine - jnp.max(mine, axis=-1, keepdims=True))
            weights = grown * (1.0 / jnp.sum(grown, axis=-1, keepdims=True))
            weights_out[rows, columns] = weights
            low.append(weights.astype(BF16))
        attended_out[rows, :] = dot(jnp.concatenate(low, axis=1), value).astype(BF16)


def feed_kernel(
    ids, tok, attended, cot, small, first_in, *refs,
):
    bufs = [ref.at[pl.ds(p * (Z - 1), Z - 1)] for ref in refs[:2] for p in range(PLANE)]
    (
        result_out, grad_middle_out, grad_attended_out, keep_out, send_out, first_out,
        w_out, w_up, w_down, acc_out, acc_up, acc_down, acc_small, flat,
    ) = refs[2:]
    step = pl.program_id(0)

    @pl.when(step == 0)
    def _():
        flat[:HEAD_ROWS, :] = first_in[...]
        place_shares(bufs, ids, flat, ROW_OUT)
        matrix_from_flat(flat, 0, D, D, w_out)
        matrix_from_flat(flat, ROW_UP - ROW_OUT, D, FF, w_up)
        matrix_from_flat(flat, ROW_DOWN - ROW_OUT, FF, D, w_down)
        acc_out[...] = jnp.zeros_like(acc_out)
        acc_up[...] = jnp.zeros_like(acc_up)
        acc_down[...] = jnp.zeros_like(acc_down)
        acc_small[...] = jnp.zeros_like(acc_small)

    gain = small_vector(small, GAIN_TWO, 2)
    middle = tok[...].astype(F32) + dot(attended[...], w_out[...]) + small_vector(small, BIAS_OUT, 2)
    normed, rate = normalize(middle)
    normed_low = (normed * gain + small_vector(small, SHIFT_TWO, 2)).astype(BF16)
    hidden = dot(normed_low, w_up[...]) + small_vector(small, BIAS_UP, 8)
    square = hidden * hidden
    slope = 0.7978845608028654
    bent = jnp.tanh(hidden * (slope + (slope * 0.044715) * square))
    half = 0.5 + 0.5 * bent
    activated = (hidden * half).astype(BF16)
    derivative = half + hidden * (0.5 - 0.5 * bent * bent) * (
        slope + (3 * slope * 0.044715) * square
    )
    result = middle + dot(activated, w_down[...]) + small_vector(small, BIAS_DOWN, 2)
    result_out[...] = result.astype(BF16)
    cotangent = cot[...]
    grad_result = cotangent.astype(F32)
    acc_down[...] += dot_tn(activated, cotangent)
    grad_hidden = (dot_nt(cotangent, w_down[...]) * derivative).astype(BF16)
    acc_up[...] += dot_tn(normed_low, grad_hidden)
    grad_normed = dot_nt(grad_hidden, w_up[...])
    grad_middle = grad_result + normalize_back(grad_normed, gain, normed, rate)
    grad_middle_out[...] = grad_middle
    grad_middle_low = grad_middle.astype(BF16)
    acc_out[...] += dot_tn(attended[...], grad_middle_low)
    grad_attended_out[...] = dot_nt(grad_middle_low, w_out[...]).astype(BF16)
    acc_small[:, 0:D] += fold_rows(grad_middle_low.astype(F32))
    acc_small[:, D : 2 * D] += fold_rows(grad_normed * normed)
    acc_small[:, 2 * D : 3 * D] += fold_rows(grad_normed)
    acc_small[:, 3 * D : 3 * D + FF] += fold_rows(grad_hidden.astype(F32))
    acc_small[:, 3 * D + FF :] += fold_rows(grad_result)

    @pl.when(step == pl.num_programs(0) - 1)
    def _():
        matrix_to_flat(acc_out, D, D, flat, 0)
        matrix_to_flat(acc_up, D, FF, flat, ROW_UP - ROW_OUT)
        matrix_to_flat(acc_down, FF, D, flat, ROW_DOWN - ROW_OUT)
        sums = jnp.sum(acc_small[...], axis=0, keepdims=True)
        base = ROW_SMALL - ROW_OUT
        flat[base : base + LATE_SMALL, :] = jnp.zeros((LATE_SMALL, LANES), F32)
        for i in range(sums.shape[1] // LANES):
            row = base + LATE_SMALL + i
            flat[row : row + 1, :] = sums[:, i * LANES : (i + 1) * LANES]
        flat[ROW_END - ROW_OUT :, :] = jnp.zeros((ROW_TOTAL - ROW_END, LANES), F32)
        first_out[...] = flat[:HEAD_ROWS, :]
        for target, out in enumerate((keep_out, send_out)):
            for p in range(PLANE):
                for z in range(Z - 1):
                    share = ids[target * PLANE + p] + (z + 1) * 2 * PLANE
                    rows = flat[pl.ds(share * SHARE - ROW_OUT, SHARE), :]
                    out[p * (Z - 1) + z] = rows.astype(out.dtype)


def attend_back_kernel(project, weights, grad_attended, grad_project):
    for s in range(BLOCK // SEQ):
        rows = slice(s * SEQ, (s + 1) * SEQ)
        query = spread_heads(project[rows, :D])
        key = spread_heads(project[rows, D : 2 * D])
        value = spread_heads(project[rows, 2 * D :])
        grad_rows = grad_attended[rows, :]
        grad_weights = dot_nt(grad_rows, value)
        scores_low, scores_turned, weights_turned = [], [], []
        for h in range(HEADS):
            columns = slice(h * SEQ, (h + 1) * SEQ)
            mine = weights[rows, columns]
            product = mine * grad_weights[:, columns]
            grad_scores = product - mine * jnp.sum(product, axis=-1, keepdims=True)
            scores_low.append(grad_scores.astype(BF16))
            scores_turned.append(grad_scores.T.astype(BF16))
            weights_turned.append(mine.T.astype(BF16))
        grad_query = dot(jnp.concatenate(scores_low, axis=1), key) * SCALE
        grad_key = dot(jnp.concatenate(scores_turned, axis=1), query) * SCALE
        grad_value = dot(jnp.concatenate(weights_turned, axis=1), spread_heads(grad_rows))
        grad_project[rows, :D] = grad_query.astype(BF16)
        grad_project[rows, D : 2 * D] = grad_key.astype(BF16)
        grad_project[rows, 2 * D :] = grad_value.astype(BF16)

def project_back_kernel(
    ids, tok, grad_project, grad_middle, w_qkv, small, first_in,
    input_grad_out, keep_out, send_out, acc_qkv, acc_small, flat,
):
    step = pl.program_id(0)

    @pl.when(step == 0)
    def _():
        acc_qkv[...] = jnp.zeros_like(acc_qkv)
        acc_small[...] = jnp.zeros_like(acc_small)

    gain = small_vector(small, GAIN_ONE, 2)
    normed, rate = normalize(tok[...].astype(F32))
    normed_low = (normed * gain + small_vector(small, SHIFT_ONE, 2)).astype(BF16)
    acc_qkv[...] += dot_tn(normed_low, grad_project[...])
    grad_normed = dot_nt(grad_project[...], w_qkv[...])
    input_grad_out[...] = grad_middle[...] + normalize_back(grad_normed, gain, normed, rate)
    acc_small[:, 0:D] += fold_rows(grad_normed * normed)
    acc_small[:, D : 2 * D] += fold_rows(grad_normed)
    acc_small[:, 2 * D : 3 * D] += fold_rows(grad_project[:, :D].astype(F32))
    acc_small[:, 3 * D :] += fold_rows(grad_project[:, 2 * D :].astype(F32))

    @pl.when(step == pl.num_programs(0) - 1)
    def _():
        matrix_to_flat(acc_qkv, D, 3 * D, flat, ROW_QKV)
        flat[ROW_OUT:, :] = first_in[...]
        sums = jnp.sum(acc_small[...], axis=0, keepdims=True)
        side = jnp.concatenate(
            [sums[:, i * LANES : (i + 1) * LANES] for i in range(LATE_SMALL)]
            + [jnp.zeros((16 - LATE_SMALL, LANES), F32)],
            axis=0,
        )
        for target, out in enumerate((keep_out, send_out)):
            for p in range(PLANE):
                share = ids[target * PLANE + p]
                rows = flat[pl.ds(share * SHARE, SHARE), :]
                padded = jnp.concatenate([rows, jnp.zeros((SIDE - SHARE, LANES), F32)], axis=0)
                mine = jnp.where(share == 2 * PLANE - 1, side, 0.0)
                out[p] = jnp.concatenate([padded, mine], axis=0).astype(out.dtype)


def add_core_kernel(kept, received, out):
    out[...] = (kept[...] + received[...].astype(F32)).astype(BF16)


def add_plane_kernel(first_in, rest_in, out, first, column):
    first[...] = sum(first_in[p].astype(F32) for p in range(PLANE))
    column[0] = first[:SHARE, :]
    column[1:] = sum(
        rest_in[p * (Z - 1) : (p + 1) * (Z - 1)].astype(F32) for p in range(PLANE)
    )
    end = SMALL_IN_SHARE + LATE_SMALL
    column[Z - 1, SMALL_IN_SHARE:end, :] += first[SIDE : SIDE + LATE_SMALL, :]
    out[...] = column[...].astype(BF16)


def add_column_kernel(received, out):
    out[...] = sum(received[z].astype(F32) for z in range(Z))


def rows_spec(columns):
    return pl.BlockSpec((BLOCK, columns), lambda i: (i, 0))


def whole_spec(item):
    return pl.BlockSpec(item.shape, lambda i: (0,) * len(item.shape))


def like(*shape, kind=F32):
    return jax.ShapeDtypeStruct(shape, kind)


SMEM_SPEC = pl.BlockSpec(memory_space=pltpu.SMEM)
PARAMS = pltpu.CompilerParams(
    dimension_semantics=("arbitrary",), vmem_limit_bytes=VMEM_BYTES
)


def cost(us):
    return pl.CostEstimate(flops=int(us * 1e9), bytes_accessed=1 << 20, transcendentals=0)


def small_call(kernel, name, ids, inputs, outs, scratch=()):
    with_ids = ids is not None
    results = pl.pallas_call(
        kernel,
        in_specs=[SMEM_SPEC] * with_ids + [pl.BlockSpec(memory_space=pltpu.VMEM)] * len(inputs),
        out_specs=[pl.BlockSpec(memory_space=pltpu.VMEM)] * len(outs),
        out_shape=list(outs),
        scratch_shapes=list(scratch),
        compiler_params=pltpu.CompilerParams(vmem_limit_bytes=VMEM_BYTES),
        cost_estimate=cost(1),
        name=name,
    )(*([ids] if with_ids else []), *inputs)
    return results if len(outs) > 1 else results[0]


def attend(ids, segments, tokens, bufs):
    rows = tokens.shape[0]
    blocked = [like(rows, 3 * D, kind=BF16), like(rows, HEADS * SEQ), like(rows, D, kind=BF16)]
    fixed = [like(D, 3 * D, kind=BF16), like(SMALL_ROWS, LANES), like(HEAD_ROWS, LANES)]
    return pl.pallas_call(
        attend_kernel,
        grid=(rows // BLOCK,),
        in_specs=[
            SMEM_SPEC,
            pl.BlockSpec((BLOCK // SEQ, 1, SEQ), lambda i: (i, 0, 0)),
            rows_spec(D),
        ]
        + [whole_spec(buf) for buf in bufs],
        out_specs=[rows_spec(item.shape[1]) for item in blocked] + [whole_spec(item) for item in fixed],
        out_shape=blocked + fixed,
        scratch_shapes=[pltpu.VMEM((FIRST_ROWS, LANES), F32)],
        compiler_params=PARAMS,
        cost_estimate=cost(7),
        name="attend",
    )(ids, segments, tokens, *bufs)


def feed(ids, tokens, attended, cotangent, small, first, bufs, send_kind):
    rows = tokens.shape[0]
    small_rows = ROW_END - ROW_SMALL - LATE_SMALL
    blocked = [like(rows, D, kind=BF16), like(rows, D), like(rows, D, kind=BF16)]
    fixed = [
        like(PLANE * (Z - 1), SHARE, LANES),
        like(PLANE * (Z - 1), SHARE, LANES, kind=send_kind),
        like(HEAD_ROWS, LANES),
    ]
    return pl.pallas_call(
        feed_kernel,
        grid=(rows // BLOCK,),
        in_specs=[SMEM_SPEC] + [rows_spec(D)] * 3 + [whole_spec(item) for item in (small, first, *bufs)],
        out_specs=[rows_spec(D)] * 3 + [whole_spec(item) for item in fixed],
        out_shape=blocked + fixed,
        scratch_shapes=[
            pltpu.VMEM((D, D), BF16),
            pltpu.VMEM((D, FF), BF16),
            pltpu.VMEM((FF, D), BF16),
            pltpu.VMEM((D, D), F32),
            pltpu.VMEM((D, FF), F32),
            pltpu.VMEM((FF, D), F32),
            pltpu.VMEM((8, small_rows * LANES), F32),
            pltpu.VMEM((ROW_TOTAL - ROW_OUT, LANES), F32),
        ],
        compiler_params=PARAMS,
        cost_estimate=cost(10),
        name="feed",
    )(ids, tokens, attended, cotangent, small, first, *bufs)


def attend_back(project, weights, grad_attended):
    return pl.pallas_call(
        attend_back_kernel,
        grid=(project.shape[0] // BLOCK,),
        in_specs=[rows_spec(item.shape[1]) for item in (project, weights, grad_attended)],
        out_specs=rows_spec(3 * D),
        out_shape=like(*project.shape, kind=BF16),
        compiler_params=PARAMS,
        cost_estimate=cost(6),
        name="attend_back",
    )(project, weights, grad_attended)


def project_back(ids, tokens, grad_project, grad_middle, w_qkv, small, first, send_kind):
    rows = tokens.shape[0]
    fixed = [
        like(PLANE, SIDE + 16, LANES),
        like(PLANE, SIDE + 16, LANES, kind=send_kind),
    ]
    return pl.pallas_call(
        project_back_kernel,
        grid=(rows // BLOCK,),
        in_specs=[SMEM_SPEC]
        + [rows_spec(item.shape[1]) for item in (tokens, grad_project, grad_middle)]
        + [whole_spec(item) for item in (w_qkv, small, first)],
        out_specs=[rows_spec(D)] + [whole_spec(item) for item in fixed],
        out_shape=[like(rows, D)] + fixed,
        scratch_shapes=[
            pltpu.VMEM((D, 3 * D), F32),
            pltpu.VMEM((8, LATE_SMALL * LANES), F32),
            pltpu.VMEM((FIRST_ROWS, LANES), F32),
        ],
        compiler_params=PARAMS,
        cost_estimate=cost(6),
        name="project_back",
    )(ids, tokens, grad_project, grad_middle, w_qkv, small, first)


def local_any(n, tokens, params, segment_ids, cotangent):
    total = n * params.shape[0]
    gathered = lax.all_gather(params, "fsdp", axis=0).reshape(total, LANES)
    shares = gathered[:ROW_TOTAL].reshape(Z, 2 * PLANE, SHARE, LANES)
    order = [p * 2 + c for c in range(2) for p in range(PLANE)]
    side = jnp.concatenate(
        [jnp.zeros((SIDE - SHARE, LANES), BF16), gathered[ROW_SMALL:ROW_TOTAL]], axis=0
    )
    firsts = [
        jnp.stack([jnp.concatenate([shares[0, p * 2 + c], side], axis=0) for p in range(PLANE)])
        for c in range(2)
    ]
    rests = [jnp.concatenate([shares[1:, p * 2 + c] for p in range(PLANE)]) for c in range(2)]
    ids = jnp.array(order, jnp.int32)
    segments = segment_ids.reshape(-1, 1, SEQ)
    project, weights, attended, w_qkv, small, first = attend(ids, segments, tokens, firsts)
    outputs, grad_middle, grad_attended, rest_keep, rest_send, first_grad = feed(
        ids, tokens, attended, cotangent, small, first, rests, F32
    )
    grad_project = attend_back(project, weights, grad_attended)
    input_grad, keep, send = project_back(
        ids, tokens, grad_project, grad_middle, w_qkv, small, first_grad, F32
    )
    first = jnp.stack([keep, send], axis=1)
    rest = jnp.stack([rest_keep, rest_send]).reshape(2, PLANE, Z - 1, SHARE, LANES).transpose(2, 1, 0, 3, 4)
    flat = jnp.concatenate(
        [
            first[:, :, :SHARE].reshape(-1, LANES),
            rest.reshape(-1, LANES),
            jnp.zeros((total - ROW_TOTAL, LANES), F32),
        ],
        axis=0,
    )
    flat = flat.at[ROW_SMALL : ROW_SMALL + LATE_SMALL].add(
        first[PLANE - 1, 1, SIDE : SIDE + LATE_SMALL]
    )
    param_grad = lax.psum_scatter(flat, "fsdp", scatter_dimension=0, tiled=True)
    return outputs, input_grad, param_grad


def index_of(z, plane, core):
    return (z * PLANE + plane) * 2 + core


COLUMNS = [[index_of(z, p, c) for z in range(Z)] for p in range(PLANE) for c in range(2)]
PLANES = [[index_of(z, p, c) for p in range(PLANE)] for z in range(Z) for c in range(2)]
CORES = [(index_of(z, p, c), index_of(z, p, 1 - c)) for z in range(Z) for p in range(PLANE) for c in range(2)]


def exchange(values, groups):
    return lax.all_to_all(values, "fsdp", 0, 0, axis_index_groups=groups, tiled=True)


def other_core(values):
    return lax.ppermute(values, "fsdp", CORES)


def add_core(keep, send):
    return small_call(
        add_core_kernel, "add_core", None, [keep, other_core(send)], [like(*keep.shape, kind=BF16)]
    )


def local_slice(tokens, params, segment_ids, cotangent):
    me = lax.axis_index("fsdp").astype(jnp.int32)
    core = me % 2
    ids = jnp.stack([p * 2 + (core ^ dc) for dc in range(2) for p in range(PLANE)])
    segments = segment_ids.reshape(-1, 1, SEQ)

    column = exchange(jnp.broadcast_to(params, (Z,) + params.shape), COLUMNS)
    first, rest = small_call(
        sort_kernel, "sort_shares", None, [column],
        [like(PLANE, SIDE + SMALL_ROWS, LANES, kind=BF16), like(PLANE * (Z - 1), SHARE, LANES, kind=BF16)],
        [pltpu.VMEM((SIDE + SMALL_ROWS, LANES), F32)],
    )
    first = exchange(first, PLANES)
    rest = exchange(rest, PLANES)
    project, weights, attended, w_qkv, small, first = attend(
        ids, segments, tokens, [first, other_core(first)]
    )
    outputs, grad_middle, grad_attended, keep, send, first_grad = feed(
        ids, tokens, attended, cotangent, small, first, [rest, other_core(rest)], BF16
    )

    grad_project = attend_back(project, weights, grad_attended)
    rest_sums, grad_project = lax.optimization_barrier((add_core(keep, send), grad_project))
    rest_sums = exchange(rest_sums, PLANES)
    input_grad, keep, send = project_back(
        ids, tokens, grad_project, grad_middle, w_qkv, small, first_grad, BF16
    )
    first_sums = exchange(add_core(keep, send), PLANES)
    column = small_call(
        add_plane_kernel, "add_plane", None, [first_sums, rest_sums],
        [like(Z, SHARE, LANES, kind=BF16)],
        [pltpu.VMEM((SIDE + 16, LANES), F32), pltpu.VMEM((Z, SHARE, LANES), F32)],
    )
    param_grad = small_call(
        add_column_kernel, "add_column", None, [exchange(column, COLUMNS)], [like(SHARE, LANES)]
    )
    return outputs, input_grad, param_grad


def solution(mesh):
    n = mesh.shape["fsdp"]
    local = local_slice if n == 2 * PLANE * Z else functools.partial(local_any, n)
    in_specs = (P("fsdp", None), P("fsdp", None), P("fsdp"), P("fsdp", None))
    out_specs = (P("fsdp", None), P("fsdp", None), P("fsdp", None))
    return jax.shard_map(local, mesh=mesh, in_specs=in_specs, out_specs=out_specs, check_vma=False)
```

```python
import functools

import jax
import jax.numpy as jnp
from jax import lax
from jax.experimental import pallas as pl
from jax.experimental.pallas import tpu as pltpu
from jax.sharding import PartitionSpec as P

D = 256
HEADS = 4
HEAD_DIM = 64
FF = 1024
SEQ = 128
LANES = 128
BLOCK = 2 * SEQ
EPSILON = 1e-05
SCALE = HEAD_DIM ** (-0.5)
VMEM_BYTES = 48 * 1024 * 1024

ROW_QKV = 0
ROW_OUT = 1536
ROW_UP = 2048
ROW_DOWN = 4096
ROW_SMALL = 6144
ROW_END = 6168
ROW_TOTAL = 6176
GAIN_ONE, SHIFT_ONE, BIAS_QUERY, BIAS_VALUE, BIAS_OUT = 0, 2, 4, 6, 8
GAIN_TWO, SHIFT_TWO, BIAS_UP, BIAS_DOWN = 10, 12, 14, 22
SMALL_ROWS = 32
LATE_SMALL = 8

SHARE = 193
Z, PLANE = 4, 4
FIRST_ROWS = 2 * PLANE * SHARE
HEAD_ROWS = FIRST_ROWS - ROW_OUT
SMALL_IN_SHARE = ROW_SMALL - (2 * PLANE * Z - 1) * SHARE
SIDE = 208

F32 = jnp.float32
BF16 = jnp.bfloat16


def dot(left, right):
    return jnp.dot(left, right, preferred_element_type=F32)


def dot_nt(left, right):
    return lax.dot_general(left, right, (((1,), (1,)), ((), ())), preferred_element_type=F32)


def dot_tn(left, right):
    return lax.dot_general(left, right, (((0,), (0,)), ((), ())), preferred_element_type=F32)


def small_vector(small, row, count):
    return jnp.concatenate([small[row + i : row + i + 1, :] for i in range(count)], axis=1)


def fold_rows(values):
    rows, columns = values.shape
    return jnp.sum(values.reshape(rows // 8, 8, columns), axis=0)


def normalize(values):
    center = values - jnp.mean(values, axis=-1, keepdims=True)
    rate = lax.rsqrt(jnp.mean(center * center, axis=-1, keepdims=True) + EPSILON)
    return center * rate, rate


def normalize_back(grad, gain, normed, rate):
    scaled = grad * gain
    return rate * (
        scaled
        - jnp.mean(scaled, axis=-1, keepdims=True)
        - normed * jnp.mean(scaled * normed, axis=-1, keepdims=True)
    )


def head_masks():
    lane = lax.broadcasted_iota(jnp.int32, (1, D), 1)
    return [(lane // HEAD_DIM == h).astype(F32).astype(BF16) for h in range(HEADS)]


def spread_heads(rows):
    return jnp.concatenate([rows * mask for mask in head_masks()], axis=0)


def matrix_from_flat(flat, start, rows, columns, out):
    per_row = columns // LANES
    for j in range(per_row):
        out[:, j * LANES : (j + 1) * LANES] = flat[
            pl.ds(start + j, rows, stride=per_row), :
        ].astype(BF16)


def matrix_to_flat(matrix, rows, columns, flat, start):
    per_row = columns // LANES
    for j in range(per_row):
        flat[pl.ds(start + j, rows, stride=per_row), :] = matrix[:, j * LANES : (j + 1) * LANES]


def place_shares(bufs, ids, flat, base):
    for slot, buf in enumerate(bufs):
        for z in range(Z - 1):
            share = ids[slot] + (z + 1) * 2 * PLANE
            flat[pl.ds(share * SHARE - base, SHARE), :] = buf[z].astype(F32)


def sort_kernel(ids, *refs):
    received, (first, rest, stage, wide) = refs[:Z], refs[Z:]
    for d in range(Z):
        stage[lax.rem(ids[0] + Z - d, Z)] = received[d][...]
    rest[...] = stage[1:]
    wide[:SHARE, :] = stage[0].astype(F32)
    wide[SHARE:SIDE, :] = jnp.zeros((SIDE - SHARE, LANES), F32)
    last = stage[Z - 1].astype(F32)
    wide[SIDE:, :] = last[SMALL_IN_SHARE:, :]
    first[...] = wide[...].astype(BF16)


def attend_kernel(
    ids, seg, tok, *refs,
):
    bufs = refs[: 2 * PLANE]
    project_out, weights_out, attended_out, w_qkv, small, first_out, flat = refs[2 * PLANE :]

    @pl.when(pl.program_id(0) == 0)
    def _():
        for slot, buf in enumerate(bufs):
            wide = buf[...].astype(F32)
            flat[pl.ds(ids[slot] * SHARE, SHARE), :] = wide[:SHARE, :]

            @pl.when(ids[slot] == 2 * PLANE - 1)
            def _():
                small[...] = wide[SIDE:, :]

        matrix_from_flat(flat, ROW_QKV, D, 3 * D, w_qkv)
        first_out[...] = flat[ROW_OUT:FIRST_ROWS, :]

    normed, _ = normalize(tok[...].astype(F32))
    normed_low = (
        normed * small_vector(small, GAIN_ONE, 2) + small_vector(small, SHIFT_ONE, 2)
    ).astype(BF16)
    bias = jnp.concatenate(
        [
            small_vector(small, BIAS_QUERY, 2),
            jnp.zeros((1, D), F32),
            small_vector(small, BIAS_VALUE, 2),
        ],
        axis=1,
    )
    project = (dot(normed_low, w_qkv[...]) + bias).astype(BF16)
    project_out[...] = project
    causal = lax.broadcasted_iota(jnp.int32, (SEQ, SEQ), 1) <= lax.broadcasted_iota(
        jnp.int32, (SEQ, SEQ), 0
    )
    for s in range(BLOCK // SEQ):
        rows = slice(s * SEQ, (s + 1) * SEQ)
        across = jnp.broadcast_to(seg[s].astype(F32), (SEQ, SEQ))
        allowed = causal & (across == across.T)
        query = project[rows, :D]
        key = spread_heads(project[rows, D : 2 * D])
        value = spread_heads(project[rows, 2 * D :])
        scores = dot_nt(query, key) * SCALE
        low = []
        for h in range(HEADS):
            columns = slice(h * SEQ, (h + 1) * SEQ)
            mine = jnp.where(allowed, scores[:, columns], -1e30)
            grown = jnp.exp(mine - jnp.max(mine, axis=-1, keepdims=True))
            weights = grown * (1.0 / jnp.sum(grown, axis=-1, keepdims=True))
            weights_out[rows, columns] = weights
            low.append(weights.astype(BF16))
        attended_out[rows, :] = dot(jnp.concatenate(low, axis=1), value).astype(BF16)


def feed_kernel(
    ids, tok, attended, cot, small, first_in, *refs,
):
    bufs = [ref.at[pl.ds(p * (Z - 1), Z - 1)] for ref in refs[:2] for p in range(PLANE)]
    (
        result_out, grad_middle_out, grad_attended_out, keep_out, send_out, first_out,
        w_out, w_up, w_down, acc_out, acc_up, acc_down, acc_small, flat,
    ) = refs[2:]
    step = pl.program_id(0)

    @pl.when(step == 0)
    def _():
        flat[:HEAD_ROWS, :] = first_in[...]
        place_shares(bufs, ids, flat, ROW_OUT)
        matrix_from_flat(flat, 0, D, D, w_out)
        matrix_from_flat(flat, ROW_UP - ROW_OUT, D, FF, w_up)
        matrix_from_flat(flat, ROW_DOWN - ROW_OUT, FF, D, w_down)
        acc_out[...] = jnp.zeros_like(acc_out)
        acc_up[...] = jnp.zeros_like(acc_up)
        acc_down[...] = jnp.zeros_like(acc_down)
        acc_small[...] = jnp.zeros_like(acc_small)

    gain = small_vector(small, GAIN_TWO, 2)
    middle = tok[...].astype(F32) + dot(attended[...], w_out[...]) + small_vector(small, BIAS_OUT, 2)
    normed, rate = normalize(middle)
    normed_low = (normed * gain + small_vector(small, SHIFT_TWO, 2)).astype(BF16)
    hidden = dot(normed_low, w_up[...]) + small_vector(small, BIAS_UP, 8)
    square = hidden * hidden
    slope = 0.7978845608028654
    bent = jnp.tanh(hidden * (slope + (slope * 0.044715) * square))
    half = 0.5 + 0.5 * bent
    activated = (hidden * half).astype(BF16)
    derivative = half + hidden * (0.5 - 0.5 * bent * bent) * (
        slope + (3 * slope * 0.044715) * square
    )
    result = middle + dot(activated, w_down[...]) + small_vector(small, BIAS_DOWN, 2)
    result_out[...] = result.astype(BF16)
    cotangent = cot[...]
    grad_result = cotangent.astype(F32)
    acc_down[...] += dot_tn(activated, cotangent)
    grad_hidden = (dot_nt(cotangent, w_down[...]) * derivative).astype(BF16)
    acc_up[...] += dot_tn(normed_low, grad_hidden)
    grad_normed = dot_nt(grad_hidden, w_up[...])
    grad_middle = grad_result + normalize_back(grad_normed, gain, normed, rate)
    grad_middle_out[...] = grad_middle
    grad_middle_low = grad_middle.astype(BF16)
    acc_out[...] += dot_tn(attended[...], grad_middle_low)
    grad_attended_out[...] = dot_nt(grad_middle_low, w_out[...]).astype(BF16)
    acc_small[:, 0:D] += fold_rows(grad_middle_low.astype(F32))
    acc_small[:, D : 2 * D] += fold_rows(grad_normed * normed)
    acc_small[:, 2 * D : 3 * D] += fold_rows(grad_normed)
    acc_small[:, 3 * D : 3 * D + FF] += fold_rows(grad_hidden.astype(F32))
    acc_small[:, 3 * D + FF :] += fold_rows(grad_result)

    @pl.when(step == pl.num_programs(0) - 1)
    def _():
        matrix_to_flat(acc_out, D, D, flat, 0)
        matrix_to_flat(acc_up, D, FF, flat, ROW_UP - ROW_OUT)
        matrix_to_flat(acc_down, FF, D, flat, ROW_DOWN - ROW_OUT)
        sums = jnp.sum(acc_small[...], axis=0, keepdims=True)
        base = ROW_SMALL - ROW_OUT
        flat[base : base + LATE_SMALL, :] = jnp.zeros((LATE_SMALL, LANES), F32)
        for i in range(sums.shape[1] // LANES):
            row = base + LATE_SMALL + i
            flat[row : row + 1, :] = sums[:, i * LANES : (i + 1) * LANES]
        flat[ROW_END - ROW_OUT :, :] = jnp.zeros((ROW_TOTAL - ROW_END, LANES), F32)
        first_out[...] = flat[:HEAD_ROWS, :]
        for target, out in enumerate((keep_out, send_out)):
            for p in range(PLANE):
                for z in range(Z - 1):
                    share = ids[target * PLANE + p] + (z + 1) * 2 * PLANE
                    rows = flat[pl.ds(share * SHARE - ROW_OUT, SHARE), :]
                    out[p * (Z - 1) + z] = rows.astype(out.dtype)


def attend_back_kernel(project, weights, grad_attended, grad_project):
    for s in range(BLOCK // SEQ):
        rows = slice(s * SEQ, (s + 1) * SEQ)
        query = spread_heads(project[rows, :D])
        key = spread_heads(project[rows, D : 2 * D])
        value = spread_heads(project[rows, 2 * D :])
        grad_rows = grad_attended[rows, :]
        grad_weights = dot_nt(grad_rows, value)
        scores_low, scores_turned, weights_turned = [], [], []
        for h in range(HEADS):
            columns = slice(h * SEQ, (h + 1) * SEQ)
            mine = weights[rows, columns]
            product = mine * grad_weights[:, columns]
            grad_scores = product - mine * jnp.sum(product, axis=-1, keepdims=True)
            scores_low.append(grad_scores.astype(BF16))
            scores_turned.append(grad_scores.T.astype(BF16))
            weights_turned.append(mine.T.astype(BF16))
        grad_query = dot(jnp.concatenate(scores_low, axis=1), key) * SCALE
        grad_key = dot(jnp.concatenate(scores_turned, axis=1), query) * SCALE
        grad_value = dot(jnp.concatenate(weights_turned, axis=1), spread_heads(grad_rows))
        grad_project[rows, :D] = grad_query.astype(BF16)
        grad_project[rows, D : 2 * D] = grad_key.astype(BF16)
        grad_project[rows, 2 * D :] = grad_value.astype(BF16)

def project_back_kernel(
    ids, tok, grad_project, grad_middle, w_qkv, small, first_in,
    input_grad_out, keep_out, send_out, acc_qkv, acc_small, flat,
):
    step = pl.program_id(0)

    @pl.when(step == 0)
    def _():
        acc_qkv[...] = jnp.zeros_like(acc_qkv)
        acc_small[...] = jnp.zeros_like(acc_small)

    gain = small_vector(small, GAIN_ONE, 2)
    normed, rate = normalize(tok[...].astype(F32))
    normed_low = (normed * gain + small_vector(small, SHIFT_ONE, 2)).astype(BF16)
    acc_qkv[...] += dot_tn(normed_low, grad_project[...])
    grad_normed = dot_nt(grad_project[...], w_qkv[...])
    input_grad_out[...] = grad_middle[...] + normalize_back(grad_normed, gain, normed, rate)
    acc_small[:, 0:D] += fold_rows(grad_normed * normed)
    acc_small[:, D : 2 * D] += fold_rows(grad_normed)
    acc_small[:, 2 * D : 3 * D] += fold_rows(grad_project[:, :D].astype(F32))
    acc_small[:, 3 * D :] += fold_rows(grad_project[:, 2 * D :].astype(F32))

    @pl.when(step == pl.num_programs(0) - 1)
    def _():
        matrix_to_flat(acc_qkv, D, 3 * D, flat, ROW_QKV)
        flat[ROW_OUT:, :] = first_in[...]
        sums = jnp.sum(acc_small[...], axis=0, keepdims=True)
        side = jnp.concatenate(
            [sums[:, i * LANES : (i + 1) * LANES] for i in range(LATE_SMALL)]
            + [jnp.zeros((16 - LATE_SMALL, LANES), F32)],
            axis=0,
        )
        for target, out in enumerate((keep_out, send_out)):
            for p in range(PLANE):
                share = ids[target * PLANE + p]
                rows = flat[pl.ds(share * SHARE, SHARE), :]
                padded = jnp.concatenate([rows, jnp.zeros((SIDE - SHARE, LANES), F32)], axis=0)
                mine = jnp.where(share == 2 * PLANE - 1, side, 0.0)
                out[p] = jnp.concatenate([padded, mine], axis=0).astype(out.dtype)


def add_first_kernel(kept, received, keep_out, *sends):
    keep_out[...] = kept[0] + received[0].astype(F32)
    for p, out in enumerate(sends):
        out[...] = (kept[p + 1] + received[p + 1].astype(F32)).astype(BF16)


def add_rest_kernel(kept, received, out):
    out[...] = (kept[...] + received[...].astype(F32)).astype(out.dtype)


def add_plane_kernel(ids, rest, first_kept, *refs):
    firsts = refs[: PLANE - 1]
    keep_out, *sends, first, column = refs[PLANE - 1 :]
    first[...] = first_kept[...] + sum(item[...].astype(F32) for item in firsts)
    column[0] = first[:SHARE, :]
    column[1:] = rest[...].astype(F32)
    end = SMALL_IN_SHARE + LATE_SMALL
    column[Z - 1, SMALL_IN_SHARE:end, :] += first[SIDE : SIDE + LATE_SMALL, :]
    keep_out[...] = column[ids[0]]
    for d, out in enumerate(sends):
        out[...] = column[lax.rem(ids[0] + d + 1, Z)].astype(BF16)


def rows_spec(columns):
    return pl.BlockSpec((BLOCK, columns), lambda i: (i, 0))


def whole_spec(item):
    return pl.BlockSpec(item.shape, lambda i: (0,) * len(item.shape))


def like(*shape, kind=F32):
    return jax.ShapeDtypeStruct(shape, kind)


SMEM_SPEC = pl.BlockSpec(memory_space=pltpu.SMEM)
PARAMS = pltpu.CompilerParams(
    dimension_semantics=("arbitrary",), vmem_limit_bytes=VMEM_BYTES
)


def cost(us):
    return pl.CostEstimate(flops=int(us * 1e9), bytes_accessed=1 << 20, transcendentals=0)


def small_call(kernel, name, ids, inputs, outs, scratch=()):
    with_ids = ids is not None
    results = pl.pallas_call(
        kernel,
        in_specs=[SMEM_SPEC] * with_ids + [pl.BlockSpec(memory_space=pltpu.VMEM)] * len(inputs),
        out_specs=[pl.BlockSpec(memory_space=pltpu.VMEM)] * len(outs),
        out_shape=list(outs),
        scratch_shapes=list(scratch),
        compiler_params=pltpu.CompilerParams(vmem_limit_bytes=VMEM_BYTES),
        cost_estimate=cost(1),
        name=name,
    )(*([ids] if with_ids else []), *inputs)
    return results if len(outs) > 1 else results[0]


def attend(ids, segments, tokens, bufs):
    rows = tokens.shape[0]
    blocked = [like(rows, 3 * D, kind=BF16), like(rows, HEADS * SEQ), like(rows, D, kind=BF16)]
    fixed = [like(D, 3 * D, kind=BF16), like(SMALL_ROWS, LANES), like(HEAD_ROWS, LANES)]
    return pl.pallas_call(
        attend_kernel,
        grid=(rows // BLOCK,),
        in_specs=[
            SMEM_SPEC,
            pl.BlockSpec((BLOCK // SEQ, 1, SEQ), lambda i: (i, 0, 0)),
            rows_spec(D),
        ]
        + [whole_spec(buf) for buf in bufs],
        out_specs=[rows_spec(item.shape[1]) for item in blocked] + [whole_spec(item) for item in fixed],
        out_shape=blocked + fixed,
        scratch_shapes=[pltpu.VMEM((FIRST_ROWS, LANES), F32)],
        compiler_params=PARAMS,
        cost_estimate=cost(7),
        name="attend",
    )(ids, segments, tokens, *bufs)


def feed(ids, tokens, attended, cotangent, small, first, bufs, send_kind):
    rows = tokens.shape[0]
    small_rows = ROW_END - ROW_SMALL - LATE_SMALL
    blocked = [like(rows, D, kind=BF16), like(rows, D), like(rows, D, kind=BF16)]
    fixed = [
        like(PLANE * (Z - 1), SHARE, LANES),
        like(PLANE * (Z - 1), SHARE, LANES, kind=send_kind),
        like(HEAD_ROWS, LANES),
    ]
    return pl.pallas_call(
        feed_kernel,
        grid=(rows // BLOCK,),
        in_specs=[SMEM_SPEC] + [rows_spec(D)] * 3 + [whole_spec(item) for item in (small, first, *bufs)],
        out_specs=[rows_spec(D)] * 3 + [whole_spec(item) for item in fixed],
        out_shape=blocked + fixed,
        scratch_shapes=[
            pltpu.VMEM((D, D), BF16),
            pltpu.VMEM((D, FF), BF16),
            pltpu.VMEM((FF, D), BF16),
            pltpu.VMEM((D, D), F32),
            pltpu.VMEM((D, FF), F32),
            pltpu.VMEM((FF, D), F32),
            pltpu.VMEM((8, small_rows * LANES), F32),
            pltpu.VMEM((ROW_TOTAL - ROW_OUT, LANES), F32),
        ],
        compiler_params=PARAMS,
        cost_estimate=cost(10),
        name="feed",
    )(ids, tokens, attended, cotangent, small, first, *bufs)


def attend_back(project, weights, grad_attended):
    return pl.pallas_call(
        attend_back_kernel,
        grid=(project.shape[0] // BLOCK,),
        in_specs=[rows_spec(item.shape[1]) for item in (project, weights, grad_attended)],
        out_specs=rows_spec(3 * D),
        out_shape=like(*project.shape, kind=BF16),
        compiler_params=PARAMS,
        cost_estimate=cost(6),
        name="attend_back",
    )(project, weights, grad_attended)


def project_back(ids, tokens, grad_project, grad_middle, w_qkv, small, first, send_kind):
    rows = tokens.shape[0]
    fixed = [
        like(PLANE, SIDE + 16, LANES),
        like(PLANE, SIDE + 16, LANES, kind=send_kind),
    ]
    return pl.pallas_call(
        project_back_kernel,
        grid=(rows // BLOCK,),
        in_specs=[SMEM_SPEC]
        + [rows_spec(item.shape[1]) for item in (tokens, grad_project, grad_middle)]
        + [whole_spec(item) for item in (w_qkv, small, first)],
        out_specs=[rows_spec(D)] + [whole_spec(item) for item in fixed],
        out_shape=[like(rows, D)] + fixed,
        scratch_shapes=[
            pltpu.VMEM((D, 3 * D), F32),
            pltpu.VMEM((8, LATE_SMALL * LANES), F32),
            pltpu.VMEM((FIRST_ROWS, LANES), F32),
        ],
        compiler_params=PARAMS,
        cost_estimate=cost(6),
        name="project_back",
    )(ids, tokens, grad_project, grad_middle, w_qkv, small, first)


def local_any(n, tokens, params, segment_ids, cotangent):
    total = n * params.shape[0]
    gathered = lax.all_gather(params, "fsdp", axis=0).reshape(total, LANES)
    shares = gathered[:ROW_TOTAL].reshape(Z, 2 * PLANE, SHARE, LANES)
    order = [p * 2 + c for c in range(2) for p in range(PLANE)]
    side = jnp.concatenate(
        [jnp.zeros((SIDE - SHARE, LANES), BF16), gathered[ROW_SMALL:ROW_TOTAL]], axis=0
    )
    firsts = [jnp.concatenate([shares[0, k], side], axis=0) for k in order]
    rests = [jnp.concatenate([shares[1:, p * 2 + c] for p in range(PLANE)]) for c in range(2)]
    ids = jnp.array(order, jnp.int32)
    segments = segment_ids.reshape(-1, 1, SEQ)
    project, weights, attended, w_qkv, small, first = attend(ids, segments, tokens, firsts)
    outputs, grad_middle, grad_attended, rest_keep, rest_send, first_grad = feed(
        ids, tokens, attended, cotangent, small, first, rests, F32
    )
    grad_project = attend_back(project, weights, grad_attended)
    input_grad, keep, send = project_back(
        ids, tokens, grad_project, grad_middle, w_qkv, small, first_grad, F32
    )
    first = jnp.stack([keep, send], axis=1)
    rest = jnp.stack([rest_keep, rest_send]).reshape(2, PLANE, Z - 1, SHARE, LANES).transpose(2, 1, 0, 3, 4)
    flat = jnp.concatenate(
        [
            first[:, :, :SHARE].reshape(-1, LANES),
            rest.reshape(-1, LANES),
            jnp.zeros((total - ROW_TOTAL, LANES), F32),
        ],
        axis=0,
    )
    flat = flat.at[ROW_SMALL : ROW_SMALL + LATE_SMALL].add(
        first[PLANE - 1, 1, SIDE : SIDE + LATE_SMALL]
    )
    param_grad = lax.psum_scatter(flat, "fsdp", scatter_dimension=0, tiled=True)
    return outputs, input_grad, param_grad


def index_of(z, plane, core):
    return (z * PLANE + plane) * 2 + core


PLANES = [[index_of(z, p, c) for p in range(PLANE)] for z in range(Z) for c in range(2)]


def move(values, step_z, step_plane, step_core):
    pairs = [
        (index_of(z, p, c), index_of((z + step_z) % Z, p ^ step_plane, c ^ step_core))
        for z in range(Z)
        for p in range(PLANE)
        for c in range(2)
    ]
    return lax.ppermute(values, "fsdp", pairs)


def local_slice(tokens, params, segment_ids, cotangent):
    me = lax.axis_index("fsdp").astype(jnp.int32)
    z, plane, core = me // (2 * PLANE), (me // 2) % PLANE, me % 2
    where = z.reshape(1)
    ids = jnp.stack([(plane ^ dp) * 2 + (core ^ dc) for dc in range(2) for dp in range(PLANE)])
    plain_ids = jnp.stack([p * 2 + (core ^ dc) for dc in range(2) for p in range(PLANE)])
    segments = segment_ids.reshape(-1, 1, SEQ)

    column = [params] + [move(params, d, 0, 0) for d in range(1, Z)]
    first, rest = small_call(
        sort_kernel, "sort_shares", where, column,
        [like(SIDE + SMALL_ROWS, LANES, kind=BF16), like(Z - 1, SHARE, LANES, kind=BF16)],
        [pltpu.VMEM((Z, SHARE, LANES), BF16), pltpu.VMEM((SIDE + SMALL_ROWS, LANES), F32)],
    )
    rest = lax.all_gather(rest, "fsdp", axis=0, axis_index_groups=PLANES, tiled=True)
    same = [first] + [move(first, 0, d, 0) for d in range(1, PLANE)]
    firsts = same + [move(item, 0, 0, 1) for item in same]
    project, weights, attended, w_qkv, small, first = attend(ids, segments, tokens, firsts)
    rest, attended = lax.optimization_barrier((rest, attended))
    outputs, grad_middle, grad_attended, keep, send, first_grad = feed(
        plain_ids, tokens, attended, cotangent, small, first, [rest, move(rest, 0, 0, 1)], BF16
    )

    grad_project = attend_back(project, weights, grad_attended)
    rest_sums = small_call(
        add_rest_kernel, "add_rest", None, [keep, move(send, 0, 0, 1)], [like(*keep.shape)]
    )
    rest_sums, grad_project = lax.optimization_barrier((rest_sums, grad_project))
    rest_sums = lax.psum_scatter(
        rest_sums, "fsdp", scatter_dimension=0, axis_index_groups=PLANES, tiled=True
    )
    input_grad, keep, send = project_back(
        ids, tokens, grad_project, grad_middle, w_qkv, small, first_grad, BF16
    )
    kept, *sends = small_call(
        add_first_kernel, "add_first", None, [keep, move(send, 0, 0, 1)],
        [like(SIDE + 16, LANES)] + [like(SIDE + 16, LANES, kind=BF16)] * (PLANE - 1),
    )
    arrived = [move(item, 0, d + 1, 0) for d, item in enumerate(sends)]
    param_grad, *sends = small_call(
        add_plane_kernel, "add_plane", where, [rest_sums, kept] + arrived,
        [like(SHARE, LANES)] + [like(SHARE, LANES, kind=BF16)] * (Z - 1),
        [pltpu.VMEM((SIDE + 16, LANES), F32), pltpu.VMEM((Z, SHARE, LANES), F32)],
    )
    for d, item in enumerate(sends):
        param_grad = param_grad + move(item, d + 1, 0, 0).astype(F32)
    return outputs, input_grad, param_grad


def solution(mesh):
    n = mesh.shape["fsdp"]
    local = local_slice if n == 2 * PLANE * Z else functools.partial(local_any, n)
    in_specs = (P("fsdp", None), P("fsdp", None), P("fsdp"), P("fsdp", None))
    out_specs = (P("fsdp", None), P("fsdp", None), P("fsdp", None))
    return jax.shard_map(local, mesh=mesh, in_specs=in_specs, out_specs=out_specs, check_vma=False)
```

```python
import functools

import jax
import jax.numpy as jnp
from jax import lax
from jax.experimental import pallas as pl
from jax.experimental.pallas import tpu as pltpu
from jax.sharding import PartitionSpec as P

D = 256
HEADS = 4
HEAD_DIM = 64
FF = 1024
SEQ = 128
LANES = 128
BLOCK = 2 * SEQ
WIDE = 4 * SEQ
CHUNK = 256
STRIP = 64
EPSILON = 1e-05
SCALE = HEAD_DIM ** (-0.5)
VMEM_BYTES = 32 * 1024 * 1024

ROW_QKV = 0
ROW_OUT = 1536
ROW_UP = 2048
ROW_DOWN = 4096
ROW_SMALL = 6144
ROW_END = 6168
ROW_TOTAL = 6176
GAIN_ONE, SHIFT_ONE, BIAS_QUERY, BIAS_VALUE, BIAS_OUT = 0, 2, 4, 6, 8
GAIN_TWO, SHIFT_TWO, BIAS_UP, BIAS_DOWN = 10, 12, 14, 22
SMALL_ROWS = 24
LATE_SMALL = 8

SHARE = 193
Z, PLANE = 4, 4
FIRST_ROWS = 2 * PLANE * SHARE
HEAD_ROWS = FIRST_ROWS - ROW_OUT
SIDE, SIDE_ROWS = 208, 16
SMALL_IN_SHARE = ROW_SMALL - (2 * PLANE * Z - 1) * SHARE

F32 = jnp.float32
BF16 = jnp.bfloat16


def dot(left, right):
    return jnp.dot(left, right, preferred_element_type=F32)


def dot_nt(left, right):
    return lax.dot_general(left, right, (((1,), (1,)), ((), ())), preferred_element_type=F32)


def dot_tn(left, right):
    return lax.dot_general(left, right, (((0,), (0,)), ((), ())), preferred_element_type=F32)


def small_vector(small, row, count):
    return jnp.concatenate([small[row + i : row + i + 1, :] for i in range(count)], axis=1)


def fold_rows(values):
    rows, columns = values.shape
    return jnp.sum(values.reshape(rows // 8, 8, columns), axis=0)


def normalize(values):
    center = values - jnp.mean(values, axis=-1, keepdims=True)
    rate = lax.rsqrt(jnp.mean(center * center, axis=-1, keepdims=True) + EPSILON)
    return center * rate, rate


def normalize_back(grad, gain, normed, rate):
    scaled = grad * gain
    return rate * (
        scaled
        - jnp.mean(scaled, axis=-1, keepdims=True)
        - normed * jnp.mean(scaled * normed, axis=-1, keepdims=True)
    )


def head_masks():
    lane = lax.broadcasted_iota(jnp.int32, (1, D), 1)
    return [(lane // HEAD_DIM == h).astype(F32).astype(BF16) for h in range(HEADS)]


def spread_heads(rows):
    return jnp.concatenate([rows * mask for mask in head_masks()], axis=0)


def matrix_from_flat(flat, start, rows, columns, out):
    per_row = columns // LANES
    for j in range(per_row):
        out[:, j * LANES : (j + 1) * LANES] = flat[
            pl.ds(start + j, rows, stride=per_row), :
        ].astype(BF16)


def turned_to_flat(turned, rows, columns, flat, start):
    per_row = columns // LANES
    for j in range(per_row):
        flat[pl.ds(start + j, rows, stride=per_row), :] = turned[j * LANES : (j + 1) * LANES, :].T


def matrix_to_flat(matrix, rows, columns, flat, start):
    per_row = columns // LANES
    for j in range(per_row):
        flat[pl.ds(start + j, rows, stride=per_row), :] = matrix[:, j * LANES : (j + 1) * LANES]


def attend_kernel(n_bufs, ids, seg, tok, *refs):
    bufs = refs[:n_bufs]
    (
        project_out, weights_out, attended_out, normed_out, w_qkv, w_out, w_up, w_down, small, flat,
    ) = refs[n_bufs:]

    @pl.when(pl.program_id(0) == 0)
    def _():
        slot = 0
        for buf in bufs:
            count, rows, _ = buf.shape

            def place(i, carry, buf=buf, slot=slot, rows=rows):
                flat[pl.ds(ids[slot + i] * rows, rows), :] = buf[i].astype(F32)
                return carry

            lax.fori_loop(0, count, place, 0)
            slot += count
        matrix_from_flat(flat, ROW_QKV, D, 3 * D, w_qkv)
        matrix_from_flat(flat, ROW_OUT, D, D, w_out)
        matrix_from_flat(flat, ROW_UP, D, FF, w_up)
        matrix_from_flat(flat, ROW_DOWN, FF, D, w_down)
        small[...] = flat[ROW_SMALL:ROW_END, :]

    normed, _ = normalize(tok[...].astype(F32))
    normed_out[...] = normed.astype(BF16)
    normed_low = (
        normed * small_vector(small, GAIN_ONE, 2) + small_vector(small, SHIFT_ONE, 2)
    ).astype(BF16)
    bias = jnp.concatenate(
        [
            small_vector(small, BIAS_QUERY, 2),
            jnp.zeros((1, D), F32),
            small_vector(small, BIAS_VALUE, 2),
        ],
        axis=1,
    )
    project = (dot(normed_low, w_qkv[...]) + bias).astype(BF16)
    project_out[...] = project
    causal = lax.broadcasted_iota(jnp.int32, (SEQ, SEQ), 1) <= lax.broadcasted_iota(
        jnp.int32, (SEQ, SEQ), 0
    )
    for s in range(BLOCK // SEQ):
        rows = slice(s * SEQ, (s + 1) * SEQ)
        across = jnp.broadcast_to(seg[s].astype(F32), (SEQ, SEQ))
        allowed = causal & (across == across.T)
        query = project[rows, :D]
        key = spread_heads(project[rows, D : 2 * D])
        value = spread_heads(project[rows, 2 * D :])
        scores = dot_nt(query, key) * SCALE
        low = []
        for h in range(HEADS):
            columns = slice(h * SEQ, (h + 1) * SEQ)
            mine = jnp.where(allowed, scores[:, columns], -1e30)
            grown = jnp.exp(mine - jnp.max(mine, axis=-1, keepdims=True))
            weights = grown * (1.0 / jnp.sum(grown, axis=-1, keepdims=True))
            weights_out[rows, columns] = weights
            low.append(weights.astype(BF16))
        attended_out[rows, :] = dot(jnp.concatenate(low, axis=1), value).astype(BF16)


def feed_kernel(
    ids, tok, attended, cot, w_out, w_up, w_down, small,
    middle_out, activated_out, grad_middle_out, grad_attended_out, keep_out, send_out, first_out,
    grad_hidden, acc_out, acc_up, acc_down, acc_small, flat,
):
    step = pl.program_id(0)

    @pl.when(step == 0)
    def _():
        acc_out[...] = jnp.zeros_like(acc_out)
        acc_up[...] = jnp.zeros_like(acc_up)
        acc_down[...] = jnp.zeros_like(acc_down)
        acc_small[...] = jnp.zeros_like(acc_small)

    gain = small_vector(small, GAIN_TWO, 2)
    middle = tok[...].astype(F32) + dot(attended[...], w_out[...]) + small_vector(small, BIAS_OUT, 2)
    middle_out[...] = middle
    normed, rate = normalize(middle)
    normed_low = (normed * gain + small_vector(small, SHIFT_TWO, 2)).astype(BF16)
    cotangent = cot[...]
    slope = 0.7978845608028654
    cubic = slope * 0.044715
    for c in range(0, FF, CHUNK):
        columns = slice(c, c + CHUNK)
        bias = small_vector(small, BIAS_UP + c // LANES, CHUNK // LANES)
        hidden_all = dot(normed_low, w_up[:, columns])
        grad_all = dot_nt(cotangent, w_down[columns, :])
        total = jnp.zeros((8, CHUNK), F32)
        for r in range(0, WIDE, STRIP):
            rows = slice(r, r + STRIP)
            hidden = hidden_all[rows] + bias
            square = hidden * hidden
            half = 0.5 + 0.5 * jnp.tanh(hidden * (slope + cubic * square))
            activated = hidden * half
            derivative = half + activated * (1.0 - half) * (2 * slope + (6 * cubic) * square)
            low = (grad_all[rows] * derivative).astype(BF16)
            activated_out[rows, columns] = activated.astype(BF16)
            grad_hidden[rows, columns] = low
            total += fold_rows(low.astype(F32))
        acc_small[:, 3 * D + c : 3 * D + c + CHUNK] += total
    grad_result = cotangent.astype(F32)
    acc_down[...] += dot_tn(cotangent, activated_out[...])
    acc_up[...] += dot_tn(normed_low, grad_hidden[...])
    grad_normed = dot_nt(grad_hidden[...], w_up[...])
    grad_middle = grad_result + normalize_back(grad_normed, gain, normed, rate)
    grad_middle_out[...] = grad_middle
    grad_middle_low = grad_middle.astype(BF16)
    acc_out[...] += dot_tn(attended[...], grad_middle_low)
    grad_attended_out[...] = dot_nt(grad_middle_low, w_out[...]).astype(BF16)
    acc_small[:, 0:D] += fold_rows(grad_middle_low.astype(F32))
    acc_small[:, D : 2 * D] += fold_rows(grad_normed * normed)
    acc_small[:, 2 * D : 3 * D] += fold_rows(grad_normed)
    acc_small[:, 3 * D + FF :] += fold_rows(grad_result)

    @pl.when(step == pl.num_programs(0) - 1)
    def _():
        matrix_to_flat(acc_out, D, D, flat, 0)
        matrix_to_flat(acc_up, D, FF, flat, ROW_UP - ROW_OUT)
        turned_to_flat(acc_down, FF, D, flat, ROW_DOWN - ROW_OUT)
        sums = jnp.sum(acc_small[...], axis=0, keepdims=True)
        base = ROW_SMALL - ROW_OUT
        flat[base : base + LATE_SMALL, :] = jnp.zeros((LATE_SMALL, LANES), F32)
        for i in range(sums.shape[1] // LANES):
            row = base + LATE_SMALL + i
            flat[row : row + 1, :] = sums[:, i * LANES : (i + 1) * LANES]
        flat[ROW_END - ROW_OUT :, :] = jnp.zeros((ROW_TOTAL - ROW_END, LANES), F32)
        first_out[...] = flat[:HEAD_ROWS, :]
        for target, out in enumerate((keep_out, send_out)):
            for p in range(PLANE):
                for z in range(1, Z):
                    share = ids[target * PLANE + p] + z * 2 * PLANE
                    rows = flat[pl.ds(share * SHARE - ROW_OUT, SHARE), :]
                    out[p * (Z - 1) + z - 1] = rows.astype(out.dtype)


def result_kernel(middle, activated, w_down, small, result_out):
    result = middle[...] + dot(activated[...], w_down[...]) + small_vector(small, BIAS_DOWN, 2)
    result_out[...] = result.astype(BF16)


def attend_back_kernel(
    ids, project, weights, grad_attended, normed_low, w_qkv, small, first_in,
    grad_project, keep_out, send_out, acc_qkv, acc_sum, flat, wide,
):
    step = pl.program_id(0)

    @pl.when(step == 0)
    def _():
        acc_qkv[...] = jnp.zeros_like(acc_qkv)
        acc_sum[...] = jnp.zeros_like(acc_sum)

    for s in range(BLOCK // SEQ):
        rows = slice(s * SEQ, (s + 1) * SEQ)
        query = spread_heads(project[rows, :D])
        key = spread_heads(project[rows, D : 2 * D])
        value = spread_heads(project[rows, 2 * D :])
        grad_rows = grad_attended[rows, :]
        grad_weights = dot_nt(grad_rows, value)
        scores_low, scores_turned, weights_turned = [], [], []
        for h in range(HEADS):
            columns = slice(h * SEQ, (h + 1) * SEQ)
            mine = weights[rows, columns]
            product = mine * grad_weights[:, columns]
            grad_scores = product - mine * jnp.sum(product, axis=-1, keepdims=True)
            scores_low.append(grad_scores.astype(BF16))
            scores_turned.append(grad_scores.T.astype(BF16))
            weights_turned.append(mine.T.astype(BF16))
        grad_query = dot(jnp.concatenate(scores_low, axis=1), key) * SCALE
        grad_key = dot(jnp.concatenate(scores_turned, axis=1), query) * SCALE
        grad_value = dot(jnp.concatenate(weights_turned, axis=1), spread_heads(grad_rows))
        grad_project[rows, :D] = grad_query.astype(BF16)
        grad_project[rows, D : 2 * D] = grad_key.astype(BF16)
        grad_project[rows, 2 * D :] = grad_value.astype(BF16)

    acc_qkv[...] += dot_tn(normed_low[...], grad_project[...])
    acc_sum[...] += fold_rows(grad_project[...].astype(F32))

    @pl.when(step == pl.num_programs(0) - 1)
    def _():
        gain = jnp.broadcast_to(small_vector(small, GAIN_ONE, 2), (LANES, D)).T
        shift = jnp.broadcast_to(small_vector(small, SHIFT_ONE, 2), (LANES, D)).T
        sums = jnp.sum(acc_sum[...], axis=0, keepdims=True)
        grad_gain = jnp.zeros((D, LANES), F32)
        grad_shift = jnp.zeros((D, LANES), F32)
        per_row = 3 * D // LANES
        for j in range(per_row):
            columns = slice(j * LANES, (j + 1) * LANES)
            weight = w_qkv[:, columns].astype(F32)
            grad_gain += acc_qkv[:, columns] * weight
            grad_shift += sums[:, columns] * weight
            flat[pl.ds(j, D, stride=per_row), :] = (
                acc_qkv[:, columns] * gain + sums[:, columns] * shift
            )
        flat[ROW_OUT:, :] = first_in[...]
        grad_gain = jnp.sum(grad_gain.T, axis=0, keepdims=True)
        grad_shift = jnp.sum(grad_shift.T, axis=0, keepdims=True)
        late = jnp.concatenate([grad_gain, grad_shift, sums[:, :D], sums[:, 2 * D :]], axis=1)
        side = jnp.concatenate(
            [late[:, i * LANES : (i + 1) * LANES] for i in range(LATE_SMALL)]
            + [jnp.zeros((SIDE_ROWS - LATE_SMALL, LANES), F32)],
            axis=0,
        )
        wide[SHARE:SIDE, :] = jnp.zeros((SIDE - SHARE, LANES), F32)
        for target, out in enumerate((keep_out, send_out)):
            for p in range(PLANE):
                share = ids[target * PLANE + p]
                wide[:SHARE, :] = flat[pl.ds(share * SHARE, SHARE), :]
                wide[SIDE:, :] = jnp.where(share == 2 * PLANE - 1, side, 0.0)
                out[p] = wide[...].astype(out.dtype)


def input_grad_kernel(tok, grad_project, grad_middle, w_qkv, small, input_grad_out):
    normed, rate = normalize(tok[...].astype(F32))
    grad_normed = dot_nt(grad_project[...], w_qkv[...])
    gain = small_vector(small, GAIN_ONE, 2)
    input_grad_out[...] = grad_middle[...] + normalize_back(grad_normed, gain, normed, rate)


def stack_kernel(*refs):
    for d, ref in enumerate(refs[:-1]):
        refs[-1][d] = ref[...]


def add_core_kernel(first, first_in, rest, rest_in, keep_out, *refs):
    sends, column = refs[:-1], refs[-1]
    end = SMALL_IN_SHARE + LATE_SMALL
    for p, out in enumerate((keep_out, *sends)):
        item = first[p] + first_in[p].astype(F32)
        span = slice(p * (Z - 1), (p + 1) * (Z - 1))
        column[0] = item[:SHARE, :]
        column[1:] = rest[span] + rest_in[span].astype(F32)
        column[Z - 1, SMALL_IN_SHARE:end, :] += item[SIDE : SIDE + LATE_SMALL, :]
        out[...] = column[...].astype(out.dtype)


def add_plane_kernel(ids, kept, *refs):
    arrived = refs[: PLANE - 1]
    keep_out, *sends, column = refs[PLANE - 1 :]
    column[...] = kept[...] + sum(item[...].astype(F32) for item in arrived)
    keep_out[...] = column[ids[0]]
    for d, out in enumerate(sends):
        out[...] = column[lax.rem(ids[0] + d + 1, Z)].astype(BF16)


def add_column_kernel(kept, *refs):
    refs[-1][...] = kept[...] + sum(item[...].astype(F32) for item in refs[:-1])


def rows_spec(columns, rows=BLOCK):
    return pl.BlockSpec((rows, columns), lambda i: (i, 0))


def whole_spec(item):
    return pl.BlockSpec(item.shape, lambda i: (0,) * len(item.shape))


def like(*shape, kind=F32):
    return jax.ShapeDtypeStruct(shape, kind)


SMEM_SPEC = pl.BlockSpec(memory_space=pltpu.SMEM)
PARAMS = pltpu.CompilerParams(
    dimension_semantics=("arbitrary",), vmem_limit_bytes=VMEM_BYTES
)


def cost(us):
    return pl.CostEstimate(flops=int(us * 1e9), bytes_accessed=1 << 20, transcendentals=0)


def small_call(kernel, name, ids, inputs, outs, scratch=()):
    with_ids = ids is not None
    results = pl.pallas_call(
        kernel,
        in_specs=[SMEM_SPEC] * with_ids + [pl.BlockSpec(memory_space=pltpu.VMEM)] * len(inputs),
        out_specs=[pl.BlockSpec(memory_space=pltpu.VMEM)] * len(outs),
        out_shape=list(outs),
        scratch_shapes=list(scratch),
        compiler_params=pltpu.CompilerParams(vmem_limit_bytes=VMEM_BYTES),
        cost_estimate=cost(1),
        name=name,
    )(*([ids] if with_ids else []), *inputs)
    return results if len(outs) > 1 else results[0]


def attend(ids, segments, tokens, bufs):
    rows = tokens.shape[0]
    total = sum(buf.shape[0] * buf.shape[1] for buf in bufs)
    blocked = [
        like(rows, 3 * D, kind=BF16), like(rows, HEADS * SEQ), like(rows, D, kind=BF16),
        like(rows, D, kind=BF16),
    ]
    fixed = [
        like(D, 3 * D, kind=BF16), like(D, D, kind=BF16), like(D, FF, kind=BF16),
        like(FF, D, kind=BF16), like(SMALL_ROWS, LANES),
    ]
    return pl.pallas_call(
        functools.partial(attend_kernel, len(bufs)),
        grid=(rows // BLOCK,),
        in_specs=[
            SMEM_SPEC,
            pl.BlockSpec((BLOCK // SEQ, 1, SEQ), lambda i: (i, 0, 0)),
            rows_spec(D),
        ]
        + [whole_spec(buf) for buf in bufs],
        out_specs=[rows_spec(item.shape[1]) for item in blocked] + [whole_spec(item) for item in fixed],
        out_shape=blocked + fixed,
        scratch_shapes=[pltpu.VMEM((total, LANES), F32)],
        compiler_params=PARAMS,
        cost_estimate=cost(7),
        name="attend",
    )(ids, segments, tokens, *bufs)


def feed(ids, tokens, attended, cotangent, w_out, w_up, w_down, small, send_kind):
    rows = tokens.shape[0]
    small_rows = SMALL_ROWS - LATE_SMALL
    blocked = [
        like(rows, D), like(rows, FF, kind=BF16), like(rows, D), like(rows, D, kind=BF16),
    ]
    fixed = [
        like(PLANE * (Z - 1), SHARE, LANES),
        like(PLANE * (Z - 1), SHARE, LANES, kind=send_kind),
        like(HEAD_ROWS, LANES),
    ]
    return pl.pallas_call(
        feed_kernel,
        grid=(rows // WIDE,),
        in_specs=[SMEM_SPEC]
        + [rows_spec(D, WIDE)] * 3
        + [whole_spec(item) for item in (w_out, w_up, w_down, small)],
        out_specs=[rows_spec(item.shape[1], WIDE) for item in blocked]
        + [whole_spec(item) for item in fixed],
        out_shape=blocked + fixed,
        scratch_shapes=[
            pltpu.VMEM((WIDE, FF), BF16),
            pltpu.VMEM((D, D), F32),
            pltpu.VMEM((D, FF), F32),
            pltpu.VMEM((D, FF), F32),
            pltpu.VMEM((8, small_rows * LANES), F32),
            pltpu.VMEM((ROW_TOTAL - ROW_OUT, LANES), F32),
        ],
        compiler_params=PARAMS,
        cost_estimate=cost(10),
        name="feed",
    )(ids, tokens, attended, cotangent, w_out, w_up, w_down, small)


def result(middle, activated, w_down, small):
    rows = middle.shape[0]
    return pl.pallas_call(
        result_kernel,
        grid=(rows // BLOCK,),
        in_specs=[rows_spec(D), rows_spec(FF), whole_spec(w_down), whole_spec(small)],
        out_specs=rows_spec(D),
        out_shape=like(rows, D, kind=BF16),
        compiler_params=PARAMS,
        cost_estimate=cost(2),
        name="result",
    )(middle, activated, w_down, small)


def attend_back(ids, project, weights, grad_attended, normed_low, w_qkv, small, first, send_kind):
    rows = project.shape[0]
    fixed = [
        like(PLANE, SIDE + SIDE_ROWS, LANES),
        like(PLANE, SIDE + SIDE_ROWS, LANES, kind=send_kind),
    ]
    blocked = (project, weights, grad_attended, normed_low)
    return pl.pallas_call(
        attend_back_kernel,
        grid=(rows // BLOCK,),
        in_specs=[SMEM_SPEC]
        + [rows_spec(item.shape[1]) for item in blocked]
        + [whole_spec(item) for item in (w_qkv, small, first)],
        out_specs=[rows_spec(3 * D)] + [whole_spec(item) for item in fixed],
        out_shape=[like(rows, 3 * D, kind=BF16)] + fixed,
        scratch_shapes=[
            pltpu.VMEM((D, 3 * D), F32),
            pltpu.VMEM((8, 3 * D), F32),
            pltpu.VMEM((FIRST_ROWS, LANES), F32),
            pltpu.VMEM((SIDE + SIDE_ROWS, LANES), F32),
        ],
        compiler_params=PARAMS,
        cost_estimate=cost(6),
        name="attend_back",
    )(ids, *blocked, w_qkv, small, first)


def input_gradient(tokens, grad_project, grad_middle, w_qkv, small):
    rows = tokens.shape[0]
    blocked = (tokens, grad_project, grad_middle)
    return pl.pallas_call(
        input_grad_kernel,
        grid=(rows // BLOCK,),
        in_specs=[rows_spec(item.shape[1]) for item in blocked] + [whole_spec(w_qkv), whole_spec(small)],
        out_specs=rows_spec(D),
        out_shape=like(rows, D),
        compiler_params=PARAMS,
        cost_estimate=cost(3),
        name="input_grad",
    )(*blocked, w_qkv, small)


def block(tokens, segment_ids, cotangent, share_ids, shares, grad_ids, send_kind, core_exchange):
    segments = segment_ids.reshape(-1, 1, SEQ)
    project, weights, attended, normed_low, w_qkv, w_out, w_up, w_down, small = attend(
        share_ids, segments, tokens, shares
    )
    middle, activated, grad_middle, grad_attended, rest, rest_send, first_grad = feed(
        grad_ids, tokens, attended, cotangent, w_out, w_up, w_down, small, send_kind
    )
    rest_in = core_exchange(rest_send)
    grad_project, first, first_send = attend_back(
        grad_ids, project, weights, grad_attended, normed_low, w_qkv, small, first_grad, send_kind
    )
    first_in = core_exchange(first_send)
    outputs = result(middle, activated, w_down, small)
    input_grad = input_gradient(tokens, grad_project, grad_middle, w_qkv, small)
    return outputs, input_grad, first, first_in, rest, rest_in


def local_any(n, tokens, params, segment_ids, cotangent):
    gathered = lax.all_gather(params, "fsdp", axis=0)
    ids = jnp.arange(n, dtype=jnp.int32)
    order = jnp.array([p * 2 + c for c in range(2) for p in range(PLANE)], jnp.int32)
    outputs, input_grad, first, first_send, rest, rest_send = block(
        tokens, segment_ids, cotangent, ids, [gathered], order, F32, lambda values: values
    )
    first = jnp.stack([first, first_send], axis=1)
    rest = jnp.stack([rest, rest_send]).reshape(2, PLANE, Z - 1, SHARE, LANES).transpose(2, 1, 0, 3, 4)
    flat = jnp.concatenate(
        [
            first[:, :, :SHARE].reshape(-1, LANES),
            rest.reshape(-1, LANES),
            jnp.zeros((n * params.shape[0] - ROW_TOTAL, LANES), F32),
        ],
        axis=0,
    )
    flat = flat.at[ROW_SMALL : ROW_SMALL + LATE_SMALL].add(
        first[PLANE - 1, 1, SIDE : SIDE + LATE_SMALL]
    )
    param_grad = lax.psum_scatter(flat, "fsdp", scatter_dimension=0, tiled=True)
    return outputs, input_grad, param_grad


def index_of(z, plane, core):
    return (z * PLANE + plane) * 2 + core


def move(values, step_z, step_plane, step_core):
    pairs = [
        (index_of(z, p, c), index_of((z + step_z) % Z, p ^ step_plane, c ^ step_core))
        for z in range(Z)
        for p in range(PLANE)
        for c in range(2)
    ]
    return lax.ppermute(values, "fsdp", pairs)


def local_slice(tokens, params, segment_ids, cotangent):
    me = lax.axis_index("fsdp").astype(jnp.int32)
    z, plane, core = me // (2 * PLANE), (me // 2) % PLANE, me % 2
    planes = [(dc, dp) for dc in range(2) for dp in range(PLANE)]
    share_ids = jnp.stack(
        [index_of((z - dz) % Z, plane ^ dp, core ^ dc) for dc, dp in planes for dz in range(Z)]
    )
    grad_ids = jnp.stack([(plane ^ dp) * 2 + (core ^ dc) for dc, dp in planes])

    column = small_call(
        stack_kernel, "stack", None, [params] + [move(params, d, 0, 0) for d in range(1, Z)],
        [like(Z, SHARE, LANES, kind=BF16)],
    )
    same = [column] + [move(column, 0, d, 0) for d in range(1, PLANE)]
    shares = same + [move(item, 0, 0, 1) for item in same]
    outputs, input_grad, first, first_in, rest, rest_in = block(
        tokens, segment_ids, cotangent, share_ids, shares, grad_ids, BF16,
        lambda values: move(values, 0, 0, 1),
    )

    part = (Z, SHARE, LANES)
    kept, *sends = small_call(
        add_core_kernel, "add_core", None, [first, first_in, rest, rest_in],
        [like(*part)] + [like(*part, kind=BF16)] * (PLANE - 1), [pltpu.VMEM(part, F32)],
    )
    arrived = [move(item, 0, d + 1, 0) for d, item in enumerate(sends)]
    kept, *sends = small_call(
        add_plane_kernel, "add_plane", z.reshape(1), [kept] + arrived,
        [like(SHARE, LANES)] + [like(SHARE, LANES, kind=BF16)] * (Z - 1), [pltpu.VMEM(part, F32)],
    )
    arrived = [move(item, d + 1, 0, 0) for d, item in enumerate(sends)]
    param_grad = small_call(
        add_column_kernel, "add_column", None, [kept] + arrived, [like(SHARE, LANES)]
    )
    return outputs, input_grad, param_grad


def solution(mesh):
    n = mesh.shape["fsdp"]
    local = local_slice if n == 2 * PLANE * Z else functools.partial(local_any, n)
    in_specs = (P("fsdp", None), P("fsdp", None), P("fsdp"), P("fsdp", None))
    out_specs = (P("fsdp", None), P("fsdp", None), P("fsdp", None))
    return jax.shard_map(local, mesh=mesh, in_specs=in_specs, out_specs=out_specs, check_vma=False)
```

```python
import functools

import jax
import jax.numpy as jnp
from jax import lax
from jax.experimental import pallas as pl
from jax.experimental.pallas import tpu as pltpu
from jax.sharding import PartitionSpec as P

D = 256
HEADS = 4
HEAD_DIM = 64
FF = 1024
SEQ = 128
LANES = 128
GROUP = 4
WIDE = GROUP * SEQ
CHUNK = 256
STRIP = 64
EPSILON = 1e-05
SCALE = HEAD_DIM ** (-0.5)
VMEM_BYTES = 24 * 1024 * 1024

ROW_QKV = 0
ROW_OUT = 1536
ROW_UP = 2048
ROW_DOWN = 4096
ROW_SMALL = 6144
ROW_END = 6168
ROW_TOTAL = 6176
GAIN_ONE, SHIFT_ONE, BIAS_QUERY, BIAS_VALUE, BIAS_OUT = 0, 2, 4, 6, 8
GAIN_TWO, SHIFT_TWO, BIAS_UP, BIAS_DOWN = 10, 12, 14, 22
SMALL_ROWS = 24
LATE_SMALL = 8

SHARE = 193
Z, PLANE = 4, 4
FIRST_ROWS = 2 * PLANE * SHARE
HEAD_ROWS = FIRST_ROWS - ROW_OUT
SIDE, SIDE_ROWS = 208, 16
SMALL_IN_SHARE = ROW_SMALL - (2 * PLANE * Z - 1) * SHARE

F32 = jnp.float32
BF16 = jnp.bfloat16


def dot(left, right):
    return jnp.dot(left, right, preferred_element_type=F32)


def dot_nt(left, right):
    return lax.dot_general(left, right, (((1,), (1,)), ((), ())), preferred_element_type=F32)


def dot_tn(left, right):
    return lax.dot_general(left, right, (((0,), (0,)), ((), ())), preferred_element_type=F32)


def small_vector(small, row, count):
    return jnp.concatenate([small[row + i : row + i + 1, :] for i in range(count)], axis=1)


def fold_rows(values):
    rows, columns = values.shape
    return jnp.sum(values.reshape(rows // 8, 8, columns), axis=0)


def normalize(values):
    center = values - jnp.mean(values, axis=-1, keepdims=True)
    rate = lax.rsqrt(jnp.mean(center * center, axis=-1, keepdims=True) + EPSILON)
    return center * rate, rate


def normalize_back(grad, gain, normed, rate):
    scaled = grad * gain
    return rate * (
        scaled
        - jnp.mean(scaled, axis=-1, keepdims=True)
        - normed * jnp.mean(scaled * normed, axis=-1, keepdims=True)
    )


def head_masks():
    lane = lax.broadcasted_iota(jnp.int32, (1, D), 1)
    return [(lane // HEAD_DIM == h).astype(F32).astype(BF16) for h in range(HEADS)]


def spread_heads(rows):
    return jnp.concatenate([rows * mask for mask in head_masks()], axis=0)


def matrix_from_flat(flat, start, rows, columns, out):
    per_row = columns // LANES
    for j in range(per_row):
        out[:, j * LANES : (j + 1) * LANES] = flat[
            pl.ds(start + j, rows, stride=per_row), :
        ].astype(BF16)


def turned_to_flat(turned, rows, columns, flat, start):
    per_row = columns // LANES
    for j in range(per_row):
        flat[pl.ds(start + j, rows, stride=per_row), :] = turned[j * LANES : (j + 1) * LANES, :].T


def matrix_to_flat(matrix, rows, columns, flat, start):
    per_row = columns // LANES
    for j in range(per_row):
        flat[pl.ds(start + j, rows, stride=per_row), :] = matrix[:, j * LANES : (j + 1) * LANES]


def prepare_kernel(tok, cot, params, normed_out, normed_turned, cot_turned, own):
    normed, _ = normalize(tok[...].astype(F32))
    normed_out[...] = normed
    normed_turned[...] = normed.astype(BF16).T
    cot_turned[...] = cot[...].T
    own[...] = params[...]


def unpack(ids, bufs, flat):
    slot = 0
    for buf in bufs:
        count, rows, _ = buf.shape

        def place(i, carry, buf=buf, slot=slot, rows=rows):
            flat[pl.ds(ids[slot + i] * rows, rows), :] = buf[i].astype(F32)
            return carry

        lax.fori_loop(0, count, place, 0)
        slot += count


def attend_kernel(n_bufs, ids, seg, normed, *refs):
    bufs = refs[:n_bufs]
    (
        project_out, weights_out, attended_out, w_qkv, w_out, w_up, w_down, small, flat,
    ) = refs[n_bufs:]
    unpack(ids, bufs, flat)
    matrix_from_flat(flat, ROW_QKV, D, 3 * D, w_qkv)
    matrix_from_flat(flat, ROW_OUT, D, D, w_out)
    matrix_from_flat(flat, ROW_UP, D, FF, w_up)
    matrix_from_flat(flat, ROW_DOWN, FF, D, w_down)
    small[...] = flat[ROW_SMALL:ROW_END, :]

    gain = small_vector(small, GAIN_ONE, 2)
    shift = small_vector(small, SHIFT_ONE, 2)
    bias = jnp.concatenate(
        [
            small_vector(small, BIAS_QUERY, 2),
            jnp.zeros((1, D), F32),
            small_vector(small, BIAS_VALUE, 2),
        ],
        axis=1,
    )
    causal = lax.broadcasted_iota(jnp.int32, (SEQ, SEQ), 1) <= lax.broadcasted_iota(
        jnp.int32, (SEQ, SEQ), 0
    )

    def some(g, carry):
        span = pl.ds(pl.multiple_of(g * WIDE, WIDE), WIDE)
        normed_low = (normed[span, :] * gain + shift).astype(BF16)
        project = (dot(normed_low, w_qkv[...]) + bias).astype(BF16)
        project_out[span, :] = project
        scores, values, allowed = [], [], []
        for s in range(GROUP):
            rows = slice(s * SEQ, (s + 1) * SEQ)
            across = jnp.broadcast_to(seg[pl.ds(g * GROUP + s, 1), :].astype(F32), (SEQ, SEQ))
            allowed.append(causal & (across == across.T))
            scores.append(
                dot_nt(project[rows, :D] * SCALE, spread_heads(project[rows, D : 2 * D]))
            )
            values.append(spread_heads(project[rows, 2 * D :]))
        weights = []
        for s in range(GROUP):
            low = []
            for h in range(HEADS):
                mine = jnp.where(allowed[s], scores[s][:, h * SEQ : (h + 1) * SEQ], -1e30)
                grown = jnp.exp(mine - jnp.max(mine, axis=-1, keepdims=True))
                low.append(
                    (grown * (1.0 / jnp.sum(grown, axis=-1, keepdims=True))).astype(BF16)
                )
            weights.append(jnp.concatenate(low, axis=1))
        weights_out[span, :] = jnp.concatenate(weights, axis=0)
        attended_out[span, :] = jnp.concatenate(
            [dot(weights[s], values[s]).astype(BF16) for s in range(GROUP)], axis=0
        )
        return carry

    lax.fori_loop(0, normed.shape[0] // WIDE, some, 0)


def feed_kernel(
    ids, tok, attended, cot, cot_turned, w_out, w_up, w_down, small,
    middle_out, activated_out, grad_middle_out, grad_attended_out, keep_out, send_out, first_out,
    normed_low_all, grad_hidden, grad_middle_low_all, acc_small, flat,
):
    acc_small[...] = jnp.zeros_like(acc_small)
    gain = small_vector(small, GAIN_TWO, 2)
    shift = small_vector(small, SHIFT_TWO, 2)
    bias_out = small_vector(small, BIAS_OUT, 2)
    slope = 0.7978845608028654
    cubic = slope * 0.044715

    def some(g, carry):
        base = pl.multiple_of(g * WIDE, WIDE)
        span = pl.ds(base, WIDE)
        middle = tok[span, :].astype(F32) + dot(attended[span, :], w_out[...]) + bias_out
        middle_out[span, :] = middle
        normed, rate = normalize(middle)
        normed_low = (normed * gain + shift).astype(BF16)
        normed_low_all[span, :] = normed_low
        cotangent = cot[span, :]
        for c in range(0, FF, CHUNK):
            columns = slice(c, c + CHUNK)
            bias = small_vector(small, BIAS_UP + c // LANES, CHUNK // LANES)
            hidden_all = dot(normed_low, w_up[:, columns])
            grad_all = dot_nt(cotangent, w_down[columns, :])
            total = jnp.zeros((8, CHUNK), F32)
            for r in range(0, WIDE, STRIP):
                rows = slice(r, r + STRIP)
                strip = pl.ds(pl.multiple_of(base + r, STRIP), STRIP)
                hidden = hidden_all[rows] + bias
                square = hidden * hidden
                half = 0.5 + 0.5 * jnp.tanh(hidden * (slope + cubic * square))
                activated = hidden * half
                derivative = half + activated * (1.0 - half) * (2 * slope + (6 * cubic) * square)
                low = (grad_all[rows] * derivative).astype(BF16)
                activated_out[strip, columns] = activated.astype(BF16)
                grad_hidden[strip, columns] = low
                total += fold_rows(low.astype(F32))
            acc_small[:, 3 * D + c : 3 * D + c + CHUNK] += total
        grad_result = cotangent.astype(F32)
        grad_normed = dot_nt(grad_hidden[span, :], w_up[...])
        grad_middle = grad_result + normalize_back(grad_normed, gain, normed, rate)
        grad_middle_out[span, :] = grad_middle
        grad_middle_low = grad_middle.astype(BF16)
        grad_middle_low_all[span, :] = grad_middle_low
        grad_attended_out[span, :] = dot_nt(grad_middle_low, w_out[...]).astype(BF16)
        acc_small[:, 0:D] += fold_rows(grad_middle_low.astype(F32))
        acc_small[:, D : 2 * D] += fold_rows(grad_normed * normed)
        acc_small[:, 2 * D : 3 * D] += fold_rows(grad_normed)
        acc_small[:, 3 * D + FF :] += fold_rows(grad_result)
        return carry

    lax.fori_loop(0, tok.shape[0] // WIDE, some, 0)
    turned_to_flat(dot(cot_turned[...], activated_out[...]), FF, D, flat, ROW_DOWN - ROW_OUT)
    matrix_to_flat(dot_tn(normed_low_all[...], grad_hidden[...]), D, FF, flat, ROW_UP - ROW_OUT)
    matrix_to_flat(dot_tn(attended[...], grad_middle_low_all[...]), D, D, flat, 0)
    sums = jnp.sum(acc_small[...], axis=0, keepdims=True)
    base = ROW_SMALL - ROW_OUT
    flat[base : base + LATE_SMALL, :] = jnp.zeros((LATE_SMALL, LANES), F32)
    for i in range(sums.shape[1] // LANES):
        row = base + LATE_SMALL + i
        flat[row : row + 1, :] = sums[:, i * LANES : (i + 1) * LANES]
    flat[ROW_END - ROW_OUT :, :] = jnp.zeros((ROW_TOTAL - ROW_END, LANES), F32)
    first_out[...] = flat[:HEAD_ROWS, :]
    for target, out in enumerate((keep_out, send_out)):
        for p in range(PLANE):
            for z in range(1, Z):
                share = ids[target * PLANE + p] + z * 2 * PLANE
                rows = flat[pl.ds(share * SHARE - ROW_OUT, SHARE), :]
                out[p * (Z - 1) + z - 1] = rows.astype(out.dtype)


def result_kernel(middle, activated, w_down, small, result_out):
    result = middle[...] + dot(activated[...], w_down[...]) + small_vector(small, BIAS_DOWN, 2)
    result_out[...] = result.astype(BF16)


def attend_back_kernel(
    ids, project, weights, grad_attended, normed_turned, w_qkv, small, first_in,
    grad_project, keep_out, send_out, flat, wide,
):
    def some(g, carry):
        base = g * WIDE
        spans = [pl.ds(pl.multiple_of(base + s * SEQ, SEQ), SEQ) for s in range(GROUP)]
        grad_weights = [
            dot_nt(grad_attended[span, :], spread_heads(project[span, 2 * D :])) for span in spans
        ]
        scores_low, scores_turned, weights_turned = [], [], []
        for s, span in enumerate(spans):
            low, turned, mine_turned = [], [], []
            for h in range(HEADS):
                columns = slice(h * SEQ, (h + 1) * SEQ)
                mine_low = weights[span, columns]
                mine = mine_low.astype(F32)
                product = mine * grad_weights[s][:, columns]
                grad_scores = (product - mine * jnp.sum(product, axis=-1, keepdims=True)) * SCALE
                low.append(grad_scores.astype(BF16))
                turned.append(low[-1].T)
                mine_turned.append(mine_low.T)
            scores_low.append(jnp.concatenate(low, axis=1))
            scores_turned.append(jnp.concatenate(turned, axis=1))
            weights_turned.append(jnp.concatenate(mine_turned, axis=1))
        for s, span in enumerate(spans):
            key = spread_heads(project[span, D : 2 * D])
            grad_project[span, :D] = dot(scores_low[s], key).astype(BF16)
            query = spread_heads(project[span, :D])
            grad_project[span, D : 2 * D] = dot(scores_turned[s], query).astype(BF16)
            grad_value = dot(weights_turned[s], spread_heads(grad_attended[span, :]))
            grad_project[span, 2 * D :] = grad_value.astype(BF16)
        return carry

    lax.fori_loop(0, project.shape[0] // WIDE, some, 0)
    products = dot(normed_turned[...], grad_project[...])
    sums = jnp.sum(fold_rows(grad_project[...].astype(F32)), axis=0, keepdims=True)
    gain = jnp.broadcast_to(small_vector(small, GAIN_ONE, 2), (LANES, D)).T
    shift = jnp.broadcast_to(small_vector(small, SHIFT_ONE, 2), (LANES, D)).T
    grad_gain = jnp.zeros((D, LANES), F32)
    grad_shift = jnp.zeros((D, LANES), F32)
    per_row = 3 * D // LANES
    for j in range(per_row):
        columns = slice(j * LANES, (j + 1) * LANES)
        weight = w_qkv[:, columns].astype(F32)
        grad_gain += products[:, columns] * weight
        grad_shift += sums[:, columns] * weight
        flat[pl.ds(j, D, stride=per_row), :] = products[:, columns] * gain + sums[:, columns] * shift
    flat[ROW_OUT:, :] = first_in[...]
    grad_gain = jnp.sum(grad_gain.T, axis=0, keepdims=True)
    grad_shift = jnp.sum(grad_shift.T, axis=0, keepdims=True)
    late = jnp.concatenate([grad_gain, grad_shift, sums[:, :D], sums[:, 2 * D :]], axis=1)
    side = jnp.concatenate(
        [late[:, i * LANES : (i + 1) * LANES] for i in range(LATE_SMALL)]
        + [jnp.zeros((SIDE_ROWS - LATE_SMALL, LANES), F32)],
        axis=0,
    )
    wide[SHARE:SIDE, :] = jnp.zeros((SIDE - SHARE, LANES), F32)
    for target, out in enumerate((keep_out, send_out)):
        for p in range(PLANE):
            share = ids[target * PLANE + p]
            wide[:SHARE, :] = flat[pl.ds(share * SHARE, SHARE), :]
            wide[SIDE:, :] = jnp.where(share == 2 * PLANE - 1, side, 0.0)
            out[p] = wide[...].astype(out.dtype)


def input_grad_kernel(tok, grad_project, grad_middle, w_qkv, small, input_grad_out):
    gain = small_vector(small, GAIN_ONE, 2)

    def some(g, carry):
        span = pl.ds(pl.multiple_of(g * WIDE, WIDE), WIDE)
        normed, rate = normalize(tok[span, :].astype(F32))
        grad_normed = dot_nt(grad_project[span, :], w_qkv[...])
        input_grad_out[span, :] = grad_middle[span, :] + normalize_back(
            grad_normed, gain, normed, rate
        )
        return carry

    lax.fori_loop(0, tok.shape[0] // WIDE, some, 0)


def stack_kernel(*refs):
    for d, ref in enumerate(refs[:-1]):
        refs[-1][d] = ref[...]


def add_core_kernel(first, first_in, rest, rest_in, keep_out, *refs):
    sends, column = refs[:-1], refs[-1]
    end = SMALL_IN_SHARE + LATE_SMALL
    for p, out in enumerate((keep_out, *sends)):
        item = first[p] + first_in[p].astype(F32)
        span = slice(p * (Z - 1), (p + 1) * (Z - 1))
        column[0] = item[:SHARE, :]
        column[1:] = rest[span] + rest_in[span].astype(F32)
        column[Z - 1, SMALL_IN_SHARE:end, :] += item[SIDE : SIDE + LATE_SMALL, :]
        out[...] = column[...].astype(out.dtype)


def add_plane_kernel(ids, kept, *refs):
    arrived = refs[: PLANE - 1]
    keep_out, *sends, column = refs[PLANE - 1 :]
    column[...] = kept[...] + sum(item[...].astype(F32) for item in arrived)
    keep_out[...] = column[ids[0]]
    for d, out in enumerate(sends):
        out[...] = column[lax.rem(ids[0] + d + 1, Z)].astype(BF16)


def add_column_kernel(kept, *refs):
    refs[-1][...] = kept[...] + sum(item[...].astype(F32) for item in refs[:-1])


def like(*shape, kind=F32):
    return jax.ShapeDtypeStruct(shape, kind)


SMEM_SPEC = pl.BlockSpec(memory_space=pltpu.SMEM)
VMEM_SPEC = pl.BlockSpec(memory_space=pltpu.VMEM)

def cost(us):
    return pl.CostEstimate(flops=int(us * 1e9), bytes_accessed=1 << 20, transcendentals=0)


def call(kernel, name, ids, inputs, outs, scratch=(), us=1):
    with_ids = ids is not None
    results = pl.pallas_call(
        kernel,
        in_specs=[SMEM_SPEC] * with_ids + [VMEM_SPEC] * len(inputs),
        out_specs=[VMEM_SPEC] * len(outs),
        out_shape=list(outs),
        scratch_shapes=list(scratch),
        compiler_params=pltpu.CompilerParams(vmem_limit_bytes=VMEM_BYTES),
        cost_estimate=cost(us),
        name=name,
    )(*([ids] if with_ids else []), *inputs)
    return results if len(outs) > 1 else results[0]


def prepare(tokens, cotangent, params):
    rows = tokens.shape[0]
    turned = like(D, rows, kind=BF16)
    return call(
        prepare_kernel, "prepare", None, [tokens, cotangent, params],
        [like(rows, D), turned, turned, like(*params.shape, kind=BF16)], us=2,
    )


def attend(ids, segments, normed, bufs):
    rows = normed.shape[0]
    total = sum(buf.shape[0] * buf.shape[1] for buf in bufs)
    shapes = [
        (rows, 3 * D), (rows, HEADS * SEQ), (rows, D), (D, 3 * D), (D, D), (D, FF), (FF, D),
    ]
    return call(
        functools.partial(attend_kernel, len(bufs)), "attend", ids, [segments, normed, *bufs],
        [like(*shape, kind=BF16) for shape in shapes] + [like(SMALL_ROWS, LANES)],
        [pltpu.VMEM((total, LANES), F32)], us=6,
    )


def feed(ids, tokens, attended, cotangent, cot_turned, w_out, w_up, w_down, small, send_kind):
    rows = tokens.shape[0]
    return call(
        feed_kernel, "feed", ids,
        [tokens, attended, cotangent, cot_turned, w_out, w_up, w_down, small],
        [
            like(rows, D),
            like(rows, FF, kind=BF16),
            like(rows, D),
            like(rows, D, kind=BF16),
            like(PLANE * (Z - 1), SHARE, LANES),
            like(PLANE * (Z - 1), SHARE, LANES, kind=send_kind),
            like(HEAD_ROWS, LANES),
        ],
        [
            pltpu.VMEM((rows, D), BF16),
            pltpu.VMEM((rows, FF), BF16),
            pltpu.VMEM((rows, D), BF16),
            pltpu.VMEM((8, (SMALL_ROWS - LATE_SMALL) * LANES), F32),
            pltpu.VMEM((ROW_TOTAL - ROW_OUT, LANES), F32),
        ],
        us=8,
    )


def result(middle, activated, w_down, small):
    return call(
        result_kernel, "result", None, [middle, activated, w_down, small],
        [like(*middle.shape, kind=BF16)], us=2,
    )


def attend_back(ids, project, weights, grad_attended, normed_turned, w_qkv, small, first, send_kind):
    shape = (PLANE, SIDE + SIDE_ROWS, LANES)
    return call(
        attend_back_kernel, "attend_back", ids,
        [project, weights, grad_attended, normed_turned, w_qkv, small, first],
        [like(*project.shape, kind=BF16), like(*shape), like(*shape, kind=send_kind)],
        [pltpu.VMEM((FIRST_ROWS, LANES), F32), pltpu.VMEM(shape[1:], F32)], us=5,
    )


def input_gradient(tokens, grad_project, grad_middle, w_qkv, small):
    return call(
        input_grad_kernel, "input_grad", None, [tokens, grad_project, grad_middle, w_qkv, small],
        [like(*tokens.shape)], us=2,
    )


def block(prepared, tokens, segment_ids, cotangent, share_ids, shares, grad_ids, send_kind, core_exchange):
    normed, normed_turned, cot_turned = prepared
    segments = segment_ids.reshape(-1, SEQ)
    project, weights, attended, w_qkv, w_out, w_up, w_down, small = attend(
        share_ids, segments, normed, shares
    )
    middle, activated, grad_middle, grad_attended, rest, rest_send, first_grad = feed(
        grad_ids, tokens, attended, cotangent, cot_turned, w_out, w_up, w_down, small, send_kind
    )
    rest_in = core_exchange(rest_send)
    grad_project, first, first_send = attend_back(
        grad_ids, project, weights, grad_attended, normed_turned, w_qkv, small, first_grad, send_kind
    )
    first_in = core_exchange(first_send)
    outputs = result(middle, activated, w_down, small)
    input_grad = input_gradient(tokens, grad_project, grad_middle, w_qkv, small)
    return outputs, input_grad, first, first_in, rest, rest_in


def local_any(n, tokens, params, segment_ids, cotangent):
    *prepared, _ = prepare(tokens, cotangent, params)
    gathered = lax.all_gather(params, "fsdp", axis=0)
    ids = jnp.arange(n, dtype=jnp.int32)
    order = jnp.array([p * 2 + c for c in range(2) for p in range(PLANE)], jnp.int32)
    outputs, input_grad, first, first_send, rest, rest_send = block(
        prepared, tokens, segment_ids, cotangent, ids, [gathered], order, F32, lambda values: values
    )
    first = jnp.stack([first, first_send], axis=1)
    rest = jnp.stack([rest, rest_send]).reshape(2, PLANE, Z - 1, SHARE, LANES).transpose(2, 1, 0, 3, 4)
    flat = jnp.concatenate(
        [
            first[:, :, :SHARE].reshape(-1, LANES),
            rest.reshape(-1, LANES),
            jnp.zeros((n * params.shape[0] - ROW_TOTAL, LANES), F32),
        ],
        axis=0,
    )
    flat = flat.at[ROW_SMALL : ROW_SMALL + LATE_SMALL].add(
        first[PLANE - 1, 1, SIDE : SIDE + LATE_SMALL]
    )
    param_grad = lax.psum_scatter(flat, "fsdp", scatter_dimension=0, tiled=True)
    return outputs, input_grad, param_grad


def index_of(z, plane, core):
    return (z * PLANE + plane) * 2 + core


def move(values, step_z, step_plane, step_core):
    pairs = [
        (index_of(z, p, c), index_of((z + step_z) % Z, p ^ step_plane, c ^ step_core))
        for z in range(Z)
        for p in range(PLANE)
        for c in range(2)
    ]
    return lax.ppermute(values, "fsdp", pairs)


def local_slice(tokens, params, segment_ids, cotangent):
    me = lax.axis_index("fsdp").astype(jnp.int32)
    z, plane, core = me // (2 * PLANE), (me // 2) % PLANE, me % 2
    planes = [(dc, dp) for dc in range(2) for dp in range(PLANE)]
    share_ids = jnp.stack(
        [index_of((z - dz) % Z, plane ^ dp, core ^ dc) for dc, dp in planes for dz in range(Z)]
    )
    grad_ids = jnp.stack([(plane ^ dp) * 2 + (core ^ dc) for dc, dp in planes])

    *prepared, own = prepare(tokens, cotangent, params)
    column = call(
        stack_kernel, "stack", None, [own] + [move(params, d, 0, 0) for d in range(1, Z)],
        [like(Z, SHARE, LANES, kind=BF16)],
    )
    same = [column] + [move(column, 0, d, 0) for d in range(1, PLANE)]
    shares = same + [move(item, 0, 0, 1) for item in same]
    outputs, input_grad, first, first_in, rest, rest_in = block(
        prepared, tokens, segment_ids, cotangent, share_ids, shares, grad_ids, BF16,
        lambda values: move(values, 0, 0, 1),
    )

    part = (Z, SHARE, LANES)
    kept, *sends = call(
        add_core_kernel, "add_core", None, [first, first_in, rest, rest_in],
        [like(*part)] + [like(*part, kind=BF16)] * (PLANE - 1), [pltpu.VMEM(part, F32)],
    )
    arrived = [move(item, 0, d + 1, 0) for d, item in enumerate(sends)]
    kept, *sends = call(
        add_plane_kernel, "add_plane", z.reshape(1), [kept] + arrived,
        [like(SHARE, LANES)] + [like(SHARE, LANES, kind=BF16)] * (Z - 1), [pltpu.VMEM(part, F32)],
    )
    arrived = [move(item, d + 1, 0, 0) for d, item in enumerate(sends)]
    param_grad = call(
        add_column_kernel, "add_column", None, [kept] + arrived, [like(SHARE, LANES)]
    )
    return outputs, input_grad, param_grad


def solution(mesh):
    n = mesh.shape["fsdp"]
    local = local_slice if n == 2 * PLANE * Z else functools.partial(local_any, n)
    in_specs = (P("fsdp", None), P("fsdp", None), P("fsdp"), P("fsdp", None))
    out_specs = (P("fsdp", None), P("fsdp", None), P("fsdp", None))
    return jax.shard_map(local, mesh=mesh, in_specs=in_specs, out_specs=out_specs, check_vma=False)
```

```python
import functools

import jax
import jax.numpy as jnp
from jax import lax
from jax.experimental import pallas as pl
from jax.experimental.pallas import tpu as pltpu
from jax.sharding import PartitionSpec as P

D = 256
HEADS = 4
HEAD_DIM = 64
FF = 1024
SEQ = 128
LANES = 128
GROUP = 4
WIDE = GROUP * SEQ
CHUNK = 256
STRIP = 64
EPSILON = 1e-05
SCALE = HEAD_DIM ** (-0.5)
VMEM_BYTES = 24 * 1024 * 1024

ROW_QKV = 0
ROW_OUT = 1536
ROW_UP = 2048
ROW_DOWN = 4096
ROW_SMALL = 6144
ROW_END = 6168
ROW_TOTAL = 6176
GAIN_ONE, SHIFT_ONE, BIAS_QUERY, BIAS_VALUE, BIAS_OUT = 0, 2, 4, 6, 8
GAIN_TWO, SHIFT_TWO, BIAS_UP, BIAS_DOWN = 10, 12, 14, 22
SMALL_ROWS = 32
LATE_SMALL = 8

SHARE = 193
Z, PLANE = 4, 4
FIRST_ROWS = 2 * PLANE * SHARE
HEAD_ROWS = FIRST_ROWS - ROW_OUT
SIDE, SIDE_ROWS = 208, 16
SMALL_IN_SHARE = ROW_SMALL - (2 * PLANE * Z - 1) * SHARE

F32 = jnp.float32
BF16 = jnp.bfloat16


def dot(left, right):
    return jnp.dot(left, right, preferred_element_type=F32)


def dot_nt(left, right):
    return lax.dot_general(left, right, (((1,), (1,)), ((), ())), preferred_element_type=F32)


def dot_tn(left, right):
    return lax.dot_general(left, right, (((0,), (0,)), ((), ())), preferred_element_type=F32)


def small_vector(small, row, count):
    return jnp.concatenate([small[row + i : row + i + 1, :] for i in range(count)], axis=1)


def fold_rows(values):
    rows, columns = values.shape
    return jnp.sum(values.reshape(rows // 8, 8, columns), axis=0)


def normalize(values):
    center = values - jnp.mean(values, axis=-1, keepdims=True)
    rate = lax.rsqrt(jnp.mean(center * center, axis=-1, keepdims=True) + EPSILON)
    return center * rate, rate


def normalize_back(grad, gain, normed, rate):
    scaled = grad * gain
    return rate * (
        scaled
        - jnp.mean(scaled, axis=-1, keepdims=True)
        - normed * jnp.mean(scaled * normed, axis=-1, keepdims=True)
    )


def head_masks():
    lane = lax.broadcasted_iota(jnp.int32, (1, D), 1)
    return [(lane // HEAD_DIM == h).astype(F32).astype(BF16) for h in range(HEADS)]


def spread_heads(rows):
    return jnp.concatenate([rows * mask for mask in head_masks()], axis=0)


def matrix_from_flat(flat, start, rows, columns, out):
    per_row = columns // LANES
    for j in range(per_row):
        out[:, j * LANES : (j + 1) * LANES] = flat[
            pl.ds(start + j, rows, stride=per_row), :
        ].astype(BF16)


def turned_to_flat(turned, rows, columns, flat, start):
    per_row = columns // LANES
    for j in range(per_row):
        flat[pl.ds(start + j, rows, stride=per_row), :] = turned[j * LANES : (j + 1) * LANES, :].T


def matrix_to_flat(matrix, rows, columns, flat, start):
    per_row = columns // LANES
    for j in range(per_row):
        flat[pl.ds(start + j, rows, stride=per_row), :] = matrix[:, j * LANES : (j + 1) * LANES]


def prepare_kernel(tok, params, normed_out, normed_turned, own):
    normed, _ = normalize(tok[...].astype(F32))
    normed_out[...] = normed
    normed_turned[...] = normed.astype(BF16).T
    own[...] = params[...]


def sort_kernel(ids, *refs):
    received, (first, rest, stage, wide) = refs[:Z], refs[Z:]
    for d in range(Z):
        stage[lax.rem(ids[0] + Z - d, Z)] = received[d][...]
    rest[...] = stage[1:]
    wide[:SHARE, :] = stage[0].astype(F32)
    wide[SHARE:SIDE, :] = jnp.zeros((SIDE - SHARE, LANES), F32)
    last = stage[Z - 1].astype(F32)
    wide[SIDE:, :] = last[SMALL_IN_SHARE:, :]
    first[...] = wide[...].astype(BF16)


def attend_kernel(ids, seg, normed, *refs):
    bufs = refs[: 2 * PLANE]
    project_out, weights_out, attended_out, w_qkv, small, first_out, flat = refs[2 * PLANE :]
    for slot, buf in enumerate(bufs):
        wide = buf[...].astype(F32)
        flat[pl.ds(ids[slot] * SHARE, SHARE), :] = wide[:SHARE, :]

        @pl.when(ids[slot] == 2 * PLANE - 1)
        def _():
            small[...] = wide[SIDE:, :]

    matrix_from_flat(flat, ROW_QKV, D, 3 * D, w_qkv)
    first_out[...] = flat[ROW_OUT:FIRST_ROWS, :]

    gain = small_vector(small, GAIN_ONE, 2)
    shift = small_vector(small, SHIFT_ONE, 2)
    bias = jnp.concatenate(
        [
            small_vector(small, BIAS_QUERY, 2),
            jnp.zeros((1, D), F32),
            small_vector(small, BIAS_VALUE, 2),
        ],
        axis=1,
    )
    causal = lax.broadcasted_iota(jnp.int32, (SEQ, SEQ), 1) <= lax.broadcasted_iota(
        jnp.int32, (SEQ, SEQ), 0
    )

    def some(g, carry):
        span = pl.ds(pl.multiple_of(g * WIDE, WIDE), WIDE)
        normed_low = (normed[span, :] * gain + shift).astype(BF16)
        project = (dot(normed_low, w_qkv[...]) + bias).astype(BF16)
        project_out[span, :] = project
        scores, values, allowed = [], [], []
        for s in range(GROUP):
            rows = slice(s * SEQ, (s + 1) * SEQ)
            across = jnp.broadcast_to(seg[pl.ds(g * GROUP + s, 1), :].astype(F32), (SEQ, SEQ))
            allowed.append(causal & (across == across.T))
            scores.append(
                dot_nt(project[rows, :D] * SCALE, spread_heads(project[rows, D : 2 * D]))
            )
            values.append(spread_heads(project[rows, 2 * D :]))
        weights = []
        for s in range(GROUP):
            low = []
            for h in range(HEADS):
                mine = jnp.where(allowed[s], scores[s][:, h * SEQ : (h + 1) * SEQ], -1e30)
                grown = jnp.exp(mine - jnp.max(mine, axis=-1, keepdims=True))
                low.append(
                    (grown * (1.0 / jnp.sum(grown, axis=-1, keepdims=True))).astype(BF16)
                )
            weights.append(jnp.concatenate(low, axis=1))
        weights_out[span, :] = jnp.concatenate(weights, axis=0)
        attended_out[span, :] = jnp.concatenate(
            [dot(weights[s], values[s]).astype(BF16) for s in range(GROUP)], axis=0
        )
        return carry

    lax.fori_loop(0, normed.shape[0] // WIDE, some, 0)


def feed_kernel(
    ids, tok, attended, cot, small, first_in, *refs,
):
    bufs = refs[: 2 * PLANE]
    (
        middle_out, activated_out, grad_middle_out, grad_attended_out, w_down, keep_out, send_out, first_out,
        w_out, w_up, grad_hidden, flat,
    ) = refs[2 * PLANE :]
    flat[:HEAD_ROWS, :] = first_in[...]
    for slot, buf in enumerate(bufs):
        for z in range(1, Z):
            share = ids[slot] + z * 2 * PLANE
            flat[pl.ds(share * SHARE - ROW_OUT, SHARE), :] = buf[z - 1].astype(F32)
    matrix_from_flat(flat, 0, D, D, w_out)
    matrix_from_flat(flat, ROW_UP - ROW_OUT, D, FF, w_up)
    matrix_from_flat(flat, ROW_DOWN - ROW_OUT, FF, D, w_down)

    gain = small_vector(small, GAIN_TWO, 2)
    middle = (
        tok[...].astype(F32) + dot(attended[...], w_out[...]) + small_vector(small, BIAS_OUT, 2)
    )
    middle_out[...] = middle
    normed, rate = normalize(middle)
    normed_low = (normed * gain + small_vector(small, SHIFT_TWO, 2)).astype(BF16)
    normed_turned = normed_low.T
    cotangent = cot[...]
    cot_turned = cotangent.T
    slope = 0.7978845608028654
    cubic = slope * 0.044715
    row_up, row_down = ROW_UP - ROW_OUT, ROW_DOWN - ROW_OUT

    def products(c):
        columns = slice(c, c + CHUNK)
        return dot(normed_low, w_up[:, columns]), dot_nt(cotangent, w_down[columns, :])

    def bend(c, hidden_all, grad_all):
        columns = slice(c, c + CHUNK)
        bias = small_vector(small, BIAS_UP + c // LANES, CHUNK // LANES)
        total = jnp.zeros((8, CHUNK), F32)
        for r in range(0, tok.shape[0], STRIP):
            rows = slice(r, r + STRIP)
            hidden = hidden_all[rows] + bias
            square = hidden * hidden
            half = 0.5 + 0.5 * jnp.tanh(hidden * (slope + cubic * square))
            activated = hidden * half
            derivative = half + activated * (1.0 - half) * (2 * slope + (6 * cubic) * square)
            low = (grad_all[rows] * derivative).astype(BF16)
            activated_out[rows, columns] = activated.astype(BF16)
            grad_hidden[rows, columns] = low
            total += fold_rows(low.astype(F32))
        return total

    def weight_gradients(c):
        columns = slice(c, c + CHUNK)
        turned_to_flat(dot(cot_turned, activated_out[:, columns]), CHUNK, D, flat, row_down + c * D // LANES)
        grads = dot(normed_turned, grad_hidden[:, columns])
        for j in range(CHUNK // LANES):
            flat[pl.ds(row_up + c // LANES + j, D, stride=FF // LANES), :] = grads[
                :, j * LANES : (j + 1) * LANES
            ]

    ahead, totals = products(0), []
    for c in range(0, FF, CHUNK):
        now = ahead
        if c + CHUNK < FF:
            ahead = products(c + CHUNK)
        if c > 0:
            weight_gradients(c - CHUNK)
        totals.append(bend(c, *now))
    grad_normed = dot_nt(grad_hidden[...], w_up[...])
    weight_gradients(FF - CHUNK)
    grad_result = cotangent.astype(F32)
    grad_middle = grad_result + normalize_back(grad_normed, gain, normed, rate)
    grad_middle_out[...] = grad_middle
    grad_middle_low = grad_middle.astype(BF16)
    grad_attended_out[...] = dot_nt(grad_middle_low, w_out[...]).astype(BF16)
    matrix_to_flat(dot_tn(attended[...], grad_middle_low), D, D, flat, 0)
    sums = jnp.concatenate(
        [
            fold_rows(grad_middle_low.astype(F32)),
            fold_rows(grad_normed * normed),
            fold_rows(grad_normed),
            *totals,
            fold_rows(grad_result),
        ],
        axis=1,
    )
    sums = jnp.sum(sums, axis=0, keepdims=True)
    base = ROW_SMALL - ROW_OUT
    flat[base : base + LATE_SMALL, :] = jnp.zeros((LATE_SMALL, LANES), F32)
    for i in range(sums.shape[1] // LANES):
        row = base + LATE_SMALL + i
        flat[row : row + 1, :] = sums[:, i * LANES : (i + 1) * LANES]
    flat[ROW_END - ROW_OUT :, :] = jnp.zeros((ROW_TOTAL - ROW_END, LANES), F32)
    first_out[...] = flat[:HEAD_ROWS, :]
    for target, out in enumerate((keep_out, send_out)):
        for p in range(PLANE):
            for z in range(1, Z):
                share = ids[target * PLANE + p] + z * 2 * PLANE
                rows = flat[pl.ds(share * SHARE - ROW_OUT, SHARE), :]
                out[p * (Z - 1) + z - 1] = rows.astype(out.dtype)


def result_kernel(middle, activated, w_down, small, result_out):
    result = middle[...] + dot(activated[...], w_down[...]) + small_vector(small, BIAS_DOWN, 2)
    result_out[...] = result.astype(BF16)


def attend_back_kernel(
    ids, project, weights, grad_attended, normed_turned, w_qkv, small, first_in,
    grad_project, keep_out, send_out, flat, wide,
):
    def some(g, carry):
        base = g * WIDE
        spans = [pl.ds(pl.multiple_of(base + s * SEQ, SEQ), SEQ) for s in range(GROUP)]
        grad_weights = [
            dot_nt(grad_attended[span, :], spread_heads(project[span, 2 * D :])) for span in spans
        ]
        scores_low, scores_turned, weights_turned = [], [], []
        for s, span in enumerate(spans):
            low, turned, mine_turned = [], [], []
            for h in range(HEADS):
                columns = slice(h * SEQ, (h + 1) * SEQ)
                mine_low = weights[span, columns]
                mine = mine_low.astype(F32)
                product = mine * grad_weights[s][:, columns]
                grad_scores = (product - mine * jnp.sum(product, axis=-1, keepdims=True)) * SCALE
                low.append(grad_scores.astype(BF16))
                turned.append(low[-1].T)
                mine_turned.append(mine_low.T)
            scores_low.append(jnp.concatenate(low, axis=1))
            scores_turned.append(jnp.concatenate(turned, axis=1))
            weights_turned.append(jnp.concatenate(mine_turned, axis=1))
        for s, span in enumerate(spans):
            key = spread_heads(project[span, D : 2 * D])
            grad_project[span, :D] = dot(scores_low[s], key).astype(BF16)
            query = spread_heads(project[span, :D])
            grad_project[span, D : 2 * D] = dot(scores_turned[s], query).astype(BF16)
            grad_value = dot(weights_turned[s], spread_heads(grad_attended[span, :]))
            grad_project[span, 2 * D :] = grad_value.astype(BF16)
        return carry

    lax.fori_loop(0, project.shape[0] // WIDE, some, 0)
    products = dot(normed_turned[...], grad_project[...])
    sums = jnp.sum(fold_rows(grad_project[...].astype(F32)), axis=0, keepdims=True)
    gain = jnp.broadcast_to(small_vector(small, GAIN_ONE, 2), (LANES, D)).T
    shift = jnp.broadcast_to(small_vector(small, SHIFT_ONE, 2), (LANES, D)).T
    grad_gain = jnp.zeros((D, LANES), F32)
    grad_shift = jnp.zeros((D, LANES), F32)
    per_row = 3 * D // LANES
    for j in range(per_row):
        columns = slice(j * LANES, (j + 1) * LANES)
        weight = w_qkv[:, columns].astype(F32)
        grad_gain += products[:, columns] * weight
        grad_shift += sums[:, columns] * weight
        flat[pl.ds(j, D, stride=per_row), :] = products[:, columns] * gain + sums[:, columns] * shift
    flat[ROW_OUT:, :] = first_in[...]
    grad_gain = jnp.sum(grad_gain.T, axis=0, keepdims=True)
    grad_shift = jnp.sum(grad_shift.T, axis=0, keepdims=True)
    late = jnp.concatenate([grad_gain, grad_shift, sums[:, :D], sums[:, 2 * D :]], axis=1)
    side = jnp.concatenate(
        [late[:, i * LANES : (i + 1) * LANES] for i in range(LATE_SMALL)]
        + [jnp.zeros((SIDE_ROWS - LATE_SMALL, LANES), F32)],
        axis=0,
    )
    wide[SHARE:SIDE, :] = jnp.zeros((SIDE - SHARE, LANES), F32)
    for target, out in enumerate((keep_out, send_out)):
        for p in range(PLANE):
            share = ids[target * PLANE + p]
            wide[:SHARE, :] = flat[pl.ds(share * SHARE, SHARE), :]
            wide[SIDE:, :] = jnp.where(share == 2 * PLANE - 1, side, 0.0)
            out[p] = wide[...].astype(out.dtype)


def input_grad_kernel(tok, grad_project, grad_middle, w_qkv, small, input_grad_out):
    gain = small_vector(small, GAIN_ONE, 2)

    def some(g, carry):
        span = pl.ds(pl.multiple_of(g * WIDE, WIDE), WIDE)
        normed, rate = normalize(tok[span, :].astype(F32))
        grad_normed = dot_nt(grad_project[span, :], w_qkv[...])
        input_grad_out[span, :] = grad_middle[span, :] + normalize_back(
            grad_normed, gain, normed, rate
        )
        return carry

    lax.fori_loop(0, tok.shape[0] // WIDE, some, 0)


def add_core_kernel(kept, received, keep_out, *sends):
    part = kept.shape[0] // PLANE
    for p, out in enumerate((keep_out, *sends)):
        span = slice(p * part, (p + 1) * part)
        out[...] = (kept[span] + received[span].astype(F32)).astype(out.dtype)


def add_plane_kernel(ids, first_kept, rest_kept, *refs):
    firsts, rests = refs[: PLANE - 1], refs[PLANE - 1 : 2 * (PLANE - 1)]
    keep_out, *sends, column = refs[2 * (PLANE - 1) :]
    first = first_kept[0] + sum(item[0].astype(F32) for item in firsts)
    column[0] = first[:SHARE, :]
    column[1:] = rest_kept[...] + sum(item[...].astype(F32) for item in rests)
    end = SMALL_IN_SHARE + LATE_SMALL
    column[Z - 1, SMALL_IN_SHARE:end, :] += first[SIDE : SIDE + LATE_SMALL, :]
    keep_out[...] = column[ids[0]]
    for d, out in enumerate(sends):
        out[...] = column[lax.rem(ids[0] + d + 1, Z)].astype(BF16)


def add_column_kernel(kept, *refs):
    refs[-1][...] = kept[...] + sum(item[...].astype(F32) for item in refs[:-1])


def like(*shape, kind=F32):
    return jax.ShapeDtypeStruct(shape, kind)


SMEM_SPEC = pl.BlockSpec(memory_space=pltpu.SMEM)
VMEM_SPEC = pl.BlockSpec(memory_space=pltpu.VMEM)

def cost(us):
    return pl.CostEstimate(flops=int(us * 5e7), bytes_accessed=1 << 20, transcendentals=0)


def call(kernel, name, ids, inputs, outs, scratch=(), us=1):
    with_ids = ids is not None
    results = pl.pallas_call(
        kernel,
        in_specs=[SMEM_SPEC] * with_ids + [VMEM_SPEC] * len(inputs),
        out_specs=[VMEM_SPEC] * len(outs),
        out_shape=list(outs),
        scratch_shapes=list(scratch),
        compiler_params=pltpu.CompilerParams(vmem_limit_bytes=VMEM_BYTES),
        cost_estimate=cost(us),
        name=name,
    )(*([ids] if with_ids else []), *inputs)
    return results if len(outs) > 1 else results[0]


def prepare(tokens, params):
    rows = tokens.shape[0]
    return call(
        prepare_kernel, "prepare", None, [tokens, params],
        [like(rows, D), like(D, rows, kind=BF16), like(*params.shape, kind=BF16)], us=2,
    )


def attend(ids, segments, normed, bufs):
    rows = normed.shape[0]
    shapes = [(rows, 3 * D), (rows, HEADS * SEQ), (rows, D), (D, 3 * D)]
    return call(
        attend_kernel, "attend", ids, [segments, normed, *bufs],
        [like(*shape, kind=BF16) for shape in shapes]
        + [like(SMALL_ROWS, LANES), like(HEAD_ROWS, LANES)],
        [pltpu.VMEM((FIRST_ROWS, LANES), F32)], us=6,
    )


def feed(ids, tokens, attended, cotangent, small, first, bufs, send_kind):
    rows = tokens.shape[0]
    return call(
        feed_kernel, "feed", ids, [tokens, attended, cotangent, small, first, *bufs],
        [
            like(rows, D),
            like(rows, FF, kind=BF16),
            like(rows, D),
            like(rows, D, kind=BF16),
            like(FF, D, kind=BF16),
            like(PLANE * (Z - 1), SHARE, LANES),
            like(PLANE * (Z - 1), SHARE, LANES, kind=send_kind),
            like(HEAD_ROWS, LANES),
        ],
        [
            pltpu.VMEM((D, D), BF16),
            pltpu.VMEM((D, FF), BF16),
            pltpu.VMEM((rows, FF), BF16),
            pltpu.VMEM((ROW_TOTAL - ROW_OUT, LANES), F32),
        ],
        us=8,
    )


def result(middle, activated, w_down, small):
    return call(
        result_kernel, "result", None, [middle, activated, w_down, small],
        [like(*middle.shape, kind=BF16)], us=2,
    )


def attend_back(ids, project, weights, grad_attended, normed_turned, w_qkv, small, first, send_kind):
    shape = (PLANE, SIDE + SIDE_ROWS, LANES)
    return call(
        attend_back_kernel, "attend_back", ids,
        [project, weights, grad_attended, normed_turned, w_qkv, small, first],
        [like(*project.shape, kind=BF16), like(*shape), like(*shape, kind=send_kind)],
        [pltpu.VMEM((FIRST_ROWS, LANES), F32), pltpu.VMEM(shape[1:], F32)], us=5,
    )


def input_gradient(tokens, grad_project, grad_middle, w_qkv, small):
    return call(
        input_grad_kernel, "input_grad", None, [tokens, grad_project, grad_middle, w_qkv, small],
        [like(*tokens.shape)], us=2,
    )


def local_any(n, tokens, params, segment_ids, cotangent):
    total = n * params.shape[0]
    normed, normed_turned, _ = prepare(tokens, params)
    gathered = lax.all_gather(params, "fsdp", axis=0).reshape(total, LANES)
    shares = gathered[:ROW_TOTAL].reshape(Z, 2 * PLANE, SHARE, LANES)
    order = [p * 2 + c for c in range(2) for p in range(PLANE)]
    side = jnp.concatenate(
        [jnp.zeros((SIDE - SHARE, LANES), BF16), gathered[ROW_SMALL:ROW_TOTAL]], axis=0
    )
    firsts = [jnp.concatenate([shares[0, k], side], axis=0) for k in order]
    rests = [shares[1:, k] for k in order]
    ids = jnp.array(order, jnp.int32)
    project, weights, attended, w_qkv, small, first = attend(
        ids, segment_ids.reshape(-1, SEQ), normed, firsts
    )
    middle, activated, grad_middle, grad_attended, w_down, rest, rest_send, first_grad = feed(
        ids, tokens, attended, cotangent, small, first, rests, F32
    )
    outputs = result(middle, activated, w_down, small)
    grad_project, first, first_send = attend_back(
        ids, project, weights, grad_attended, normed_turned, w_qkv, small, first_grad, F32
    )
    input_grad = input_gradient(tokens, grad_project, grad_middle, w_qkv, small)
    first = jnp.stack([first, first_send], axis=1)
    rest = jnp.stack([rest, rest_send]).reshape(2, PLANE, Z - 1, SHARE, LANES).transpose(2, 1, 0, 3, 4)
    flat = jnp.concatenate(
        [
            first[:, :, :SHARE].reshape(-1, LANES),
            rest.reshape(-1, LANES),
            jnp.zeros((total - ROW_TOTAL, LANES), F32),
        ],
        axis=0,
    )
    flat = flat.at[ROW_SMALL : ROW_SMALL + LATE_SMALL].add(
        first[PLANE - 1, 1, SIDE : SIDE + LATE_SMALL]
    )
    param_grad = lax.psum_scatter(flat, "fsdp", scatter_dimension=0, tiled=True)
    return outputs, input_grad, param_grad


def index_of(z, plane, core):
    return (z * PLANE + plane) * 2 + core


def move(values, step_z, step_plane, step_core):
    pairs = [
        (index_of(z, p, c), index_of((z + step_z) % Z, p ^ step_plane, c ^ step_core))
        for z in range(Z)
        for p in range(PLANE)
        for c in range(2)
    ]
    return lax.ppermute(values, "fsdp", pairs)


STEPS = (3, 1, 2)


def add_core(keep, send):
    part = (keep.shape[0] // PLANE,) + keep.shape[1:]
    return call(
        add_core_kernel, "add_core", None, [keep, send],
        [like(*part)] + [like(*part, kind=BF16)] * (PLANE - 1),
    )


def local_slice(tokens, params, segment_ids, cotangent):
    me = lax.axis_index("fsdp").astype(jnp.int32)
    z, plane, core = me // (2 * PLANE), (me // 2) % PLANE, me % 2
    where = z.reshape(1)
    ids = jnp.stack(
        [(plane ^ dp) * 2 + (core ^ dc) for dc in range(2) for dp in (0, *STEPS)]
    )

    normed, normed_turned, own = prepare(tokens, params)
    first, rest = call(
        sort_kernel, "sort_shares", where, [own] + [move(params, d, 0, 0) for d in range(1, Z)],
        [like(SIDE + SMALL_ROWS, LANES, kind=BF16), like(Z - 1, SHARE, LANES, kind=BF16)],
        [pltpu.VMEM((Z, SHARE, LANES), BF16), pltpu.VMEM((SIDE + SMALL_ROWS, LANES), F32)],
    )
    firsts = [first] + [move(first, 0, d, 0) for d in STEPS]
    rests = [move(rest, 0, d, 0) for d in STEPS]
    firsts = firsts + [move(item, 0, 0, 1) for item in firsts]
    project, weights, attended, w_qkv, small, first = attend(
        ids, segment_ids.reshape(-1, SEQ), normed, firsts
    )
    *rests, attended = lax.optimization_barrier((*rests, attended))
    rests = [rest] + rests
    rests = rests + [move(item, 0, 0, 1) for item in rests]
    middle, activated, grad_middle, grad_attended, w_down, keep, send, first_grad = feed(
        ids, tokens, attended, cotangent, small, first, rests, BF16
    )

    received = move(send, 0, 0, 1)
    outputs = result(middle, activated, w_down, small)
    received, outputs = lax.optimization_barrier((received, outputs))
    rest_kept, *sends = add_core(keep, received)
    *sends, grad_attended = lax.optimization_barrier((*sends, grad_attended))
    rest_sums = [move(item, 0, d, 0) for item, d in zip(sends, STEPS)]
    grad_project, keep, send = attend_back(
        ids, project, weights, grad_attended, normed_turned, w_qkv, small, first_grad, BF16
    )
    rest_sums[0], keep = lax.optimization_barrier((rest_sums[0], keep))
    first_kept, *sends = add_core(keep, move(send, 0, 0, 1))
    first_sums = [move(item, 0, d, 0) for item, d in zip(sends, STEPS)]
    input_grad = input_gradient(tokens, grad_project, grad_middle, w_qkv, small)
    kept, *sends = call(
        add_plane_kernel, "add_plane", where, [first_kept, rest_kept] + first_sums + rest_sums,
        [like(SHARE, LANES)] + [like(SHARE, LANES, kind=BF16)] * (Z - 1),
        [pltpu.VMEM((Z, SHARE, LANES), F32)],
    )
    arrived = [move(item, d + 1, 0, 0) for d, item in enumerate(sends)]
    param_grad = call(
        add_column_kernel, "add_column", None, [kept] + arrived, [like(SHARE, LANES)]
    )
    return outputs, input_grad, param_grad


def solution(mesh):
    n = mesh.shape["fsdp"]
    local = local_slice if n == 2 * PLANE * Z else functools.partial(local_any, n)
    in_specs = (P("fsdp", None), P("fsdp", None), P("fsdp"), P("fsdp", None))
    out_specs = (P("fsdp", None), P("fsdp", None), P("fsdp", None))
    return jax.shard_map(local, mesh=mesh, in_specs=in_specs, out_specs=out_specs, check_vma=False)
```

```python
import functools

import jax
import jax.numpy as jnp
from jax import lax
from jax.experimental import pallas as pl
from jax.experimental.pallas import tpu as pltpu
from jax.sharding import PartitionSpec as P

D = 256
HEADS = 4
HEAD_DIM = 64
FF = 1024
SEQ = 128
LANES = 128
GROUP = 4
WIDE = GROUP * SEQ
CHUNK = 256
STRIP = 64
EPSILON = 1e-05
SCALE = HEAD_DIM ** (-0.5)
VMEM_BYTES = 24 * 1024 * 1024

ROW_QKV = 0
ROW_OUT = 1536
ROW_UP = 2048
ROW_DOWN = 4096
ROW_SMALL = 6144
ROW_END = 6168
ROW_TOTAL = 6176
GAIN_ONE, SHIFT_ONE, BIAS_QUERY, BIAS_VALUE, BIAS_OUT = 0, 2, 4, 6, 8
GAIN_TWO, SHIFT_TWO, BIAS_UP, BIAS_DOWN = 10, 12, 14, 22
SMALL_ROWS = 32
LATE_SMALL = 8

SHARE = 193
Z, PLANE = 4, 4
FIRST_ROWS = 2 * PLANE * SHARE
HEAD_ROWS = FIRST_ROWS - ROW_OUT
SIDE, SIDE_ROWS = 208, 16
SMALL_IN_SHARE = ROW_SMALL - (2 * PLANE * Z - 1) * SHARE

F32 = jnp.float32
BF16 = jnp.bfloat16


def dot(left, right):
    return jnp.dot(left, right, preferred_element_type=F32)


def dot_nt(left, right):
    return lax.dot_general(left, right, (((1,), (1,)), ((), ())), preferred_element_type=F32)


def dot_tn(left, right):
    return lax.dot_general(left, right, (((0,), (0,)), ((), ())), preferred_element_type=F32)


def small_vector(small, row, count):
    return jnp.concatenate([small[row + i : row + i + 1, :] for i in range(count)], axis=1)


def fold_rows(values):
    rows, columns = values.shape
    return jnp.sum(values.reshape(rows // 8, 8, columns), axis=0)


def normalize(values):
    center = values - jnp.mean(values, axis=-1, keepdims=True)
    rate = lax.rsqrt(jnp.mean(center * center, axis=-1, keepdims=True) + EPSILON)
    return center * rate, rate


def normalize_back(grad, gain, normed, rate):
    scaled = grad * gain
    return rate * (
        scaled
        - jnp.mean(scaled, axis=-1, keepdims=True)
        - normed * jnp.mean(scaled * normed, axis=-1, keepdims=True)
    )


def head_masks():
    lane = lax.broadcasted_iota(jnp.int32, (1, D), 1)
    return [(lane // HEAD_DIM == h).astype(F32).astype(BF16) for h in range(HEADS)]


def spread_heads(rows):
    return jnp.concatenate([rows * mask for mask in head_masks()], axis=0)


def matrix_from_flat(flat, start, rows, columns, out):
    per_row = columns // LANES
    for j in range(per_row):
        out[:, j * LANES : (j + 1) * LANES] = flat[
            pl.ds(start + j, rows, stride=per_row), :
        ].astype(BF16)


def turned_to_flat(turned, rows, columns, flat, start):
    per_row = columns // LANES
    for j in range(per_row):
        flat[pl.ds(start + j, rows, stride=per_row), :] = turned[j * LANES : (j + 1) * LANES, :].T


def matrix_to_flat(matrix, rows, columns, flat, start):
    per_row = columns // LANES
    for j in range(per_row):
        flat[pl.ds(start + j, rows, stride=per_row), :] = matrix[:, j * LANES : (j + 1) * LANES]


def prepare_kernel(tok, params, seg, normed_out, normed_turned, own, allowed):
    normed, _ = normalize(tok[...].astype(F32))
    normed_out[...] = normed
    normed_turned[...] = normed.astype(BF16).T
    own[...] = params[...]
    causal = lax.broadcasted_iota(jnp.int32, (SEQ, SEQ), 1) <= lax.broadcasted_iota(
        jnp.int32, (SEQ, SEQ), 0
    )
    for s in range(seg.shape[0]):
        across = jnp.broadcast_to(seg[s : s + 1, :].astype(F32), (SEQ, SEQ))
        allowed[s * SEQ : (s + 1) * SEQ, :] = (causal & (across == across.T)).astype(F32)


def sort_kernel(ids, *refs):
    received, (first, rest, stage, wide) = refs[:Z], refs[Z:]
    for d in range(Z):
        stage[lax.rem(ids[0] + Z - d, Z)] = received[d][...]
    rest[...] = stage[1:]
    wide[:SHARE, :] = stage[0].astype(F32)
    wide[SHARE:SIDE, :] = jnp.zeros((SIDE - SHARE, LANES), F32)
    last = stage[Z - 1].astype(F32)
    wide[SIDE:, :] = last[SMALL_IN_SHARE:, :]
    first[...] = wide[...].astype(BF16)


def attend_kernel(ids, allowed, normed, *refs):
    bufs = [ref.at[p] for ref in refs[:2] for p in range(PLANE)]
    project_out, weights_out, attended_out, w_qkv, small, first_out, flat = refs[2:]
    for slot, buf in enumerate(bufs):
        wide = buf[...].astype(F32)
        flat[pl.ds(ids[slot] * SHARE, SHARE), :] = wide[:SHARE, :]

        @pl.when(ids[slot] == 2 * PLANE - 1)
        def _():
            small[...] = wide[SIDE:, :]

    matrix_from_flat(flat, ROW_QKV, D, 3 * D, w_qkv)
    first_out[...] = flat[ROW_OUT:FIRST_ROWS, :]

    gain = small_vector(small, GAIN_ONE, 2)
    shift = small_vector(small, SHIFT_ONE, 2)
    bias = jnp.concatenate(
        [
            small_vector(small, BIAS_QUERY, 2),
            jnp.zeros((1, D), F32),
            small_vector(small, BIAS_VALUE, 2),
        ],
        axis=1,
    )
    def some(g, carry):
        span = pl.ds(pl.multiple_of(g * WIDE, WIDE), WIDE)
        normed_low = (normed[span, :] * gain + shift).astype(BF16)
        project = (dot(normed_low, w_qkv[...]) + bias).astype(BF16)
        project_out[span, :] = project
        scores, values = [], []
        for s in range(GROUP):
            rows = slice(s * SEQ, (s + 1) * SEQ)
            scores.append(
                dot_nt(project[rows, :D] * SCALE, spread_heads(project[rows, D : 2 * D]))
            )
            values.append(spread_heads(project[rows, 2 * D :]))
        weights = []
        for s in range(GROUP):
            low = []
            open_pairs = allowed[pl.ds(pl.multiple_of(g * WIDE + s * SEQ, SEQ), SEQ), :] > 0.5
            for h in range(HEADS):
                mine = jnp.where(open_pairs, scores[s][:, h * SEQ : (h + 1) * SEQ], -1e30)
                grown = jnp.exp(mine - jnp.max(mine, axis=-1, keepdims=True))
                low.append(
                    (grown * (1.0 / jnp.sum(grown, axis=-1, keepdims=True))).astype(BF16)
                )
            weights.append(jnp.concatenate(low, axis=1))
        weights_out[span, :] = jnp.concatenate(weights, axis=0)
        attended_out[span, :] = jnp.concatenate(
            [dot(weights[s], values[s]).astype(BF16) for s in range(GROUP)], axis=0
        )
        return carry

    lax.fori_loop(0, normed.shape[0] // WIDE, some, 0)


def feed_kernel(
    ids, tok, attended, cot, small, first_in, *refs,
):
    bufs = []
    for own, others in (refs[0:2], refs[2:4]):
        bufs.append(own)
        bufs += [others.at[pl.ds(p * (Z - 1), Z - 1)] for p in range(PLANE - 1)]
    (
        middle_out, activated_out, grad_middle_out, grad_attended_out, w_down, keep_out, send_out, first_out,
        w_out, w_up, grad_hidden, flat,
    ) = refs[4:]
    flat[:HEAD_ROWS, :] = first_in[...]
    for slot, buf in enumerate(bufs):
        for z in range(1, Z):
            share = ids[slot] + z * 2 * PLANE
            flat[pl.ds(share * SHARE - ROW_OUT, SHARE), :] = buf[z - 1].astype(F32)
    matrix_from_flat(flat, 0, D, D, w_out)
    matrix_from_flat(flat, ROW_UP - ROW_OUT, D, FF, w_up)
    matrix_from_flat(flat, ROW_DOWN - ROW_OUT, FF, D, w_down)

    gain = small_vector(small, GAIN_TWO, 2)
    middle = (
        tok[...].astype(F32) + dot(attended[...], w_out[...]) + small_vector(small, BIAS_OUT, 2)
    )
    middle_out[...] = middle
    normed, rate = normalize(middle)
    normed_low = (normed * gain + small_vector(small, SHIFT_TWO, 2)).astype(BF16)
    normed_turned = normed_low.T
    cotangent = cot[...]
    cot_turned = cotangent.T
    slope = 0.7978845608028654
    cubic = slope * 0.044715
    row_up, row_down = ROW_UP - ROW_OUT, ROW_DOWN - ROW_OUT

    def products(c):
        columns = slice(c, c + CHUNK)
        return dot(normed_low, w_up[:, columns]), dot_nt(cotangent, w_down[columns, :])

    def bend(c, hidden_all, grad_all):
        columns = slice(c, c + CHUNK)
        bias = small_vector(small, BIAS_UP + c // LANES, CHUNK // LANES)
        total = jnp.zeros((8, CHUNK), F32)
        for r in range(0, tok.shape[0], STRIP):
            rows = slice(r, r + STRIP)
            hidden = hidden_all[rows] + bias
            square = hidden * hidden
            half = 0.5 + 0.5 * jnp.tanh(hidden * (slope + cubic * square))
            activated = hidden * half
            derivative = half + activated * (1.0 - half) * (2 * slope + (6 * cubic) * square)
            low = (grad_all[rows] * derivative).astype(BF16)
            activated_out[rows, columns] = activated.astype(BF16)
            grad_hidden[rows, columns] = low
            total += fold_rows(low.astype(F32))
        return total

    def weight_gradients(c):
        columns = slice(c, c + CHUNK)
        turned_to_flat(dot(cot_turned, activated_out[:, columns]), CHUNK, D, flat, row_down + c * D // LANES)
        grads = dot(normed_turned, grad_hidden[:, columns])
        for j in range(CHUNK // LANES):
            flat[pl.ds(row_up + c // LANES + j, D, stride=FF // LANES), :] = grads[
                :, j * LANES : (j + 1) * LANES
            ]

    ahead, totals = products(0), []
    for c in range(0, FF, CHUNK):
        now = ahead
        if c + CHUNK < FF:
            ahead = products(c + CHUNK)
        if c > 0:
            weight_gradients(c - CHUNK)
        totals.append(bend(c, *now))
    grad_normed = dot_nt(grad_hidden[...], w_up[...])
    weight_gradients(FF - CHUNK)
    grad_result = cotangent.astype(F32)
    grad_middle = grad_result + normalize_back(grad_normed, gain, normed, rate)
    grad_middle_out[...] = grad_middle
    grad_middle_low = grad_middle.astype(BF16)
    grad_attended_out[...] = dot_nt(grad_middle_low, w_out[...]).astype(BF16)
    matrix_to_flat(dot_tn(attended[...], grad_middle_low), D, D, flat, 0)
    sums = jnp.concatenate(
        [
            fold_rows(grad_middle_low.astype(F32)),
            fold_rows(grad_normed * normed),
            fold_rows(grad_normed),
            *totals,
            fold_rows(grad_result),
        ],
        axis=1,
    )
    sums = jnp.sum(sums, axis=0, keepdims=True)
    base = ROW_SMALL - ROW_OUT
    flat[base : base + LATE_SMALL, :] = jnp.zeros((LATE_SMALL, LANES), F32)
    for i in range(sums.shape[1] // LANES):
        row = base + LATE_SMALL + i
        flat[row : row + 1, :] = sums[:, i * LANES : (i + 1) * LANES]
    flat[ROW_END - ROW_OUT :, :] = jnp.zeros((ROW_TOTAL - ROW_END, LANES), F32)
    first_out[...] = flat[:HEAD_ROWS, :]
    for target, out in enumerate((keep_out, send_out)):
        for p in range(PLANE):
            for z in range(1, Z):
                share = ids[target * PLANE + p] + z * 2 * PLANE
                rows = flat[pl.ds(share * SHARE - ROW_OUT, SHARE), :]
                out[p * (Z - 1) + z - 1] = rows.astype(out.dtype)


def result_kernel(middle, activated, w_down, small, result_out):
    result = middle[...] + dot(activated[...], w_down[...]) + small_vector(small, BIAS_DOWN, 2)
    result_out[...] = result.astype(BF16)


def attend_back_kernel(project, weights, grad_attended, grad_project):
    def some(g, carry):
        base = g * WIDE
        spans = [pl.ds(pl.multiple_of(base + s * SEQ, SEQ), SEQ) for s in range(GROUP)]
        grad_weights = [
            dot_nt(grad_attended[span, :], spread_heads(project[span, 2 * D :])) for span in spans
        ]
        scores_low, scores_turned, weights_turned = [], [], []
        for s, span in enumerate(spans):
            low, turned, mine_turned = [], [], []
            for h in range(HEADS):
                columns = slice(h * SEQ, (h + 1) * SEQ)
                mine_low = weights[span, columns]
                mine = mine_low.astype(F32)
                product = mine * grad_weights[s][:, columns]
                grad_scores = (product - mine * jnp.sum(product, axis=-1, keepdims=True)) * SCALE
                low.append(grad_scores.astype(BF16))
                turned.append(low[-1].T)
                mine_turned.append(mine_low.T)
            scores_low.append(jnp.concatenate(low, axis=1))
            scores_turned.append(jnp.concatenate(turned, axis=1))
            weights_turned.append(jnp.concatenate(mine_turned, axis=1))
        for s, span in enumerate(spans):
            key = spread_heads(project[span, D : 2 * D])
            grad_project[span, :D] = dot(scores_low[s], key).astype(BF16)
            query = spread_heads(project[span, :D])
            grad_project[span, D : 2 * D] = dot(scores_turned[s], query).astype(BF16)
            grad_value = dot(weights_turned[s], spread_heads(grad_attended[span, :]))
            grad_project[span, 2 * D :] = grad_value.astype(BF16)
        return carry

    lax.fori_loop(0, project.shape[0] // WIDE, some, 0)


def project_back_kernel(
    ids, grad_project, normed_turned, w_qkv, small, first_in, keep_out, send_out, flat, wide
):
    products = dot(normed_turned[...], grad_project[...])
    sums = jnp.sum(fold_rows(grad_project[...].astype(F32)), axis=0, keepdims=True)
    gain = jnp.broadcast_to(small_vector(small, GAIN_ONE, 2), (LANES, D)).T
    shift = jnp.broadcast_to(small_vector(small, SHIFT_ONE, 2), (LANES, D)).T
    grad_gain = jnp.zeros((D, LANES), F32)
    grad_shift = jnp.zeros((D, LANES), F32)
    per_row = 3 * D // LANES
    for j in range(per_row):
        columns = slice(j * LANES, (j + 1) * LANES)
        weight = w_qkv[:, columns].astype(F32)
        grad_gain += products[:, columns] * weight
        grad_shift += sums[:, columns] * weight
        flat[pl.ds(j, D, stride=per_row), :] = products[:, columns] * gain + sums[:, columns] * shift
    flat[ROW_OUT:, :] = first_in[...]
    grad_gain = jnp.sum(grad_gain.T, axis=0, keepdims=True)
    grad_shift = jnp.sum(grad_shift.T, axis=0, keepdims=True)
    late = jnp.concatenate([grad_gain, grad_shift, sums[:, :D], sums[:, 2 * D :]], axis=1)
    side = jnp.concatenate(
        [late[:, i * LANES : (i + 1) * LANES] for i in range(LATE_SMALL)]
        + [jnp.zeros((SIDE_ROWS - LATE_SMALL, LANES), F32)],
        axis=0,
    )
    wide[SHARE:SIDE, :] = jnp.zeros((SIDE - SHARE, LANES), F32)
    for target, out in enumerate((keep_out, send_out)):
        for p in range(PLANE):
            share = ids[target * PLANE + p]
            wide[:SHARE, :] = flat[pl.ds(share * SHARE, SHARE), :]
            wide[SIDE:, :] = jnp.where(share == 2 * PLANE - 1, side, 0.0)
            out[p] = wide[...].astype(out.dtype)


def input_grad_kernel(tok, grad_project, grad_middle, w_qkv, small, input_grad_out):
    gain = small_vector(small, GAIN_ONE, 2)

    def some(g, carry):
        span = pl.ds(pl.multiple_of(g * WIDE, WIDE), WIDE)
        normed, rate = normalize(tok[span, :].astype(F32))
        grad_normed = dot_nt(grad_project[span, :], w_qkv[...])
        input_grad_out[span, :] = grad_middle[span, :] + normalize_back(
            grad_normed, gain, normed, rate
        )
        return carry

    lax.fori_loop(0, tok.shape[0] // WIDE, some, 0)


def stack_kernel(*refs):
    row = 0
    for ref in refs[:-1]:
        refs[-1][row : row + ref.shape[0]] = ref[...]
        row += ref.shape[0]


def add_core_kernel(kept, received, keep_out, *sends):
    part = kept.shape[0] // PLANE
    for p, out in enumerate((keep_out, *sends)):
        span = slice(p * part, (p + 1) * part)
        out[...] = (kept[span] + received[span].astype(F32)).astype(out.dtype)


def add_plane_kernel(ids, first_kept, rest_kept, *refs):
    firsts, rests = refs[: PLANE - 1], refs[PLANE - 1 : 2 * (PLANE - 1)]
    keep_out, *sends, column = refs[2 * (PLANE - 1) :]
    first = first_kept[0] + sum(item[0].astype(F32) for item in firsts)
    column[0] = first[:SHARE, :]
    column[1:] = rest_kept[...] + sum(item[...].astype(F32) for item in rests)
    end = SMALL_IN_SHARE + LATE_SMALL
    column[Z - 1, SMALL_IN_SHARE:end, :] += first[SIDE : SIDE + LATE_SMALL, :]
    keep_out[...] = column[ids[0]]
    for d, out in enumerate(sends):
        out[...] = column[lax.rem(ids[0] + d + 1, Z)].astype(BF16)


def add_column_kernel(kept, *refs):
    refs[-1][...] = kept[...] + sum(item[...].astype(F32) for item in refs[:-1])


def like(*shape, kind=F32):
    return jax.ShapeDtypeStruct(shape, kind)


SMEM_SPEC = pl.BlockSpec(memory_space=pltpu.SMEM)
VMEM_SPEC = pl.BlockSpec(memory_space=pltpu.VMEM)

def cost(us):
    return pl.CostEstimate(flops=int(us * 1e9), bytes_accessed=1 << 20, transcendentals=0)


def call(kernel, name, ids, inputs, outs, scratch=(), us=1):
    with_ids = ids is not None
    results = pl.pallas_call(
        kernel,
        in_specs=[SMEM_SPEC] * with_ids + [VMEM_SPEC] * len(inputs),
        out_specs=[VMEM_SPEC] * len(outs),
        out_shape=list(outs),
        scratch_shapes=list(scratch),
        compiler_params=pltpu.CompilerParams(vmem_limit_bytes=VMEM_BYTES),
        cost_estimate=cost(us),
        name=name,
    )(*([ids] if with_ids else []), *inputs)
    return results if len(outs) > 1 else results[0]


def prepare(tokens, params, segment_ids):
    rows = tokens.shape[0]
    return call(
        prepare_kernel, "prepare", None, [tokens, params, segment_ids.reshape(-1, SEQ)],
        [
            like(rows, D),
            like(D, rows, kind=BF16),
            like(*params.shape, kind=BF16),
            like(rows, SEQ),
        ],
        us=2,
    )


def stack(items):
    shape = (sum(item.shape[0] for item in items),) + items[0].shape[1:]
    return call(stack_kernel, "stack", None, items, [like(*shape, kind=items[0].dtype)])


def attend(ids, allowed, normed, bufs):
    rows = normed.shape[0]
    shapes = [(rows, 3 * D), (rows, HEADS * SEQ), (rows, D), (D, 3 * D)]
    return call(
        attend_kernel, "attend", ids, [allowed, normed, *bufs],
        [like(*shape, kind=BF16) for shape in shapes]
        + [like(SMALL_ROWS, LANES), like(HEAD_ROWS, LANES)],
        [pltpu.VMEM((FIRST_ROWS, LANES), F32)], us=6,
    )


def feed(ids, tokens, attended, cotangent, small, first, bufs, send_kind):
    rows = tokens.shape[0]
    return call(
        feed_kernel, "feed", ids, [tokens, attended, cotangent, small, first, *bufs],
        [
            like(rows, D),
            like(rows, FF, kind=BF16),
            like(rows, D),
            like(rows, D, kind=BF16),
            like(FF, D, kind=BF16),
            like(PLANE * (Z - 1), SHARE, LANES),
            like(PLANE * (Z - 1), SHARE, LANES, kind=send_kind),
            like(HEAD_ROWS, LANES),
        ],
        [
            pltpu.VMEM((D, D), BF16),
            pltpu.VMEM((D, FF), BF16),
            pltpu.VMEM((rows, FF), BF16),
            pltpu.VMEM((ROW_TOTAL - ROW_OUT, LANES), F32),
        ],
        us=8,
    )


def result(middle, activated, w_down, small):
    return call(
        result_kernel, "result", None, [middle, activated, w_down, small],
        [like(*middle.shape, kind=BF16)], us=2,
    )


def attend_back(project, weights, grad_attended):
    return call(
        attend_back_kernel, "attend_back", None, [project, weights, grad_attended],
        [like(*project.shape, kind=BF16)], us=3,
    )


def project_back(ids, grad_project, normed_turned, w_qkv, small, first, send_kind):
    shape = (PLANE, SIDE + SIDE_ROWS, LANES)
    return call(
        project_back_kernel, "project_back", ids, [grad_project, normed_turned, w_qkv, small, first],
        [like(*shape), like(*shape, kind=send_kind)],
        [pltpu.VMEM((FIRST_ROWS, LANES), F32), pltpu.VMEM(shape[1:], F32)], us=1,
    )


def input_gradient(tokens, grad_project, grad_middle, w_qkv, small):
    return call(
        input_grad_kernel, "input_grad", None, [tokens, grad_project, grad_middle, w_qkv, small],
        [like(*tokens.shape)], us=2,
    )


def local_any(n, tokens, params, segment_ids, cotangent):
    total = n * params.shape[0]
    normed, normed_turned, _, allowed = prepare(tokens, params, segment_ids)
    gathered = lax.all_gather(params, "fsdp", axis=0).reshape(total, LANES)
    shares = gathered[:ROW_TOTAL].reshape(Z, 2 * PLANE, SHARE, LANES)
    order = [p * 2 + c for c in range(2) for p in range(PLANE)]
    side = jnp.concatenate(
        [jnp.zeros((SIDE - SHARE, LANES), BF16), gathered[ROW_SMALL:ROW_TOTAL]], axis=0
    )
    firsts = [
        jnp.stack([jnp.concatenate([shares[0, k], side], axis=0) for k in group])
        for group in (order[:PLANE], order[PLANE:])
    ]
    rests = []
    for group in (order[:PLANE], order[PLANE:]):
        rests += [shares[1:, group[0]], jnp.concatenate([shares[1:, k] for k in group[1:]])]
    ids = jnp.array(order, jnp.int32)
    project, weights, attended, w_qkv, small, first = attend(ids, allowed, normed, firsts)
    middle, activated, grad_middle, grad_attended, w_down, rest, rest_send, first_grad = feed(
        ids, tokens, attended, cotangent, small, first, rests, F32
    )
    outputs = result(middle, activated, w_down, small)
    grad_project = attend_back(project, weights, grad_attended)
    first, first_send = project_back(ids, grad_project, normed_turned, w_qkv, small, first_grad, F32)
    input_grad = input_gradient(tokens, grad_project, grad_middle, w_qkv, small)
    first = jnp.stack([first, first_send], axis=1)
    rest = jnp.stack([rest, rest_send]).reshape(2, PLANE, Z - 1, SHARE, LANES).transpose(2, 1, 0, 3, 4)
    flat = jnp.concatenate(
        [
            first[:, :, :SHARE].reshape(-1, LANES),
            rest.reshape(-1, LANES),
            jnp.zeros((total - ROW_TOTAL, LANES), F32),
        ],
        axis=0,
    )
    flat = flat.at[ROW_SMALL : ROW_SMALL + LATE_SMALL].add(
        first[PLANE - 1, 1, SIDE : SIDE + LATE_SMALL]
    )
    param_grad = lax.psum_scatter(flat, "fsdp", scatter_dimension=0, tiled=True)
    return outputs, input_grad, param_grad


def index_of(z, plane, core):
    return (z * PLANE + plane) * 2 + core


def move(values, step_z, step_plane, step_core):
    pairs = [
        (index_of(z, p, c), index_of((z + step_z) % Z, p ^ step_plane, c ^ step_core))
        for z in range(Z)
        for p in range(PLANE)
        for c in range(2)
    ]
    return lax.ppermute(values, "fsdp", pairs)


STEPS = (3, 1, 2)


def add_core(keep, send):
    part = (keep.shape[0] // PLANE,) + keep.shape[1:]
    return call(
        add_core_kernel, "add_core", None, [keep, send],
        [like(*part)] + [like(*part, kind=BF16)] * (PLANE - 1),
    )


def local_slice(tokens, params, segment_ids, cotangent):
    me = lax.axis_index("fsdp").astype(jnp.int32)
    z, plane, core = me // (2 * PLANE), (me // 2) % PLANE, me % 2
    where = z.reshape(1)
    ids = jnp.stack(
        [(plane ^ dp) * 2 + (core ^ dc) for dc in range(2) for dp in (0, *STEPS)]
    )

    normed, normed_turned, own, allowed = prepare(tokens, params, segment_ids)
    first, rest = call(
        sort_kernel, "sort_shares", where, [own] + [move(params, d, 0, 0) for d in range(1, Z)],
        [like(SIDE + SMALL_ROWS, LANES, kind=BF16), like(Z - 1, SHARE, LANES, kind=BF16)],
        [pltpu.VMEM((Z, SHARE, LANES), BF16), pltpu.VMEM((SIDE + SMALL_ROWS, LANES), F32)],
    )
    firsts = [move(first, 0, d, 0) for d in STEPS]
    rests = [move(rest, 0, d, 0) for d in STEPS]
    firsts = stack([item[None] for item in (first, *firsts)])
    project, weights, attended, w_qkv, small, first = attend(
        ids, allowed, normed, [firsts, move(firsts, 0, 0, 1)]
    )
    *rests, attended = lax.optimization_barrier((*rests, attended))
    rests = stack(rests)
    rests = [rest, rests, move(rest, 0, 0, 1), move(rests, 0, 0, 1)]
    middle, activated, grad_middle, grad_attended, w_down, keep, send, first_grad = feed(
        ids, tokens, attended, cotangent, small, first, rests, BF16
    )

    received = move(send, 0, 0, 1)
    outputs = result(middle, activated, w_down, small)
    received, outputs = lax.optimization_barrier((received, outputs))
    rest_kept, *sends = add_core(keep, received)
    *sends, grad_attended = lax.optimization_barrier((*sends, grad_attended))
    rest_sums = [move(item, 0, d, 0) for item, d in zip(sends, STEPS)]
    grad_project = attend_back(project, weights, grad_attended)
    rest_sums[0], grad_project = lax.optimization_barrier((rest_sums[0], grad_project))
    keep, send = project_back(ids, grad_project, normed_turned, w_qkv, small, first_grad, BF16)
    first_kept, *sends = add_core(keep, move(send, 0, 0, 1))
    first_sums = [move(item, 0, d, 0) for item, d in zip(sends, STEPS)]
    input_grad = input_gradient(tokens, grad_project, grad_middle, w_qkv, small)
    kept, *sends = call(
        add_plane_kernel, "add_plane", where, [first_kept, rest_kept] + first_sums + rest_sums,
        [like(SHARE, LANES)] + [like(SHARE, LANES, kind=BF16)] * (Z - 1),
        [pltpu.VMEM((Z, SHARE, LANES), F32)],
    )
    arrived = [move(item, d + 1, 0, 0) for d, item in enumerate(sends)]
    param_grad = call(
        add_column_kernel, "add_column", None, [kept] + arrived, [like(SHARE, LANES)]
    )
    return outputs, input_grad, param_grad


def solution(mesh):
    n = mesh.shape["fsdp"]
    local = local_slice if n == 2 * PLANE * Z else functools.partial(local_any, n)
    in_specs = (P("fsdp", None), P("fsdp", None), P("fsdp"), P("fsdp", None))
    out_specs = (P("fsdp", None), P("fsdp", None), P("fsdp", None))
    return jax.shard_map(local, mesh=mesh, in_specs=in_specs, out_specs=out_specs, check_vma=False)
```

```python
import functools

import jax
import jax.numpy as jnp
from jax import lax
from jax.experimental import pallas as pl
from jax.experimental.pallas import tpu as pltpu
from jax.sharding import PartitionSpec as P

D = 256
HEADS = 4
HEAD_DIM = 64
FF = 1024
SEQ = 128
LANES = 128
GROUP = 4
WIDE = GROUP * SEQ
CHUNK = 256
STRIP = 64
EPSILON = 1e-05
SCALE = HEAD_DIM ** (-0.5)
VMEM_BYTES = 24 * 1024 * 1024

ROW_QKV = 0
ROW_OUT = 1536
ROW_UP = 2048
ROW_DOWN = 4096
ROW_SMALL = 6144
ROW_END = 6168
ROW_TOTAL = 6176
GAIN_ONE, SHIFT_ONE, BIAS_QUERY, BIAS_VALUE, BIAS_OUT = 0, 2, 4, 6, 8
GAIN_TWO, SHIFT_TWO, BIAS_UP, BIAS_DOWN = 10, 12, 14, 22
SMALL_ROWS = 32
LATE_SMALL = 8

SHARE = 193
Z, PLANE = 4, 4
FIRST_ROWS = 2 * PLANE * SHARE
HEAD_ROWS = FIRST_ROWS - ROW_OUT
SIDE, SIDE_ROWS = 208, 16
SMALL_IN_SHARE = ROW_SMALL - (2 * PLANE * Z - 1) * SHARE

F32 = jnp.float32
BF16 = jnp.bfloat16


def dot(left, right):
    return jnp.dot(left, right, preferred_element_type=F32)


def dot_nt(left, right):
    return lax.dot_general(left, right, (((1,), (1,)), ((), ())), preferred_element_type=F32)


def dot_tn(left, right):
    return lax.dot_general(left, right, (((0,), (0,)), ((), ())), preferred_element_type=F32)


def small_vector(small, row, count):
    return jnp.concatenate([small[row + i : row + i + 1, :] for i in range(count)], axis=1)


def fold_rows(values):
    rows, columns = values.shape
    return jnp.sum(values.reshape(rows // 8, 8, columns), axis=0)


def normalize(values):
    center = values - jnp.mean(values, axis=-1, keepdims=True)
    rate = lax.rsqrt(jnp.mean(center * center, axis=-1, keepdims=True) + EPSILON)
    return center * rate, rate


def normalize_back(grad, gain, normed, rate):
    scaled = grad * gain
    return rate * (
        scaled
        - jnp.mean(scaled, axis=-1, keepdims=True)
        - normed * jnp.mean(scaled * normed, axis=-1, keepdims=True)
    )


def head_masks():
    lane = lax.broadcasted_iota(jnp.int32, (1, D), 1)
    return [(lane // HEAD_DIM == h).astype(F32).astype(BF16) for h in range(HEADS)]


def spread_heads(rows):
    return jnp.concatenate([rows * mask for mask in head_masks()], axis=0)


def matrix_from_flat(flat, start, rows, columns, out):
    per_row = columns // LANES
    for j in range(per_row):
        out[:, j * LANES : (j + 1) * LANES] = flat[
            pl.ds(start + j, rows, stride=per_row), :
        ].astype(BF16)


def turned_to_flat(turned, rows, columns, flat, start):
    per_row = columns // LANES
    for j in range(per_row):
        flat[pl.ds(start + j, rows, stride=per_row), :] = turned[j * LANES : (j + 1) * LANES, :].T


def matrix_to_flat(matrix, rows, columns, flat, start):
    per_row = columns // LANES
    for j in range(per_row):
        flat[pl.ds(start + j, rows, stride=per_row), :] = matrix[:, j * LANES : (j + 1) * LANES]


def prepare_kernel(tok, params, seg, normed_out, normed_turned, own, allowed):
    normed, _ = normalize(tok[...].astype(F32))
    normed_out[...] = normed
    normed_turned[...] = normed.astype(BF16).T
    own[...] = params[...]
    causal = lax.broadcasted_iota(jnp.int32, (SEQ, SEQ), 1) <= lax.broadcasted_iota(
        jnp.int32, (SEQ, SEQ), 0
    )
    for s in range(seg.shape[0]):
        across = jnp.broadcast_to(seg[s : s + 1, :].astype(F32), (SEQ, SEQ))
        allowed[s * SEQ : (s + 1) * SEQ, :] = (causal & (across == across.T)).astype(F32)


def sort_kernel(ids, *refs):
    received, (first, rest, stage, wide) = refs[:Z], refs[Z:]
    for d in range(Z):
        stage[lax.rem(ids[0] + Z - d, Z)] = received[d][...]
    rest[...] = stage[1:]
    wide[:SHARE, :] = stage[0].astype(F32)
    wide[SHARE:SIDE, :] = jnp.zeros((SIDE - SHARE, LANES), F32)
    last = stage[Z - 1].astype(F32)
    wide[SIDE:, :] = last[SMALL_IN_SHARE:, :]
    first[...] = wide[...].astype(BF16)


def attend_kernel(ids, allowed, normed, *refs):
    bufs = refs[: 2 * PLANE]
    project_out, weights_out, attended_out, w_qkv, small, first_out, flat = refs[2 * PLANE :]
    for slot, buf in enumerate(bufs):
        wide = buf[...].astype(F32)
        flat[pl.ds(ids[slot] * SHARE, SHARE), :] = wide[:SHARE, :]

        @pl.when(ids[slot] == 2 * PLANE - 1)
        def _():
            small[...] = wide[SIDE:, :]

    matrix_from_flat(flat, ROW_QKV, D, 3 * D, w_qkv)
    first_out[...] = flat[ROW_OUT:FIRST_ROWS, :]

    gain = small_vector(small, GAIN_ONE, 2)
    shift = small_vector(small, SHIFT_ONE, 2)
    bias = jnp.concatenate(
        [
            small_vector(small, BIAS_QUERY, 2),
            jnp.zeros((1, D), F32),
            small_vector(small, BIAS_VALUE, 2),
        ],
        axis=1,
    )
    def some(g, carry):
        span = pl.ds(pl.multiple_of(g * WIDE, WIDE), WIDE)
        normed_low = (normed[span, :] * gain + shift).astype(BF16)
        project = (dot(normed_low, w_qkv[...]) + bias).astype(BF16)
        project_out[span, :] = project
        scores, values = [], []
        for s in range(GROUP):
            rows = slice(s * SEQ, (s + 1) * SEQ)
            scores.append(
                dot_nt(project[rows, :D] * SCALE, spread_heads(project[rows, D : 2 * D]))
            )
            values.append(spread_heads(project[rows, 2 * D :]))
        weights = []
        for s in range(GROUP):
            low = []
            open_pairs = allowed[pl.ds(pl.multiple_of(g * WIDE + s * SEQ, SEQ), SEQ), :] > 0.5
            for h in range(HEADS):
                mine = jnp.where(open_pairs, scores[s][:, h * SEQ : (h + 1) * SEQ], -1e30)
                grown = jnp.exp(mine - jnp.max(mine, axis=-1, keepdims=True))
                low.append(
                    (grown * (1.0 / jnp.sum(grown, axis=-1, keepdims=True))).astype(BF16)
                )
            weights.append(jnp.concatenate(low, axis=1))
        weights_out[span, :] = jnp.concatenate(weights, axis=0)
        attended_out[span, :] = jnp.concatenate(
            [dot(weights[s], values[s]).astype(BF16) for s in range(GROUP)], axis=0
        )
        return carry

    lax.fori_loop(0, normed.shape[0] // WIDE, some, 0)


def feed_kernel(
    ids, tok, attended, cot, small, first_in, *refs,
):
    bufs = []
    for own, others in (refs[0:2], refs[2:4]):
        bufs.append(own)
        bufs += [others.at[pl.ds(p * (Z - 1), Z - 1)] for p in range(PLANE - 1)]
    (
        middle_out, activated_out, grad_middle_out, grad_attended_out, w_down, keep_out, send_out, first_out,
        w_out, w_up, grad_hidden, flat,
    ) = refs[4:]
    flat[:HEAD_ROWS, :] = first_in[...]
    for slot, buf in enumerate(bufs):
        for z in range(1, Z):
            share = ids[slot] + z * 2 * PLANE
            flat[pl.ds(share * SHARE - ROW_OUT, SHARE), :] = buf[z - 1].astype(F32)
    matrix_from_flat(flat, 0, D, D, w_out)
    matrix_from_flat(flat, ROW_UP - ROW_OUT, D, FF, w_up)
    matrix_from_flat(flat, ROW_DOWN - ROW_OUT, FF, D, w_down)

    gain = small_vector(small, GAIN_TWO, 2)
    middle = (
        tok[...].astype(F32) + dot(attended[...], w_out[...]) + small_vector(small, BIAS_OUT, 2)
    )
    middle_out[...] = middle
    normed, rate = normalize(middle)
    normed_low = (normed * gain + small_vector(small, SHIFT_TWO, 2)).astype(BF16)
    normed_turned = normed_low.T
    cotangent = cot[...]
    cot_turned = cotangent.T
    slope = 0.7978845608028654
    cubic = slope * 0.044715
    row_up, row_down = ROW_UP - ROW_OUT, ROW_DOWN - ROW_OUT

    def products(c):
        columns = slice(c, c + CHUNK)
        return dot(normed_low, w_up[:, columns]), dot_nt(cotangent, w_down[columns, :])

    def bend(c, hidden_all, grad_all):
        columns = slice(c, c + CHUNK)
        bias = small_vector(small, BIAS_UP + c // LANES, CHUNK // LANES)
        total = jnp.zeros((8, CHUNK), F32)
        for r in range(0, tok.shape[0], STRIP):
            rows = slice(r, r + STRIP)
            hidden = hidden_all[rows] + bias
            square = hidden * hidden
            half = 0.5 + 0.5 * jnp.tanh(hidden * (slope + cubic * square))
            activated = hidden * half
            derivative = half + activated * (1.0 - half) * (2 * slope + (6 * cubic) * square)
            low = (grad_all[rows] * derivative).astype(BF16)
            activated_out[rows, columns] = activated.astype(BF16)
            grad_hidden[rows, columns] = low
            total += fold_rows(low.astype(F32))
        return total

    def weight_gradients(c):
        columns = slice(c, c + CHUNK)
        turned_to_flat(dot(cot_turned, activated_out[:, columns]), CHUNK, D, flat, row_down + c * D // LANES)
        grads = dot(normed_turned, grad_hidden[:, columns])
        for j in range(CHUNK // LANES):
            flat[pl.ds(row_up + c // LANES + j, D, stride=FF // LANES), :] = grads[
                :, j * LANES : (j + 1) * LANES
            ]

    ahead, totals = products(0), []
    for c in range(0, FF, CHUNK):
        now = ahead
        if c + CHUNK < FF:
            ahead = products(c + CHUNK)
        if c > 0:
            weight_gradients(c - CHUNK)
        totals.append(bend(c, *now))
    grad_normed = dot_nt(grad_hidden[...], w_up[...])
    weight_gradients(FF - CHUNK)
    grad_result = cotangent.astype(F32)
    grad_middle = grad_result + normalize_back(grad_normed, gain, normed, rate)
    grad_middle_out[...] = grad_middle
    grad_middle_low = grad_middle.astype(BF16)
    grad_attended_out[...] = dot_nt(grad_middle_low, w_out[...]).astype(BF16)
    matrix_to_flat(dot_tn(attended[...], grad_middle_low), D, D, flat, 0)
    sums = jnp.concatenate(
        [
            fold_rows(grad_middle_low.astype(F32)),
            fold_rows(grad_normed * normed),
            fold_rows(grad_normed),
            *totals,
            fold_rows(grad_result),
        ],
        axis=1,
    )
    sums = jnp.sum(sums, axis=0, keepdims=True)
    base = ROW_SMALL - ROW_OUT
    flat[base : base + LATE_SMALL, :] = jnp.zeros((LATE_SMALL, LANES), F32)
    for i in range(sums.shape[1] // LANES):
        row = base + LATE_SMALL + i
        flat[row : row + 1, :] = sums[:, i * LANES : (i + 1) * LANES]
    flat[ROW_END - ROW_OUT :, :] = jnp.zeros((ROW_TOTAL - ROW_END, LANES), F32)
    first_out[...] = flat[:HEAD_ROWS, :]
    for target, out in enumerate((keep_out, send_out)):
        for p in range(PLANE):
            for z in range(1, Z):
                share = ids[target * PLANE + p] + z * 2 * PLANE
                rows = flat[pl.ds(share * SHARE - ROW_OUT, SHARE), :]
                out[p * (Z - 1) + z - 1] = rows.astype(out.dtype)


def result_kernel(middle, activated, w_down, small, result_out):
    result = middle[...] + dot(activated[...], w_down[...]) + small_vector(small, BIAS_DOWN, 2)
    result_out[...] = result.astype(BF16)


def attend_back_kernel(
    ids, project, weights, grad_attended, normed_turned, w_qkv, small, first_in,
    grad_project, keep_out, send_out, flat, wide,
):
    def some(g, carry):
        base = g * WIDE
        spans = [pl.ds(pl.multiple_of(base + s * SEQ, SEQ), SEQ) for s in range(GROUP)]
        grad_weights = [
            dot_nt(grad_attended[span, :], spread_heads(project[span, 2 * D :])) for span in spans
        ]
        scores_low, scores_turned, weights_turned = [], [], []
        for s, span in enumerate(spans):
            low, turned, mine_turned = [], [], []
            for h in range(HEADS):
                columns = slice(h * SEQ, (h + 1) * SEQ)
                mine_low = weights[span, columns]
                mine = mine_low.astype(F32)
                product = mine * grad_weights[s][:, columns]
                grad_scores = (product - mine * jnp.sum(product, axis=-1, keepdims=True)) * SCALE
                low.append(grad_scores.astype(BF16))
                turned.append(low[-1].T)
                mine_turned.append(mine_low.T)
            scores_low.append(jnp.concatenate(low, axis=1))
            scores_turned.append(jnp.concatenate(turned, axis=1))
            weights_turned.append(jnp.concatenate(mine_turned, axis=1))
        for s, span in enumerate(spans):
            key = spread_heads(project[span, D : 2 * D])
            grad_project[span, :D] = dot(scores_low[s], key).astype(BF16)
            query = spread_heads(project[span, :D])
            grad_project[span, D : 2 * D] = dot(scores_turned[s], query).astype(BF16)
            grad_value = dot(weights_turned[s], spread_heads(grad_attended[span, :]))
            grad_project[span, 2 * D :] = grad_value.astype(BF16)
        return carry

    lax.fori_loop(0, project.shape[0] // WIDE, some, 0)
    products = dot(normed_turned[...], grad_project[...])
    sums = jnp.sum(fold_rows(grad_project[...].astype(F32)), axis=0, keepdims=True)
    gain = jnp.broadcast_to(small_vector(small, GAIN_ONE, 2), (LANES, D)).T
    shift = jnp.broadcast_to(small_vector(small, SHIFT_ONE, 2), (LANES, D)).T
    grad_gain = jnp.zeros((D, LANES), F32)
    grad_shift = jnp.zeros((D, LANES), F32)
    per_row = 3 * D // LANES
    for j in range(per_row):
        columns = slice(j * LANES, (j + 1) * LANES)
        weight = w_qkv[:, columns].astype(F32)
        grad_gain += products[:, columns] * weight
        grad_shift += sums[:, columns] * weight
        flat[pl.ds(j, D, stride=per_row), :] = products[:, columns] * gain + sums[:, columns] * shift
    flat[ROW_OUT:, :] = first_in[...]
    grad_gain = jnp.sum(grad_gain.T, axis=0, keepdims=True)
    grad_shift = jnp.sum(grad_shift.T, axis=0, keepdims=True)
    late = jnp.concatenate([grad_gain, grad_shift, sums[:, :D], sums[:, 2 * D :]], axis=1)
    side = jnp.concatenate(
        [late[:, i * LANES : (i + 1) * LANES] for i in range(LATE_SMALL)]
        + [jnp.zeros((SIDE_ROWS - LATE_SMALL, LANES), F32)],
        axis=0,
    )
    wide[SHARE:SIDE, :] = jnp.zeros((SIDE - SHARE, LANES), F32)
    for target, out in enumerate((keep_out, send_out)):
        for p in range(PLANE):
            share = ids[target * PLANE + p]
            wide[:SHARE, :] = flat[pl.ds(share * SHARE, SHARE), :]
            wide[SIDE:, :] = jnp.where(share == 2 * PLANE - 1, side, 0.0)
            out[p] = wide[...].astype(out.dtype)


def input_grad_kernel(tok, grad_project, grad_middle, w_qkv, small, input_grad_out):
    gain = small_vector(small, GAIN_ONE, 2)

    def some(g, carry):
        span = pl.ds(pl.multiple_of(g * WIDE, WIDE), WIDE)
        normed, rate = normalize(tok[span, :].astype(F32))
        grad_normed = dot_nt(grad_project[span, :], w_qkv[...])
        input_grad_out[span, :] = grad_middle[span, :] + normalize_back(
            grad_normed, gain, normed, rate
        )
        return carry

    lax.fori_loop(0, tok.shape[0] // WIDE, some, 0)


def stack_kernel(*refs):
    row = 0
    for ref in refs[:-1]:
        refs[-1][row : row + ref.shape[0]] = ref[...]
        row += ref.shape[0]


def add_core_kernel(first, first_in, rest, rest_in, keep_out, *refs):
    sends, column = refs[:-1], refs[-1]
    end = SMALL_IN_SHARE + LATE_SMALL
    for p, out in enumerate((keep_out, *sends)):
        item = first[p] + first_in[p].astype(F32)
        span = slice(p * (Z - 1), (p + 1) * (Z - 1))
        column[0] = item[:SHARE, :]
        column[1:] = rest[span] + rest_in[span].astype(F32)
        column[Z - 1, SMALL_IN_SHARE:end, :] += item[SIDE : SIDE + LATE_SMALL, :]
        out[...] = column[...].astype(out.dtype)


def add_plane_kernel(ids, kept, *refs):
    arrived = refs[: PLANE - 1]
    keep_out, *sends, column = refs[PLANE - 1 :]
    column[...] = kept[...] + sum(item[...].astype(F32) for item in arrived)
    keep_out[...] = column[ids[0]]
    for d, out in enumerate(sends):
        out[...] = column[lax.rem(ids[0] + d + 1, Z)].astype(BF16)


def add_column_kernel(kept, *refs):
    refs[-1][...] = kept[...] + sum(item[...].astype(F32) for item in refs[:-1])


def like(*shape, kind=F32):
    return jax.ShapeDtypeStruct(shape, kind)


SMEM_SPEC = pl.BlockSpec(memory_space=pltpu.SMEM)
VMEM_SPEC = pl.BlockSpec(memory_space=pltpu.VMEM)

def cost(us):
    return pl.CostEstimate(flops=int(us * 1e9), bytes_accessed=1 << 20, transcendentals=0)


def call(kernel, name, ids, inputs, outs, scratch=(), us=1):
    with_ids = ids is not None
    results = pl.pallas_call(
        kernel,
        in_specs=[SMEM_SPEC] * with_ids + [VMEM_SPEC] * len(inputs),
        out_specs=[VMEM_SPEC] * len(outs),
        out_shape=list(outs),
        scratch_shapes=list(scratch),
        compiler_params=pltpu.CompilerParams(vmem_limit_bytes=VMEM_BYTES),
        cost_estimate=cost(us),
        name=name,
    )(*([ids] if with_ids else []), *inputs)
    return results if len(outs) > 1 else results[0]


def prepare(tokens, params, segment_ids):
    rows = tokens.shape[0]
    return call(
        prepare_kernel, "prepare", None, [tokens, params, segment_ids.reshape(-1, SEQ)],
        [
            like(rows, D),
            like(D, rows, kind=BF16),
            like(*params.shape, kind=BF16),
            like(rows, SEQ),
        ],
        us=2,
    )


def stack(items):
    shape = (sum(item.shape[0] for item in items),) + items[0].shape[1:]
    return call(stack_kernel, "stack", None, items, [like(*shape, kind=items[0].dtype)])


def attend(ids, allowed, normed, bufs):
    rows = normed.shape[0]
    shapes = [(rows, 3 * D), (rows, HEADS * SEQ), (rows, D), (D, 3 * D)]
    return call(
        attend_kernel, "attend", ids, [allowed, normed, *bufs],
        [like(*shape, kind=BF16) for shape in shapes]
        + [like(SMALL_ROWS, LANES), like(HEAD_ROWS, LANES)],
        [pltpu.VMEM((FIRST_ROWS, LANES), F32)], us=0.2,
    )


def feed(ids, tokens, attended, cotangent, small, first, bufs, send_kind):
    rows = tokens.shape[0]
    return call(
        feed_kernel, "feed", ids, [tokens, attended, cotangent, small, first, *bufs],
        [
            like(rows, D),
            like(rows, FF, kind=BF16),
            like(rows, D),
            like(rows, D, kind=BF16),
            like(FF, D, kind=BF16),
            like(PLANE * (Z - 1), SHARE, LANES),
            like(PLANE * (Z - 1), SHARE, LANES, kind=send_kind),
            like(HEAD_ROWS, LANES),
        ],
        [
            pltpu.VMEM((D, D), BF16),
            pltpu.VMEM((D, FF), BF16),
            pltpu.VMEM((rows, FF), BF16),
            pltpu.VMEM((ROW_TOTAL - ROW_OUT, LANES), F32),
        ],
        us=8,
    )


def result(middle, activated, w_down, small):
    return call(
        result_kernel, "result", None, [middle, activated, w_down, small],
        [like(*middle.shape, kind=BF16)], us=2,
    )


def attend_back(ids, project, weights, grad_attended, normed_turned, w_qkv, small, first, send_kind):
    shape = (PLANE, SIDE + SIDE_ROWS, LANES)
    return call(
        attend_back_kernel, "attend_back", ids,
        [project, weights, grad_attended, normed_turned, w_qkv, small, first],
        [like(*project.shape, kind=BF16), like(*shape), like(*shape, kind=send_kind)],
        [pltpu.VMEM((FIRST_ROWS, LANES), F32), pltpu.VMEM(shape[1:], F32)], us=4,
    )


def input_gradient(tokens, grad_project, grad_middle, w_qkv, small):
    return call(
        input_grad_kernel, "input_grad", None, [tokens, grad_project, grad_middle, w_qkv, small],
        [like(*tokens.shape)], us=2,
    )


def local_any(n, tokens, params, segment_ids, cotangent):
    total = n * params.shape[0]
    normed, normed_turned, _, allowed = prepare(tokens, params, segment_ids)
    gathered = lax.all_gather(params, "fsdp", axis=0).reshape(total, LANES)
    shares = gathered[:ROW_TOTAL].reshape(Z, 2 * PLANE, SHARE, LANES)
    order = [p * 2 + c for c in range(2) for p in range(PLANE)]
    side = jnp.concatenate(
        [jnp.zeros((SIDE - SHARE, LANES), BF16), gathered[ROW_SMALL:ROW_TOTAL]], axis=0
    )
    firsts = [jnp.concatenate([shares[0, k], side], axis=0) for k in order]
    rests = []
    for group in (order[:PLANE], order[PLANE:]):
        rests += [shares[1:, group[0]], jnp.concatenate([shares[1:, k] for k in group[1:]])]
    ids = jnp.array(order, jnp.int32)
    project, weights, attended, w_qkv, small, first = attend(ids, allowed, normed, firsts)
    middle, activated, grad_middle, grad_attended, w_down, rest, rest_send, first_grad = feed(
        ids, tokens, attended, cotangent, small, first, rests, F32
    )
    outputs = result(middle, activated, w_down, small)
    grad_project, first, first_send = attend_back(
        ids, project, weights, grad_attended, normed_turned, w_qkv, small, first_grad, F32
    )
    input_grad = input_gradient(tokens, grad_project, grad_middle, w_qkv, small)
    first = jnp.stack([first, first_send], axis=1)
    rest = jnp.stack([rest, rest_send]).reshape(2, PLANE, Z - 1, SHARE, LANES).transpose(2, 1, 0, 3, 4)
    flat = jnp.concatenate(
        [
            first[:, :, :SHARE].reshape(-1, LANES),
            rest.reshape(-1, LANES),
            jnp.zeros((total - ROW_TOTAL, LANES), F32),
        ],
        axis=0,
    )
    flat = flat.at[ROW_SMALL : ROW_SMALL + LATE_SMALL].add(
        first[PLANE - 1, 1, SIDE : SIDE + LATE_SMALL]
    )
    param_grad = lax.psum_scatter(flat, "fsdp", scatter_dimension=0, tiled=True)
    return outputs, input_grad, param_grad


def index_of(z, plane, core):
    return (z * PLANE + plane) * 2 + core


def move(values, step_z, step_plane, step_core):
    pairs = [
        (index_of(z, p, c), index_of((z + step_z) % Z, p ^ step_plane, c ^ step_core))
        for z in range(Z)
        for p in range(PLANE)
        for c in range(2)
    ]
    return lax.ppermute(values, "fsdp", pairs)


STEPS = (3, 1, 2)


def local_slice(tokens, params, segment_ids, cotangent):
    me = lax.axis_index("fsdp").astype(jnp.int32)
    z, plane, core = me // (2 * PLANE), (me // 2) % PLANE, me % 2
    where = z.reshape(1)
    ids = jnp.stack(
        [(plane ^ dp) * 2 + (core ^ dc) for dc in range(2) for dp in (0, *STEPS)]
    )

    normed, normed_turned, own, allowed = prepare(tokens, params, segment_ids)
    first, rest = call(
        sort_kernel, "sort_shares", where, [own] + [move(params, d, 0, 0) for d in range(1, Z)],
        [like(SIDE + SMALL_ROWS, LANES, kind=BF16), like(Z - 1, SHARE, LANES, kind=BF16)],
        [pltpu.VMEM((Z, SHARE, LANES), BF16), pltpu.VMEM((SIDE + SMALL_ROWS, LANES), F32)],
    )
    firsts = [first] + [move(first, 0, d, 0) for d in STEPS]
    rests = [move(rest, 0, d, 0) for d in STEPS]
    firsts = firsts + [move(item, 0, 0, 1) for item in firsts]
    project, weights, attended, w_qkv, small, first = attend(ids, allowed, normed, firsts)
    *rests, attended = lax.optimization_barrier((*rests, attended))
    rests = stack(rests)
    rests = [rest, rests, move(rest, 0, 0, 1), move(rests, 0, 0, 1)]
    middle, activated, grad_middle, grad_attended, w_down, rest, send, first_grad = feed(
        ids, tokens, attended, cotangent, small, first, rests, BF16
    )

    rest_in = move(send, 0, 0, 1)
    grad_project, first, send = attend_back(
        ids, project, weights, grad_attended, normed_turned, w_qkv, small, first_grad, BF16
    )
    first_in = move(send, 0, 0, 1)
    part = (Z, SHARE, LANES)
    kept, *sends = call(
        add_core_kernel, "add_core", None, [first, first_in, rest, rest_in],
        [like(*part)] + [like(*part, kind=BF16)] * (PLANE - 1), [pltpu.VMEM(part, F32)],
    )
    arrived = [move(item, 0, d, 0) for item, d in zip(sends, STEPS)]
    outputs = result(middle, activated, w_down, small)
    input_grad = input_gradient(tokens, grad_project, grad_middle, w_qkv, small)
    kept, *sends = call(
        add_plane_kernel, "add_plane", where, [kept] + arrived,
        [like(SHARE, LANES)] + [like(SHARE, LANES, kind=BF16)] * (Z - 1), [pltpu.VMEM(part, F32)],
    )
    arrived = [move(item, d + 1, 0, 0) for d, item in enumerate(sends)]
    param_grad = call(
        add_column_kernel, "add_column", None, [kept] + arrived, [like(SHARE, LANES)]
    )
    return outputs, input_grad, param_grad


def solution(mesh):
    n = mesh.shape["fsdp"]
    local = local_slice if n == 2 * PLANE * Z else functools.partial(local_any, n)
    in_specs = (P("fsdp", None), P("fsdp", None), P("fsdp"), P("fsdp", None))
    out_specs = (P("fsdp", None), P("fsdp", None), P("fsdp", None))
    return jax.shard_map(local, mesh=mesh, in_specs=in_specs, out_specs=out_specs, check_vma=False)
```

```python
import functools

import jax
import jax.numpy as jnp
from jax import lax
from jax.experimental import pallas as pl
from jax.experimental.pallas import tpu as pltpu
from jax.sharding import PartitionSpec as P

D = 256
HEADS = 4
HEAD_DIM = 64
FF = 1024
SEQ = 128
LANES = 128
GROUP = 4
WIDE = GROUP * SEQ
CHUNK = 256
STRIP = 64
EPSILON = 1e-05
SCALE = HEAD_DIM ** (-0.5)
VMEM_BYTES = 24 * 1024 * 1024

ROW_QKV = 0
ROW_OUT = 1536
ROW_UP = 2048
ROW_DOWN = 4096
ROW_SMALL = 6144
ROW_END = 6168
ROW_TOTAL = 6176
GAIN_ONE, SHIFT_ONE, BIAS_QUERY, BIAS_VALUE, BIAS_OUT = 0, 2, 4, 6, 8
GAIN_TWO, SHIFT_TWO, BIAS_UP, BIAS_DOWN = 10, 12, 14, 22
SMALL_ROWS = 32
LATE_SMALL = 8

SHARE = 193
Z, PLANE = 4, 4
FIRST_ROWS = 2 * PLANE * SHARE
HEAD_ROWS = FIRST_ROWS - ROW_OUT
SIDE, SIDE_ROWS = 208, 16
SMALL_IN_SHARE = ROW_SMALL - (2 * PLANE * Z - 1) * SHARE

F32 = jnp.float32
BF16 = jnp.bfloat16


def dot(left, right):
    return jnp.dot(left, right, preferred_element_type=F32)


def dot_nt(left, right):
    return lax.dot_general(left, right, (((1,), (1,)), ((), ())), preferred_element_type=F32)


def dot_tn(left, right):
    return lax.dot_general(left, right, (((0,), (0,)), ((), ())), preferred_element_type=F32)


def small_vector(small, row, count):
    return jnp.concatenate([small[row + i : row + i + 1, :] for i in range(count)], axis=1)


def fold_rows(values):
    rows, columns = values.shape
    return jnp.sum(values.reshape(rows // 8, 8, columns), axis=0)


def normalize(values):
    center = values - jnp.mean(values, axis=-1, keepdims=True)
    rate = lax.rsqrt(jnp.mean(center * center, axis=-1, keepdims=True) + EPSILON)
    return center * rate, rate


def normalize_back(grad, gain, normed, rate):
    scaled = grad * gain
    return rate * (
        scaled
        - jnp.mean(scaled, axis=-1, keepdims=True)
        - normed * jnp.mean(scaled * normed, axis=-1, keepdims=True)
    )


def head_masks():
    lane = lax.broadcasted_iota(jnp.int32, (1, D), 1)
    return [(lane // HEAD_DIM == h).astype(F32).astype(BF16) for h in range(HEADS)]


def spread_heads(rows):
    return jnp.concatenate([rows * mask for mask in head_masks()], axis=0)


def matrix_from_flat(flat, start, rows, columns, out):
    per_row = columns // LANES
    for j in range(per_row):
        out[:, j * LANES : (j + 1) * LANES] = flat[
            pl.ds(start + j, rows, stride=per_row), :
        ].astype(BF16)


def turned_to_flat(turned, rows, columns, flat, start):
    per_row = columns // LANES
    for j in range(per_row):
        flat[pl.ds(start + j, rows, stride=per_row), :] = turned[j * LANES : (j + 1) * LANES, :].T


def matrix_to_flat(matrix, rows, columns, flat, start):
    per_row = columns // LANES
    for j in range(per_row):
        flat[pl.ds(start + j, rows, stride=per_row), :] = matrix[:, j * LANES : (j + 1) * LANES]


def prepare_kernel(tok, params, seg, normed_out, normed_turned, own, allowed):
    normed, _ = normalize(tok[...].astype(F32))
    normed_out[...] = normed
    normed_turned[...] = normed.astype(BF16).T
    own[...] = params[...]
    causal = lax.broadcasted_iota(jnp.int32, (SEQ, SEQ), 1) <= lax.broadcasted_iota(
        jnp.int32, (SEQ, SEQ), 0
    )
    for s in range(seg.shape[0]):
        across = jnp.broadcast_to(seg[s : s + 1, :].astype(F32), (SEQ, SEQ))
        allowed[s * SEQ : (s + 1) * SEQ, :] = (causal & (across == across.T)).astype(F32)


def sort_kernel(ids, *refs):
    received, (first, rest, stage, wide) = refs[:Z], refs[Z:]
    for d in range(Z):
        stage[lax.rem(ids[0] + Z - d, Z)] = received[d][...]
    rest[...] = stage[1:]
    wide[:SHARE, :] = stage[0].astype(F32)
    wide[SHARE:SIDE, :] = jnp.zeros((SIDE - SHARE, LANES), F32)
    last = stage[Z - 1].astype(F32)
    wide[SIDE:, :] = last[SMALL_IN_SHARE:, :]
    first[...] = wide[...].astype(BF16)


def attend_kernel(ids, allowed, normed, *refs):
    bufs = refs[: 2 * PLANE]
    project_out, weights_out, attended_out, w_qkv, small, first_out, flat = refs[2 * PLANE :]
    for slot, buf in enumerate(bufs):
        wide = buf[...].astype(F32)
        flat[pl.ds(ids[slot] * SHARE, SHARE), :] = wide[:SHARE, :]

        @pl.when(ids[slot] == 2 * PLANE - 1)
        def _():
            small[...] = wide[SIDE:, :]

    matrix_from_flat(flat, ROW_QKV, D, 3 * D, w_qkv)
    first_out[...] = flat[ROW_OUT:FIRST_ROWS, :]

    gain = small_vector(small, GAIN_ONE, 2)
    shift = small_vector(small, SHIFT_ONE, 2)
    bias = jnp.concatenate(
        [
            small_vector(small, BIAS_QUERY, 2),
            jnp.zeros((1, D), F32),
            small_vector(small, BIAS_VALUE, 2),
        ],
        axis=1,
    )
    for g in range(normed.shape[0] // WIDE):
        span = slice(g * WIDE, (g + 1) * WIDE)
        normed_low = (normed[span, :] * gain + shift).astype(BF16)
        project = (dot(normed_low, w_qkv[...]) + bias).astype(BF16)
        project_out[span, :] = project
        scores, values = [], []
        for s in range(GROUP):
            rows = slice(s * SEQ, (s + 1) * SEQ)
            scores.append(
                dot_nt(project[rows, :D] * SCALE, spread_heads(project[rows, D : 2 * D]))
            )
            values.append(spread_heads(project[rows, 2 * D :]))
        weights = []
        for s in range(GROUP):
            low = []
            open_pairs = allowed[g * WIDE + s * SEQ : g * WIDE + (s + 1) * SEQ, :] > 0.5
            for h in range(HEADS):
                mine = jnp.where(open_pairs, scores[s][:, h * SEQ : (h + 1) * SEQ], -1e30)
                grown = jnp.exp(mine - jnp.max(mine, axis=-1, keepdims=True))
                low.append(
                    (grown * (1.0 / jnp.sum(grown, axis=-1, keepdims=True))).astype(BF16)
                )
            weights.append(jnp.concatenate(low, axis=1))
        weights_out[span, :] = jnp.concatenate(weights, axis=0)
        attended_out[span, :] = jnp.concatenate(
            [dot(weights[s], values[s]).astype(BF16) for s in range(GROUP)], axis=0
        )


def feed_kernel(
    ids, tok, attended, cot, small, first_in, *refs,
):
    bufs = []
    for own, others in (refs[0:2], refs[2:4]):
        bufs.append(own)
        bufs += [others.at[pl.ds(p * (Z - 1), Z - 1)] for p in range(PLANE - 1)]
    (
        middle_out, activated_out, grad_middle_out, grad_attended_out, w_down, keep_out, send_out, first_out,
        w_out, w_up, grad_hidden, flat,
    ) = refs[4:]
    flat[:HEAD_ROWS, :] = first_in[...]
    for slot, buf in enumerate(bufs):
        for z in range(1, Z):
            share = ids[slot] + z * 2 * PLANE
            flat[pl.ds(share * SHARE - ROW_OUT, SHARE), :] = buf[z - 1].astype(F32)
    matrix_from_flat(flat, 0, D, D, w_out)
    matrix_from_flat(flat, ROW_UP - ROW_OUT, D, FF, w_up)
    matrix_from_flat(flat, ROW_DOWN - ROW_OUT, FF, D, w_down)

    gain = small_vector(small, GAIN_TWO, 2)
    shift = small_vector(small, SHIFT_TWO, 2)
    bias_out = small_vector(small, BIAS_OUT, 2)
    slope = 0.7978845608028654
    cubic = slope * 0.044715
    row_up, row_down = ROW_UP - ROW_OUT, ROW_DOWN - ROW_OUT
    spans = [slice(r, r + WIDE) for r in range(0, tok.shape[0], WIDE)]
    cot_turned = cot[...].T

    def head(span):
        middle = tok[span, :].astype(F32) + dot(attended[span, :], w_out[...]) + bias_out
        middle_out[span, :] = middle
        normed, rate = normalize(middle)
        normed_low = (normed * gain + shift).astype(BF16)
        return normed, rate, normed_low, normed_low.T

    def products(span, normed_low, c):
        columns = slice(c, c + CHUNK)
        return dot(normed_low, w_up[:, columns]), dot_nt(cot[span, :], w_down[columns, :])

    def bend(span, c, hidden_all, grad_all):
        columns = slice(c, c + CHUNK)
        bias = small_vector(small, BIAS_UP + c // LANES, CHUNK // LANES)
        total = jnp.zeros((8, CHUNK), F32)
        for r in range(0, WIDE, STRIP):
            rows = slice(r, r + STRIP)
            hidden = hidden_all[rows] + bias
            square = hidden * hidden
            half = 0.5 + 0.5 * jnp.tanh(hidden * (slope + cubic * square))
            activated = hidden * half
            derivative = half + activated * (1.0 - half) * (2 * slope + (6 * cubic) * square)
            low = (grad_all[rows] * derivative).astype(BF16)
            activated_out[span.start + r : span.start + r + STRIP, columns] = activated.astype(BF16)
            grad_hidden[span.start + r : span.start + r + STRIP, columns] = low
            total += fold_rows(low.astype(F32))
        return total

    def weight_gradients(normed_turned, c):
        columns = slice(c, c + CHUNK)
        turned_to_flat(dot(cot_turned, activated_out[:, columns]), CHUNK, D, flat, row_down + c * D // LANES)
        grads = dot(normed_turned, grad_hidden[:, columns])
        for j in range(CHUNK // LANES):
            flat[pl.ds(row_up + c // LANES + j, D, stride=FF // LANES), :] = grads[
                :, j * LANES : (j + 1) * LANES
            ]

    def tail(span, normed, rate):
        grad_normed = dot_nt(grad_hidden[span, :], w_up[...])
        grad_result = cot[span, :].astype(F32)
        grad_middle = grad_result + normalize_back(grad_normed, gain, normed, rate)
        grad_middle_out[span, :] = grad_middle
        low = grad_middle.astype(BF16)
        grad_attended_out[span, :] = dot_nt(low, w_out[...]).astype(BF16)
        sums = [low.astype(F32), grad_normed * normed, grad_normed, grad_result]
        return dot_tn(attended[span, :], low), [fold_rows(item) for item in sums]

    chunks = range(0, FF, CHUNK)
    heads = [head(spans[0])]
    totals = [0.0] * len(chunks)
    grad_out, sums = 0.0, [0.0] * 4
    for n, span in enumerate(spans):
        normed, rate, normed_low, _ = heads[n]
        ahead = products(span, normed_low, 0)
        if n + 1 < len(spans):
            heads.append(head(spans[n + 1]))
        if n > 0:
            added, more = tail(spans[n - 1], *heads[n - 1][:2])
            grad_out, sums = grad_out + added, [a + b for a, b in zip(sums, more)]
        if n + 1 == len(spans):
            normed_turned = jnp.concatenate([item[3] for item in heads], axis=1)
        for i, c in enumerate(chunks):
            now = ahead
            if c + CHUNK < FF:
                ahead = products(span, normed_low, c + CHUNK)
            if n + 1 == len(spans) and c > 0:
                weight_gradients(normed_turned, c - CHUNK)
            totals[i] += bend(span, c, *now)
    added, more = tail(spans[-1], *heads[-1][:2])
    grad_out, sums = grad_out + added, [a + b for a, b in zip(sums, more)]
    weight_gradients(normed_turned, FF - CHUNK)
    matrix_to_flat(grad_out, D, D, flat, 0)
    sums = jnp.concatenate([*sums[:3], *totals, sums[3]], axis=1)
    sums = jnp.sum(sums, axis=0, keepdims=True)
    base = ROW_SMALL - ROW_OUT
    flat[base : base + LATE_SMALL, :] = jnp.zeros((LATE_SMALL, LANES), F32)
    for i in range(sums.shape[1] // LANES):
        row = base + LATE_SMALL + i
        flat[row : row + 1, :] = sums[:, i * LANES : (i + 1) * LANES]
    flat[ROW_END - ROW_OUT :, :] = jnp.zeros((ROW_TOTAL - ROW_END, LANES), F32)
    first_out[...] = flat[:HEAD_ROWS, :]
    for target, out in enumerate((keep_out, send_out)):
        for p in range(PLANE):
            for z in range(1, Z):
                share = ids[target * PLANE + p] + z * 2 * PLANE
                rows = flat[pl.ds(share * SHARE - ROW_OUT, SHARE), :]
                out[p * (Z - 1) + z - 1] = rows.astype(out.dtype)


def result_kernel(middle, activated, w_down, small, result_out):
    result = middle[...] + dot(activated[...], w_down[...]) + small_vector(small, BIAS_DOWN, 2)
    result_out[...] = result.astype(BF16)


def attend_back_kernel(
    ids, project, weights, grad_attended, normed_turned, w_qkv, small, first_in,
    grad_project, keep_out, send_out, flat, wide,
):
    products, sums = 0.0, 0.0
    for g in range(project.shape[0] // WIDE):
        spans = [slice(r, r + SEQ) for r in range(g * WIDE, (g + 1) * WIDE, SEQ)]
        grad_weights = [
            dot_nt(grad_attended[span, :], spread_heads(project[span, 2 * D :])) for span in spans
        ]
        scores_low, scores_turned, weights_turned = [], [], []
        for s, span in enumerate(spans):
            low, turned, mine_turned = [], [], []
            for h in range(HEADS):
                columns = slice(h * SEQ, (h + 1) * SEQ)
                mine_low = weights[span, columns]
                mine = mine_low.astype(F32)
                product = mine * grad_weights[s][:, columns]
                grad_scores = (product - mine * jnp.sum(product, axis=-1, keepdims=True)) * SCALE
                low.append(grad_scores.astype(BF16))
                turned.append(low[-1].T)
                mine_turned.append(mine_low.T)
            scores_low.append(jnp.concatenate(low, axis=1))
            scores_turned.append(jnp.concatenate(turned, axis=1))
            weights_turned.append(jnp.concatenate(mine_turned, axis=1))
        for s, span in enumerate(spans):
            key = spread_heads(project[span, D : 2 * D])
            grad_project[span, :D] = dot(scores_low[s], key).astype(BF16)
            query = spread_heads(project[span, :D])
            grad_project[span, D : 2 * D] = dot(scores_turned[s], query).astype(BF16)
            grad_value = dot(weights_turned[s], spread_heads(grad_attended[span, :]))
            grad_project[span, 2 * D :] = grad_value.astype(BF16)
        span = slice(g * WIDE, (g + 1) * WIDE)
        products += dot(normed_turned[:, span], grad_project[span, :])
        sums += fold_rows(grad_project[span, :].astype(F32))
    sums = jnp.sum(sums, axis=0, keepdims=True)
    gain = jnp.broadcast_to(small_vector(small, GAIN_ONE, 2), (LANES, D)).T
    shift = jnp.broadcast_to(small_vector(small, SHIFT_ONE, 2), (LANES, D)).T
    grad_gain = jnp.zeros((D, LANES), F32)
    grad_shift = jnp.zeros((D, LANES), F32)
    per_row = 3 * D // LANES
    for j in range(per_row):
        columns = slice(j * LANES, (j + 1) * LANES)
        weight = w_qkv[:, columns].astype(F32)
        grad_gain += products[:, columns] * weight
        grad_shift += sums[:, columns] * weight
        flat[pl.ds(j, D, stride=per_row), :] = products[:, columns] * gain + sums[:, columns] * shift
    flat[ROW_OUT:, :] = first_in[...]
    grad_gain = jnp.sum(grad_gain.T, axis=0, keepdims=True)
    grad_shift = jnp.sum(grad_shift.T, axis=0, keepdims=True)
    late = jnp.concatenate([grad_gain, grad_shift, sums[:, :D], sums[:, 2 * D :]], axis=1)
    side = jnp.concatenate(
        [late[:, i * LANES : (i + 1) * LANES] for i in range(LATE_SMALL)]
        + [jnp.zeros((SIDE_ROWS - LATE_SMALL, LANES), F32)],
        axis=0,
    )
    wide[SHARE:SIDE, :] = jnp.zeros((SIDE - SHARE, LANES), F32)
    for target, out in enumerate((keep_out, send_out)):
        for p in range(PLANE):
            share = ids[target * PLANE + p]
            wide[:SHARE, :] = flat[pl.ds(share * SHARE, SHARE), :]
            wide[SIDE:, :] = jnp.where(share == 2 * PLANE - 1, side, 0.0)
            out[p] = wide[...].astype(out.dtype)


def input_grad_kernel(tok, grad_project, grad_middle, w_qkv, small, input_grad_out):
    gain = small_vector(small, GAIN_ONE, 2)

    def some(g, carry):
        span = pl.ds(pl.multiple_of(g * WIDE, WIDE), WIDE)
        normed, rate = normalize(tok[span, :].astype(F32))
        grad_normed = dot_nt(grad_project[span, :], w_qkv[...])
        input_grad_out[span, :] = grad_middle[span, :] + normalize_back(
            grad_normed, gain, normed, rate
        )
        return carry

    lax.fori_loop(0, tok.shape[0] // WIDE, some, 0)


def stack_kernel(*refs):
    row = 0
    for ref in refs[:-1]:
        refs[-1][row : row + ref.shape[0]] = ref[...]
        row += ref.shape[0]


def add_core_kernel(first, first_in, rest, rest_in, keep_out, *refs):
    sends, column = refs[:-1], refs[-1]
    end = SMALL_IN_SHARE + LATE_SMALL
    for p, out in enumerate((keep_out, *sends)):
        item = first[p] + first_in[p].astype(F32)
        span = slice(p * (Z - 1), (p + 1) * (Z - 1))
        column[0] = item[:SHARE, :]
        column[1:] = rest[span] + rest_in[span].astype(F32)
        column[Z - 1, SMALL_IN_SHARE:end, :] += item[SIDE : SIDE + LATE_SMALL, :]
        out[...] = column[...].astype(out.dtype)


def add_plane_kernel(ids, kept, *refs):
    arrived = refs[: PLANE - 1]
    keep_out, *sends, column = refs[PLANE - 1 :]
    column[...] = kept[...] + sum(item[...].astype(F32) for item in arrived)
    keep_out[...] = column[ids[0]]
    for d, out in enumerate(sends):
        out[...] = column[lax.rem(ids[0] + d + 1, Z)].astype(BF16)


def add_column_kernel(kept, *refs):
    refs[-1][...] = kept[...] + sum(item[...].astype(F32) for item in refs[:-1])


def like(*shape, kind=F32):
    return jax.ShapeDtypeStruct(shape, kind)


SMEM_SPEC = pl.BlockSpec(memory_space=pltpu.SMEM)
VMEM_SPEC = pl.BlockSpec(memory_space=pltpu.VMEM)

def cost(us):
    return pl.CostEstimate(flops=int(us * 1e9), bytes_accessed=1 << 20, transcendentals=0)


def call(kernel, name, ids, inputs, outs, scratch=(), us=1):
    with_ids = ids is not None
    results = pl.pallas_call(
        kernel,
        in_specs=[SMEM_SPEC] * with_ids + [VMEM_SPEC] * len(inputs),
        out_specs=[VMEM_SPEC] * len(outs),
        out_shape=list(outs),
        scratch_shapes=list(scratch),
        compiler_params=pltpu.CompilerParams(vmem_limit_bytes=VMEM_BYTES),
        cost_estimate=cost(us),
        name=name,
    )(*([ids] if with_ids else []), *inputs)
    return results if len(outs) > 1 else results[0]


def prepare(tokens, params, segment_ids):
    rows = tokens.shape[0]
    return call(
        prepare_kernel, "prepare", None, [tokens, params, segment_ids.reshape(-1, SEQ)],
        [
            like(rows, D),
            like(D, rows, kind=BF16),
            like(*params.shape, kind=BF16),
            like(rows, SEQ),
        ],
        us=2,
    )


def stack(items):
    shape = (sum(item.shape[0] for item in items),) + items[0].shape[1:]
    return call(stack_kernel, "stack", None, items, [like(*shape, kind=items[0].dtype)])


def attend(ids, allowed, normed, bufs):
    rows = normed.shape[0]
    shapes = [(rows, 3 * D), (rows, HEADS * SEQ), (rows, D), (D, 3 * D)]
    return call(
        attend_kernel, "attend", ids, [allowed, normed, *bufs],
        [like(*shape, kind=BF16) for shape in shapes]
        + [like(SMALL_ROWS, LANES), like(HEAD_ROWS, LANES)],
        [pltpu.VMEM((FIRST_ROWS, LANES), F32)], us=0.2,
    )


def feed(ids, tokens, attended, cotangent, small, first, bufs, send_kind):
    rows = tokens.shape[0]
    return call(
        feed_kernel, "feed", ids, [tokens, attended, cotangent, small, first, *bufs],
        [
            like(rows, D),
            like(rows, FF, kind=BF16),
            like(rows, D),
            like(rows, D, kind=BF16),
            like(FF, D, kind=BF16),
            like(PLANE * (Z - 1), SHARE, LANES),
            like(PLANE * (Z - 1), SHARE, LANES, kind=send_kind),
            like(HEAD_ROWS, LANES),
        ],
        [
            pltpu.VMEM((D, D), BF16),
            pltpu.VMEM((D, FF), BF16),
            pltpu.VMEM((rows, FF), BF16),
            pltpu.VMEM((ROW_TOTAL - ROW_OUT, LANES), F32),
        ],
        us=8,
    )


def result(middle, activated, w_down, small):
    return call(
        result_kernel, "result", None, [middle, activated, w_down, small],
        [like(*middle.shape, kind=BF16)], us=2,
    )


def attend_back(ids, project, weights, grad_attended, normed_turned, w_qkv, small, first, send_kind):
    shape = (PLANE, SIDE + SIDE_ROWS, LANES)
    return call(
        attend_back_kernel, "attend_back", ids,
        [project, weights, grad_attended, normed_turned, w_qkv, small, first],
        [like(*project.shape, kind=BF16), like(*shape), like(*shape, kind=send_kind)],
        [pltpu.VMEM((FIRST_ROWS, LANES), F32), pltpu.VMEM(shape[1:], F32)], us=4,
    )


def input_gradient(tokens, grad_project, grad_middle, w_qkv, small):
    return call(
        input_grad_kernel, "input_grad", None, [tokens, grad_project, grad_middle, w_qkv, small],
        [like(*tokens.shape)], us=2,
    )


def local_any(n, tokens, params, segment_ids, cotangent):
    total = n * params.shape[0]
    normed, normed_turned, _, allowed = prepare(tokens, params, segment_ids)
    gathered = lax.all_gather(params, "fsdp", axis=0).reshape(total, LANES)
    shares = gathered[:ROW_TOTAL].reshape(Z, 2 * PLANE, SHARE, LANES)
    order = [p * 2 + c for c in range(2) for p in range(PLANE)]
    side = jnp.concatenate(
        [jnp.zeros((SIDE - SHARE, LANES), BF16), gathered[ROW_SMALL:ROW_TOTAL]], axis=0
    )
    firsts = [jnp.concatenate([shares[0, k], side], axis=0) for k in order]
    rests = []
    for group in (order[:PLANE], order[PLANE:]):
        rests += [shares[1:, group[0]], jnp.concatenate([shares[1:, k] for k in group[1:]])]
    ids = jnp.array(order, jnp.int32)
    project, weights, attended, w_qkv, small, first = attend(ids, allowed, normed, firsts)
    middle, activated, grad_middle, grad_attended, w_down, rest, rest_send, first_grad = feed(
        ids, tokens, attended, cotangent, small, first, rests, F32
    )
    outputs = result(middle, activated, w_down, small)
    grad_project, first, first_send = attend_back(
        ids, project, weights, grad_attended, normed_turned, w_qkv, small, first_grad, F32
    )
    input_grad = input_gradient(tokens, grad_project, grad_middle, w_qkv, small)
    first = jnp.stack([first, first_send], axis=1)
    rest = jnp.stack([rest, rest_send]).reshape(2, PLANE, Z - 1, SHARE, LANES).transpose(2, 1, 0, 3, 4)
    flat = jnp.concatenate(
        [
            first[:, :, :SHARE].reshape(-1, LANES),
            rest.reshape(-1, LANES),
            jnp.zeros((total - ROW_TOTAL, LANES), F32),
        ],
        axis=0,
    )
    flat = flat.at[ROW_SMALL : ROW_SMALL + LATE_SMALL].add(
        first[PLANE - 1, 1, SIDE : SIDE + LATE_SMALL]
    )
    param_grad = lax.psum_scatter(flat, "fsdp", scatter_dimension=0, tiled=True)
    return outputs, input_grad, param_grad


def index_of(z, plane, core):
    return (z * PLANE + plane) * 2 + core


def move(values, step_z, step_plane, step_core):
    pairs = [
        (index_of(z, p, c), index_of((z + step_z) % Z, p ^ step_plane, c ^ step_core))
        for z in range(Z)
        for p in range(PLANE)
        for c in range(2)
    ]
    return lax.ppermute(values, "fsdp", pairs)


STEPS = (3, 1, 2)


def local_slice(tokens, params, segment_ids, cotangent):
    me = lax.axis_index("fsdp").astype(jnp.int32)
    z, plane, core = me // (2 * PLANE), (me // 2) % PLANE, me % 2
    where = z.reshape(1)
    ids = jnp.stack(
        [(plane ^ dp) * 2 + (core ^ dc) for dc in range(2) for dp in (0, *STEPS)]
    )

    normed, normed_turned, own, allowed = prepare(tokens, params, segment_ids)
    first, rest = call(
        sort_kernel, "sort_shares", where, [own] + [move(params, d, 0, 0) for d in range(1, Z)],
        [like(SIDE + SMALL_ROWS, LANES, kind=BF16), like(Z - 1, SHARE, LANES, kind=BF16)],
        [pltpu.VMEM((Z, SHARE, LANES), BF16), pltpu.VMEM((SIDE + SMALL_ROWS, LANES), F32)],
    )
    firsts = [first] + [move(first, 0, d, 0) for d in STEPS]
    rests = [move(rest, 0, d, 0) for d in STEPS]
    firsts = firsts + [move(item, 0, 0, 1) for item in firsts]
    project, weights, attended, w_qkv, small, first = attend(ids, allowed, normed, firsts)
    *rests, attended = lax.optimization_barrier((*rests, attended))
    rests = stack(rests)
    rests = [rest, rests, move(rest, 0, 0, 1), move(rests, 0, 0, 1)]
    middle, activated, grad_middle, grad_attended, w_down, rest, send, first_grad = feed(
        ids, tokens, attended, cotangent, small, first, rests, BF16
    )

    rest_in = move(send, 0, 0, 1)
    grad_project, first, send = attend_back(
        ids, project, weights, grad_attended, normed_turned, w_qkv, small, first_grad, BF16
    )
    first_in = move(send, 0, 0, 1)
    part = (Z, SHARE, LANES)
    kept, *sends = call(
        add_core_kernel, "add_core", None, [first, first_in, rest, rest_in],
        [like(*part)] + [like(*part, kind=BF16)] * (PLANE - 1), [pltpu.VMEM(part, F32)],
    )
    arrived = [move(item, 0, d, 0) for item, d in zip(sends, STEPS)]
    outputs = result(middle, activated, w_down, small)
    input_grad = input_gradient(tokens, grad_project, grad_middle, w_qkv, small)
    kept, *sends = call(
        add_plane_kernel, "add_plane", where, [kept] + arrived,
        [like(SHARE, LANES)] + [like(SHARE, LANES, kind=BF16)] * (Z - 1), [pltpu.VMEM(part, F32)],
    )
    arrived = [move(item, d + 1, 0, 0) for d, item in enumerate(sends)]
    param_grad = call(
        add_column_kernel, "add_column", None, [kept] + arrived, [like(SHARE, LANES)]
    )
    return outputs, input_grad, param_grad


def solution(mesh):
    n = mesh.shape["fsdp"]
    local = local_slice if n == 2 * PLANE * Z else functools.partial(local_any, n)
    in_specs = (P("fsdp", None), P("fsdp", None), P("fsdp"), P("fsdp", None))
    out_specs = (P("fsdp", None), P("fsdp", None), P("fsdp", None))
    return jax.shard_map(local, mesh=mesh, in_specs=in_specs, out_specs=out_specs, check_vma=False)
```

```python
import functools

import jax
import jax.numpy as jnp
from jax import lax
from jax.experimental import pallas as pl
from jax.experimental.pallas import tpu as pltpu
from jax.sharding import PartitionSpec as P

D = 256
HEADS = 4
HEAD_DIM = 64
FF = 1024
SEQ = 128
LANES = 128
GROUP = 4
WIDE = GROUP * SEQ
CHUNK = 256
STRIP = 64
EPSILON = 1e-05
SCALE = HEAD_DIM ** (-0.5)
VMEM_BYTES = 24 * 1024 * 1024

ROW_QKV = 0
ROW_OUT = 1536
ROW_UP = 2048
ROW_DOWN = 4096
ROW_SMALL = 6144
ROW_END = 6168
ROW_TOTAL = 6176
GAIN_ONE, SHIFT_ONE, BIAS_QUERY, BIAS_VALUE, BIAS_OUT = 0, 2, 4, 6, 8
GAIN_TWO, SHIFT_TWO, BIAS_UP, BIAS_DOWN = 10, 12, 14, 22
SMALL_ROWS = 32
LATE_SMALL = 8

SHARE = 193
Z, PLANE = 4, 4
FIRST_ROWS = 2 * PLANE * SHARE
HEAD_ROWS = FIRST_ROWS - ROW_OUT
SIDE, SIDE_ROWS = 208, 16
PARTS = (slice(0, 96), slice(96, SHARE))
SMALL_IN_SHARE = ROW_SMALL - (2 * PLANE * Z - 1) * SHARE

F32 = jnp.float32
BF16 = jnp.bfloat16


def dot(left, right):
    return jnp.dot(left, right, preferred_element_type=F32)


def dot_nt(left, right):
    return lax.dot_general(left, right, (((1,), (1,)), ((), ())), preferred_element_type=F32)


def dot_tn(left, right):
    return lax.dot_general(left, right, (((0,), (0,)), ((), ())), preferred_element_type=F32)


def small_vector(small, row, count):
    return jnp.concatenate([small[row + i : row + i + 1, :] for i in range(count)], axis=1)


def fold_rows(values):
    rows, columns = values.shape
    return jnp.sum(values.reshape(rows // 8, 8, columns), axis=0)


def normalize(values):
    center = values - jnp.mean(values, axis=-1, keepdims=True)
    rate = lax.rsqrt(jnp.mean(center * center, axis=-1, keepdims=True) + EPSILON)
    return center * rate, rate


def normalize_back(grad, gain, normed, rate):
    scaled = grad * gain
    return rate * (
        scaled
        - jnp.mean(scaled, axis=-1, keepdims=True)
        - normed * jnp.mean(scaled * normed, axis=-1, keepdims=True)
    )


def head_masks():
    lane = lax.broadcasted_iota(jnp.int32, (1, D), 1)
    return [(lane // HEAD_DIM == h).astype(F32).astype(BF16) for h in range(HEADS)]


def spread_heads(rows):
    return jnp.concatenate([rows * mask for mask in head_masks()], axis=0)


def matrix_from_flat(flat, start, rows, columns, out):
    per_row = columns // LANES
    for j in range(per_row):
        out[:, j * LANES : (j + 1) * LANES] = flat[
            pl.ds(start + j, rows, stride=per_row), :
        ].astype(BF16)


def turned_to_flat(turned, rows, columns, flat, start):
    per_row = columns // LANES
    for j in range(per_row):
        flat[pl.ds(start + j, rows, stride=per_row), :] = turned[j * LANES : (j + 1) * LANES, :].T


def matrix_to_flat(matrix, rows, columns, flat, start):
    per_row = columns // LANES
    for j in range(per_row):
        flat[pl.ds(start + j, rows, stride=per_row), :] = matrix[:, j * LANES : (j + 1) * LANES]


def prepare_kernel(tok, params, seg, normed_out, normed_turned, own, allowed):
    normed, _ = normalize(tok[...].astype(F32))
    normed_out[...] = normed
    normed_turned[...] = normed.astype(BF16).T
    own[...] = params[...]
    causal = lax.broadcasted_iota(jnp.int32, (SEQ, SEQ), 1) <= lax.broadcasted_iota(
        jnp.int32, (SEQ, SEQ), 0
    )
    for s in range(seg.shape[0]):
        across = jnp.broadcast_to(seg[s : s + 1, :].astype(F32), (SEQ, SEQ))
        allowed[s * SEQ : (s + 1) * SEQ, :] = (causal & (across == across.T)).astype(F32)


def sort_kernel(ids, *refs):
    received, (first, rest, stage, wide) = refs[:Z], refs[Z:]
    for d in range(Z):
        stage[lax.rem(ids[0] + Z - d, Z)] = received[d][...]
    rest[...] = stage[1:]
    wide[:SHARE, :] = stage[0].astype(F32)
    wide[SHARE:SIDE, :] = jnp.zeros((SIDE - SHARE, LANES), F32)
    last = stage[Z - 1].astype(F32)
    wide[SIDE:, :] = last[SMALL_IN_SHARE:, :]
    first[...] = wide[...].astype(BF16)


def attend_kernel(ids, allowed, normed, *refs):
    bufs = refs[: 2 * PLANE]
    project_out, weights_out, attended_out, w_qkv, small, first_out, flat = refs[2 * PLANE :]
    for slot, buf in enumerate(bufs):
        wide = buf[...].astype(F32)
        flat[pl.ds(ids[slot] * SHARE, SHARE), :] = wide[:SHARE, :]

        @pl.when(ids[slot] == 2 * PLANE - 1)
        def _():
            small[...] = wide[SIDE:, :]

    matrix_from_flat(flat, ROW_QKV, D, 3 * D, w_qkv)
    first_out[...] = flat[ROW_OUT:FIRST_ROWS, :]

    gain = small_vector(small, GAIN_ONE, 2)
    shift = small_vector(small, SHIFT_ONE, 2)
    bias = jnp.concatenate(
        [
            small_vector(small, BIAS_QUERY, 2),
            jnp.zeros((1, D), F32),
            small_vector(small, BIAS_VALUE, 2),
        ],
        axis=1,
    )
    for g in range(normed.shape[0] // WIDE):
        span = slice(g * WIDE, (g + 1) * WIDE)
        normed_low = (normed[span, :] * gain + shift).astype(BF16)
        project = (dot(normed_low, w_qkv[...]) + bias).astype(BF16)
        project_out[span, :] = project
        scores, values = [], []
        for s in range(GROUP):
            rows = slice(s * SEQ, (s + 1) * SEQ)
            scores.append(
                dot_nt(project[rows, :D] * SCALE, spread_heads(project[rows, D : 2 * D]))
            )
            values.append(spread_heads(project[rows, 2 * D :]))
        weights = []
        for s in range(GROUP):
            low = []
            open_pairs = allowed[g * WIDE + s * SEQ : g * WIDE + (s + 1) * SEQ, :] > 0.5
            for h in range(HEADS):
                mine = jnp.where(open_pairs, scores[s][:, h * SEQ : (h + 1) * SEQ], -1e30)
                grown = jnp.exp(mine - jnp.max(mine, axis=-1, keepdims=True))
                low.append(
                    (grown * (1.0 / jnp.sum(grown, axis=-1, keepdims=True))).astype(BF16)
                )
            weights.append(jnp.concatenate(low, axis=1))
        weights_out[span, :] = jnp.concatenate(weights, axis=0)
        attended_out[span, :] = jnp.concatenate(
            [dot(weights[s], values[s]).astype(BF16) for s in range(GROUP)], axis=0
        )


def feed_kernel(
    ids, tok, attended, cot, small, first_in, *refs,
):
    bufs = []
    for own, others in (refs[0:2], refs[2:4]):
        bufs.append(own)
        bufs += [others.at[pl.ds(p * (Z - 1), Z - 1)] for p in range(PLANE - 1)]
    (
        middle_out, activated_out, grad_middle_out, grad_attended_out, w_down, keep_out, send_out, first_out,
        w_out, w_up, grad_hidden, flat,
    ) = refs[4:]
    flat[:HEAD_ROWS, :] = first_in[...]
    for slot, buf in enumerate(bufs):
        for z in range(1, Z):
            share = ids[slot] + z * 2 * PLANE
            flat[pl.ds(share * SHARE - ROW_OUT, SHARE), :] = buf[z - 1].astype(F32)
    matrix_from_flat(flat, 0, D, D, w_out)
    matrix_from_flat(flat, ROW_UP - ROW_OUT, D, FF, w_up)
    matrix_from_flat(flat, ROW_DOWN - ROW_OUT, FF, D, w_down)

    gain = small_vector(small, GAIN_TWO, 2)
    middle = (
        tok[...].astype(F32) + dot(attended[...], w_out[...]) + small_vector(small, BIAS_OUT, 2)
    )
    middle_out[...] = middle
    normed, rate = normalize(middle)
    normed_low = (normed * gain + small_vector(small, SHIFT_TWO, 2)).astype(BF16)
    normed_turned = normed_low.T
    cotangent = cot[...]
    cot_turned = cotangent.T
    slope = 0.7978845608028654
    cubic = slope * 0.044715
    row_up, row_down = ROW_UP - ROW_OUT, ROW_DOWN - ROW_OUT

    def products(c):
        columns = slice(c, c + CHUNK)
        return dot(normed_low, w_up[:, columns]), dot_nt(cotangent, w_down[columns, :])

    def bend(c, hidden_all, grad_all):
        columns = slice(c, c + CHUNK)
        bias = small_vector(small, BIAS_UP + c // LANES, CHUNK // LANES)
        total = jnp.zeros((8, CHUNK), F32)
        for r in range(0, tok.shape[0], STRIP):
            rows = slice(r, r + STRIP)
            hidden = hidden_all[rows] + bias
            square = hidden * hidden
            half = 0.5 + 0.5 * jnp.tanh(hidden * (slope + cubic * square))
            activated = hidden * half
            derivative = half + activated * (1.0 - half) * (2 * slope + (6 * cubic) * square)
            low = (grad_all[rows] * derivative).astype(BF16)
            activated_out[rows, columns] = activated.astype(BF16)
            grad_hidden[rows, columns] = low
            total += fold_rows(low.astype(F32))
        return total

    def weight_gradients(c):
        columns = slice(c, c + CHUNK)
        turned_to_flat(dot(cot_turned, activated_out[:, columns]), CHUNK, D, flat, row_down + c * D // LANES)
        grads = dot(normed_turned, grad_hidden[:, columns])
        for j in range(CHUNK // LANES):
            flat[pl.ds(row_up + c // LANES + j, D, stride=FF // LANES), :] = grads[
                :, j * LANES : (j + 1) * LANES
            ]

    ahead, totals = products(0), []
    for c in range(0, FF, CHUNK):
        now = ahead
        if c + CHUNK < FF:
            ahead = products(c + CHUNK)
        if c > 0:
            weight_gradients(c - CHUNK)
        totals.append(bend(c, *now))
    grad_normed = dot_nt(grad_hidden[...], w_up[...])
    weight_gradients(FF - CHUNK)
    grad_result = cotangent.astype(F32)
    grad_middle = grad_result + normalize_back(grad_normed, gain, normed, rate)
    grad_middle_out[...] = grad_middle
    grad_middle_low = grad_middle.astype(BF16)
    grad_attended_out[...] = dot_nt(grad_middle_low, w_out[...]).astype(BF16)
    matrix_to_flat(dot_tn(attended[...], grad_middle_low), D, D, flat, 0)
    sums = jnp.concatenate(
        [
            fold_rows(grad_middle_low.astype(F32)),
            fold_rows(grad_normed * normed),
            fold_rows(grad_normed),
            *totals,
            fold_rows(grad_result),
        ],
        axis=1,
    )
    sums = jnp.sum(sums, axis=0, keepdims=True)
    base = ROW_SMALL - ROW_OUT
    flat[base : base + LATE_SMALL, :] = jnp.zeros((LATE_SMALL, LANES), F32)
    for i in range(sums.shape[1] // LANES):
        row = base + LATE_SMALL + i
        flat[row : row + 1, :] = sums[:, i * LANES : (i + 1) * LANES]
    flat[ROW_END - ROW_OUT :, :] = jnp.zeros((ROW_TOTAL - ROW_END, LANES), F32)
    first_out[...] = flat[:HEAD_ROWS, :]
    for target, out in enumerate((keep_out, send_out)):
        for p in range(PLANE):
            for z in range(1, Z):
                share = ids[target * PLANE + p] + z * 2 * PLANE
                rows = flat[pl.ds(share * SHARE - ROW_OUT, SHARE), :]
                out[p * (Z - 1) + z - 1] = rows.astype(out.dtype)


def result_kernel(middle, activated, w_down, small, result_out):
    result = middle[...] + dot(activated[...], w_down[...]) + small_vector(small, BIAS_DOWN, 2)
    result_out[...] = result.astype(BF16)


def attend_back_kernel(
    ids, project, weights, grad_attended, normed_turned, w_qkv, small, first_in,
    grad_project, keep_out, send_out, flat, wide,
):
    products, sums = 0.0, 0.0
    for g in range(project.shape[0] // WIDE):
        spans = [slice(r, r + SEQ) for r in range(g * WIDE, (g + 1) * WIDE, SEQ)]
        grad_weights = [
            dot_nt(grad_attended[span, :], spread_heads(project[span, 2 * D :])) for span in spans
        ]
        scores_low, scores_turned, weights_turned = [], [], []
        for s, span in enumerate(spans):
            low, turned, mine_turned = [], [], []
            for h in range(HEADS):
                columns = slice(h * SEQ, (h + 1) * SEQ)
                mine_low = weights[span, columns]
                mine = mine_low.astype(F32)
                product = mine * grad_weights[s][:, columns]
                grad_scores = (product - mine * jnp.sum(product, axis=-1, keepdims=True)) * SCALE
                low.append(grad_scores.astype(BF16))
                turned.append(low[-1].T)
                mine_turned.append(mine_low.T)
            scores_low.append(jnp.concatenate(low, axis=1))
            scores_turned.append(jnp.concatenate(turned, axis=1))
            weights_turned.append(jnp.concatenate(mine_turned, axis=1))
        for s, span in enumerate(spans):
            key = spread_heads(project[span, D : 2 * D])
            grad_project[span, :D] = dot(scores_low[s], key).astype(BF16)
            query = spread_heads(project[span, :D])
            grad_project[span, D : 2 * D] = dot(scores_turned[s], query).astype(BF16)
            grad_value = dot(weights_turned[s], spread_heads(grad_attended[span, :]))
            grad_project[span, 2 * D :] = grad_value.astype(BF16)
        span = slice(g * WIDE, (g + 1) * WIDE)
        products += dot(normed_turned[:, span], grad_project[span, :])
        sums += fold_rows(grad_project[span, :].astype(F32))
    sums = jnp.sum(sums, axis=0, keepdims=True)
    gain = jnp.broadcast_to(small_vector(small, GAIN_ONE, 2), (LANES, D)).T
    shift = jnp.broadcast_to(small_vector(small, SHIFT_ONE, 2), (LANES, D)).T
    grad_gain = jnp.zeros((D, LANES), F32)
    grad_shift = jnp.zeros((D, LANES), F32)
    per_row = 3 * D // LANES
    for j in range(per_row):
        columns = slice(j * LANES, (j + 1) * LANES)
        weight = w_qkv[:, columns].astype(F32)
        grad_gain += products[:, columns] * weight
        grad_shift += sums[:, columns] * weight
        flat[pl.ds(j, D, stride=per_row), :] = products[:, columns] * gain + sums[:, columns] * shift
    flat[ROW_OUT:, :] = first_in[...]
    grad_gain = jnp.sum(grad_gain.T, axis=0, keepdims=True)
    grad_shift = jnp.sum(grad_shift.T, axis=0, keepdims=True)
    late = jnp.concatenate([grad_gain, grad_shift, sums[:, :D], sums[:, 2 * D :]], axis=1)
    side = jnp.concatenate(
        [late[:, i * LANES : (i + 1) * LANES] for i in range(LATE_SMALL)]
        + [jnp.zeros((SIDE_ROWS - LATE_SMALL, LANES), F32)],
        axis=0,
    )
    wide[SHARE:SIDE, :] = jnp.zeros((SIDE - SHARE, LANES), F32)
    for target, out in enumerate((keep_out, send_out)):
        for p in range(PLANE):
            share = ids[target * PLANE + p]
            wide[:SHARE, :] = flat[pl.ds(share * SHARE, SHARE), :]
            wide[SIDE:, :] = jnp.where(share == 2 * PLANE - 1, side, 0.0)
            out[p] = wide[...].astype(out.dtype)


def input_grad_kernel(tok, grad_project, grad_middle, w_qkv, small, input_grad_out):
    gain = small_vector(small, GAIN_ONE, 2)

    def some(g, carry):
        span = pl.ds(pl.multiple_of(g * WIDE, WIDE), WIDE)
        normed, rate = normalize(tok[span, :].astype(F32))
        grad_normed = dot_nt(grad_project[span, :], w_qkv[...])
        input_grad_out[span, :] = grad_middle[span, :] + normalize_back(
            grad_normed, gain, normed, rate
        )
        return carry

    lax.fori_loop(0, tok.shape[0] // WIDE, some, 0)


def stack_kernel(*refs):
    row = 0
    for ref in refs[:-1]:
        refs[-1][row : row + ref.shape[0]] = ref[...]
        row += ref.shape[0]


def add_core_kernel(first, first_in, rest, rest_in, *refs):
    outs, column = refs[:-1], refs[-1]
    end = SMALL_IN_SHARE + LATE_SMALL
    for p in range(PLANE):
        item = first[p] + first_in[p].astype(F32)
        span = slice(p * (Z - 1), (p + 1) * (Z - 1))
        column[0] = item[:SHARE, :]
        column[1:] = rest[span] + rest_in[span].astype(F32)
        column[Z - 1, SMALL_IN_SHARE:end, :] += item[SIDE : SIDE + LATE_SMALL, :]
        for part, rows in enumerate(PARTS):
            out = outs[p * len(PARTS) + part]
            out[...] = column[:, rows, :].astype(out.dtype)


def add_plane_kernel(ids, kept, *refs):
    arrived = refs[: PLANE - 1]
    keep_out, *sends, column = refs[PLANE - 1 :]
    column[...] = kept[...] + sum(item[...].astype(F32) for item in arrived)
    keep_out[...] = column[ids[0]]
    for d, out in enumerate(sends):
        out[...] = column[lax.rem(ids[0] + d + 1, Z)].astype(BF16)


def add_column_kernel(*refs):
    for part, rows in enumerate(PARTS):
        kept, *arrived = refs[part * Z : (part + 1) * Z]
        refs[-1][rows, :] = kept[...] + sum(item[...].astype(F32) for item in arrived)


def like(*shape, kind=F32):
    return jax.ShapeDtypeStruct(shape, kind)


SMEM_SPEC = pl.BlockSpec(memory_space=pltpu.SMEM)
VMEM_SPEC = pl.BlockSpec(memory_space=pltpu.VMEM)

def cost(us):
    return pl.CostEstimate(flops=int(us * 1e9), bytes_accessed=1 << 20, transcendentals=0)


def call(kernel, name, ids, inputs, outs, scratch=(), us=1):
    with_ids = ids is not None
    results = pl.pallas_call(
        kernel,
        in_specs=[SMEM_SPEC] * with_ids + [VMEM_SPEC] * len(inputs),
        out_specs=[VMEM_SPEC] * len(outs),
        out_shape=list(outs),
        scratch_shapes=list(scratch),
        compiler_params=pltpu.CompilerParams(vmem_limit_bytes=VMEM_BYTES),
        cost_estimate=cost(us),
        name=name,
    )(*([ids] if with_ids else []), *inputs)
    return results if len(outs) > 1 else results[0]


def prepare(tokens, params, segment_ids):
    rows = tokens.shape[0]
    return call(
        prepare_kernel, "prepare", None, [tokens, params, segment_ids.reshape(-1, SEQ)],
        [
            like(rows, D),
            like(D, rows, kind=BF16),
            like(*params.shape, kind=BF16),
            like(rows, SEQ),
        ],
        us=2,
    )


def stack(items):
    shape = (sum(item.shape[0] for item in items),) + items[0].shape[1:]
    return call(stack_kernel, "stack", None, items, [like(*shape, kind=items[0].dtype)])


def attend(ids, allowed, normed, bufs):
    rows = normed.shape[0]
    shapes = [(rows, 3 * D), (rows, HEADS * SEQ), (rows, D), (D, 3 * D)]
    return call(
        attend_kernel, "attend", ids, [allowed, normed, *bufs],
        [like(*shape, kind=BF16) for shape in shapes]
        + [like(SMALL_ROWS, LANES), like(HEAD_ROWS, LANES)],
        [pltpu.VMEM((FIRST_ROWS, LANES), F32)], us=0.2,
    )


def feed(ids, tokens, attended, cotangent, small, first, bufs, send_kind):
    rows = tokens.shape[0]
    return call(
        feed_kernel, "feed", ids, [tokens, attended, cotangent, small, first, *bufs],
        [
            like(rows, D),
            like(rows, FF, kind=BF16),
            like(rows, D),
            like(rows, D, kind=BF16),
            like(FF, D, kind=BF16),
            like(PLANE * (Z - 1), SHARE, LANES),
            like(PLANE * (Z - 1), SHARE, LANES, kind=send_kind),
            like(HEAD_ROWS, LANES),
        ],
        [
            pltpu.VMEM((D, D), BF16),
            pltpu.VMEM((D, FF), BF16),
            pltpu.VMEM((rows, FF), BF16),
            pltpu.VMEM((ROW_TOTAL - ROW_OUT, LANES), F32),
        ],
        us=8,
    )


def result(middle, activated, w_down, small):
    return call(
        result_kernel, "result", None, [middle, activated, w_down, small],
        [like(*middle.shape, kind=BF16)], us=2,
    )


def attend_back(ids, project, weights, grad_attended, normed_turned, w_qkv, small, first, send_kind):
    shape = (PLANE, SIDE + SIDE_ROWS, LANES)
    return call(
        attend_back_kernel, "attend_back", ids,
        [project, weights, grad_attended, normed_turned, w_qkv, small, first],
        [like(*project.shape, kind=BF16), like(*shape), like(*shape, kind=send_kind)],
        [pltpu.VMEM((FIRST_ROWS, LANES), F32), pltpu.VMEM(shape[1:], F32)], us=4,
    )


def input_gradient(tokens, grad_project, grad_middle, w_qkv, small):
    return call(
        input_grad_kernel, "input_grad", None, [tokens, grad_project, grad_middle, w_qkv, small],
        [like(*tokens.shape)], us=2,
    )


def local_any(n, tokens, params, segment_ids, cotangent):
    total = n * params.shape[0]
    normed, normed_turned, _, allowed = prepare(tokens, params, segment_ids)
    gathered = lax.all_gather(params, "fsdp", axis=0).reshape(total, LANES)
    shares = gathered[:ROW_TOTAL].reshape(Z, 2 * PLANE, SHARE, LANES)
    order = [p * 2 + c for c in range(2) for p in range(PLANE)]
    side = jnp.concatenate(
        [jnp.zeros((SIDE - SHARE, LANES), BF16), gathered[ROW_SMALL:ROW_TOTAL]], axis=0
    )
    firsts = [jnp.concatenate([shares[0, k], side], axis=0) for k in order]
    rests = []
    for group in (order[:PLANE], order[PLANE:]):
        rests += [shares[1:, group[0]], jnp.concatenate([shares[1:, k] for k in group[1:]])]
    ids = jnp.array(order, jnp.int32)
    project, weights, attended, w_qkv, small, first = attend(ids, allowed, normed, firsts)
    middle, activated, grad_middle, grad_attended, w_down, rest, rest_send, first_grad = feed(
        ids, tokens, attended, cotangent, small, first, rests, F32
    )
    outputs = result(middle, activated, w_down, small)
    grad_project, first, first_send = attend_back(
        ids, project, weights, grad_attended, normed_turned, w_qkv, small, first_grad, F32
    )
    input_grad = input_gradient(tokens, grad_project, grad_middle, w_qkv, small)
    first = jnp.stack([first, first_send], axis=1)
    rest = jnp.stack([rest, rest_send]).reshape(2, PLANE, Z - 1, SHARE, LANES).transpose(2, 1, 0, 3, 4)
    flat = jnp.concatenate(
        [
            first[:, :, :SHARE].reshape(-1, LANES),
            rest.reshape(-1, LANES),
            jnp.zeros((total - ROW_TOTAL, LANES), F32),
        ],
        axis=0,
    )
    flat = flat.at[ROW_SMALL : ROW_SMALL + LATE_SMALL].add(
        first[PLANE - 1, 1, SIDE : SIDE + LATE_SMALL]
    )
    param_grad = lax.psum_scatter(flat, "fsdp", scatter_dimension=0, tiled=True)
    return outputs, input_grad, param_grad


def index_of(z, plane, core):
    return (z * PLANE + plane) * 2 + core


def move(values, step_z, step_plane, step_core):
    pairs = [
        (index_of(z, p, c), index_of((z + step_z) % Z, p ^ step_plane, c ^ step_core))
        for z in range(Z)
        for p in range(PLANE)
        for c in range(2)
    ]
    return lax.ppermute(values, "fsdp", pairs)


STEPS = (3, 1, 2)


def local_slice(tokens, params, segment_ids, cotangent):
    me = lax.axis_index("fsdp").astype(jnp.int32)
    z, plane, core = me // (2 * PLANE), (me // 2) % PLANE, me % 2
    where = z.reshape(1)
    ids = jnp.stack(
        [(plane ^ dp) * 2 + (core ^ dc) for dc in range(2) for dp in (0, *STEPS)]
    )

    normed, normed_turned, own, allowed = prepare(tokens, params, segment_ids)
    first, rest = call(
        sort_kernel, "sort_shares", where, [own] + [move(params, d, 0, 0) for d in range(1, Z)],
        [like(SIDE + SMALL_ROWS, LANES, kind=BF16), like(Z - 1, SHARE, LANES, kind=BF16)],
        [pltpu.VMEM((Z, SHARE, LANES), BF16), pltpu.VMEM((SIDE + SMALL_ROWS, LANES), F32)],
    )
    firsts = [first] + [move(first, 0, d, 0) for d in STEPS]
    rests = [move(rest, 0, d, 0) for d in STEPS]
    firsts = firsts + [move(item, 0, 0, 1) for item in firsts]
    project, weights, attended, w_qkv, small, first = attend(ids, allowed, normed, firsts)
    *rests, attended = lax.optimization_barrier((*rests, attended))
    rests = stack(rests)
    rests = [rest, rests, move(rest, 0, 0, 1), move(rests, 0, 0, 1)]
    middle, activated, grad_middle, grad_attended, w_down, rest, send, first_grad = feed(
        ids, tokens, attended, cotangent, small, first, rests, BF16
    )

    rest_in = move(send, 0, 0, 1)
    grad_project, first, send = attend_back(
        ids, project, weights, grad_attended, normed_turned, w_qkv, small, first_grad, BF16
    )
    first_in = move(send, 0, 0, 1)
    parts = [(Z, rows.stop - rows.start, LANES) for rows in PARTS]
    sums = call(
        add_core_kernel, "add_core", None, [first, first_in, rest, rest_in],
        [like(*part, kind=BF16 if p else F32) for p in range(PLANE) for part in parts],
        [pltpu.VMEM((Z, SHARE, LANES), F32)],
    )
    sums = [sums[n::2] for n in range(2)]
    grad_project, *sums[0] = lax.optimization_barrier((grad_project, *sums[0]))
    outputs = result(middle, activated, w_down, small)
    input_grad = input_gradient(tokens, grad_project, grad_middle, w_qkv, small)
    input_grad, *sums[1] = lax.optimization_barrier((input_grad, *sums[1]))
    arrived = [[move(item, 0, d, 0) for item, d in zip(part[1:], STEPS)] for part in sums]
    columns = []
    for n, part in enumerate(parts):
        kept, *sends = call(
            add_plane_kernel, "add_plane", where, [sums[n][0]] + arrived[n],
            [like(*part[1:])] + [like(*part[1:], kind=BF16)] * (Z - 1), [pltpu.VMEM(part, F32)],
        )
        columns += [kept] + [move(item, d + 1, 0, 0) for d, item in enumerate(sends)]
    param_grad = call(add_column_kernel, "add_column", None, columns, [like(SHARE, LANES)])
    return outputs, input_grad, param_grad


def solution(mesh):
    n = mesh.shape["fsdp"]
    local = local_slice if n == 2 * PLANE * Z else functools.partial(local_any, n)
    in_specs = (P("fsdp", None), P("fsdp", None), P("fsdp"), P("fsdp", None))
    out_specs = (P("fsdp", None), P("fsdp", None), P("fsdp", None))
    return jax.shard_map(local, mesh=mesh, in_specs=in_specs, out_specs=out_specs, check_vma=False)
```

```python
import functools

import jax
import jax.numpy as jnp
from jax import lax
from jax.experimental import pallas as pl
from jax.experimental.pallas import tpu as pltpu
from jax.sharding import PartitionSpec as P

D = 256
HEADS = 4
HEAD_DIM = 64
FF = 1024
SEQ = 128
LANES = 128
GROUP = 4
WIDE = GROUP * SEQ
CHUNK = 256
STRIP = 64
EPSILON = 1e-05
SCALE = HEAD_DIM ** (-0.5)
VMEM_BYTES = 24 * 1024 * 1024

ROW_QKV = 0
ROW_OUT = 1536
ROW_UP = 2048
ROW_DOWN = 4096
ROW_SMALL = 6144
ROW_END = 6168
ROW_TOTAL = 6176
GAIN_ONE, SHIFT_ONE, BIAS_QUERY, BIAS_VALUE, BIAS_OUT = 0, 2, 4, 6, 8
GAIN_TWO, SHIFT_TWO, BIAS_UP, BIAS_DOWN = 10, 12, 14, 22
SMALL_ROWS = 32
LATE_SMALL = 8

SHARE = 193
Z, PLANE = 4, 4
FIRST_ROWS = 2 * PLANE * SHARE
HEAD_ROWS = FIRST_ROWS - ROW_OUT
SIDE, SIDE_ROWS = 208, 16
SLOTS, NO_SHARE = 10, 2 * PLANE
STEPS = (3, 1, 2)
PARTS = (slice(0, 96), slice(96, SHARE))
SMALL_IN_SHARE = ROW_SMALL - (2 * PLANE * Z - 1) * SHARE

F32 = jnp.float32
BF16 = jnp.bfloat16


def dot(left, right):
    return jnp.dot(left, right, preferred_element_type=F32)


def dot_nt(left, right):
    return lax.dot_general(left, right, (((1,), (1,)), ((), ())), preferred_element_type=F32)


def dot_tn(left, right):
    return lax.dot_general(left, right, (((0,), (0,)), ((), ())), preferred_element_type=F32)


def small_vector(small, row, count):
    return jnp.concatenate([small[row + i : row + i + 1, :] for i in range(count)], axis=1)


def fold_rows(values):
    rows, columns = values.shape
    return jnp.sum(values.reshape(rows // 8, 8, columns), axis=0)


def normalize(values):
    center = values - jnp.mean(values, axis=-1, keepdims=True)
    rate = lax.rsqrt(jnp.mean(center * center, axis=-1, keepdims=True) + EPSILON)
    return center * rate, rate


def normalize_back(grad, gain, normed, rate):
    scaled = grad * gain
    return rate * (
        scaled
        - jnp.mean(scaled, axis=-1, keepdims=True)
        - normed * jnp.mean(scaled * normed, axis=-1, keepdims=True)
    )


def head_masks():
    lane = lax.broadcasted_iota(jnp.int32, (1, D), 1)
    return [(lane // HEAD_DIM == h).astype(F32).astype(BF16) for h in range(HEADS)]


def spread_heads(rows):
    return jnp.concatenate([rows * mask for mask in head_masks()], axis=0)


def matrix_from_flat(flat, start, rows, columns, out):
    per_row = columns // LANES
    for j in range(per_row):
        out[:, j * LANES : (j + 1) * LANES] = flat[
            pl.ds(start + j, rows, stride=per_row), :
        ].astype(BF16)


def turned_to_flat(turned, rows, columns, flat, start):
    per_row = columns // LANES
    for j in range(per_row):
        flat[pl.ds(start + j, rows, stride=per_row), :] = turned[j * LANES : (j + 1) * LANES, :].T


def matrix_to_flat(matrix, rows, columns, flat, start):
    per_row = columns // LANES
    for j in range(per_row):
        flat[pl.ds(start + j, rows, stride=per_row), :] = matrix[:, j * LANES : (j + 1) * LANES]


def prepare_kernel(tok, params, seg, normed_out, normed_turned, own, allowed):
    normed, _ = normalize(tok[...].astype(F32))
    normed_out[...] = normed
    normed_turned[...] = normed.astype(BF16).T
    own[...] = params[...]
    causal = lax.broadcasted_iota(jnp.int32, (SEQ, SEQ), 1) <= lax.broadcasted_iota(
        jnp.int32, (SEQ, SEQ), 0
    )
    for s in range(seg.shape[0]):
        across = jnp.broadcast_to(seg[s : s + 1, :].astype(F32), (SEQ, SEQ))
        allowed[s * SEQ : (s + 1) * SEQ, :] = (causal & (across == across.T)).astype(F32)


def sort_kernel(ids, *refs):
    received, (first, rest, stage, wide) = refs[:Z], refs[Z:]
    for d in range(Z):
        stage[lax.rem(ids[0] + Z - d, Z)] = received[d][...]
    rest[...] = stage[1:]
    wide[:SHARE, :] = stage[0].astype(F32)
    wide[SHARE:SIDE, :] = jnp.zeros((SIDE - SHARE, LANES), F32)
    last = stage[Z - 1].astype(F32)
    wide[SIDE:, :] = last[SMALL_IN_SHARE:, :]
    first[0] = wide[...].astype(BF16)


def attend_kernel(ids, allowed, normed, *refs):
    bufs = [ref.at[i] for ref in refs[:3] for i in range(ref.shape[0])]
    project_out, weights_out, attended_out, w_qkv, small, first_out, flat = refs[3:]
    for slot, buf in enumerate(bufs):
        wide = buf[...].astype(F32)
        flat[pl.ds(ids[slot] * SHARE, SHARE), :] = wide[:SHARE, :]

        @pl.when(ids[slot] == 2 * PLANE - 1)
        def _():
            small[...] = wide[SIDE:, :]

    matrix_from_flat(flat, ROW_QKV, D, 3 * D, w_qkv)
    first_out[...] = flat[ROW_OUT:FIRST_ROWS, :]

    gain = small_vector(small, GAIN_ONE, 2)
    shift = small_vector(small, SHIFT_ONE, 2)
    bias = jnp.concatenate(
        [
            small_vector(small, BIAS_QUERY, 2),
            jnp.zeros((1, D), F32),
            small_vector(small, BIAS_VALUE, 2),
        ],
        axis=1,
    )
    for g in range(normed.shape[0] // WIDE):
        span = slice(g * WIDE, (g + 1) * WIDE)
        normed_low = (normed[span, :] * gain + shift).astype(BF16)
        project = (dot(normed_low, w_qkv[...]) + bias).astype(BF16)
        project_out[span, :] = project
        scores, values = [], []
        for s in range(GROUP):
            rows = slice(s * SEQ, (s + 1) * SEQ)
            scores.append(
                dot_nt(project[rows, :D] * SCALE, spread_heads(project[rows, D : 2 * D]))
            )
            values.append(spread_heads(project[rows, 2 * D :]))
        weights = []
        for s in range(GROUP):
            low = []
            open_pairs = allowed[g * WIDE + s * SEQ : g * WIDE + (s + 1) * SEQ, :] > 0.5
            for h in range(HEADS):
                mine = jnp.where(open_pairs, scores[s][:, h * SEQ : (h + 1) * SEQ], -1e30)
                grown = jnp.exp(mine - jnp.max(mine, axis=-1, keepdims=True))
                low.append(
                    (grown * (1.0 / jnp.sum(grown, axis=-1, keepdims=True))).astype(BF16)
                )
            weights.append(jnp.concatenate(low, axis=1))
        weights_out[span, :] = jnp.concatenate(weights, axis=0)
        attended_out[span, :] = jnp.concatenate(
            [dot(weights[s], values[s]).astype(BF16) for s in range(GROUP)], axis=0
        )


def feed_kernel(
    ids, tok, attended, cot, small, first_in, *refs,
):
    bufs = [ref.at[pl.ds(i, Z - 1)] for ref in refs[:3] for i in range(0, ref.shape[0], Z - 1)]
    (
        middle_out, activated_out, grad_middle_out, grad_attended_out, w_down, keep_out, send_out, first_out,
        w_out, w_up, grad_hidden, flat,
    ) = refs[3:]
    flat[:HEAD_ROWS, :] = first_in[...]
    for slot, buf in enumerate(bufs):
        for z in range(1, Z):
            row = (ids[slot] + z * 2 * PLANE) * SHARE - ROW_OUT
            row = jnp.where(ids[slot] == NO_SHARE, ROW_TOTAL - ROW_OUT, row)
            flat[pl.ds(row, SHARE), :] = buf[z - 1].astype(F32)
    matrix_from_flat(flat, 0, D, D, w_out)
    matrix_from_flat(flat, ROW_UP - ROW_OUT, D, FF, w_up)
    matrix_from_flat(flat, ROW_DOWN - ROW_OUT, FF, D, w_down)

    gain = small_vector(small, GAIN_TWO, 2)
    middle = (
        tok[...].astype(F32) + dot(attended[...], w_out[...]) + small_vector(small, BIAS_OUT, 2)
    )
    middle_out[...] = middle
    normed, rate = normalize(middle)
    normed_low = (normed * gain + small_vector(small, SHIFT_TWO, 2)).astype(BF16)
    normed_turned = normed_low.T
    cotangent = cot[...]
    cot_turned = cotangent.T
    slope = 0.7978845608028654
    cubic = slope * 0.044715
    row_up, row_down = ROW_UP - ROW_OUT, ROW_DOWN - ROW_OUT

    def products(c):
        columns = slice(c, c + CHUNK)
        return dot(normed_low, w_up[:, columns]), dot_nt(cotangent, w_down[columns, :])

    def bend(c, hidden_all, grad_all):
        columns = slice(c, c + CHUNK)
        bias = small_vector(small, BIAS_UP + c // LANES, CHUNK // LANES)
        total = jnp.zeros((8, CHUNK), F32)
        for r in range(0, tok.shape[0], STRIP):
            rows = slice(r, r + STRIP)
            hidden = hidden_all[rows] + bias
            square = hidden * hidden
            half = 0.5 + 0.5 * jnp.tanh(hidden * (slope + cubic * square))
            activated = hidden * half
            derivative = half + activated * (1.0 - half) * (2 * slope + (6 * cubic) * square)
            low = (grad_all[rows] * derivative).astype(BF16)
            activated_out[rows, columns] = activated.astype(BF16)
            grad_hidden[rows, columns] = low
            total += fold_rows(low.astype(F32))
        return total

    def weight_gradients(c):
        columns = slice(c, c + CHUNK)
        turned_to_flat(dot(cot_turned, activated_out[:, columns]), CHUNK, D, flat, row_down + c * D // LANES)
        grads = dot(normed_turned, grad_hidden[:, columns])
        for j in range(CHUNK // LANES):
            flat[pl.ds(row_up + c // LANES + j, D, stride=FF // LANES), :] = grads[
                :, j * LANES : (j + 1) * LANES
            ]

    ahead, totals = products(0), []
    for c in range(0, FF, CHUNK):
        now = ahead
        if c + CHUNK < FF:
            ahead = products(c + CHUNK)
        if c > 0:
            weight_gradients(c - CHUNK)
        totals.append(bend(c, *now))
    grad_normed = dot_nt(grad_hidden[...], w_up[...])
    weight_gradients(FF - CHUNK)
    grad_result = cotangent.astype(F32)
    grad_middle = grad_result + normalize_back(grad_normed, gain, normed, rate)
    grad_middle_out[...] = grad_middle
    grad_middle_low = grad_middle.astype(BF16)
    grad_attended_out[...] = dot_nt(grad_middle_low, w_out[...]).astype(BF16)
    matrix_to_flat(dot_tn(attended[...], grad_middle_low), D, D, flat, 0)
    sums = jnp.concatenate(
        [
            fold_rows(grad_middle_low.astype(F32)),
            fold_rows(grad_normed * normed),
            fold_rows(grad_normed),
            *totals,
            fold_rows(grad_result),
        ],
        axis=1,
    )
    sums = jnp.sum(sums, axis=0, keepdims=True)
    base = ROW_SMALL - ROW_OUT
    flat[base : base + LATE_SMALL, :] = jnp.zeros((LATE_SMALL, LANES), F32)
    for i in range(sums.shape[1] // LANES):
        row = base + LATE_SMALL + i
        flat[row : row + 1, :] = sums[:, i * LANES : (i + 1) * LANES]
    flat[ROW_END - ROW_OUT : ROW_TOTAL - ROW_OUT, :] = jnp.zeros((ROW_TOTAL - ROW_END, LANES), F32)
    first_out[...] = flat[:HEAD_ROWS, :]
    for target, out in enumerate((keep_out, send_out)):
        for p in range(PLANE):
            for z in range(1, Z):
                share = ids[SLOTS + target * PLANE + p] + z * 2 * PLANE
                rows = flat[pl.ds(share * SHARE - ROW_OUT, SHARE), :]
                out[p * (Z - 1) + z - 1] = rows.astype(out.dtype)


def result_kernel(middle, activated, w_down, small, result_out):
    result = middle[...] + dot(activated[...], w_down[...]) + small_vector(small, BIAS_DOWN, 2)
    result_out[...] = result.astype(BF16)


def attend_back_kernel(
    ids, project, weights, grad_attended, normed_turned, w_qkv, small, first_in,
    grad_project, keep_out, send_out, flat, wide,
):
    products, sums = 0.0, 0.0
    for g in range(project.shape[0] // WIDE):
        spans = [slice(r, r + SEQ) for r in range(g * WIDE, (g + 1) * WIDE, SEQ)]
        grad_weights = [
            dot_nt(grad_attended[span, :], spread_heads(project[span, 2 * D :])) for span in spans
        ]
        scores_low, scores_turned, weights_turned = [], [], []
        for s, span in enumerate(spans):
            low, turned, mine_turned = [], [], []
            for h in range(HEADS):
                columns = slice(h * SEQ, (h + 1) * SEQ)
                mine_low = weights[span, columns]
                mine = mine_low.astype(F32)
                product = mine * grad_weights[s][:, columns]
                grad_scores = (product - mine * jnp.sum(product, axis=-1, keepdims=True)) * SCALE
                low.append(grad_scores.astype(BF16))
                turned.append(low[-1].T)
                mine_turned.append(mine_low.T)
            scores_low.append(jnp.concatenate(low, axis=1))
            scores_turned.append(jnp.concatenate(turned, axis=1))
            weights_turned.append(jnp.concatenate(mine_turned, axis=1))
        for s, span in enumerate(spans):
            key = spread_heads(project[span, D : 2 * D])
            grad_project[span, :D] = dot(scores_low[s], key).astype(BF16)
            query = spread_heads(project[span, :D])
            grad_project[span, D : 2 * D] = dot(scores_turned[s], query).astype(BF16)
            grad_value = dot(weights_turned[s], spread_heads(grad_attended[span, :]))
            grad_project[span, 2 * D :] = grad_value.astype(BF16)
        span = slice(g * WIDE, (g + 1) * WIDE)
        products += dot(normed_turned[:, span], grad_project[span, :])
        sums += fold_rows(grad_project[span, :].astype(F32))
    sums = jnp.sum(sums, axis=0, keepdims=True)
    gain = jnp.broadcast_to(small_vector(small, GAIN_ONE, 2), (LANES, D)).T
    shift = jnp.broadcast_to(small_vector(small, SHIFT_ONE, 2), (LANES, D)).T
    grad_gain = jnp.zeros((D, LANES), F32)
    grad_shift = jnp.zeros((D, LANES), F32)
    per_row = 3 * D // LANES
    for j in range(per_row):
        columns = slice(j * LANES, (j + 1) * LANES)
        weight = w_qkv[:, columns].astype(F32)
        grad_gain += products[:, columns] * weight
        grad_shift += sums[:, columns] * weight
        flat[pl.ds(j, D, stride=per_row), :] = products[:, columns] * gain + sums[:, columns] * shift
    flat[ROW_OUT:, :] = first_in[...]
    grad_gain = jnp.sum(grad_gain.T, axis=0, keepdims=True)
    grad_shift = jnp.sum(grad_shift.T, axis=0, keepdims=True)
    late = jnp.concatenate([grad_gain, grad_shift, sums[:, :D], sums[:, 2 * D :]], axis=1)
    side = jnp.concatenate(
        [late[:, i * LANES : (i + 1) * LANES] for i in range(LATE_SMALL)]
        + [jnp.zeros((SIDE_ROWS - LATE_SMALL, LANES), F32)],
        axis=0,
    )
    wide[SHARE:SIDE, :] = jnp.zeros((SIDE - SHARE, LANES), F32)
    for target, out in enumerate((keep_out, send_out)):
        for p in range(PLANE):
            share = ids[target * PLANE + p]
            wide[:SHARE, :] = flat[pl.ds(share * SHARE, SHARE), :]
            wide[SIDE:, :] = jnp.where(share == 2 * PLANE - 1, side, 0.0)
            out[p] = wide[...].astype(out.dtype)


def input_grad_kernel(tok, grad_project, grad_middle, w_qkv, small, input_grad_out):
    gain = small_vector(small, GAIN_ONE, 2)

    def some(g, carry):
        span = pl.ds(pl.multiple_of(g * WIDE, WIDE), WIDE)
        normed, rate = normalize(tok[span, :].astype(F32))
        grad_normed = dot_nt(grad_project[span, :], w_qkv[...])
        input_grad_out[span, :] = grad_middle[span, :] + normalize_back(
            grad_normed, gain, normed, rate
        )
        return carry

    lax.fori_loop(0, tok.shape[0] // WIDE, some, 0)


def stack_kernel(*refs):
    row = 0
    for ref in refs[:-1]:
        refs[-1][row : row + ref.shape[0]] = ref[...]
        row += ref.shape[0]


def add_core_kernel(first, first_in, rest, rest_in, *refs):
    outs, column = refs[:-1], refs[-1]
    end = SMALL_IN_SHARE + LATE_SMALL
    for p in range(PLANE):
        item = first[p] + first_in[p].astype(F32)
        span = slice(p * (Z - 1), (p + 1) * (Z - 1))
        column[0] = item[:SHARE, :]
        column[1:] = rest[span] + rest_in[span].astype(F32)
        column[Z - 1, SMALL_IN_SHARE:end, :] += item[SIDE : SIDE + LATE_SMALL, :]
        for part, rows in enumerate(PARTS):
            out = outs[p * len(PARTS) + part]
            out[...] = column[:, rows, :].astype(out.dtype)


def add_plane_kernel(ids, kept, *refs):
    arrived = refs[: PLANE - 1]
    keep_out, *sends, column = refs[PLANE - 1 :]
    column[...] = kept[...] + sum(item[...].astype(F32) for item in arrived)
    keep_out[...] = column[ids[0]]
    for d, out in enumerate(sends):
        out[...] = column[lax.rem(ids[0] + d + 1, Z)].astype(BF16)


def add_column_kernel(*refs):
    for part, rows in enumerate(PARTS):
        kept, *arrived = refs[part * Z : (part + 1) * Z]
        refs[-1][rows, :] = kept[...] + sum(item[...].astype(F32) for item in arrived)


def like(*shape, kind=F32):
    return jax.ShapeDtypeStruct(shape, kind)


SMEM_SPEC = pl.BlockSpec(memory_space=pltpu.SMEM)
VMEM_SPEC = pl.BlockSpec(memory_space=pltpu.VMEM)

def cost(us):
    return pl.CostEstimate(flops=int(us * 1e9), bytes_accessed=1 << 20, transcendentals=0)


def call(kernel, name, ids, inputs, outs, scratch=(), us=1):
    with_ids = ids is not None
    results = pl.pallas_call(
        kernel,
        in_specs=[SMEM_SPEC] * with_ids + [VMEM_SPEC] * len(inputs),
        out_specs=[VMEM_SPEC] * len(outs),
        out_shape=list(outs),
        scratch_shapes=list(scratch),
        compiler_params=pltpu.CompilerParams(vmem_limit_bytes=VMEM_BYTES),
        cost_estimate=cost(us),
        name=name,
    )(*([ids] if with_ids else []), *inputs)
    return results if len(outs) > 1 else results[0]


def prepare(tokens, params, segment_ids):
    rows = tokens.shape[0]
    return call(
        prepare_kernel, "prepare", None, [tokens, params, segment_ids.reshape(-1, SEQ)],
        [
            like(rows, D),
            like(D, rows, kind=BF16),
            like(*params.shape, kind=BF16),
            like(rows, SEQ),
        ],
        us=2,
    )


def slot_ids(plane, core, choose):
    mine, others = choose(core == 0, 1, 2), choose(core == 0, 2, 1)
    pairs = [
        (plane, core, True), (plane ^ mine, core, True), (plane ^ 3, core, core == 1),
        (plane ^ others, core ^ 1, True), (plane ^ 3, core ^ 1, core == 0),
    ]
    return [
        choose(there, p * 2 + c, NO_SHARE)
        for p, first, there in pairs
        for c in (first, first ^ 1)
    ]


def stack(items):
    shape = (sum(item.shape[0] for item in items),) + items[0].shape[1:]
    return call(stack_kernel, "stack", None, items, [like(*shape, kind=items[0].dtype)])


def attend(ids, allowed, normed, bufs):
    rows = normed.shape[0]
    shapes = [(rows, 3 * D), (rows, HEADS * SEQ), (rows, D), (D, 3 * D)]
    return call(
        attend_kernel, "attend", ids, [allowed, normed, *bufs],
        [like(*shape, kind=BF16) for shape in shapes]
        + [like(SMALL_ROWS, LANES), like(HEAD_ROWS, LANES)],
        [pltpu.VMEM((FIRST_ROWS + SHARE, LANES), F32)], us=0.2,
    )


def feed(ids, tokens, attended, cotangent, small, first, bufs, send_kind):
    rows = tokens.shape[0]
    return call(
        feed_kernel, "feed", ids, [tokens, attended, cotangent, small, first, *bufs],
        [
            like(rows, D),
            like(rows, FF, kind=BF16),
            like(rows, D),
            like(rows, D, kind=BF16),
            like(FF, D, kind=BF16),
            like(PLANE * (Z - 1), SHARE, LANES),
            like(PLANE * (Z - 1), SHARE, LANES, kind=send_kind),
            like(HEAD_ROWS, LANES),
        ],
        [
            pltpu.VMEM((D, D), BF16),
            pltpu.VMEM((D, FF), BF16),
            pltpu.VMEM((rows, FF), BF16),
            pltpu.VMEM((ROW_TOTAL - ROW_OUT + SHARE, LANES), F32),
        ],
        us=8,
    )


def result(middle, activated, w_down, small):
    return call(
        result_kernel, "result", None, [middle, activated, w_down, small],
        [like(*middle.shape, kind=BF16)], us=2,
    )


def attend_back(ids, project, weights, grad_attended, normed_turned, w_qkv, small, first, send_kind):
    shape = (PLANE, SIDE + SIDE_ROWS, LANES)
    return call(
        attend_back_kernel, "attend_back", ids,
        [project, weights, grad_attended, normed_turned, w_qkv, small, first],
        [like(*project.shape, kind=BF16), like(*shape), like(*shape, kind=send_kind)],
        [pltpu.VMEM((FIRST_ROWS, LANES), F32), pltpu.VMEM(shape[1:], F32)], us=4,
    )


def input_gradient(tokens, grad_project, grad_middle, w_qkv, small):
    return call(
        input_grad_kernel, "input_grad", None, [tokens, grad_project, grad_middle, w_qkv, small],
        [like(*tokens.shape)], us=2,
    )


def local_any(n, tokens, params, segment_ids, cotangent):
    total = n * params.shape[0]
    normed, normed_turned, _, allowed = prepare(tokens, params, segment_ids)
    gathered = lax.all_gather(params, "fsdp", axis=0).reshape(total, LANES)
    shares = gathered[:ROW_TOTAL].reshape(Z, 2 * PLANE, SHARE, LANES)
    order = [p * 2 + c for c in range(2) for p in (0, *STEPS)]
    side = jnp.concatenate(
        [jnp.zeros((SIDE - SHARE, LANES), BF16), gathered[ROW_SMALL:ROW_TOTAL]], axis=0
    )
    places = slot_ids(0, 0, lambda there, yes, no: yes if there else no)
    firsts = [
        jnp.concatenate([shares[0, k % NO_SHARE], side], axis=0)[None] for k in places
    ]
    rests = [shares[1:, k % NO_SHARE] for k in places]
    firsts, rests = (
        [jnp.concatenate(items[i:j]) for i, j in ((0, 2), (2, 6), (6, SLOTS))]
        for items in (firsts, rests)
    )
    in_ids, ids = jnp.array(places, jnp.int32), jnp.array(order, jnp.int32)
    project, weights, attended, w_qkv, small, first = attend(in_ids, allowed, normed, firsts)
    middle, activated, grad_middle, grad_attended, w_down, rest, rest_send, first_grad = feed(
        jnp.concatenate([in_ids, ids]), tokens, attended, cotangent, small, first, rests, F32
    )
    outputs = result(middle, activated, w_down, small)
    grad_project, first, first_send = attend_back(
        ids, project, weights, grad_attended, normed_turned, w_qkv, small, first_grad, F32
    )
    input_grad = input_gradient(tokens, grad_project, grad_middle, w_qkv, small)
    back = [order.index(k) for k in range(2 * PLANE)]
    first = jnp.concatenate([first, first_send])[jnp.array(back)].reshape(PLANE, 2, -1, LANES)
    rest = jnp.concatenate([rest, rest_send]).reshape(2 * PLANE, Z - 1, SHARE, LANES)
    rest = rest[jnp.array(back)].transpose(1, 0, 2, 3)
    flat = jnp.concatenate(
        [
            first[:, :, :SHARE].reshape(-1, LANES),
            rest.reshape(-1, LANES),
            jnp.zeros((total - ROW_TOTAL, LANES), F32),
        ],
        axis=0,
    )
    flat = flat.at[ROW_SMALL : ROW_SMALL + LATE_SMALL].add(
        first[PLANE - 1, 1, SIDE : SIDE + LATE_SMALL]
    )
    param_grad = lax.psum_scatter(flat, "fsdp", scatter_dimension=0, tiled=True)
    return outputs, input_grad, param_grad


def index_of(z, plane, core):
    return (z * PLANE + plane) * 2 + core


def move(values, step_z, step_plane, step_core):
    pairs = [
        (index_of(z, p, c), index_of((z + step_z) % Z, p ^ step_plane, c ^ step_core))
        for z in range(Z)
        for p in range(PLANE)
        for c in range(2)
    ]
    return lax.ppermute(values, "fsdp", pairs)


def to_neighbour(values):
    return lax.ppermute(
        values, "fsdp",
        [
            (index_of(z, p, c), index_of(z, p ^ (1 + c), c))
            for z in range(Z)
            for p in range(PLANE)
            for c in range(2)
        ],
    )


def to_diagonal(values):
    return lax.ppermute(
        values, "fsdp",
        [(index_of(z, p, 1), index_of(z, p ^ 3, 1)) for z in range(Z) for p in range(PLANE)],
    )


def spread(own):
    pair = stack([own, move(own, 0, 0, 1)])
    return pair, [to_neighbour(pair), to_diagonal(pair)]


def local_slice(tokens, params, segment_ids, cotangent):
    me = lax.axis_index("fsdp").astype(jnp.int32)
    z, plane, core = me // (2 * PLANE), (me // 2) % PLANE, me % 2
    where = z.reshape(1)
    in_ids = jnp.stack(slot_ids(plane, core, jnp.where)).astype(jnp.int32)
    ids = jnp.stack(
        [(plane ^ dp) * 2 + (core ^ dc) for dc in range(2) for dp in (0, *STEPS)]
    )

    normed, normed_turned, own, allowed = prepare(tokens, params, segment_ids)
    first, rest = call(
        sort_kernel, "sort_shares", where, [own] + [move(params, d, 0, 0) for d in range(1, Z)],
        [like(1, SIDE + SMALL_ROWS, LANES, kind=BF16), like(Z - 1, SHARE, LANES, kind=BF16)],
        [pltpu.VMEM((Z, SHARE, LANES), BF16), pltpu.VMEM((SIDE + SMALL_ROWS, LANES), F32)],
    )
    pair, received = spread(first)
    rest_pair, rest_received = spread(rest)
    received = stack(received)
    project, weights, attended, w_qkv, small, first = attend(
        in_ids, allowed, normed, [pair, received, move(received, 0, 0, 1)]
    )
    *rest_received, attended = lax.optimization_barrier((*rest_received, attended))
    rest_received = stack(rest_received)
    rests = [rest_pair, rest_received, move(rest_received, 0, 0, 1)]
    middle, activated, grad_middle, grad_attended, w_down, rest, send, first_grad = feed(
        jnp.concatenate([in_ids, ids]), tokens, attended, cotangent, small, first, rests, BF16
    )

    rest_in = move(send, 0, 0, 1)
    grad_project, first, send = attend_back(
        ids, project, weights, grad_attended, normed_turned, w_qkv, small, first_grad, BF16
    )
    first_in = move(send, 0, 0, 1)
    input_grad = input_gradient(tokens, grad_project, grad_middle, w_qkv, small)
    first_in, input_grad = lax.optimization_barrier((first_in, input_grad))
    parts = [(Z, rows.stop - rows.start, LANES) for rows in PARTS]
    sums = call(
        add_core_kernel, "add_core", None, [first, first_in, rest, rest_in],
        [like(*part, kind=BF16 if p else F32) for p in range(PLANE) for part in parts],
        [pltpu.VMEM((Z, SHARE, LANES), F32)],
    )
    sums = [sums[n::2] for n in range(2)]
    outputs = result(middle, activated, w_down, small)
    arrived = [[move(item, 0, d, 0) for item, d in zip(part[1:], STEPS)] for part in sums]
    columns = []
    for n, part in enumerate(parts):
        kept, *sends = call(
            add_plane_kernel, "add_plane", where, [sums[n][0]] + arrived[n],
            [like(*part[1:])] + [like(*part[1:], kind=BF16)] * (Z - 1), [pltpu.VMEM(part, F32)],
        )
        columns += [kept] + [move(item, d + 1, 0, 0) for d, item in enumerate(sends)]
    param_grad = call(add_column_kernel, "add_column", None, columns, [like(SHARE, LANES)])
    return outputs, input_grad, param_grad


def solution(mesh):
    n = mesh.shape["fsdp"]
    local = local_slice if n == 2 * PLANE * Z else functools.partial(local_any, n)
    in_specs = (P("fsdp", None), P("fsdp", None), P("fsdp"), P("fsdp", None))
    out_specs = (P("fsdp", None), P("fsdp", None), P("fsdp", None))
    return jax.shard_map(local, mesh=mesh, in_specs=in_specs, out_specs=out_specs, check_vma=False)
```

```python
import functools

import jax
import jax.numpy as jnp
from jax import lax
from jax.experimental import pallas as pl
from jax.experimental.pallas import tpu as pltpu
from jax.sharding import PartitionSpec as P

D = 256
HEADS = 4
HEAD_DIM = 64
FF = 1024
SEQ = 128
LANES = 128
GROUP = 4
WIDE = GROUP * SEQ
CHUNK = 256
STRIP = 64
EPSILON = 1e-05
SCALE = HEAD_DIM ** (-0.5)
VMEM_BYTES = 24 * 1024 * 1024

ROW_QKV = 0
ROW_OUT = 1536
ROW_UP = 2048
ROW_DOWN = 4096
ROW_SMALL = 6144
ROW_END = 6168
ROW_TOTAL = 6176
GAIN_ONE, SHIFT_ONE, BIAS_QUERY, BIAS_VALUE, BIAS_OUT = 0, 2, 4, 6, 8
GAIN_TWO, SHIFT_TWO, BIAS_UP, BIAS_DOWN = 10, 12, 14, 22
SMALL_ROWS = 32
LATE_SMALL = 8

SHARE = 193
Z, PLANE = 4, 4
FIRST_ROWS = 2 * PLANE * SHARE
HEAD_ROWS = FIRST_ROWS - ROW_OUT
SIDE, SIDE_ROWS = 208, 16
SMALL_IN_SHARE = ROW_SMALL - (2 * PLANE * Z - 1) * SHARE

F32 = jnp.float32
BF16 = jnp.bfloat16


def dot(left, right):
    return jnp.dot(left, right, preferred_element_type=F32)


def dot_nt(left, right):
    return lax.dot_general(left, right, (((1,), (1,)), ((), ())), preferred_element_type=F32)


def dot_tn(left, right):
    return lax.dot_general(left, right, (((0,), (0,)), ((), ())), preferred_element_type=F32)


def small_vector(small, row, count):
    return jnp.concatenate([small[row + i : row + i + 1, :] for i in range(count)], axis=1)


def fold_rows(values):
    rows, columns = values.shape
    return jnp.sum(values.reshape(rows // 8, 8, columns), axis=0)


def normalize(values):
    center = values - jnp.mean(values, axis=-1, keepdims=True)
    rate = lax.rsqrt(jnp.mean(center * center, axis=-1, keepdims=True) + EPSILON)
    return center * rate, rate


def normalize_back(grad, gain, normed, rate):
    scaled = grad * gain
    return rate * (
        scaled
        - jnp.mean(scaled, axis=-1, keepdims=True)
        - normed * jnp.mean(scaled * normed, axis=-1, keepdims=True)
    )


def head_masks():
    lane = lax.broadcasted_iota(jnp.int32, (1, D), 1)
    return [(lane // HEAD_DIM == h).astype(F32).astype(BF16) for h in range(HEADS)]


def spread_heads(rows):
    return jnp.concatenate([rows * mask for mask in head_masks()], axis=0)


def matrix_from_flat(flat, start, rows, columns, out):
    per_row = columns // LANES
    for j in range(per_row):
        out[:, j * LANES : (j + 1) * LANES] = flat[
            pl.ds(start + j, rows, stride=per_row), :
        ].astype(BF16)


def matrix_to_flat(matrix, rows, columns, flat, start):
    per_row = columns // LANES
    for j in range(per_row):
        flat[pl.ds(start + j, rows, stride=per_row), :] = matrix[:, j * LANES : (j + 1) * LANES]


def prepare_kernel(tok, params, seg, normed_out, normed_turned, own, allowed):
    normed, _ = normalize(tok[...].astype(F32))
    normed_out[...] = normed
    normed_turned[...] = normed.astype(BF16).T
    own[...] = params[...]
    causal = lax.broadcasted_iota(jnp.int32, (SEQ, SEQ), 0) <= lax.broadcasted_iota(
        jnp.int32, (SEQ, SEQ), 1
    )
    for s in range(seg.shape[0]):
        across = jnp.broadcast_to(seg[s : s + 1, :].astype(F32), (SEQ, SEQ))
        allowed[s * SEQ : (s + 1) * SEQ, :] = (causal & (across == across.T)).astype(F32)


def sort_kernel(ids, *refs):
    received, (first, rest, stage, wide) = refs[:Z], refs[Z:]
    for d in range(Z):
        stage[lax.rem(ids[0] + Z - d, Z)] = received[d][...]
    rest[...] = stage[1:]
    wide[:SHARE, :] = stage[0].astype(F32)
    wide[SHARE:SIDE, :] = jnp.zeros((SIDE - SHARE, LANES), F32)
    last = stage[Z - 1].astype(F32)
    wide[SIDE:, :] = last[SMALL_IN_SHARE:, :]
    first[...] = wide[...].astype(BF16)


def attend_kernel(ids, allowed, normed, *refs):
    bufs = refs[: 2 * PLANE]
    project_out, weights_out, attended_out, w_qkv, small, first_out, flat = refs[2 * PLANE :]
    for slot, buf in enumerate(bufs):
        wide = buf[...].astype(F32)
        flat[pl.ds(ids[slot] * SHARE, SHARE), :] = wide[:SHARE, :]

        @pl.when(ids[slot] == 2 * PLANE - 1)
        def _():
            small[...] = wide[SIDE:, :]

    matrix_from_flat(flat, ROW_QKV, D, 3 * D, w_qkv)
    first_out[...] = flat[ROW_OUT:FIRST_ROWS, :]

    gain = small_vector(small, GAIN_ONE, 2)
    shift = small_vector(small, SHIFT_ONE, 2)
    bias = jnp.concatenate(
        [
            small_vector(small, BIAS_QUERY, 2),
            jnp.zeros((1, D), F32),
            small_vector(small, BIAS_VALUE, 2),
        ],
        axis=1,
    )
    project_out[...] = (
        dot((normed[...] * gain + shift).astype(BF16), w_qkv[...]) + bias
    ).astype(BF16)
    for g in range(normed.shape[0] // WIDE):
        starts = range(g * WIDE, (g + 1) * WIDE, SEQ)
        scores = [
            dot_nt(
                spread_heads(project_out[r : r + SEQ, D : 2 * D]),
                project_out[r : r + SEQ, :D] * SCALE,
            )
            for r in starts
        ]
        weights = []
        for r, score in zip(starts, scores):
            open_pairs = allowed[r : r + SEQ, :] > 0.5
            turned = []
            for h in range(HEADS):
                mine = jnp.where(open_pairs, score[h * SEQ : (h + 1) * SEQ, :], -1e30)
                grown = jnp.exp(mine - jnp.max(mine, axis=0, keepdims=True))
                low = (grown * (1.0 / jnp.sum(grown, axis=0, keepdims=True))).astype(BF16)
                weights_out[r : r + SEQ, h * SEQ : (h + 1) * SEQ] = low
                turned.append(low.T)
            weights.append(jnp.concatenate(turned, axis=1))
        for r, weight in zip(starts, weights):
            value = spread_heads(project_out[r : r + SEQ, 2 * D :])
            attended_out[r : r + SEQ, :] = dot(weight, value).astype(BF16)


def feed_kernel(
    ids, tok, attended, cot, small, first_in, *refs,
):
    bufs = []
    for own, others in (refs[0:2], refs[2:4]):
        bufs.append(own)
        bufs += [others.at[pl.ds(p * (Z - 1), Z - 1)] for p in range(PLANE - 1)]
    (
        middle_out, activated_out, grad_middle_out, grad_attended_out, w_down, keep_out, send_out, first_out,
        w_out, w_up, grad_hidden, flat,
    ) = refs[4:]
    flat[:HEAD_ROWS, :] = first_in[...]
    for slot, buf in enumerate(bufs):
        for z in range(1, Z):
            share = ids[slot] + z * 2 * PLANE
            flat[pl.ds(share * SHARE - ROW_OUT, SHARE), :] = buf[z - 1].astype(F32)
    matrix_from_flat(flat, 0, D, D, w_out)
    matrix_from_flat(flat, ROW_UP - ROW_OUT, D, FF, w_up)
    matrix_from_flat(flat, ROW_DOWN - ROW_OUT, FF, D, w_down)

    gain = small_vector(small, GAIN_TWO, 2)
    middle = (
        tok[...].astype(F32) + dot(attended[...], w_out[...]) + small_vector(small, BIAS_OUT, 2)
    )
    middle_out[...] = middle
    normed, rate = normalize(middle)
    normed_low = (normed * gain + small_vector(small, SHIFT_TWO, 2)).astype(BF16)
    normed_turned = normed_low.T
    cotangent = cot[...]
    slope = 0.7978845608028654
    cubic = slope * 0.044715
    row_up, row_down = ROW_UP - ROW_OUT, ROW_DOWN - ROW_OUT

    def products(c):
        columns = slice(c, c + CHUNK)
        return dot(normed_low, w_up[:, columns]), dot_nt(cotangent, w_down[columns, :])

    def bend(c, hidden_all, grad_all):
        columns = slice(c, c + CHUNK)
        bias = small_vector(small, BIAS_UP + c // LANES, CHUNK // LANES)
        total = jnp.zeros((8, CHUNK), F32)
        for r in range(0, tok.shape[0], STRIP):
            rows = slice(r, r + STRIP)
            hidden = hidden_all[rows] + bias
            square = hidden * hidden
            half = 0.5 + 0.5 * jnp.tanh(hidden * (slope + cubic * square))
            activated = hidden * half
            derivative = half + activated * (1.0 - half) * (2 * slope + (6 * cubic) * square)
            low = (grad_all[rows] * derivative).astype(BF16)
            activated_out[rows, columns] = activated.astype(BF16)
            grad_hidden[rows, columns] = low
            total += fold_rows(low.astype(F32))
        return total

    def weight_gradients(c):
        columns = slice(c, c + CHUNK)
        if (c // CHUNK) % 2:
            start, rows = c - CHUNK, 2 * CHUNK
            turned = activated_out[:, start : start + rows].T
            matrix_to_flat(dot(turned, cotangent), rows, D, flat, row_down + start * D // LANES)
        grads = dot(normed_turned, grad_hidden[:, columns])
        for j in range(CHUNK // LANES):
            flat[pl.ds(row_up + c // LANES + j, D, stride=FF // LANES), :] = grads[
                :, j * LANES : (j + 1) * LANES
            ]

    ahead, totals = products(0), []
    for c in range(0, FF, CHUNK):
        now = ahead
        if c + CHUNK < FF:
            ahead = products(c + CHUNK)
        if c > 0:
            weight_gradients(c - CHUNK)
        totals.append(bend(c, *now))
    grad_normed = dot_nt(grad_hidden[...], w_up[...])
    weight_gradients(FF - CHUNK)
    grad_result = cotangent.astype(F32)
    grad_middle = grad_result + normalize_back(grad_normed, gain, normed, rate)
    grad_middle_out[...] = grad_middle
    grad_middle_low = grad_middle.astype(BF16)
    grad_attended_out[...] = dot_nt(grad_middle_low, w_out[...]).astype(BF16)
    matrix_to_flat(dot_tn(attended[...], grad_middle_low), D, D, flat, 0)
    sums = jnp.concatenate(
        [
            fold_rows(grad_middle_low.astype(F32)),
            fold_rows(grad_normed * normed),
            fold_rows(grad_normed),
            *totals,
            fold_rows(grad_result),
        ],
        axis=1,
    )
    sums = jnp.sum(sums, axis=0, keepdims=True)
    base = ROW_SMALL - ROW_OUT
    flat[base : base + LATE_SMALL, :] = jnp.zeros((LATE_SMALL, LANES), F32)
    for i in range(sums.shape[1] // LANES):
        row = base + LATE_SMALL + i
        flat[row : row + 1, :] = sums[:, i * LANES : (i + 1) * LANES]
    flat[ROW_END - ROW_OUT :, :] = jnp.zeros((ROW_TOTAL - ROW_END, LANES), F32)
    first_out[...] = flat[:HEAD_ROWS, :]
    for target, out in enumerate((keep_out, send_out)):
        for p in range(PLANE):
            for z in range(1, Z):
                share = ids[target * PLANE + p] + z * 2 * PLANE
                rows = flat[pl.ds(share * SHARE - ROW_OUT, SHARE), :]
                out[p * (Z - 1) + z - 1] = rows.astype(out.dtype)


def result_kernel(middle, activated, w_down, small, result_out):
    result = middle[...] + dot(activated[...], w_down[...]) + small_vector(small, BIAS_DOWN, 2)
    result_out[...] = result.astype(BF16)


def attend_back_kernel(
    ids, project, weights, grad_attended, normed_turned, w_qkv, small, first_in,
    grad_project, keep_out, send_out, flat, wide,
):
    products, sums = 0.0, 0.0
    for g in range(project.shape[0] // WIDE):
        spans = [slice(r, r + SEQ) for r in range(g * WIDE, (g + 1) * WIDE, SEQ)]
        grad_weights = [
            dot_nt(spread_heads(project[span, 2 * D :]), grad_attended[span, :]) for span in spans
        ]
        scores_low, scores_turned = [], []
        for span, grads in zip(spans, grad_weights):
            low, turned = [], []
            for h in range(HEADS):
                mine = weights[span, h * SEQ : (h + 1) * SEQ].astype(F32)
                product = mine * grads[h * SEQ : (h + 1) * SEQ, :]
                grad_scores = (product - mine * jnp.sum(product, axis=0, keepdims=True)) * SCALE
                turned.append(grad_scores.astype(BF16))
                low.append(turned[-1].T)
            scores_low.append(jnp.concatenate(low, axis=1))
            scores_turned.append(jnp.concatenate(turned, axis=1))
        for s, span in enumerate(spans):
            key = spread_heads(project[span, D : 2 * D])
            grad_project[span, :D] = dot(scores_low[s], key).astype(BF16)
            query = spread_heads(project[span, :D])
            grad_project[span, D : 2 * D] = dot(scores_turned[s], query).astype(BF16)
            grad_value = dot(weights[span, :], spread_heads(grad_attended[span, :]))
            grad_project[span, 2 * D :] = grad_value.astype(BF16)
        span = slice(g * WIDE, (g + 1) * WIDE)
        products += dot(normed_turned[:, span], grad_project[span, :])
        sums += fold_rows(grad_project[span, :].astype(F32))
    sums = jnp.sum(sums, axis=0, keepdims=True)
    gain = jnp.broadcast_to(small_vector(small, GAIN_ONE, 2), (LANES, D)).T
    shift = jnp.broadcast_to(small_vector(small, SHIFT_ONE, 2), (LANES, D)).T
    grad_gain = jnp.zeros((D, LANES), F32)
    grad_shift = jnp.zeros((D, LANES), F32)
    per_row = 3 * D // LANES
    for j in range(per_row):
        columns = slice(j * LANES, (j + 1) * LANES)
        weight = w_qkv[:, columns].astype(F32)
        grad_gain += products[:, columns] * weight
        grad_shift += sums[:, columns] * weight
        flat[pl.ds(j, D, stride=per_row), :] = products[:, columns] * gain + sums[:, columns] * shift
    flat[ROW_OUT:, :] = first_in[...]
    grad_gain = jnp.sum(grad_gain.T, axis=0, keepdims=True)
    grad_shift = jnp.sum(grad_shift.T, axis=0, keepdims=True)
    late = jnp.concatenate([grad_gain, grad_shift, sums[:, :D], sums[:, 2 * D :]], axis=1)
    side = jnp.concatenate(
        [late[:, i * LANES : (i + 1) * LANES] for i in range(LATE_SMALL)]
        + [jnp.zeros((SIDE_ROWS - LATE_SMALL, LANES), F32)],
        axis=0,
    )
    wide[SHARE:SIDE, :] = jnp.zeros((SIDE - SHARE, LANES), F32)
    for target, out in enumerate((keep_out, send_out)):
        for p in range(PLANE):
            share = ids[target * PLANE + p]
            wide[:SHARE, :] = flat[pl.ds(share * SHARE, SHARE), :]
            wide[SIDE:, :] = jnp.where(share == 2 * PLANE - 1, side, 0.0)
            out[p] = wide[...].astype(out.dtype)


def input_grad_kernel(tok, grad_project, grad_middle, w_qkv, small, input_grad_out):
    gain = small_vector(small, GAIN_ONE, 2)

    def some(g, carry):
        span = pl.ds(pl.multiple_of(g * WIDE, WIDE), WIDE)
        normed, rate = normalize(tok[span, :].astype(F32))
        grad_normed = dot_nt(grad_project[span, :], w_qkv[...])
        input_grad_out[span, :] = grad_middle[span, :] + normalize_back(
            grad_normed, gain, normed, rate
        )
        return carry

    lax.fori_loop(0, tok.shape[0] // WIDE, some, 0)


def stack_kernel(*refs):
    row = 0
    for ref in refs[:-1]:
        refs[-1][row : row + ref.shape[0]] = ref[...]
        row += ref.shape[0]


def add_core_kernel(first, first_in, rest, rest_in, keep_out, *refs):
    sends, column = refs[:-1], refs[-1]
    end = SMALL_IN_SHARE + LATE_SMALL
    for p, out in enumerate((keep_out, *sends)):
        item = first[p] + first_in[p].astype(F32)
        span = slice(p * (Z - 1), (p + 1) * (Z - 1))
        column[0] = item[:SHARE, :]
        column[1:] = rest[span] + rest_in[span].astype(F32)
        column[Z - 1, SMALL_IN_SHARE:end, :] += item[SIDE : SIDE + LATE_SMALL, :]
        out[...] = column[...].astype(out.dtype)


def add_plane_kernel(ids, kept, *refs):
    arrived = refs[: PLANE - 1]
    keep_out, *sends, column = refs[PLANE - 1 :]
    column[...] = kept[...] + sum(item[...].astype(F32) for item in arrived)
    keep_out[...] = column[ids[0]]
    for d, out in enumerate(sends):
        out[...] = column[lax.rem(ids[0] + d + 1, Z)].astype(BF16)


def add_column_kernel(kept, *refs):
    refs[-1][...] = kept[...] + sum(item[...].astype(F32) for item in refs[:-1])


def like(*shape, kind=F32):
    return jax.ShapeDtypeStruct(shape, kind)


SMEM_SPEC = pl.BlockSpec(memory_space=pltpu.SMEM)
VMEM_SPEC = pl.BlockSpec(memory_space=pltpu.VMEM)

def cost(us):
    return pl.CostEstimate(flops=int(us * 1e9), bytes_accessed=1 << 20, transcendentals=0)


def call(kernel, name, ids, inputs, outs, scratch=(), us=1):
    with_ids = ids is not None
    results = pl.pallas_call(
        kernel,
        in_specs=[SMEM_SPEC] * with_ids + [VMEM_SPEC] * len(inputs),
        out_specs=[VMEM_SPEC] * len(outs),
        out_shape=list(outs),
        scratch_shapes=list(scratch),
        compiler_params=pltpu.CompilerParams(vmem_limit_bytes=VMEM_BYTES),
        cost_estimate=cost(us),
        name=name,
    )(*([ids] if with_ids else []), *inputs)
    return results if len(outs) > 1 else results[0]


def prepare(tokens, params, segment_ids):
    rows = tokens.shape[0]
    return call(
        prepare_kernel, "prepare", None, [tokens, params, segment_ids.reshape(-1, SEQ)],
        [
            like(rows, D),
            like(D, rows, kind=BF16),
            like(*params.shape, kind=BF16),
            like(rows, SEQ),
        ],
        us=2,
    )


def stack(items):
    shape = (sum(item.shape[0] for item in items),) + items[0].shape[1:]
    return call(stack_kernel, "stack", None, items, [like(*shape, kind=items[0].dtype)])


def attend(ids, allowed, normed, bufs):
    rows = normed.shape[0]
    shapes = [(rows, 3 * D), (rows, HEADS * SEQ), (rows, D), (D, 3 * D)]
    return call(
        attend_kernel, "attend", ids, [allowed, normed, *bufs],
        [like(*shape, kind=BF16) for shape in shapes]
        + [like(SMALL_ROWS, LANES), like(HEAD_ROWS, LANES)],
        [pltpu.VMEM((FIRST_ROWS, LANES), F32)], us=0.2,
    )


def feed(ids, tokens, attended, cotangent, small, first, bufs, send_kind):
    rows = tokens.shape[0]
    return call(
        feed_kernel, "feed", ids, [tokens, attended, cotangent, small, first, *bufs],
        [
            like(rows, D),
            like(rows, FF, kind=BF16),
            like(rows, D),
            like(rows, D, kind=BF16),
            like(FF, D, kind=BF16),
            like(PLANE * (Z - 1), SHARE, LANES),
            like(PLANE * (Z - 1), SHARE, LANES, kind=send_kind),
            like(HEAD_ROWS, LANES),
        ],
        [
            pltpu.VMEM((D, D), BF16),
            pltpu.VMEM((D, FF), BF16),
            pltpu.VMEM((rows, FF), BF16),
            pltpu.VMEM((ROW_TOTAL - ROW_OUT, LANES), F32),
        ],
        us=8,
    )


def result(middle, activated, w_down, small):
    return call(
        result_kernel, "result", None, [middle, activated, w_down, small],
        [like(*middle.shape, kind=BF16)], us=2,
    )


def attend_back(ids, project, weights, grad_attended, normed_turned, w_qkv, small, first, send_kind):
    shape = (PLANE, SIDE + SIDE_ROWS, LANES)
    return call(
        attend_back_kernel, "attend_back", ids,
        [project, weights, grad_attended, normed_turned, w_qkv, small, first],
        [like(*project.shape, kind=BF16), like(*shape), like(*shape, kind=send_kind)],
        [pltpu.VMEM((FIRST_ROWS, LANES), F32), pltpu.VMEM(shape[1:], F32)], us=4,
    )


def input_gradient(tokens, grad_project, grad_middle, w_qkv, small):
    return call(
        input_grad_kernel, "input_grad", None, [tokens, grad_project, grad_middle, w_qkv, small],
        [like(*tokens.shape)], us=2,
    )


def local_any(n, tokens, params, segment_ids, cotangent):
    total = n * params.shape[0]
    normed, normed_turned, _, allowed = prepare(tokens, params, segment_ids)
    gathered = lax.all_gather(params, "fsdp", axis=0).reshape(total, LANES)
    shares = gathered[:ROW_TOTAL].reshape(Z, 2 * PLANE, SHARE, LANES)
    order = [p * 2 + c for c in range(2) for p in range(PLANE)]
    side = jnp.concatenate(
        [jnp.zeros((SIDE - SHARE, LANES), BF16), gathered[ROW_SMALL:ROW_TOTAL]], axis=0
    )
    firsts = [jnp.concatenate([shares[0, k], side], axis=0) for k in order]
    rests = []
    for group in (order[:PLANE], order[PLANE:]):
        rests += [shares[1:, group[0]], jnp.concatenate([shares[1:, k] for k in group[1:]])]
    ids = jnp.array(order, jnp.int32)
    project, weights, attended, w_qkv, small, first = attend(ids, allowed, normed, firsts)
    middle, activated, grad_middle, grad_attended, w_down, rest, rest_send, first_grad = feed(
        ids, tokens, attended, cotangent, small, first, rests, F32
    )
    outputs = result(middle, activated, w_down, small)
    grad_project, first, first_send = attend_back(
        ids, project, weights, grad_attended, normed_turned, w_qkv, small, first_grad, F32
    )
    input_grad = input_gradient(tokens, grad_project, grad_middle, w_qkv, small)
    first = jnp.stack([first, first_send], axis=1)
    rest = jnp.stack([rest, rest_send]).reshape(2, PLANE, Z - 1, SHARE, LANES).transpose(2, 1, 0, 3, 4)
    flat = jnp.concatenate(
        [
            first[:, :, :SHARE].reshape(-1, LANES),
            rest.reshape(-1, LANES),
            jnp.zeros((total - ROW_TOTAL, LANES), F32),
        ],
        axis=0,
    )
    flat = flat.at[ROW_SMALL : ROW_SMALL + LATE_SMALL].add(
        first[PLANE - 1, 1, SIDE : SIDE + LATE_SMALL]
    )
    param_grad = lax.psum_scatter(flat, "fsdp", scatter_dimension=0, tiled=True)
    return outputs, input_grad, param_grad


def index_of(z, plane, core):
    return (z * PLANE + plane) * 2 + core


def move(values, step_z, step_plane, step_core):
    pairs = [
        (index_of(z, p, c), index_of((z + step_z) % Z, p ^ step_plane, c ^ step_core))
        for z in range(Z)
        for p in range(PLANE)
        for c in range(2)
    ]
    return lax.ppermute(values, "fsdp", pairs)


STEPS = (3, 1, 2)


def local_slice(tokens, params, segment_ids, cotangent):
    me = lax.axis_index("fsdp").astype(jnp.int32)
    z, plane, core = me // (2 * PLANE), (me // 2) % PLANE, me % 2
    where = z.reshape(1)
    ids = jnp.stack(
        [(plane ^ dp) * 2 + (core ^ dc) for dc in range(2) for dp in (0, *STEPS)]
    )

    normed, normed_turned, own, allowed = prepare(tokens, params, segment_ids)
    first, rest = call(
        sort_kernel, "sort_shares", where, [own] + [move(params, d, 0, 0) for d in range(1, Z)],
        [like(SIDE + SMALL_ROWS, LANES, kind=BF16), like(Z - 1, SHARE, LANES, kind=BF16)],
        [pltpu.VMEM((Z, SHARE, LANES), BF16), pltpu.VMEM((SIDE + SMALL_ROWS, LANES), F32)],
    )
    firsts = [first] + [move(first, 0, d, 0) for d in STEPS]
    rests = [move(rest, 0, d, 0) for d in STEPS]
    firsts = firsts + [move(item, 0, 0, 1) for item in firsts]
    project, weights, attended, w_qkv, small, first = attend(ids, allowed, normed, firsts)
    *rests, attended = lax.optimization_barrier((*rests, attended))
    rests = stack(rests)
    rests = [rest, rests, move(rest, 0, 0, 1), move(rests, 0, 0, 1)]
    middle, activated, grad_middle, grad_attended, w_down, rest, send, first_grad = feed(
        ids, tokens, attended, cotangent, small, first, rests, BF16
    )

    rest_in = move(send, 0, 0, 1)
    grad_project, first, send = attend_back(
        ids, project, weights, grad_attended, normed_turned, w_qkv, small, first_grad, BF16
    )
    first_in = move(send, 0, 0, 1)
    part = (Z, SHARE, LANES)
    kept, *sends = call(
        add_core_kernel, "add_core", None, [first, first_in, rest, rest_in],
        [like(*part)] + [like(*part, kind=BF16)] * (PLANE - 1), [pltpu.VMEM(part, F32)],
    )
    arrived = [move(item, 0, d, 0) for item, d in zip(sends, STEPS)]
    outputs = result(middle, activated, w_down, small)
    input_grad = input_gradient(tokens, grad_project, grad_middle, w_qkv, small)
    kept, *sends = call(
        add_plane_kernel, "add_plane", where, [kept] + arrived,
        [like(SHARE, LANES)] + [like(SHARE, LANES, kind=BF16)] * (Z - 1), [pltpu.VMEM(part, F32)],
    )
    arrived = [move(item, d + 1, 0, 0) for d, item in enumerate(sends)]
    param_grad = call(
        add_column_kernel, "add_column", None, [kept] + arrived, [like(SHARE, LANES)]
    )
    return outputs, input_grad, param_grad


def solution(mesh):
    n = mesh.shape["fsdp"]
    local = local_slice if n == 2 * PLANE * Z else functools.partial(local_any, n)
    in_specs = (P("fsdp", None), P("fsdp", None), P("fsdp"), P("fsdp", None))
    out_specs = (P("fsdp", None), P("fsdp", None), P("fsdp", None))
    return jax.shard_map(local, mesh=mesh, in_specs=in_specs, out_specs=out_specs, check_vma=False)
```

```python
import functools

import jax
import jax.numpy as jnp
from jax import lax
from jax.experimental import pallas as pl
from jax.experimental.pallas import tpu as pltpu
from jax.sharding import PartitionSpec as P

D = 256
HEADS = 4
HEAD_DIM = 64
FF = 1024
SEQ = 128
LANES = 128
GROUP = 4
WIDE = GROUP * SEQ
CHUNK = 256
STRIP = 64
EPSILON = 1e-05
SCALE = HEAD_DIM ** (-0.5)
VMEM_BYTES = 24 * 1024 * 1024

ROW_QKV = 0
ROW_OUT = 1536
ROW_UP = 2048
ROW_DOWN = 4096
ROW_SMALL = 6144
ROW_END = 6168
ROW_TOTAL = 6176
GAIN_ONE, SHIFT_ONE, BIAS_QUERY, BIAS_VALUE, BIAS_OUT = 0, 2, 4, 6, 8
GAIN_TWO, SHIFT_TWO, BIAS_UP, BIAS_DOWN = 10, 12, 14, 22
SMALL_ROWS = 32
LATE_SMALL = 8

SHARE = 193
Z, PLANE = 4, 4
FIRST_ROWS = 2 * PLANE * SHARE
HEAD_ROWS = FIRST_ROWS - ROW_OUT
SIDE, SIDE_ROWS = 208, 16
SMALL_IN_SHARE = ROW_SMALL - (2 * PLANE * Z - 1) * SHARE

F32 = jnp.float32
BF16 = jnp.bfloat16


def dot(left, right):
    return jnp.dot(left, right, preferred_element_type=F32)


def dot_nt(left, right):
    return lax.dot_general(left, right, (((1,), (1,)), ((), ())), preferred_element_type=F32)


def dot_tn(left, right):
    return lax.dot_general(left, right, (((0,), (0,)), ((), ())), preferred_element_type=F32)


def small_vector(small, row, count):
    return jnp.concatenate([small[row + i : row + i + 1, :] for i in range(count)], axis=1)


def fold_rows(values):
    rows, columns = values.shape
    return jnp.sum(values.reshape(rows // 8, 8, columns), axis=0)


def normalize(values):
    center = values - jnp.mean(values, axis=-1, keepdims=True)
    rate = lax.rsqrt(jnp.mean(center * center, axis=-1, keepdims=True) + EPSILON)
    return center * rate, rate


def normalize_back(grad, gain, normed, rate):
    scaled = grad * gain
    return rate * (
        scaled
        - jnp.mean(scaled, axis=-1, keepdims=True)
        - normed * jnp.mean(scaled * normed, axis=-1, keepdims=True)
    )


def head_masks():
    lane = lax.broadcasted_iota(jnp.int32, (1, D), 1)
    return [(lane // HEAD_DIM == h).astype(F32).astype(BF16) for h in range(HEADS)]


def spread_heads(rows):
    return jnp.concatenate([rows * mask for mask in head_masks()], axis=0)


def matrix_from_flat(flat, start, rows, columns, out):
    per_row = columns // LANES
    for j in range(per_row):
        out[:, j * LANES : (j + 1) * LANES] = flat[
            pl.ds(start + j, rows, stride=per_row), :
        ].astype(BF16)


def matrix_to_flat(matrix, rows, columns, flat, start):
    per_row = columns // LANES
    for j in range(per_row):
        flat[pl.ds(start + j, rows, stride=per_row), :] = matrix[:, j * LANES : (j + 1) * LANES]


def copy_kernel(params, own):
    own[...] = params[...]


def prepare_kernel(tok, seg, normed_out, normed_turned, allowed):
    normed, _ = normalize(tok[...].astype(F32))
    normed_out[...] = normed
    normed_turned[...] = normed.astype(BF16).T
    causal = lax.broadcasted_iota(jnp.int32, (SEQ, SEQ), 0) <= lax.broadcasted_iota(
        jnp.int32, (SEQ, SEQ), 1
    )
    for s in range(seg.shape[0]):
        across = jnp.broadcast_to(seg[s : s + 1, :].astype(F32), (SEQ, SEQ))
        allowed[s * SEQ : (s + 1) * SEQ, :] = (causal & (across == across.T)).astype(F32)


def sort_kernel(ids, *refs):
    received, (first, rest, stage, wide) = refs[:Z], refs[Z:]
    for d in range(Z):
        stage[lax.rem(ids[0] + Z - d, Z)] = received[d][...]
    rest[...] = stage[1:]
    wide[:SHARE, :] = stage[0].astype(F32)
    wide[SHARE:SIDE, :] = jnp.zeros((SIDE - SHARE, LANES), F32)
    last = stage[Z - 1].astype(F32)
    wide[SIDE:, :] = last[SMALL_IN_SHARE:, :]
    first[...] = wide[...].astype(BF16)


def attend_kernel(ids, allowed, normed, *refs):
    bufs = refs[: 2 * PLANE]
    project_out, weights_out, attended_out, w_qkv, small, first_out, flat = refs[2 * PLANE :]
    for slot, buf in enumerate(bufs):
        wide = buf[...].astype(F32)
        flat[pl.ds(ids[slot] * SHARE, SHARE), :] = wide[:SHARE, :]

        @pl.when(ids[slot] == 2 * PLANE - 1)
        def _():
            small[...] = wide[SIDE:, :]

    matrix_from_flat(flat, ROW_QKV, D, 3 * D, w_qkv)
    first_out[...] = flat[ROW_OUT:FIRST_ROWS, :]

    gain = small_vector(small, GAIN_ONE, 2)
    shift = small_vector(small, SHIFT_ONE, 2)
    bias = jnp.concatenate(
        [
            small_vector(small, BIAS_QUERY, 2),
            jnp.zeros((1, D), F32),
            small_vector(small, BIAS_VALUE, 2),
        ],
        axis=1,
    )
    project_out[...] = (
        dot((normed[...] * gain + shift).astype(BF16), w_qkv[...]) + bias
    ).astype(BF16)
    for g in range(normed.shape[0] // WIDE):
        starts = range(g * WIDE, (g + 1) * WIDE, SEQ)
        scores = [
            dot_nt(
                spread_heads(project_out[r : r + SEQ, D : 2 * D]),
                project_out[r : r + SEQ, :D] * SCALE,
            )
            for r in starts
        ]
        weights = []
        for r, score in zip(starts, scores):
            open_pairs = allowed[r : r + SEQ, :] > 0.5
            turned = []
            for h in range(HEADS):
                mine = jnp.where(open_pairs, score[h * SEQ : (h + 1) * SEQ, :], -1e30)
                grown = jnp.exp(mine - jnp.max(mine, axis=0, keepdims=True))
                low = (grown * (1.0 / jnp.sum(grown, axis=0, keepdims=True))).astype(BF16)
                weights_out[r : r + SEQ, h * SEQ : (h + 1) * SEQ] = low
                turned.append(low.T)
            weights.append(jnp.concatenate(turned, axis=1))
        for r, weight in zip(starts, weights):
            value = spread_heads(project_out[r : r + SEQ, 2 * D :])
            attended_out[r : r + SEQ, :] = dot(weight, value).astype(BF16)


def feed_kernel(
    ids, tok, attended, cot, small, first_in, *refs,
):
    bufs = []
    for own, others in (refs[0:2], refs[2:4]):
        bufs.append(own)
        bufs += [others.at[pl.ds(p * (Z - 1), Z - 1)] for p in range(PLANE - 1)]
    (
        middle_out, activated_out, grad_middle_out, grad_attended_out, w_down, keep_out, send_out, first_out,
        w_out, w_up, grad_hidden, flat,
    ) = refs[4:]
    flat[:HEAD_ROWS, :] = first_in[...]
    for slot, buf in enumerate(bufs):
        for z in range(1, Z):
            share = ids[slot] + z * 2 * PLANE
            flat[pl.ds(share * SHARE - ROW_OUT, SHARE), :] = buf[z - 1].astype(F32)
    matrix_from_flat(flat, 0, D, D, w_out)
    matrix_from_flat(flat, ROW_UP - ROW_OUT, D, FF, w_up)
    matrix_from_flat(flat, ROW_DOWN - ROW_OUT, FF, D, w_down)

    gain = small_vector(small, GAIN_TWO, 2)
    middle = (
        tok[...].astype(F32) + dot(attended[...], w_out[...]) + small_vector(small, BIAS_OUT, 2)
    )
    middle_out[...] = middle
    normed, rate = normalize(middle)
    normed_low = (normed * gain + small_vector(small, SHIFT_TWO, 2)).astype(BF16)
    normed_turned = normed_low.T
    cotangent = cot[...]
    slope = 0.7978845608028654
    cubic = slope * 0.044715
    row_up, row_down = ROW_UP - ROW_OUT, ROW_DOWN - ROW_OUT

    def products(c):
        columns = slice(c, c + CHUNK)
        return dot(normed_low, w_up[:, columns]), dot_nt(cotangent, w_down[columns, :])

    def bend(c, hidden_all, grad_all):
        columns = slice(c, c + CHUNK)
        bias = small_vector(small, BIAS_UP + c // LANES, CHUNK // LANES)
        total = jnp.zeros((8, CHUNK), F32)
        for r in range(0, tok.shape[0], STRIP):
            rows = slice(r, r + STRIP)
            hidden = hidden_all[rows] + bias
            square = hidden * hidden
            half = 0.5 + 0.5 * jnp.tanh(hidden * (slope + cubic * square))
            activated = hidden * half
            derivative = half + activated * (1.0 - half) * (2 * slope + (6 * cubic) * square)
            low = (grad_all[rows] * derivative).astype(BF16)
            activated_out[rows, columns] = activated.astype(BF16)
            grad_hidden[rows, columns] = low
            total += fold_rows(low.astype(F32))
        return total

    def weight_gradients(c):
        columns = slice(c, c + CHUNK)
        if (c // CHUNK) % 2:
            start, rows = c - CHUNK, 2 * CHUNK
            turned = activated_out[:, start : start + rows].T
            matrix_to_flat(dot(turned, cotangent), rows, D, flat, row_down + start * D // LANES)
        grads = dot(normed_turned, grad_hidden[:, columns])
        for j in range(CHUNK // LANES):
            flat[pl.ds(row_up + c // LANES + j, D, stride=FF // LANES), :] = grads[
                :, j * LANES : (j + 1) * LANES
            ]

    ahead, totals = products(0), []
    for c in range(0, FF, CHUNK):
        now = ahead
        if c + CHUNK < FF:
            ahead = products(c + CHUNK)
        if c > 0:
            weight_gradients(c - CHUNK)
        totals.append(bend(c, *now))
    grad_normed = dot_nt(grad_hidden[...], w_up[...])
    weight_gradients(FF - CHUNK)
    grad_result = cotangent.astype(F32)
    grad_middle = grad_result + normalize_back(grad_normed, gain, normed, rate)
    grad_middle_out[...] = grad_middle
    grad_middle_low = grad_middle.astype(BF16)
    grad_attended_out[...] = dot_nt(grad_middle_low, w_out[...]).astype(BF16)
    matrix_to_flat(dot_tn(attended[...], grad_middle_low), D, D, flat, 0)
    sums = jnp.concatenate(
        [
            fold_rows(grad_middle_low.astype(F32)),
            fold_rows(grad_normed * normed),
            fold_rows(grad_normed),
            *totals,
            fold_rows(grad_result),
        ],
        axis=1,
    )
    sums = jnp.sum(sums, axis=0, keepdims=True)
    base = ROW_SMALL - ROW_OUT
    flat[base : base + LATE_SMALL, :] = jnp.zeros((LATE_SMALL, LANES), F32)
    for i in range(sums.shape[1] // LANES):
        row = base + LATE_SMALL + i
        flat[row : row + 1, :] = sums[:, i * LANES : (i + 1) * LANES]
    flat[ROW_END - ROW_OUT :, :] = jnp.zeros((ROW_TOTAL - ROW_END, LANES), F32)
    first_out[...] = flat[:HEAD_ROWS, :]
    for target, out in enumerate((keep_out, send_out)):
        for p in range(PLANE):
            for z in range(1, Z):
                share = ids[target * PLANE + p] + z * 2 * PLANE
                rows = flat[pl.ds(share * SHARE - ROW_OUT, SHARE), :]
                out[p * (Z - 1) + z - 1] = rows.astype(out.dtype)


def result_kernel(middle, activated, w_down, small, result_out):
    result = middle[...] + dot(activated[...], w_down[...]) + small_vector(small, BIAS_DOWN, 2)
    result_out[...] = result.astype(BF16)


def attend_back_kernel(
    ids, project, weights, grad_attended, normed_turned, w_qkv, small, first_in,
    grad_project, keep_out, send_out, flat, wide,
):
    products, sums = 0.0, 0.0
    for g in range(project.shape[0] // WIDE):
        spans = [slice(r, r + SEQ) for r in range(g * WIDE, (g + 1) * WIDE, SEQ)]
        grad_weights = [
            dot_nt(spread_heads(project[span, 2 * D :]), grad_attended[span, :]) for span in spans
        ]
        scores_low, scores_turned = [], []
        for span, grads in zip(spans, grad_weights):
            low, turned = [], []
            for h in range(HEADS):
                mine = weights[span, h * SEQ : (h + 1) * SEQ].astype(F32)
                product = mine * grads[h * SEQ : (h + 1) * SEQ, :]
                grad_scores = (product - mine * jnp.sum(product, axis=0, keepdims=True)) * SCALE
                turned.append(grad_scores.astype(BF16))
                low.append(turned[-1].T)
            scores_low.append(jnp.concatenate(low, axis=1))
            scores_turned.append(jnp.concatenate(turned, axis=1))
        for s, span in enumerate(spans):
            key = spread_heads(project[span, D : 2 * D])
            grad_project[span, :D] = dot(scores_low[s], key).astype(BF16)
            query = spread_heads(project[span, :D])
            grad_project[span, D : 2 * D] = dot(scores_turned[s], query).astype(BF16)
            grad_value = dot(weights[span, :], spread_heads(grad_attended[span, :]))
            grad_project[span, 2 * D :] = grad_value.astype(BF16)
        span = slice(g * WIDE, (g + 1) * WIDE)
        products += dot(normed_turned[:, span], grad_project[span, :])
        sums += fold_rows(grad_project[span, :].astype(F32))
    sums = jnp.sum(sums, axis=0, keepdims=True)
    gain = jnp.broadcast_to(small_vector(small, GAIN_ONE, 2), (LANES, D)).T
    shift = jnp.broadcast_to(small_vector(small, SHIFT_ONE, 2), (LANES, D)).T
    grad_gain = jnp.zeros((D, LANES), F32)
    grad_shift = jnp.zeros((D, LANES), F32)
    per_row = 3 * D // LANES
    for j in range(per_row):
        columns = slice(j * LANES, (j + 1) * LANES)
        weight = w_qkv[:, columns].astype(F32)
        grad_gain += products[:, columns] * weight
        grad_shift += sums[:, columns] * weight
        flat[pl.ds(j, D, stride=per_row), :] = products[:, columns] * gain + sums[:, columns] * shift
    flat[ROW_OUT:, :] = first_in[...]
    grad_gain = jnp.sum(grad_gain.T, axis=0, keepdims=True)
    grad_shift = jnp.sum(grad_shift.T, axis=0, keepdims=True)
    late = jnp.concatenate([grad_gain, grad_shift, sums[:, :D], sums[:, 2 * D :]], axis=1)
    side = jnp.concatenate(
        [late[:, i * LANES : (i + 1) * LANES] for i in range(LATE_SMALL)]
        + [jnp.zeros((SIDE_ROWS - LATE_SMALL, LANES), F32)],
        axis=0,
    )
    wide[SHARE:SIDE, :] = jnp.zeros((SIDE - SHARE, LANES), F32)
    for target, out in enumerate((keep_out, send_out)):
        for p in range(PLANE):
            share = ids[target * PLANE + p]
            wide[:SHARE, :] = flat[pl.ds(share * SHARE, SHARE), :]
            wide[SIDE:, :] = jnp.where(share == 2 * PLANE - 1, side, 0.0)
            out[p] = wide[...].astype(out.dtype)


def input_grad_kernel(tok, grad_project, grad_middle, w_qkv, small, input_grad_out):
    gain = small_vector(small, GAIN_ONE, 2)

    def some(g, carry):
        span = pl.ds(pl.multiple_of(g * WIDE, WIDE), WIDE)
        normed, rate = normalize(tok[span, :].astype(F32))
        grad_normed = dot_nt(grad_project[span, :], w_qkv[...])
        input_grad_out[span, :] = grad_middle[span, :] + normalize_back(
            grad_normed, gain, normed, rate
        )
        return carry

    lax.fori_loop(0, tok.shape[0] // WIDE, some, 0)


def stack_kernel(*refs):
    row = 0
    for ref in refs[:-1]:
        refs[-1][row : row + ref.shape[0]] = ref[...]
        row += ref.shape[0]


def add_core_kernel(first, first_in, rest, rest_in, keep_out, *refs):
    sends, column = refs[:-1], refs[-1]
    end = SMALL_IN_SHARE + LATE_SMALL
    for p, out in enumerate((keep_out, *sends)):
        item = first[p] + first_in[p].astype(F32)
        span = slice(p * (Z - 1), (p + 1) * (Z - 1))
        column[0] = item[:SHARE, :]
        column[1:] = rest[span] + rest_in[span].astype(F32)
        column[Z - 1, SMALL_IN_SHARE:end, :] += item[SIDE : SIDE + LATE_SMALL, :]
        out[...] = column[...].astype(out.dtype)


def add_plane_kernel(ids, kept, *refs):
    arrived = refs[: PLANE - 1]
    keep_out, *sends, column = refs[PLANE - 1 :]
    column[...] = kept[...] + sum(item[...].astype(F32) for item in arrived)
    keep_out[...] = column[ids[0]]
    for d, out in enumerate(sends):
        out[...] = column[lax.rem(ids[0] + d + 1, Z)].astype(BF16)


def add_column_kernel(kept, *refs):
    refs[-1][...] = kept[...] + sum(item[...].astype(F32) for item in refs[:-1])


def like(*shape, kind=F32):
    return jax.ShapeDtypeStruct(shape, kind)


SMEM_SPEC = pl.BlockSpec(memory_space=pltpu.SMEM)
VMEM_SPEC = pl.BlockSpec(memory_space=pltpu.VMEM)

def cost(us):
    return pl.CostEstimate(flops=int(us * 1e9), bytes_accessed=1 << 20, transcendentals=0)


def call(kernel, name, ids, inputs, outs, scratch=(), us=1):
    with_ids = ids is not None
    results = pl.pallas_call(
        kernel,
        in_specs=[SMEM_SPEC] * with_ids + [VMEM_SPEC] * len(inputs),
        out_specs=[VMEM_SPEC] * len(outs),
        out_shape=list(outs),
        scratch_shapes=list(scratch),
        compiler_params=pltpu.CompilerParams(vmem_limit_bytes=VMEM_BYTES),
        cost_estimate=cost(us),
        name=name,
    )(*([ids] if with_ids else []), *inputs)
    return results if len(outs) > 1 else results[0]


def prepare(tokens, segment_ids):
    rows = tokens.shape[0]
    return call(
        prepare_kernel, "prepare", None, [tokens, segment_ids.reshape(-1, SEQ)],
        [
            like(rows, D),
            like(D, rows, kind=BF16),
            like(rows, SEQ),
        ],
        us=2,
    )


def stack(items):
    shape = (sum(item.shape[0] for item in items),) + items[0].shape[1:]
    return call(stack_kernel, "stack", None, items, [like(*shape, kind=items[0].dtype)])


def attend(ids, allowed, normed, bufs):
    rows = normed.shape[0]
    shapes = [(rows, 3 * D), (rows, HEADS * SEQ), (rows, D), (D, 3 * D)]
    return call(
        attend_kernel, "attend", ids, [allowed, normed, *bufs],
        [like(*shape, kind=BF16) for shape in shapes]
        + [like(SMALL_ROWS, LANES), like(HEAD_ROWS, LANES)],
        [pltpu.VMEM((FIRST_ROWS, LANES), F32)], us=0.2,
    )


def feed(ids, tokens, attended, cotangent, small, first, bufs, send_kind):
    rows = tokens.shape[0]
    return call(
        feed_kernel, "feed", ids, [tokens, attended, cotangent, small, first, *bufs],
        [
            like(rows, D),
            like(rows, FF, kind=BF16),
            like(rows, D),
            like(rows, D, kind=BF16),
            like(FF, D, kind=BF16),
            like(PLANE * (Z - 1), SHARE, LANES),
            like(PLANE * (Z - 1), SHARE, LANES, kind=send_kind),
            like(HEAD_ROWS, LANES),
        ],
        [
            pltpu.VMEM((D, D), BF16),
            pltpu.VMEM((D, FF), BF16),
            pltpu.VMEM((rows, FF), BF16),
            pltpu.VMEM((ROW_TOTAL - ROW_OUT, LANES), F32),
        ],
        us=8,
    )


def result(middle, activated, w_down, small):
    return call(
        result_kernel, "result", None, [middle, activated, w_down, small],
        [like(*middle.shape, kind=BF16)], us=2,
    )


def attend_back(ids, project, weights, grad_attended, normed_turned, w_qkv, small, first, send_kind):
    shape = (PLANE, SIDE + SIDE_ROWS, LANES)
    return call(
        attend_back_kernel, "attend_back", ids,
        [project, weights, grad_attended, normed_turned, w_qkv, small, first],
        [like(*project.shape, kind=BF16), like(*shape), like(*shape, kind=send_kind)],
        [pltpu.VMEM((FIRST_ROWS, LANES), F32), pltpu.VMEM(shape[1:], F32)], us=4,
    )


def input_gradient(tokens, grad_project, grad_middle, w_qkv, small):
    return call(
        input_grad_kernel, "input_grad", None, [tokens, grad_project, grad_middle, w_qkv, small],
        [like(*tokens.shape)], us=2,
    )


def local_any(n, tokens, params, segment_ids, cotangent):
    total = n * params.shape[0]
    normed, normed_turned, allowed = prepare(tokens, segment_ids)
    gathered = lax.all_gather(params, "fsdp", axis=0).reshape(total, LANES)
    shares = gathered[:ROW_TOTAL].reshape(Z, 2 * PLANE, SHARE, LANES)
    order = [p * 2 + c for c in range(2) for p in range(PLANE)]
    side = jnp.concatenate(
        [jnp.zeros((SIDE - SHARE, LANES), BF16), gathered[ROW_SMALL:ROW_TOTAL]], axis=0
    )
    firsts = [jnp.concatenate([shares[0, k], side], axis=0) for k in order]
    rests = []
    for group in (order[:PLANE], order[PLANE:]):
        rests += [shares[1:, group[0]], jnp.concatenate([shares[1:, k] for k in group[1:]])]
    ids = jnp.array(order, jnp.int32)
    project, weights, attended, w_qkv, small, first = attend(ids, allowed, normed, firsts)
    middle, activated, grad_middle, grad_attended, w_down, rest, rest_send, first_grad = feed(
        ids, tokens, attended, cotangent, small, first, rests, F32
    )
    outputs = result(middle, activated, w_down, small)
    grad_project, first, first_send = attend_back(
        ids, project, weights, grad_attended, normed_turned, w_qkv, small, first_grad, F32
    )
    input_grad = input_gradient(tokens, grad_project, grad_middle, w_qkv, small)
    first = jnp.stack([first, first_send], axis=1)
    rest = jnp.stack([rest, rest_send]).reshape(2, PLANE, Z - 1, SHARE, LANES).transpose(2, 1, 0, 3, 4)
    flat = jnp.concatenate(
        [
            first[:, :, :SHARE].reshape(-1, LANES),
            rest.reshape(-1, LANES),
            jnp.zeros((total - ROW_TOTAL, LANES), F32),
        ],
        axis=0,
    )
    flat = flat.at[ROW_SMALL : ROW_SMALL + LATE_SMALL].add(
        first[PLANE - 1, 1, SIDE : SIDE + LATE_SMALL]
    )
    param_grad = lax.psum_scatter(flat, "fsdp", scatter_dimension=0, tiled=True)
    return outputs, input_grad, param_grad


def index_of(z, plane, core):
    return (z * PLANE + plane) * 2 + core


def move(values, step_z, step_plane, step_core):
    pairs = [
        (index_of(z, p, c), index_of((z + step_z) % Z, p ^ step_plane, c ^ step_core))
        for z in range(Z)
        for p in range(PLANE)
        for c in range(2)
    ]
    return lax.ppermute(values, "fsdp", pairs)


STEPS = (3, 1, 2)


def local_slice(tokens, params, segment_ids, cotangent):
    me = lax.axis_index("fsdp").astype(jnp.int32)
    z, plane, core = me // (2 * PLANE), (me // 2) % PLANE, me % 2
    where = z.reshape(1)
    ids = jnp.stack(
        [(plane ^ dp) * 2 + (core ^ dc) for dc in range(2) for dp in (0, *STEPS)]
    )

    own = call(copy_kernel, "own", None, [params], [like(*params.shape, kind=BF16)])
    first, rest = call(
        sort_kernel, "sort_shares", where, [own] + [move(params, d, 0, 0) for d in range(1, Z)],
        [like(SIDE + SMALL_ROWS, LANES, kind=BF16), like(Z - 1, SHARE, LANES, kind=BF16)],
        [pltpu.VMEM((Z, SHARE, LANES), BF16), pltpu.VMEM((SIDE + SMALL_ROWS, LANES), F32)],
    )
    first, late_tokens, late_segments = lax.optimization_barrier((first, tokens, segment_ids))
    normed, normed_turned, allowed = prepare(late_tokens, late_segments)
    firsts = [first] + [move(first, 0, d, 0) for d in STEPS]
    rests = [move(rest, 0, d, 0) for d in STEPS]
    firsts = firsts + [move(item, 0, 0, 1) for item in firsts]
    project, weights, attended, w_qkv, small, first = attend(ids, allowed, normed, firsts)
    *rests, attended = lax.optimization_barrier((*rests, attended))
    rests = stack(rests)
    rests = [rest, rests, move(rest, 0, 0, 1), move(rests, 0, 0, 1)]
    middle, activated, grad_middle, grad_attended, w_down, rest, send, first_grad = feed(
        ids, tokens, attended, cotangent, small, first, rests, BF16
    )

    rest_in = move(send, 0, 0, 1)
    grad_project, first, send = attend_back(
        ids, project, weights, grad_attended, normed_turned, w_qkv, small, first_grad, BF16
    )
    first_in = move(send, 0, 0, 1)
    part = (Z, SHARE, LANES)
    kept, *sends = call(
        add_core_kernel, "add_core", None, [first, first_in, rest, rest_in],
        [like(*part)] + [like(*part, kind=BF16)] * (PLANE - 1), [pltpu.VMEM(part, F32)],
    )
    arrived = [move(item, 0, d, 0) for item, d in zip(sends, STEPS)]
    outputs = result(middle, activated, w_down, small)
    input_grad = input_gradient(tokens, grad_project, grad_middle, w_qkv, small)
    kept, *sends = call(
        add_plane_kernel, "add_plane", where, [kept] + arrived,
        [like(SHARE, LANES)] + [like(SHARE, LANES, kind=BF16)] * (Z - 1), [pltpu.VMEM(part, F32)],
    )
    arrived = [move(item, d + 1, 0, 0) for d, item in enumerate(sends)]
    param_grad = call(
        add_column_kernel, "add_column", None, [kept] + arrived, [like(SHARE, LANES)]
    )
    return outputs, input_grad, param_grad


def solution(mesh):
    n = mesh.shape["fsdp"]
    local = local_slice if n == 2 * PLANE * Z else functools.partial(local_any, n)
    in_specs = (P("fsdp", None), P("fsdp", None), P("fsdp"), P("fsdp", None))
    out_specs = (P("fsdp", None), P("fsdp", None), P("fsdp", None))
    return jax.shard_map(local, mesh=mesh, in_specs=in_specs, out_specs=out_specs, check_vma=False)
```

```python
import functools

import jax
import jax.numpy as jnp
from jax import lax
from jax.experimental import pallas as pl
from jax.experimental.pallas import tpu as pltpu
from jax.sharding import PartitionSpec as P

D = 256
HEADS = 4
HEAD_DIM = 64
FF = 1024
SEQ = 128
LANES = 128
GROUP = 4
WIDE = GROUP * SEQ
CHUNK = 256
STRIP = 64
EPSILON = 1e-05
SCALE = HEAD_DIM ** (-0.5)
VMEM_BYTES = 24 * 1024 * 1024

ROW_QKV = 0
ROW_OUT = 1536
ROW_UP = 2048
ROW_DOWN = 4096
ROW_SMALL = 6144
ROW_END = 6168
ROW_TOTAL = 6176
GAIN_ONE, SHIFT_ONE, BIAS_QUERY, BIAS_VALUE, BIAS_OUT = 0, 2, 4, 6, 8
GAIN_TWO, SHIFT_TWO, BIAS_UP, BIAS_DOWN = 10, 12, 14, 22
SMALL_ROWS = 32
LATE_SMALL = 8

SHARE = 193
Z, PLANE = 4, 4
FIRST_ROWS = 2 * PLANE * SHARE
HEAD_ROWS = FIRST_ROWS - ROW_OUT
SIDE, SIDE_ROWS = 208, 16
FIRST_GROUPS = ((0, 2), (2, 4))
SMALL_IN_SHARE = ROW_SMALL - (2 * PLANE * Z - 1) * SHARE

F32 = jnp.float32
BF16 = jnp.bfloat16


def dot(left, right):
    return jnp.dot(left, right, preferred_element_type=F32)


def dot_nt(left, right):
    return lax.dot_general(left, right, (((1,), (1,)), ((), ())), preferred_element_type=F32)


def dot_tn(left, right):
    return lax.dot_general(left, right, (((0,), (0,)), ((), ())), preferred_element_type=F32)


def small_vector(small, row, count):
    return jnp.concatenate([small[row + i : row + i + 1, :] for i in range(count)], axis=1)


def fold_rows(values):
    rows, columns = values.shape
    return jnp.sum(values.reshape(rows // 8, 8, columns), axis=0)


def normalize(values):
    center = values - jnp.mean(values, axis=-1, keepdims=True)
    rate = lax.rsqrt(jnp.mean(center * center, axis=-1, keepdims=True) + EPSILON)
    return center * rate, rate


def normalize_back(grad, gain, normed, rate):
    scaled = grad * gain
    return rate * (
        scaled
        - jnp.mean(scaled, axis=-1, keepdims=True)
        - normed * jnp.mean(scaled * normed, axis=-1, keepdims=True)
    )


def head_masks():
    lane = lax.broadcasted_iota(jnp.int32, (1, D), 1)
    return [(lane // HEAD_DIM == h).astype(F32).astype(BF16) for h in range(HEADS)]


def spread_heads(rows):
    return jnp.concatenate([rows * mask for mask in head_masks()], axis=0)


def matrix_from_flat(flat, start, rows, columns, out):
    per_row = columns // LANES
    for j in range(per_row):
        out[:, j * LANES : (j + 1) * LANES] = flat[
            pl.ds(start + j, rows, stride=per_row), :
        ].astype(BF16)


def matrix_to_flat(matrix, rows, columns, flat, start):
    per_row = columns // LANES
    for j in range(per_row):
        flat[pl.ds(start + j, rows, stride=per_row), :] = matrix[:, j * LANES : (j + 1) * LANES]


def prepare_kernel(tok, params, seg, normed_out, normed_turned, own, allowed):
    normed, _ = normalize(tok[...].astype(F32))
    normed_out[...] = normed
    normed_turned[...] = normed.astype(BF16).T
    own[...] = params[...]
    causal = lax.broadcasted_iota(jnp.int32, (SEQ, SEQ), 0) <= lax.broadcasted_iota(
        jnp.int32, (SEQ, SEQ), 1
    )
    for s in range(seg.shape[0]):
        across = jnp.broadcast_to(seg[s : s + 1, :].astype(F32), (SEQ, SEQ))
        allowed[s * SEQ : (s + 1) * SEQ, :] = (causal & (across == across.T)).astype(F32)


def sort_kernel(ids, *refs):
    received, (first, rest, stage, wide) = refs[:Z], refs[Z:]
    for d in range(Z):
        stage[lax.rem(ids[0] + Z - d, Z)] = received[d][...]
    rest[...] = stage[1:]
    wide[:SHARE, :] = stage[0].astype(F32)
    wide[SHARE:SIDE, :] = jnp.zeros((SIDE - SHARE, LANES), F32)
    last = stage[Z - 1].astype(F32)
    wide[SIDE:, :] = last[SMALL_IN_SHARE:, :]
    first[0] = wide[...].astype(BF16)


def attend_kernel(ids, allowed, normed, *refs):
    bufs = [ref.at[i] for ref in refs[:4] for i in range(ref.shape[0])]
    project_out, weights_out, attended_out, w_qkv, small, first_out, flat = refs[4:]
    for slot, buf in enumerate(bufs):
        wide = buf[...].astype(F32)
        flat[pl.ds(ids[slot] * SHARE, SHARE), :] = wide[:SHARE, :]

        @pl.when(ids[slot] == 2 * PLANE - 1)
        def _():
            small[...] = wide[SIDE:, :]

    matrix_from_flat(flat, ROW_QKV, D, 3 * D, w_qkv)
    first_out[...] = flat[ROW_OUT:FIRST_ROWS, :]

    gain = small_vector(small, GAIN_ONE, 2)
    shift = small_vector(small, SHIFT_ONE, 2)
    bias = jnp.concatenate(
        [
            small_vector(small, BIAS_QUERY, 2),
            jnp.zeros((1, D), F32),
            small_vector(small, BIAS_VALUE, 2),
        ],
        axis=1,
    )
    project_out[...] = (
        dot((normed[...] * gain + shift).astype(BF16), w_qkv[...]) + bias
    ).astype(BF16)
    for g in range(normed.shape[0] // WIDE):
        starts = range(g * WIDE, (g + 1) * WIDE, SEQ)
        scores = [
            dot_nt(
                spread_heads(project_out[r : r + SEQ, D : 2 * D]),
                project_out[r : r + SEQ, :D] * SCALE,
            )
            for r in starts
        ]
        weights = []
        for r, score in zip(starts, scores):
            open_pairs = allowed[r : r + SEQ, :] > 0.5
            turned = []
            for h in range(HEADS):
                mine = jnp.where(open_pairs, score[h * SEQ : (h + 1) * SEQ, :], -1e30)
                grown = jnp.exp(mine - jnp.max(mine, axis=0, keepdims=True))
                low = (grown * (1.0 / jnp.sum(grown, axis=0, keepdims=True))).astype(BF16)
                weights_out[r : r + SEQ, h * SEQ : (h + 1) * SEQ] = low
                turned.append(low.T)
            weights.append(jnp.concatenate(turned, axis=1))
        for r, weight in zip(starts, weights):
            value = spread_heads(project_out[r : r + SEQ, 2 * D :])
            attended_out[r : r + SEQ, :] = dot(weight, value).astype(BF16)


def feed_kernel(
    ids, tok, attended, cot, small, first_in, *refs,
):
    bufs = []
    for own, others in (refs[0:2], refs[2:4]):
        bufs.append(own)
        bufs += [others.at[pl.ds(p * (Z - 1), Z - 1)] for p in range(PLANE - 1)]
    (
        middle_out, activated_out, grad_middle_out, grad_attended_out, w_down, keep_out, send_out, first_out,
        w_out, w_up, grad_hidden, flat,
    ) = refs[4:]
    flat[:HEAD_ROWS, :] = first_in[...]
    for slot, buf in enumerate(bufs):
        for z in range(1, Z):
            share = ids[slot] + z * 2 * PLANE
            flat[pl.ds(share * SHARE - ROW_OUT, SHARE), :] = buf[z - 1].astype(F32)
    matrix_from_flat(flat, 0, D, D, w_out)
    matrix_from_flat(flat, ROW_UP - ROW_OUT, D, FF, w_up)
    matrix_from_flat(flat, ROW_DOWN - ROW_OUT, FF, D, w_down)

    gain = small_vector(small, GAIN_TWO, 2)
    middle = (
        tok[...].astype(F32) + dot(attended[...], w_out[...]) + small_vector(small, BIAS_OUT, 2)
    )
    middle_out[...] = middle
    normed, rate = normalize(middle)
    normed_low = (normed * gain + small_vector(small, SHIFT_TWO, 2)).astype(BF16)
    normed_turned = normed_low.T
    cotangent = cot[...]
    slope = 0.7978845608028654
    cubic = slope * 0.044715
    row_up, row_down = ROW_UP - ROW_OUT, ROW_DOWN - ROW_OUT

    def products(c):
        columns = slice(c, c + CHUNK)
        return dot(normed_low, w_up[:, columns]), dot_nt(cotangent, w_down[columns, :])

    def bend(c, hidden_all, grad_all):
        columns = slice(c, c + CHUNK)
        bias = small_vector(small, BIAS_UP + c // LANES, CHUNK // LANES)
        total = jnp.zeros((8, CHUNK), F32)
        for r in range(0, tok.shape[0], STRIP):
            rows = slice(r, r + STRIP)
            hidden = hidden_all[rows] + bias
            square = hidden * hidden
            half = 0.5 + 0.5 * jnp.tanh(hidden * (slope + cubic * square))
            activated = hidden * half
            derivative = half + activated * (1.0 - half) * (2 * slope + (6 * cubic) * square)
            low = (grad_all[rows] * derivative).astype(BF16)
            activated_out[rows, columns] = activated.astype(BF16)
            grad_hidden[rows, columns] = low
            total += fold_rows(low.astype(F32))
        return total

    def weight_gradients(c):
        columns = slice(c, c + CHUNK)
        if (c // CHUNK) % 2:
            start, rows = c - CHUNK, 2 * CHUNK
            turned = activated_out[:, start : start + rows].T
            matrix_to_flat(dot(turned, cotangent), rows, D, flat, row_down + start * D // LANES)
        grads = dot(normed_turned, grad_hidden[:, columns])
        for j in range(CHUNK // LANES):
            flat[pl.ds(row_up + c // LANES + j, D, stride=FF // LANES), :] = grads[
                :, j * LANES : (j + 1) * LANES
            ]

    ahead, totals = products(0), []
    for c in range(0, FF, CHUNK):
        now = ahead
        if c + CHUNK < FF:
            ahead = products(c + CHUNK)
        if c > 0:
            weight_gradients(c - CHUNK)
        totals.append(bend(c, *now))
    grad_normed = dot_nt(grad_hidden[...], w_up[...])
    weight_gradients(FF - CHUNK)
    grad_result = cotangent.astype(F32)
    grad_middle = grad_result + normalize_back(grad_normed, gain, normed, rate)
    grad_middle_out[...] = grad_middle
    grad_middle_low = grad_middle.astype(BF16)
    grad_attended_out[...] = dot_nt(grad_middle_low, w_out[...]).astype(BF16)
    matrix_to_flat(dot_tn(attended[...], grad_middle_low), D, D, flat, 0)
    sums = jnp.concatenate(
        [
            fold_rows(grad_middle_low.astype(F32)),
            fold_rows(grad_normed * normed),
            fold_rows(grad_normed),
            *totals,
            fold_rows(grad_result),
        ],
        axis=1,
    )
    sums = jnp.sum(sums, axis=0, keepdims=True)
    base = ROW_SMALL - ROW_OUT
    flat[base : base + LATE_SMALL, :] = jnp.zeros((LATE_SMALL, LANES), F32)
    for i in range(sums.shape[1] // LANES):
        row = base + LATE_SMALL + i
        flat[row : row + 1, :] = sums[:, i * LANES : (i + 1) * LANES]
    flat[ROW_END - ROW_OUT :, :] = jnp.zeros((ROW_TOTAL - ROW_END, LANES), F32)
    first_out[...] = flat[:HEAD_ROWS, :]
    for target, out in enumerate((keep_out, send_out)):
        for p in range(PLANE):
            for z in range(1, Z):
                share = ids[target * PLANE + p] + z * 2 * PLANE
                rows = flat[pl.ds(share * SHARE - ROW_OUT, SHARE), :]
                out[p * (Z - 1) + z - 1] = rows.astype(out.dtype)


def result_kernel(middle, activated, w_down, small, result_out):
    result = middle[...] + dot(activated[...], w_down[...]) + small_vector(small, BIAS_DOWN, 2)
    result_out[...] = result.astype(BF16)


def attend_back_kernel(
    ids, project, weights, grad_attended, normed_turned, w_qkv, small, first_in,
    grad_project, keep_out, send_out, flat, wide,
):
    products, sums = 0.0, 0.0
    for g in range(project.shape[0] // WIDE):
        spans = [slice(r, r + SEQ) for r in range(g * WIDE, (g + 1) * WIDE, SEQ)]
        grad_weights = [
            dot_nt(spread_heads(project[span, 2 * D :]), grad_attended[span, :]) for span in spans
        ]
        scores_low, scores_turned = [], []
        for span, grads in zip(spans, grad_weights):
            low, turned = [], []
            for h in range(HEADS):
                mine = weights[span, h * SEQ : (h + 1) * SEQ].astype(F32)
                product = mine * grads[h * SEQ : (h + 1) * SEQ, :]
                grad_scores = (product - mine * jnp.sum(product, axis=0, keepdims=True)) * SCALE
                turned.append(grad_scores.astype(BF16))
                low.append(turned[-1].T)
            scores_low.append(jnp.concatenate(low, axis=1))
            scores_turned.append(jnp.concatenate(turned, axis=1))
        for s, span in enumerate(spans):
            key = spread_heads(project[span, D : 2 * D])
            grad_project[span, :D] = dot(scores_low[s], key).astype(BF16)
            query = spread_heads(project[span, :D])
            grad_project[span, D : 2 * D] = dot(scores_turned[s], query).astype(BF16)
            grad_value = dot(weights[span, :], spread_heads(grad_attended[span, :]))
            grad_project[span, 2 * D :] = grad_value.astype(BF16)
        span = slice(g * WIDE, (g + 1) * WIDE)
        products += dot(normed_turned[:, span], grad_project[span, :])
        sums += fold_rows(grad_project[span, :].astype(F32))
    sums = jnp.sum(sums, axis=0, keepdims=True)
    gain = jnp.broadcast_to(small_vector(small, GAIN_ONE, 2), (LANES, D)).T
    shift = jnp.broadcast_to(small_vector(small, SHIFT_ONE, 2), (LANES, D)).T
    grad_gain = jnp.zeros((D, LANES), F32)
    grad_shift = jnp.zeros((D, LANES), F32)
    per_row = 3 * D // LANES
    for j in range(per_row):
        columns = slice(j * LANES, (j + 1) * LANES)
        weight = w_qkv[:, columns].astype(F32)
        grad_gain += products[:, columns] * weight
        grad_shift += sums[:, columns] * weight
        flat[pl.ds(j, D, stride=per_row), :] = products[:, columns] * gain + sums[:, columns] * shift
    flat[ROW_OUT:, :] = first_in[...]
    grad_gain = jnp.sum(grad_gain.T, axis=0, keepdims=True)
    grad_shift = jnp.sum(grad_shift.T, axis=0, keepdims=True)
    late = jnp.concatenate([grad_gain, grad_shift, sums[:, :D], sums[:, 2 * D :]], axis=1)
    side = jnp.concatenate(
        [late[:, i * LANES : (i + 1) * LANES] for i in range(LATE_SMALL)]
        + [jnp.zeros((SIDE_ROWS - LATE_SMALL, LANES), F32)],
        axis=0,
    )
    wide[SHARE:SIDE, :] = jnp.zeros((SIDE - SHARE, LANES), F32)
    for target, out in enumerate((keep_out, send_out)):
        for p in range(PLANE):
            share = ids[target * PLANE + p]
            wide[:SHARE, :] = flat[pl.ds(share * SHARE, SHARE), :]
            wide[SIDE:, :] = jnp.where(share == 2 * PLANE - 1, side, 0.0)
            out[p] = wide[...].astype(out.dtype)


def input_grad_kernel(tok, grad_project, grad_middle, w_qkv, small, input_grad_out):
    gain = small_vector(small, GAIN_ONE, 2)

    def some(g, carry):
        span = pl.ds(pl.multiple_of(g * WIDE, WIDE), WIDE)
        normed, rate = normalize(tok[span, :].astype(F32))
        grad_normed = dot_nt(grad_project[span, :], w_qkv[...])
        input_grad_out[span, :] = grad_middle[span, :] + normalize_back(
            grad_normed, gain, normed, rate
        )
        return carry

    lax.fori_loop(0, tok.shape[0] // WIDE, some, 0)


def stack_kernel(*refs):
    row = 0
    for ref in refs[:-1]:
        refs[-1][row : row + ref.shape[0]] = ref[...]
        row += ref.shape[0]


def add_core_kernel(first, first_in, rest, rest_in, keep_out, *refs):
    sends, column = refs[:-1], refs[-1]
    end = SMALL_IN_SHARE + LATE_SMALL
    for p, out in enumerate((keep_out, *sends)):
        item = first[p] + first_in[p].astype(F32)
        span = slice(p * (Z - 1), (p + 1) * (Z - 1))
        column[0] = item[:SHARE, :]
        column[1:] = rest[span] + rest_in[span].astype(F32)
        column[Z - 1, SMALL_IN_SHARE:end, :] += item[SIDE : SIDE + LATE_SMALL, :]
        out[...] = column[...].astype(out.dtype)


def add_plane_kernel(ids, kept, *refs):
    arrived = refs[: PLANE - 1]
    keep_out, *sends, column = refs[PLANE - 1 :]
    column[...] = kept[...] + sum(item[...].astype(F32) for item in arrived)
    keep_out[...] = column[ids[0]]
    for d, out in enumerate(sends):
        out[...] = column[lax.rem(ids[0] + d + 1, Z)].astype(BF16)


def add_column_kernel(kept, *refs):
    refs[-1][...] = kept[...] + sum(item[...].astype(F32) for item in refs[:-1])


def like(*shape, kind=F32):
    return jax.ShapeDtypeStruct(shape, kind)


SMEM_SPEC = pl.BlockSpec(memory_space=pltpu.SMEM)
VMEM_SPEC = pl.BlockSpec(memory_space=pltpu.VMEM)

def cost(us):
    return pl.CostEstimate(flops=int(us * 1e9), bytes_accessed=1 << 20, transcendentals=0)


def call(kernel, name, ids, inputs, outs, scratch=(), us=1):
    with_ids = ids is not None
    results = pl.pallas_call(
        kernel,
        in_specs=[SMEM_SPEC] * with_ids + [VMEM_SPEC] * len(inputs),
        out_specs=[VMEM_SPEC] * len(outs),
        out_shape=list(outs),
        scratch_shapes=list(scratch),
        compiler_params=pltpu.CompilerParams(vmem_limit_bytes=VMEM_BYTES),
        cost_estimate=cost(us),
        name=name,
    )(*([ids] if with_ids else []), *inputs)
    return results if len(outs) > 1 else results[0]


def prepare(tokens, params, segment_ids):
    rows = tokens.shape[0]
    return call(
        prepare_kernel, "prepare", None, [tokens, params, segment_ids.reshape(-1, SEQ)],
        [
            like(rows, D),
            like(D, rows, kind=BF16),
            like(*params.shape, kind=BF16),
            like(rows, SEQ),
        ],
        us=2,
    )


def stack(items):
    shape = (sum(item.shape[0] for item in items),) + items[0].shape[1:]
    return call(stack_kernel, "stack", None, items, [like(*shape, kind=items[0].dtype)], us=0.01)


def attend(ids, allowed, normed, bufs):
    rows = normed.shape[0]
    shapes = [(rows, 3 * D), (rows, HEADS * SEQ), (rows, D), (D, 3 * D)]
    return call(
        attend_kernel, "attend", ids, [allowed, normed, *bufs],
        [like(*shape, kind=BF16) for shape in shapes]
        + [like(SMALL_ROWS, LANES), like(HEAD_ROWS, LANES)],
        [pltpu.VMEM((FIRST_ROWS, LANES), F32)], us=0.01,
    )


def feed(ids, tokens, attended, cotangent, small, first, bufs, send_kind):
    rows = tokens.shape[0]
    return call(
        feed_kernel, "feed", ids, [tokens, attended, cotangent, small, first, *bufs],
        [
            like(rows, D),
            like(rows, FF, kind=BF16),
            like(rows, D),
            like(rows, D, kind=BF16),
            like(FF, D, kind=BF16),
            like(PLANE * (Z - 1), SHARE, LANES),
            like(PLANE * (Z - 1), SHARE, LANES, kind=send_kind),
            like(HEAD_ROWS, LANES),
        ],
        [
            pltpu.VMEM((D, D), BF16),
            pltpu.VMEM((D, FF), BF16),
            pltpu.VMEM((rows, FF), BF16),
            pltpu.VMEM((ROW_TOTAL - ROW_OUT, LANES), F32),
        ],
        us=8,
    )


def result(middle, activated, w_down, small):
    return call(
        result_kernel, "result", None, [middle, activated, w_down, small],
        [like(*middle.shape, kind=BF16)], us=2,
    )


def attend_back(ids, project, weights, grad_attended, normed_turned, w_qkv, small, first, send_kind):
    shape = (PLANE, SIDE + SIDE_ROWS, LANES)
    return call(
        attend_back_kernel, "attend_back", ids,
        [project, weights, grad_attended, normed_turned, w_qkv, small, first],
        [like(*project.shape, kind=BF16), like(*shape), like(*shape, kind=send_kind)],
        [pltpu.VMEM((FIRST_ROWS, LANES), F32), pltpu.VMEM(shape[1:], F32)], us=4,
    )


def input_gradient(tokens, grad_project, grad_middle, w_qkv, small):
    return call(
        input_grad_kernel, "input_grad", None, [tokens, grad_project, grad_middle, w_qkv, small],
        [like(*tokens.shape)], us=2,
    )


def local_any(n, tokens, params, segment_ids, cotangent):
    total = n * params.shape[0]
    normed, normed_turned, _, allowed = prepare(tokens, params, segment_ids)
    gathered = lax.all_gather(params, "fsdp", axis=0).reshape(total, LANES)
    shares = gathered[:ROW_TOTAL].reshape(Z, 2 * PLANE, SHARE, LANES)
    order = [p * 2 + c for c in range(2) for p in range(PLANE)]
    side = jnp.concatenate(
        [jnp.zeros((SIDE - SHARE, LANES), BF16), gathered[ROW_SMALL:ROW_TOTAL]], axis=0
    )
    firsts = [jnp.concatenate([shares[0, k], side], axis=0)[None] for k in order]
    firsts = [
        jnp.concatenate(firsts[c + i : c + j]) for c in (0, PLANE) for i, j in FIRST_GROUPS
    ]
    rests = []
    for group in (order[:PLANE], order[PLANE:]):
        rests += [shares[1:, group[0]], jnp.concatenate([shares[1:, k] for k in group[1:]])]
    ids = jnp.array(order, jnp.int32)
    project, weights, attended, w_qkv, small, first = attend(ids, allowed, normed, firsts)
    middle, activated, grad_middle, grad_attended, w_down, rest, rest_send, first_grad = feed(
        ids, tokens, attended, cotangent, small, first, rests, F32
    )
    outputs = result(middle, activated, w_down, small)
    grad_project, first, first_send = attend_back(
        ids, project, weights, grad_attended, normed_turned, w_qkv, small, first_grad, F32
    )
    input_grad = input_gradient(tokens, grad_project, grad_middle, w_qkv, small)
    first = jnp.stack([first, first_send], axis=1)
    rest = jnp.stack([rest, rest_send]).reshape(2, PLANE, Z - 1, SHARE, LANES).transpose(2, 1, 0, 3, 4)
    flat = jnp.concatenate(
        [
            first[:, :, :SHARE].reshape(-1, LANES),
            rest.reshape(-1, LANES),
            jnp.zeros((total - ROW_TOTAL, LANES), F32),
        ],
        axis=0,
    )
    flat = flat.at[ROW_SMALL : ROW_SMALL + LATE_SMALL].add(
        first[PLANE - 1, 1, SIDE : SIDE + LATE_SMALL]
    )
    param_grad = lax.psum_scatter(flat, "fsdp", scatter_dimension=0, tiled=True)
    return outputs, input_grad, param_grad


def index_of(z, plane, core):
    return (z * PLANE + plane) * 2 + core


def move(values, step_z, step_plane, step_core):
    pairs = [
        (index_of(z, p, c), index_of((z + step_z) % Z, p ^ step_plane, c ^ step_core))
        for z in range(Z)
        for p in range(PLANE)
        for c in range(2)
    ]
    return lax.ppermute(values, "fsdp", pairs)


STEPS = (3, 1, 2)


def local_slice(tokens, params, segment_ids, cotangent):
    me = lax.axis_index("fsdp").astype(jnp.int32)
    z, plane, core = me // (2 * PLANE), (me // 2) % PLANE, me % 2
    where = z.reshape(1)
    ids = jnp.stack(
        [(plane ^ dp) * 2 + (core ^ dc) for dc in range(2) for dp in (0, *STEPS)]
    )

    normed, normed_turned, own, allowed = prepare(tokens, params, segment_ids)
    first, rest = call(
        sort_kernel, "sort_shares", where, [own] + [move(params, d, 0, 0) for d in range(1, Z)],
        [like(1, SIDE + SMALL_ROWS, LANES, kind=BF16), like(Z - 1, SHARE, LANES, kind=BF16)],
        [pltpu.VMEM((Z, SHARE, LANES), BF16), pltpu.VMEM((SIDE + SMALL_ROWS, LANES), F32)],
    )
    firsts = [first] + [move(first, 0, d, 0) for d in STEPS]
    rests = [move(rest, 0, d, 0) for d in STEPS]
    firsts = [stack(firsts[i:j]) if j > i + 1 else firsts[i] for i, j in FIRST_GROUPS]
    firsts = firsts + [move(item, 0, 0, 1) for item in firsts]
    project, weights, attended, w_qkv, small, first = attend(ids, allowed, normed, firsts)
    *rests, attended = lax.optimization_barrier((*rests, attended))
    rests = stack(rests)
    rests = [rest, rests, move(rest, 0, 0, 1), move(rests, 0, 0, 1)]
    middle, activated, grad_middle, grad_attended, w_down, rest, send, first_grad = feed(
        ids, tokens, attended, cotangent, small, first, rests, BF16
    )

    rest_in = move(send, 0, 0, 1)
    grad_project, first, send = attend_back(
        ids, project, weights, grad_attended, normed_turned, w_qkv, small, first_grad, BF16
    )
    first_in = move(send, 0, 0, 1)
    part = (Z, SHARE, LANES)
    kept, *sends = call(
        add_core_kernel, "add_core", None, [first, first_in, rest, rest_in],
        [like(*part)] + [like(*part, kind=BF16)] * (PLANE - 1), [pltpu.VMEM(part, F32)],
    )
    arrived = [move(item, 0, d, 0) for item, d in zip(sends, STEPS)]
    outputs = result(middle, activated, w_down, small)
    input_grad = input_gradient(tokens, grad_project, grad_middle, w_qkv, small)
    kept, *sends = call(
        add_plane_kernel, "add_plane", where, [kept] + arrived,
        [like(SHARE, LANES)] + [like(SHARE, LANES, kind=BF16)] * (Z - 1), [pltpu.VMEM(part, F32)],
    )
    arrived = [move(item, d + 1, 0, 0) for d, item in enumerate(sends)]
    param_grad = call(
        add_column_kernel, "add_column", None, [kept] + arrived, [like(SHARE, LANES)]
    )
    return outputs, input_grad, param_grad


def solution(mesh):
    n = mesh.shape["fsdp"]
    local = local_slice if n == 2 * PLANE * Z else functools.partial(local_any, n)
    in_specs = (P("fsdp", None), P("fsdp", None), P("fsdp"), P("fsdp", None))
    out_specs = (P("fsdp", None), P("fsdp", None), P("fsdp", None))
    return jax.shard_map(local, mesh=mesh, in_specs=in_specs, out_specs=out_specs, check_vma=False)
```

```python
import functools

import jax
import jax.numpy as jnp
from jax import lax
from jax.experimental import pallas as pl
from jax.experimental.pallas import tpu as pltpu
from jax.sharding import PartitionSpec as P

D = 256
HEADS = 4
HEAD_DIM = 64
FF = 1024
SEQ = 128
LANES = 128
GROUP = 4
WIDE = GROUP * SEQ
CHUNK = 256
STRIP = 64
EPSILON = 1e-05
SCALE = HEAD_DIM ** (-0.5)
VMEM_BYTES = 24 * 1024 * 1024

ROW_QKV = 0
ROW_OUT = 1536
ROW_UP = 2048
ROW_DOWN = 4096
ROW_SMALL = 6144
ROW_END = 6168
ROW_TOTAL = 6176
GAIN_ONE, SHIFT_ONE, BIAS_QUERY, BIAS_VALUE, BIAS_OUT = 0, 2, 4, 6, 8
GAIN_TWO, SHIFT_TWO, BIAS_UP, BIAS_DOWN = 10, 12, 14, 22
SMALL_ROWS = 32
LATE_SMALL = 8

SHARE = 193
Z, PLANE = 4, 4
FIRST_ROWS = 2 * PLANE * SHARE
HEAD_ROWS = FIRST_ROWS - ROW_OUT
SIDE, SIDE_ROWS = 208, 16
FIRST_GROUPS = ((0, 2), (2, 4))
SMALL_IN_SHARE = ROW_SMALL - (2 * PLANE * Z - 1) * SHARE

F32 = jnp.float32
BF16 = jnp.bfloat16


def dot(left, right):
    return jnp.dot(left, right, preferred_element_type=F32)


def dot_nt(left, right):
    return lax.dot_general(left, right, (((1,), (1,)), ((), ())), preferred_element_type=F32)


def dot_tn(left, right):
    return lax.dot_general(left, right, (((0,), (0,)), ((), ())), preferred_element_type=F32)


def small_vector(small, row, count):
    return jnp.concatenate([small[row + i : row + i + 1, :] for i in range(count)], axis=1)


def fold_rows(values):
    rows, columns = values.shape
    return jnp.sum(values.reshape(rows // 8, 8, columns), axis=0)


def normalize(values):
    center = values - jnp.mean(values, axis=-1, keepdims=True)
    rate = lax.rsqrt(jnp.mean(center * center, axis=-1, keepdims=True) + EPSILON)
    return center * rate, rate


def normalize_back(grad, gain, normed, rate):
    scaled = grad * gain
    return rate * (
        scaled
        - jnp.mean(scaled, axis=-1, keepdims=True)
        - normed * jnp.mean(scaled * normed, axis=-1, keepdims=True)
    )


def head_masks():
    lane = lax.broadcasted_iota(jnp.int32, (1, D), 1)
    return [(lane // HEAD_DIM == h).astype(F32).astype(BF16) for h in range(HEADS)]


def spread_heads(rows):
    return jnp.concatenate([rows * mask for mask in head_masks()], axis=0)


def matrix_from_flat(flat, start, rows, columns, out):
    per_row = columns // LANES
    for j in range(per_row):
        out[:, j * LANES : (j + 1) * LANES] = flat[
            pl.ds(start + j, rows, stride=per_row), :
        ].astype(BF16)


def matrix_to_flat(matrix, rows, columns, flat, start):
    per_row = columns // LANES
    for j in range(per_row):
        flat[pl.ds(start + j, rows, stride=per_row), :] = matrix[:, j * LANES : (j + 1) * LANES]


def prepare_kernel(tok, params, seg, normed_out, normed_turned, own, allowed):
    normed, _ = normalize(tok[...].astype(F32))
    normed_out[...] = normed
    normed_turned[...] = normed.astype(BF16).T
    own[...] = params[...]
    causal = lax.broadcasted_iota(jnp.int32, (SEQ, SEQ), 0) <= lax.broadcasted_iota(
        jnp.int32, (SEQ, SEQ), 1
    )
    for s in range(seg.shape[0]):
        across = jnp.broadcast_to(seg[s : s + 1, :].astype(F32), (SEQ, SEQ))
        allowed[s * SEQ : (s + 1) * SEQ, :] = (causal & (across == across.T)).astype(F32)


def sort_kernel(ids, *refs):
    received, (first, rest, stage, wide) = refs[:Z], refs[Z:]
    for d in range(Z):
        stage[lax.rem(ids[0] + Z - d, Z)] = received[d][...]
    rest[...] = stage[1:]
    wide[:SHARE, :] = stage[0].astype(F32)
    wide[SHARE:SIDE, :] = jnp.zeros((SIDE - SHARE, LANES), F32)
    last = stage[Z - 1].astype(F32)
    wide[SIDE:, :] = last[SMALL_IN_SHARE:, :]
    first[0] = wide[...].astype(BF16)


def attend_kernel(ids, allowed, normed, *refs):
    bufs = [ref.at[i] for ref in refs[:4] for i in range(ref.shape[0])]
    project_out, weights_out, attended_out, w_qkv, small, first_out, flat = refs[4:]
    for slot, buf in enumerate(bufs):
        wide = buf[...].astype(F32)
        flat[pl.ds(ids[slot] * SHARE, SHARE), :] = wide[:SHARE, :]

        @pl.when(ids[slot] == 2 * PLANE - 1)
        def _():
            small[...] = wide[SIDE:, :]

    matrix_from_flat(flat, ROW_QKV, D, 3 * D, w_qkv)
    first_out[...] = flat[ROW_OUT:FIRST_ROWS, :]

    gain = small_vector(small, GAIN_ONE, 2)
    shift = small_vector(small, SHIFT_ONE, 2)
    bias = jnp.concatenate(
        [
            small_vector(small, BIAS_QUERY, 2),
            jnp.zeros((1, D), F32),
            small_vector(small, BIAS_VALUE, 2),
        ],
        axis=1,
    )
    project_out[...] = (
        dot((normed[...] * gain + shift).astype(BF16), w_qkv[...]) + bias
    ).astype(BF16)
    for g in range(normed.shape[0] // WIDE):
        starts = range(g * WIDE, (g + 1) * WIDE, SEQ)
        scores = [
            dot_nt(
                spread_heads(project_out[r : r + SEQ, D : 2 * D]),
                project_out[r : r + SEQ, :D] * SCALE,
            )
            for r in starts
        ]
        weights = []
        for r, score in zip(starts, scores):
            open_pairs = allowed[r : r + SEQ, :] > 0.5
            turned = []
            for h in range(HEADS):
                mine = jnp.where(open_pairs, score[h * SEQ : (h + 1) * SEQ, :], -1e30)
                grown = jnp.exp(mine - jnp.max(mine, axis=0, keepdims=True))
                low = (grown * (1.0 / jnp.sum(grown, axis=0, keepdims=True))).astype(BF16)
                weights_out[r : r + SEQ, h * SEQ : (h + 1) * SEQ] = low
                turned.append(low.T)
            weights.append(jnp.concatenate(turned, axis=1))
        for r, weight in zip(starts, weights):
            value = spread_heads(project_out[r : r + SEQ, 2 * D :])
            attended_out[r : r + SEQ, :] = dot(weight, value).astype(BF16)


def feed_kernel(
    ids, tok, attended, cot, small, first_in, *refs,
):
    bufs = []
    for own, others in (refs[0:2], refs[2:4]):
        bufs.append(own)
        bufs += [others.at[pl.ds(p * (Z - 1), Z - 1)] for p in range(PLANE - 1)]
    (
        middle_out, activated_out, grad_middle_out, grad_attended_out, w_down, keep_out, send_out, first_out,
        w_out, w_up, grad_hidden, flat,
    ) = refs[4:]
    flat[:HEAD_ROWS, :] = first_in[...]
    for slot, buf in enumerate(bufs):
        for z in range(1, Z):
            share = ids[slot] + z * 2 * PLANE
            flat[pl.ds(share * SHARE - ROW_OUT, SHARE), :] = buf[z - 1].astype(F32)
    matrix_from_flat(flat, 0, D, D, w_out)

    gain = small_vector(small, GAIN_TWO, 2)
    middle = (
        tok[...].astype(F32) + dot(attended[...], w_out[...]) + small_vector(small, BIAS_OUT, 2)
    )
    middle_out[...] = middle
    normed, rate = normalize(middle)
    normed_low = (normed * gain + small_vector(small, SHIFT_TWO, 2)).astype(BF16)
    matrix_from_flat(flat, ROW_UP - ROW_OUT, D, FF, w_up)
    matrix_from_flat(flat, ROW_DOWN - ROW_OUT, FF, D, w_down)
    normed_turned = normed_low.T
    cotangent = cot[...]
    slope = 0.7978845608028654
    cubic = slope * 0.044715
    row_up, row_down = ROW_UP - ROW_OUT, ROW_DOWN - ROW_OUT

    def products(c):
        columns = slice(c, c + CHUNK)
        return dot(normed_low, w_up[:, columns]), dot_nt(cotangent, w_down[columns, :])

    def bend(c, hidden_all, grad_all):
        columns = slice(c, c + CHUNK)
        bias = small_vector(small, BIAS_UP + c // LANES, CHUNK // LANES)
        total = jnp.zeros((8, CHUNK), F32)
        for r in range(0, tok.shape[0], STRIP):
            rows = slice(r, r + STRIP)
            hidden = hidden_all[rows] + bias
            square = hidden * hidden
            half = 0.5 + 0.5 * jnp.tanh(hidden * (slope + cubic * square))
            activated = hidden * half
            derivative = half + activated * (1.0 - half) * (2 * slope + (6 * cubic) * square)
            low = (grad_all[rows] * derivative).astype(BF16)
            activated_out[rows, columns] = activated.astype(BF16)
            grad_hidden[rows, columns] = low
            total += fold_rows(low.astype(F32))
        return total

    def weight_gradients(c):
        columns = slice(c, c + CHUNK)
        if (c // CHUNK) % 2:
            start, rows = c - CHUNK, 2 * CHUNK
            turned = activated_out[:, start : start + rows].T
            matrix_to_flat(dot(turned, cotangent), rows, D, flat, row_down + start * D // LANES)
        grads = dot(normed_turned, grad_hidden[:, columns])
        for j in range(CHUNK // LANES):
            flat[pl.ds(row_up + c // LANES + j, D, stride=FF // LANES), :] = grads[
                :, j * LANES : (j + 1) * LANES
            ]

    ahead, totals = products(0), []
    for c in range(0, FF, CHUNK):
        now = ahead
        if c + CHUNK < FF:
            ahead = products(c + CHUNK)
        if c > 0:
            weight_gradients(c - CHUNK)
        totals.append(bend(c, *now))
    grad_normed = dot_nt(grad_hidden[...], w_up[...])
    weight_gradients(FF - CHUNK)
    grad_result = cotangent.astype(F32)
    grad_middle = grad_result + normalize_back(grad_normed, gain, normed, rate)
    grad_middle_out[...] = grad_middle
    grad_middle_low = grad_middle.astype(BF16)
    grad_attended_out[...] = dot_nt(grad_middle_low, w_out[...]).astype(BF16)
    matrix_to_flat(dot_tn(attended[...], grad_middle_low), D, D, flat, 0)
    sums = jnp.concatenate(
        [
            fold_rows(grad_middle_low.astype(F32)),
            fold_rows(grad_normed * normed),
            fold_rows(grad_normed),
            *totals,
            fold_rows(grad_result),
        ],
        axis=1,
    )
    sums = jnp.sum(sums, axis=0, keepdims=True)
    base = ROW_SMALL - ROW_OUT
    flat[base : base + LATE_SMALL, :] = jnp.zeros((LATE_SMALL, LANES), F32)
    for i in range(sums.shape[1] // LANES):
        row = base + LATE_SMALL + i
        flat[row : row + 1, :] = sums[:, i * LANES : (i + 1) * LANES]
    flat[ROW_END - ROW_OUT :, :] = jnp.zeros((ROW_TOTAL - ROW_END, LANES), F32)
    first_out[...] = flat[:HEAD_ROWS, :]
    for target, out in enumerate((keep_out, send_out)):
        for p in range(PLANE):
            for z in range(1, Z):
                share = ids[target * PLANE + p] + z * 2 * PLANE
                rows = flat[pl.ds(share * SHARE - ROW_OUT, SHARE), :]
                out[p * (Z - 1) + z - 1] = rows.astype(out.dtype)


def result_kernel(middle, activated, w_down, small, result_out):
    result = middle[...] + dot(activated[...], w_down[...]) + small_vector(small, BIAS_DOWN, 2)
    result_out[...] = result.astype(BF16)


def attend_back_kernel(
    ids, project, weights, grad_attended, normed_turned, w_qkv, small, first_in,
    grad_project, keep_out, send_out, flat, wide,
):
    products, sums = 0.0, 0.0
    for g in range(project.shape[0] // WIDE):
        spans = [slice(r, r + SEQ) for r in range(g * WIDE, (g + 1) * WIDE, SEQ)]
        grad_weights = [
            dot_nt(spread_heads(project[span, 2 * D :]), grad_attended[span, :]) for span in spans
        ]
        scores_low, scores_turned = [], []
        for span, grads in zip(spans, grad_weights):
            low, turned = [], []
            for h in range(HEADS):
                mine = weights[span, h * SEQ : (h + 1) * SEQ].astype(F32)
                product = mine * grads[h * SEQ : (h + 1) * SEQ, :]
                grad_scores = (product - mine * jnp.sum(product, axis=0, keepdims=True)) * SCALE
                turned.append(grad_scores.astype(BF16))
                low.append(turned[-1].T)
            scores_low.append(jnp.concatenate(low, axis=1))
            scores_turned.append(jnp.concatenate(turned, axis=1))
        for s, span in enumerate(spans):
            key = spread_heads(project[span, D : 2 * D])
            grad_project[span, :D] = dot(scores_low[s], key).astype(BF16)
            query = spread_heads(project[span, :D])
            grad_project[span, D : 2 * D] = dot(scores_turned[s], query).astype(BF16)
            grad_value = dot(weights[span, :], spread_heads(grad_attended[span, :]))
            grad_project[span, 2 * D :] = grad_value.astype(BF16)
        span = slice(g * WIDE, (g + 1) * WIDE)
        products += dot(normed_turned[:, span], grad_project[span, :])
        sums += fold_rows(grad_project[span, :].astype(F32))
    sums = jnp.sum(sums, axis=0, keepdims=True)
    gain = jnp.broadcast_to(small_vector(small, GAIN_ONE, 2), (LANES, D)).T
    shift = jnp.broadcast_to(small_vector(small, SHIFT_ONE, 2), (LANES, D)).T
    grad_gain = jnp.zeros((D, LANES), F32)
    grad_shift = jnp.zeros((D, LANES), F32)
    per_row = 3 * D // LANES
    for j in range(per_row):
        columns = slice(j * LANES, (j + 1) * LANES)
        weight = w_qkv[:, columns].astype(F32)
        grad_gain += products[:, columns] * weight
        grad_shift += sums[:, columns] * weight
        flat[pl.ds(j, D, stride=per_row), :] = products[:, columns] * gain + sums[:, columns] * shift
    flat[ROW_OUT:, :] = first_in[...]
    grad_gain = jnp.sum(grad_gain.T, axis=0, keepdims=True)
    grad_shift = jnp.sum(grad_shift.T, axis=0, keepdims=True)
    late = jnp.concatenate([grad_gain, grad_shift, sums[:, :D], sums[:, 2 * D :]], axis=1)
    side = jnp.concatenate(
        [late[:, i * LANES : (i + 1) * LANES] for i in range(LATE_SMALL)]
        + [jnp.zeros((SIDE_ROWS - LATE_SMALL, LANES), F32)],
        axis=0,
    )
    wide[SHARE:SIDE, :] = jnp.zeros((SIDE - SHARE, LANES), F32)
    for target, out in enumerate((keep_out, send_out)):
        for p in range(PLANE):
            share = ids[target * PLANE + p]
            wide[:SHARE, :] = flat[pl.ds(share * SHARE, SHARE), :]
            wide[SIDE:, :] = jnp.where(share == 2 * PLANE - 1, side, 0.0)
            out[p] = wide[...].astype(out.dtype)


def input_grad_kernel(tok, grad_project, grad_middle, w_qkv, small, input_grad_out):
    gain = small_vector(small, GAIN_ONE, 2)

    def some(g, carry):
        span = pl.ds(pl.multiple_of(g * WIDE, WIDE), WIDE)
        normed, rate = normalize(tok[span, :].astype(F32))
        grad_normed = dot_nt(grad_project[span, :], w_qkv[...])
        input_grad_out[span, :] = grad_middle[span, :] + normalize_back(
            grad_normed, gain, normed, rate
        )
        return carry

    lax.fori_loop(0, tok.shape[0] // WIDE, some, 0)


def stack_kernel(*refs):
    row = 0
    for ref in refs[:-1]:
        refs[-1][row : row + ref.shape[0]] = ref[...]
        row += ref.shape[0]


def add_core_kernel(first, first_in, rest, rest_in, keep_out, *refs):
    sends, column = refs[:-1], refs[-1]
    start = (Z - 1) * SHARE + SMALL_IN_SHARE
    for p, out in enumerate((keep_out, *sends)):
        item = first[p] + first_in[p].astype(F32)
        column[:SHARE, :] = item[:SHARE, :]
        for z in range(1, Z):
            slot = p * (Z - 1) + z - 1
            column[z * SHARE : (z + 1) * SHARE, :] = rest[slot] + rest_in[slot].astype(F32)
        column[start : start + LATE_SMALL, :] += item[SIDE : SIDE + LATE_SMALL, :]
        out[...] = column[...].astype(out.dtype)


def add_plane_kernel(ids, kept, *refs):
    arrived = refs[: PLANE - 1]
    keep_out, *sends, column = refs[PLANE - 1 :]
    column[...] = kept[...] + sum(item[...].astype(F32) for item in arrived)
    keep_out[...] = column[pl.ds(ids[0] * SHARE, SHARE), :]
    for d, out in enumerate(sends):
        out[...] = column[pl.ds(lax.rem(ids[0] + d + 1, Z) * SHARE, SHARE), :].astype(BF16)


def add_column_kernel(kept, *refs):
    refs[-1][...] = kept[...] + sum(item[...].astype(F32) for item in refs[:-1])


def like(*shape, kind=F32):
    return jax.ShapeDtypeStruct(shape, kind)


SMEM_SPEC = pl.BlockSpec(memory_space=pltpu.SMEM)
VMEM_SPEC = pl.BlockSpec(memory_space=pltpu.VMEM)

def cost(us):
    return pl.CostEstimate(flops=int(us * 1e9), bytes_accessed=1 << 20, transcendentals=0)


def call(kernel, name, ids, inputs, outs, scratch=(), us=1):
    with_ids = ids is not None
    results = pl.pallas_call(
        kernel,
        in_specs=[SMEM_SPEC] * with_ids + [VMEM_SPEC] * len(inputs),
        out_specs=[VMEM_SPEC] * len(outs),
        out_shape=list(outs),
        scratch_shapes=list(scratch),
        compiler_params=pltpu.CompilerParams(vmem_limit_bytes=VMEM_BYTES),
        cost_estimate=cost(us),
        name=name,
    )(*([ids] if with_ids else []), *inputs)
    return results if len(outs) > 1 else results[0]


def prepare(tokens, params, segment_ids):
    rows = tokens.shape[0]
    return call(
        prepare_kernel, "prepare", None, [tokens, params, segment_ids.reshape(-1, SEQ)],
        [
            like(rows, D),
            like(D, rows, kind=BF16),
            like(*params.shape, kind=BF16),
            like(rows, SEQ),
        ],
        us=2,
    )


def stack(items):
    shape = (sum(item.shape[0] for item in items),) + items[0].shape[1:]
    return call(stack_kernel, "stack", None, items, [like(*shape, kind=items[0].dtype)], us=0.01)


def attend(ids, allowed, normed, bufs):
    rows = normed.shape[0]
    shapes = [(rows, 3 * D), (rows, HEADS * SEQ), (rows, D), (D, 3 * D)]
    return call(
        attend_kernel, "attend", ids, [allowed, normed, *bufs],
        [like(*shape, kind=BF16) for shape in shapes]
        + [like(SMALL_ROWS, LANES), like(HEAD_ROWS, LANES)],
        [pltpu.VMEM((FIRST_ROWS, LANES), F32)], us=0.01,
    )


def feed(ids, tokens, attended, cotangent, small, first, bufs, send_kind):
    rows = tokens.shape[0]
    return call(
        feed_kernel, "feed", ids, [tokens, attended, cotangent, small, first, *bufs],
        [
            like(rows, D),
            like(rows, FF, kind=BF16),
            like(rows, D),
            like(rows, D, kind=BF16),
            like(FF, D, kind=BF16),
            like(PLANE * (Z - 1), SHARE, LANES),
            like(PLANE * (Z - 1), SHARE, LANES, kind=send_kind),
            like(HEAD_ROWS, LANES),
        ],
        [
            pltpu.VMEM((D, D), BF16),
            pltpu.VMEM((D, FF), BF16),
            pltpu.VMEM((rows, FF), BF16),
            pltpu.VMEM((ROW_TOTAL - ROW_OUT, LANES), F32),
        ],
        us=8,
    )


def result(middle, activated, w_down, small):
    return call(
        result_kernel, "result", None, [middle, activated, w_down, small],
        [like(*middle.shape, kind=BF16)], us=2,
    )


def attend_back(ids, project, weights, grad_attended, normed_turned, w_qkv, small, first, send_kind):
    shape = (PLANE, SIDE + SIDE_ROWS, LANES)
    return call(
        attend_back_kernel, "attend_back", ids,
        [project, weights, grad_attended, normed_turned, w_qkv, small, first],
        [like(*project.shape, kind=BF16), like(*shape), like(*shape, kind=send_kind)],
        [pltpu.VMEM((FIRST_ROWS, LANES), F32), pltpu.VMEM(shape[1:], F32)], us=4,
    )


def input_gradient(tokens, grad_project, grad_middle, w_qkv, small):
    return call(
        input_grad_kernel, "input_grad", None, [tokens, grad_project, grad_middle, w_qkv, small],
        [like(*tokens.shape)], us=2,
    )


def local_any(n, tokens, params, segment_ids, cotangent):
    total = n * params.shape[0]
    normed, normed_turned, _, allowed = prepare(tokens, params, segment_ids)
    gathered = lax.all_gather(params, "fsdp", axis=0).reshape(total, LANES)
    shares = gathered[:ROW_TOTAL].reshape(Z, 2 * PLANE, SHARE, LANES)
    order = [p * 2 + c for c in range(2) for p in range(PLANE)]
    side = jnp.concatenate(
        [jnp.zeros((SIDE - SHARE, LANES), BF16), gathered[ROW_SMALL:ROW_TOTAL]], axis=0
    )
    firsts = [jnp.concatenate([shares[0, k], side], axis=0)[None] for k in order]
    firsts = [
        jnp.concatenate(firsts[c + i : c + j]) for c in (0, PLANE) for i, j in FIRST_GROUPS
    ]
    rests = []
    for group in (order[:PLANE], order[PLANE:]):
        rests += [shares[1:, group[0]], jnp.concatenate([shares[1:, k] for k in group[1:]])]
    ids = jnp.array(order, jnp.int32)
    project, weights, attended, w_qkv, small, first = attend(ids, allowed, normed, firsts)
    middle, activated, grad_middle, grad_attended, w_down, rest, rest_send, first_grad = feed(
        ids, tokens, attended, cotangent, small, first, rests, F32
    )
    outputs = result(middle, activated, w_down, small)
    grad_project, first, first_send = attend_back(
        ids, project, weights, grad_attended, normed_turned, w_qkv, small, first_grad, F32
    )
    input_grad = input_gradient(tokens, grad_project, grad_middle, w_qkv, small)
    first = jnp.stack([first, first_send], axis=1)
    rest = jnp.stack([rest, rest_send]).reshape(2, PLANE, Z - 1, SHARE, LANES).transpose(2, 1, 0, 3, 4)
    flat = jnp.concatenate(
        [
            first[:, :, :SHARE].reshape(-1, LANES),
            rest.reshape(-1, LANES),
            jnp.zeros((total - ROW_TOTAL, LANES), F32),
        ],
        axis=0,
    )
    flat = flat.at[ROW_SMALL : ROW_SMALL + LATE_SMALL].add(
        first[PLANE - 1, 1, SIDE : SIDE + LATE_SMALL]
    )
    param_grad = lax.psum_scatter(flat, "fsdp", scatter_dimension=0, tiled=True)
    return outputs, input_grad, param_grad


def index_of(z, plane, core):
    return (z * PLANE + plane) * 2 + core


def move(values, step_z, step_plane, step_core):
    pairs = [
        (index_of(z, p, c), index_of((z + step_z) % Z, p ^ step_plane, c ^ step_core))
        for z in range(Z)
        for p in range(PLANE)
        for c in range(2)
    ]
    return lax.ppermute(values, "fsdp", pairs)


STEPS = (3, 1, 2)


def local_slice(tokens, params, segment_ids, cotangent):
    me = lax.axis_index("fsdp").astype(jnp.int32)
    z, plane, core = me // (2 * PLANE), (me // 2) % PLANE, me % 2
    where = z.reshape(1)
    ids = jnp.stack(
        [(plane ^ dp) * 2 + (core ^ dc) for dc in range(2) for dp in (0, *STEPS)]
    )

    normed, normed_turned, own, allowed = prepare(tokens, params, segment_ids)
    first, rest = call(
        sort_kernel, "sort_shares", where, [own] + [move(params, d, 0, 0) for d in range(1, Z)],
        [like(1, SIDE + SMALL_ROWS, LANES, kind=BF16), like(Z - 1, SHARE, LANES, kind=BF16)],
        [pltpu.VMEM((Z, SHARE, LANES), BF16), pltpu.VMEM((SIDE + SMALL_ROWS, LANES), F32)],
    )
    firsts = [first] + [move(first, 0, d, 0) for d in STEPS]
    rests = [move(rest, 0, d, 0) for d in STEPS]
    firsts = [stack(firsts[i:j]) if j > i + 1 else firsts[i] for i, j in FIRST_GROUPS]
    firsts = firsts + [move(item, 0, 0, 1) for item in firsts]
    project, weights, attended, w_qkv, small, first = attend(ids, allowed, normed, firsts)
    *rests, attended = lax.optimization_barrier((*rests, attended))
    rests = stack(rests)
    rests = [rest, rests, move(rest, 0, 0, 1), move(rests, 0, 0, 1)]
    middle, activated, grad_middle, grad_attended, w_down, rest, send, first_grad = feed(
        ids, tokens, attended, cotangent, small, first, rests, BF16
    )

    rest_in = move(send, 0, 0, 1)
    grad_project, first, send = attend_back(
        ids, project, weights, grad_attended, normed_turned, w_qkv, small, first_grad, BF16
    )
    first_in = move(send, 0, 0, 1)
    part = (Z * SHARE, LANES)
    kept, *sends = call(
        add_core_kernel, "add_core", None, [first, first_in, rest, rest_in],
        [like(*part)] + [like(*part, kind=BF16)] * (PLANE - 1), [pltpu.VMEM(part, F32)],
    )
    arrived = [move(item, 0, d, 0) for item, d in zip(sends, STEPS)]
    outputs = result(middle, activated, w_down, small)
    input_grad = input_gradient(tokens, grad_project, grad_middle, w_qkv, small)
    kept, *sends = call(
        add_plane_kernel, "add_plane", where, [kept] + arrived,
        [like(SHARE, LANES)] + [like(SHARE, LANES, kind=BF16)] * (Z - 1), [pltpu.VMEM(part, F32)],
    )
    arrived = [move(item, d + 1, 0, 0) for d, item in enumerate(sends)]
    param_grad = call(
        add_column_kernel, "add_column", None, [kept] + arrived, [like(SHARE, LANES)]
    )
    return outputs, input_grad, param_grad


def solution(mesh):
    n = mesh.shape["fsdp"]
    local = local_slice if n == 2 * PLANE * Z else functools.partial(local_any, n)
    in_specs = (P("fsdp", None), P("fsdp", None), P("fsdp"), P("fsdp", None))
    out_specs = (P("fsdp", None), P("fsdp", None), P("fsdp", None))
    return jax.shard_map(local, mesh=mesh, in_specs=in_specs, out_specs=out_specs, check_vma=False)
```

```python
import functools

import jax
import jax.numpy as jnp
from jax import lax
from jax.experimental import pallas as pl
from jax.experimental.pallas import tpu as pltpu
from jax.sharding import PartitionSpec as P

D = 256
HEADS = 4
HEAD_DIM = 64
FF = 1024
SEQ = 128
LANES = 128
GROUP = 4
WIDE = GROUP * SEQ
CHUNK = 256
STRIP = 64
EPSILON = 1e-05
SCALE = HEAD_DIM ** (-0.5)
VMEM_BYTES = 24 * 1024 * 1024

ROW_QKV = 0
ROW_OUT = 1536
ROW_UP = 2048
ROW_DOWN = 4096
ROW_SMALL = 6144
ROW_END = 6168
ROW_TOTAL = 6176
GAIN_ONE, SHIFT_ONE, BIAS_QUERY, BIAS_VALUE, BIAS_OUT = 0, 2, 4, 6, 8
GAIN_TWO, SHIFT_TWO, BIAS_UP, BIAS_DOWN = 10, 12, 14, 22
SMALL_ROWS = 32
LATE_SMALL = 8

SHARE = 193
Z, PLANE = 4, 4
FIRST_ROWS = 2 * PLANE * SHARE
HEAD_ROWS = FIRST_ROWS - ROW_OUT
SIDE, SIDE_ROWS = 208, 16
FIRST_GROUPS = ((0, 2), (2, 4))
DIAGONAL_ROWS = SIDE + SMALL_ROWS + (Z - 1) * SIDE
SMALL_IN_SHARE = ROW_SMALL - (2 * PLANE * Z - 1) * SHARE

F32 = jnp.float32
BF16 = jnp.bfloat16


def dot(left, right):
    return jnp.dot(left, right, preferred_element_type=F32)


def dot_nt(left, right):
    return lax.dot_general(left, right, (((1,), (1,)), ((), ())), preferred_element_type=F32)


def dot_tn(left, right):
    return lax.dot_general(left, right, (((0,), (0,)), ((), ())), preferred_element_type=F32)


def small_vector(small, row, count):
    return jnp.concatenate([small[row + i : row + i + 1, :] for i in range(count)], axis=1)


def fold_rows(values):
    rows, columns = values.shape
    return jnp.sum(values.reshape(rows // 8, 8, columns), axis=0)


def normalize(values):
    center = values - jnp.mean(values, axis=-1, keepdims=True)
    rate = lax.rsqrt(jnp.mean(center * center, axis=-1, keepdims=True) + EPSILON)
    return center * rate, rate


def normalize_back(grad, gain, normed, rate):
    scaled = grad * gain
    return rate * (
        scaled
        - jnp.mean(scaled, axis=-1, keepdims=True)
        - normed * jnp.mean(scaled * normed, axis=-1, keepdims=True)
    )


def head_masks():
    lane = lax.broadcasted_iota(jnp.int32, (1, D), 1)
    return [(lane // HEAD_DIM == h).astype(F32).astype(BF16) for h in range(HEADS)]


def spread_heads(rows):
    return jnp.concatenate([rows * mask for mask in head_masks()], axis=0)


def matrix_from_flat(flat, start, rows, columns, out):
    per_row = columns // LANES
    for j in range(per_row):
        out[:, j * LANES : (j + 1) * LANES] = flat[
            pl.ds(start + j, rows, stride=per_row), :
        ].astype(BF16)


def matrix_to_flat(matrix, rows, columns, flat, start):
    per_row = columns // LANES
    for j in range(per_row):
        flat[pl.ds(start + j, rows, stride=per_row), :] = matrix[:, j * LANES : (j + 1) * LANES]


def prepare_kernel(tok, params, seg, normed_out, normed_turned, own, allowed):
    normed, _ = normalize(tok[...].astype(F32))
    normed_out[...] = normed
    normed_turned[...] = normed.astype(BF16).T
    own[...] = params[...]
    causal = lax.broadcasted_iota(jnp.int32, (SEQ, SEQ), 0) <= lax.broadcasted_iota(
        jnp.int32, (SEQ, SEQ), 1
    )
    for s in range(seg.shape[0]):
        across = jnp.broadcast_to(seg[s : s + 1, :].astype(F32), (SEQ, SEQ))
        allowed[s * SEQ : (s + 1) * SEQ, :] = (causal & (across == across.T)).astype(F32)


def sort_kernel(ids, *refs):
    received, (first, rest, both, stage, wide) = refs[:Z], refs[Z:]
    for d in range(Z):
        stage[lax.rem(ids[0] + Z - d, Z)] = received[d][...]
    rest[...] = stage[1:]
    wide[:SHARE, :] = stage[0].astype(F32)
    wide[SHARE:SIDE, :] = jnp.zeros((SIDE - SHARE, LANES), F32)
    last = stage[Z - 1].astype(F32)
    wide[SIDE:, :] = last[SMALL_IN_SHARE:, :]
    first[0] = wide[...].astype(BF16)
    both[: SIDE + SMALL_ROWS, :] = wide[...].astype(BF16)
    for z in range(1, Z):
        wide[:SHARE, :] = stage[z].astype(F32)
        row = SIDE + SMALL_ROWS + (z - 1) * SIDE
        both[row : row + SIDE, :] = wide[:SIDE, :].astype(BF16)


def attend_kernel(ids, allowed, normed, *refs):
    bufs = [ref.at[i] for ref in refs[:4] for i in range(ref.shape[0])]
    project_out, weights_out, attended_out, w_qkv, small, first_out, flat = refs[4:]
    for slot, buf in enumerate(bufs):
        wide = buf[...].astype(F32)
        flat[pl.ds(ids[slot] * SHARE, SHARE), :] = wide[:SHARE, :]

        @pl.when(ids[slot] == 2 * PLANE - 1)
        def _():
            small[...] = wide[SIDE:, :]

    matrix_from_flat(flat, ROW_QKV, D, 3 * D, w_qkv)
    first_out[...] = flat[ROW_OUT:FIRST_ROWS, :]

    gain = small_vector(small, GAIN_ONE, 2)
    shift = small_vector(small, SHIFT_ONE, 2)
    bias = jnp.concatenate(
        [
            small_vector(small, BIAS_QUERY, 2),
            jnp.zeros((1, D), F32),
            small_vector(small, BIAS_VALUE, 2),
        ],
        axis=1,
    )
    project_out[...] = (
        dot((normed[...] * gain + shift).astype(BF16), w_qkv[...]) + bias
    ).astype(BF16)
    for g in range(normed.shape[0] // WIDE):
        starts = range(g * WIDE, (g + 1) * WIDE, SEQ)
        scores = [
            dot_nt(
                spread_heads(project_out[r : r + SEQ, D : 2 * D]),
                project_out[r : r + SEQ, :D] * SCALE,
            )
            for r in starts
        ]
        weights = []
        for r, score in zip(starts, scores):
            open_pairs = allowed[r : r + SEQ, :] > 0.5
            turned = []
            for h in range(HEADS):
                mine = jnp.where(open_pairs, score[h * SEQ : (h + 1) * SEQ, :], -1e30)
                grown = jnp.exp(mine - jnp.max(mine, axis=0, keepdims=True))
                low = (grown * (1.0 / jnp.sum(grown, axis=0, keepdims=True))).astype(BF16)
                weights_out[r : r + SEQ, h * SEQ : (h + 1) * SEQ] = low
                turned.append(low.T)
            weights.append(jnp.concatenate(turned, axis=1))
        for r, weight in zip(starts, weights):
            value = spread_heads(project_out[r : r + SEQ, 2 * D :])
            attended_out[r : r + SEQ, :] = dot(weight, value).astype(BF16)


def feed_kernel(
    ids, tok, attended, cot, small, first_in, *refs,
):
    bufs = []
    for own, others in (refs[0:2], refs[2:4]):
        bufs.append(own)
        bufs += [others.at[pl.ds(p * (Z - 1), Z - 1)] for p in range(PLANE - 1)]
    (
        middle_out, activated_out, grad_middle_out, grad_attended_out, w_down, keep_out, send_out, first_out,
        w_out, w_up, grad_hidden, flat,
    ) = refs[4:]
    flat[:HEAD_ROWS, :] = first_in[...]
    for slot, buf in enumerate(bufs):
        for z in range(1, Z):
            share = ids[slot] + z * 2 * PLANE
            flat[pl.ds(share * SHARE - ROW_OUT, SHARE), :] = buf[z - 1].astype(F32)
    matrix_from_flat(flat, 0, D, D, w_out)
    matrix_from_flat(flat, ROW_UP - ROW_OUT, D, FF, w_up)
    matrix_from_flat(flat, ROW_DOWN - ROW_OUT, FF, D, w_down)

    gain = small_vector(small, GAIN_TWO, 2)
    middle = (
        tok[...].astype(F32) + dot(attended[...], w_out[...]) + small_vector(small, BIAS_OUT, 2)
    )
    middle_out[...] = middle
    normed, rate = normalize(middle)
    normed_low = (normed * gain + small_vector(small, SHIFT_TWO, 2)).astype(BF16)
    normed_turned = normed_low.T
    cotangent = cot[...]
    slope = 0.7978845608028654
    cubic = slope * 0.044715
    row_up, row_down = ROW_UP - ROW_OUT, ROW_DOWN - ROW_OUT

    def products(c):
        columns = slice(c, c + CHUNK)
        return dot(normed_low, w_up[:, columns]), dot_nt(cotangent, w_down[columns, :])

    def bend(c, hidden_all, grad_all):
        columns = slice(c, c + CHUNK)
        bias = small_vector(small, BIAS_UP + c // LANES, CHUNK // LANES)
        total = jnp.zeros((8, CHUNK), F32)
        for r in range(0, tok.shape[0], STRIP):
            rows = slice(r, r + STRIP)
            hidden = hidden_all[rows] + bias
            square = hidden * hidden
            half = 0.5 + 0.5 * jnp.tanh(hidden * (slope + cubic * square))
            activated = hidden * half
            derivative = half + activated * (1.0 - half) * (2 * slope + (6 * cubic) * square)
            low = (grad_all[rows] * derivative).astype(BF16)
            activated_out[rows, columns] = activated.astype(BF16)
            grad_hidden[rows, columns] = low
            total += fold_rows(low.astype(F32))
        return total

    def weight_gradients(c):
        columns = slice(c, c + CHUNK)
        if (c // CHUNK) % 2:
            start, rows = c - CHUNK, 2 * CHUNK
            turned = activated_out[:, start : start + rows].T
            matrix_to_flat(dot(turned, cotangent), rows, D, flat, row_down + start * D // LANES)
        grads = dot(normed_turned, grad_hidden[:, columns])
        for j in range(CHUNK // LANES):
            flat[pl.ds(row_up + c // LANES + j, D, stride=FF // LANES), :] = grads[
                :, j * LANES : (j + 1) * LANES
            ]

    ahead, totals = products(0), []
    for c in range(0, FF, CHUNK):
        now = ahead
        if c + CHUNK < FF:
            ahead = products(c + CHUNK)
        if c > 0:
            weight_gradients(c - CHUNK)
        totals.append(bend(c, *now))
    grad_normed = dot_nt(grad_hidden[...], w_up[...])
    weight_gradients(FF - CHUNK)
    grad_result = cotangent.astype(F32)
    grad_middle = grad_result + normalize_back(grad_normed, gain, normed, rate)
    grad_middle_out[...] = grad_middle
    grad_middle_low = grad_middle.astype(BF16)
    grad_attended_out[...] = dot_nt(grad_middle_low, w_out[...]).astype(BF16)
    matrix_to_flat(dot_tn(attended[...], grad_middle_low), D, D, flat, 0)
    sums = jnp.concatenate(
        [
            fold_rows(grad_middle_low.astype(F32)),
            fold_rows(grad_normed * normed),
            fold_rows(grad_normed),
            *totals,
            fold_rows(grad_result),
        ],
        axis=1,
    )
    sums = jnp.sum(sums, axis=0, keepdims=True)
    base = ROW_SMALL - ROW_OUT
    flat[base : base + LATE_SMALL, :] = jnp.zeros((LATE_SMALL, LANES), F32)
    for i in range(sums.shape[1] // LANES):
        row = base + LATE_SMALL + i
        flat[row : row + 1, :] = sums[:, i * LANES : (i + 1) * LANES]
    flat[ROW_END - ROW_OUT :, :] = jnp.zeros((ROW_TOTAL - ROW_END, LANES), F32)
    first_out[...] = flat[:HEAD_ROWS, :]
    for target, out in enumerate((keep_out, send_out)):
        for p in range(PLANE):
            for z in range(1, Z):
                share = ids[target * PLANE + p] + z * 2 * PLANE
                rows = flat[pl.ds(share * SHARE - ROW_OUT, SHARE), :]
                out[p * (Z - 1) + z - 1] = rows.astype(out.dtype)


def result_kernel(middle, activated, w_down, small, result_out):
    result = middle[...] + dot(activated[...], w_down[...]) + small_vector(small, BIAS_DOWN, 2)
    result_out[...] = result.astype(BF16)


def attend_back_kernel(
    ids, project, weights, grad_attended, normed_turned, w_qkv, small, first_in,
    grad_project, keep_out, send_out, flat, wide,
):
    products, sums = 0.0, 0.0
    for g in range(project.shape[0] // WIDE):
        spans = [slice(r, r + SEQ) for r in range(g * WIDE, (g + 1) * WIDE, SEQ)]
        grad_weights = [
            dot_nt(spread_heads(project[span, 2 * D :]), grad_attended[span, :]) for span in spans
        ]
        scores_low, scores_turned = [], []
        for span, grads in zip(spans, grad_weights):
            low, turned = [], []
            for h in range(HEADS):
                mine = weights[span, h * SEQ : (h + 1) * SEQ].astype(F32)
                product = mine * grads[h * SEQ : (h + 1) * SEQ, :]
                grad_scores = (product - mine * jnp.sum(product, axis=0, keepdims=True)) * SCALE
                turned.append(grad_scores.astype(BF16))
                low.append(turned[-1].T)
            scores_low.append(jnp.concatenate(low, axis=1))
            scores_turned.append(jnp.concatenate(turned, axis=1))
        for s, span in enumerate(spans):
            key = spread_heads(project[span, D : 2 * D])
            grad_project[span, :D] = dot(scores_low[s], key).astype(BF16)
            query = spread_heads(project[span, :D])
            grad_project[span, D : 2 * D] = dot(scores_turned[s], query).astype(BF16)
            grad_value = dot(weights[span, :], spread_heads(grad_attended[span, :]))
            grad_project[span, 2 * D :] = grad_value.astype(BF16)
        span = slice(g * WIDE, (g + 1) * WIDE)
        products += dot(normed_turned[:, span], grad_project[span, :])
        sums += fold_rows(grad_project[span, :].astype(F32))
    sums = jnp.sum(sums, axis=0, keepdims=True)
    gain = jnp.broadcast_to(small_vector(small, GAIN_ONE, 2), (LANES, D)).T
    shift = jnp.broadcast_to(small_vector(small, SHIFT_ONE, 2), (LANES, D)).T
    grad_gain = jnp.zeros((D, LANES), F32)
    grad_shift = jnp.zeros((D, LANES), F32)
    per_row = 3 * D // LANES
    for j in range(per_row):
        columns = slice(j * LANES, (j + 1) * LANES)
        weight = w_qkv[:, columns].astype(F32)
        grad_gain += products[:, columns] * weight
        grad_shift += sums[:, columns] * weight
        flat[pl.ds(j, D, stride=per_row), :] = products[:, columns] * gain + sums[:, columns] * shift
    flat[ROW_OUT:, :] = first_in[...]
    grad_gain = jnp.sum(grad_gain.T, axis=0, keepdims=True)
    grad_shift = jnp.sum(grad_shift.T, axis=0, keepdims=True)
    late = jnp.concatenate([grad_gain, grad_shift, sums[:, :D], sums[:, 2 * D :]], axis=1)
    side = jnp.concatenate(
        [late[:, i * LANES : (i + 1) * LANES] for i in range(LATE_SMALL)]
        + [jnp.zeros((SIDE_ROWS - LATE_SMALL, LANES), F32)],
        axis=0,
    )
    wide[SHARE:SIDE, :] = jnp.zeros((SIDE - SHARE, LANES), F32)
    for target, out in enumerate((keep_out, send_out)):
        for p in range(PLANE):
            share = ids[target * PLANE + p]
            wide[:SHARE, :] = flat[pl.ds(share * SHARE, SHARE), :]
            wide[SIDE:, :] = jnp.where(share == 2 * PLANE - 1, side, 0.0)
            out[p] = wide[...].astype(out.dtype)


def input_grad_kernel(tok, grad_project, grad_middle, w_qkv, small, input_grad_out):
    gain = small_vector(small, GAIN_ONE, 2)

    def some(g, carry):
        span = pl.ds(pl.multiple_of(g * WIDE, WIDE), WIDE)
        normed, rate = normalize(tok[span, :].astype(F32))
        grad_normed = dot_nt(grad_project[span, :], w_qkv[...])
        input_grad_out[span, :] = grad_middle[span, :] + normalize_back(
            grad_normed, gain, normed, rate
        )
        return carry

    lax.fori_loop(0, tok.shape[0] // WIDE, some, 0)


def stack_first_kernel(own, both, out):
    out[0] = own[0]
    out[1] = both[: SIDE + SMALL_ROWS, :]


def stack_rest_kernel(both, *refs):
    others, out = refs[:-1], refs[-1]
    for z in range(Z - 1):
        row = SIDE + SMALL_ROWS + z * SIDE
        out[z] = both[row : row + SIDE, :].astype(F32)[:SHARE, :].astype(BF16)
    for i, item in enumerate(others, 1):
        out[i * (Z - 1) : (i + 1) * (Z - 1)] = item[...]


def stack_kernel(*refs):
    row = 0
    for ref in refs[:-1]:
        refs[-1][row : row + ref.shape[0]] = ref[...]
        row += ref.shape[0]


def add_core_kernel(first, first_in, rest, rest_in, keep_out, *refs):
    sends, column = refs[:-1], refs[-1]
    end = SMALL_IN_SHARE + LATE_SMALL
    for p, out in enumerate((keep_out, *sends)):
        item = first[p] + first_in[p].astype(F32)
        span = slice(p * (Z - 1), (p + 1) * (Z - 1))
        column[0] = item[:SHARE, :]
        column[1:] = rest[span] + rest_in[span].astype(F32)
        column[Z - 1, SMALL_IN_SHARE:end, :] += item[SIDE : SIDE + LATE_SMALL, :]
        out[...] = column[...].astype(out.dtype)


def add_plane_kernel(ids, kept, *refs):
    arrived = refs[: PLANE - 1]
    keep_out, *sends, column = refs[PLANE - 1 :]
    column[...] = kept[...] + sum(item[...].astype(F32) for item in arrived)
    keep_out[...] = column[ids[0]]
    for d, out in enumerate(sends):
        out[...] = column[lax.rem(ids[0] + d + 1, Z)].astype(BF16)


def add_column_kernel(kept, *refs):
    refs[-1][...] = kept[...] + sum(item[...].astype(F32) for item in refs[:-1])


def like(*shape, kind=F32):
    return jax.ShapeDtypeStruct(shape, kind)


SMEM_SPEC = pl.BlockSpec(memory_space=pltpu.SMEM)
VMEM_SPEC = pl.BlockSpec(memory_space=pltpu.VMEM)

def cost(us):
    return pl.CostEstimate(flops=int(us * 1e9), bytes_accessed=1 << 20, transcendentals=0)


def call(kernel, name, ids, inputs, outs, scratch=(), us=1):
    with_ids = ids is not None
    results = pl.pallas_call(
        kernel,
        in_specs=[SMEM_SPEC] * with_ids + [VMEM_SPEC] * len(inputs),
        out_specs=[VMEM_SPEC] * len(outs),
        out_shape=list(outs),
        scratch_shapes=list(scratch),
        compiler_params=pltpu.CompilerParams(vmem_limit_bytes=VMEM_BYTES),
        cost_estimate=cost(us),
        name=name,
    )(*([ids] if with_ids else []), *inputs)
    return results if len(outs) > 1 else results[0]


def prepare(tokens, params, segment_ids):
    rows = tokens.shape[0]
    return call(
        prepare_kernel, "prepare", None, [tokens, params, segment_ids.reshape(-1, SEQ)],
        [
            like(rows, D),
            like(D, rows, kind=BF16),
            like(*params.shape, kind=BF16),
            like(rows, SEQ),
        ],
        us=2,
    )


def stack(items):
    shape = (sum(item.shape[0] for item in items),) + items[0].shape[1:]
    return call(stack_kernel, "stack", None, items, [like(*shape, kind=items[0].dtype)], us=0.01)


def attend(ids, allowed, normed, bufs):
    rows = normed.shape[0]
    shapes = [(rows, 3 * D), (rows, HEADS * SEQ), (rows, D), (D, 3 * D)]
    return call(
        attend_kernel, "attend", ids, [allowed, normed, *bufs],
        [like(*shape, kind=BF16) for shape in shapes]
        + [like(SMALL_ROWS, LANES), like(HEAD_ROWS, LANES)],
        [pltpu.VMEM((FIRST_ROWS, LANES), F32)], us=0.01,
    )


def feed(ids, tokens, attended, cotangent, small, first, bufs, send_kind):
    rows = tokens.shape[0]
    return call(
        feed_kernel, "feed", ids, [tokens, attended, cotangent, small, first, *bufs],
        [
            like(rows, D),
            like(rows, FF, kind=BF16),
            like(rows, D),
            like(rows, D, kind=BF16),
            like(FF, D, kind=BF16),
            like(PLANE * (Z - 1), SHARE, LANES),
            like(PLANE * (Z - 1), SHARE, LANES, kind=send_kind),
            like(HEAD_ROWS, LANES),
        ],
        [
            pltpu.VMEM((D, D), BF16),
            pltpu.VMEM((D, FF), BF16),
            pltpu.VMEM((rows, FF), BF16),
            pltpu.VMEM((ROW_TOTAL - ROW_OUT, LANES), F32),
        ],
        us=8,
    )


def result(middle, activated, w_down, small):
    return call(
        result_kernel, "result", None, [middle, activated, w_down, small],
        [like(*middle.shape, kind=BF16)], us=2,
    )


def attend_back(ids, project, weights, grad_attended, normed_turned, w_qkv, small, first, send_kind):
    shape = (PLANE, SIDE + SIDE_ROWS, LANES)
    return call(
        attend_back_kernel, "attend_back", ids,
        [project, weights, grad_attended, normed_turned, w_qkv, small, first],
        [like(*project.shape, kind=BF16), like(*shape), like(*shape, kind=send_kind)],
        [pltpu.VMEM((FIRST_ROWS, LANES), F32), pltpu.VMEM(shape[1:], F32)], us=4,
    )


def input_gradient(tokens, grad_project, grad_middle, w_qkv, small):
    return call(
        input_grad_kernel, "input_grad", None, [tokens, grad_project, grad_middle, w_qkv, small],
        [like(*tokens.shape)], us=2,
    )


def local_any(n, tokens, params, segment_ids, cotangent):
    total = n * params.shape[0]
    normed, normed_turned, _, allowed = prepare(tokens, params, segment_ids)
    gathered = lax.all_gather(params, "fsdp", axis=0).reshape(total, LANES)
    shares = gathered[:ROW_TOTAL].reshape(Z, 2 * PLANE, SHARE, LANES)
    order = [p * 2 + c for c in range(2) for p in range(PLANE)]
    side = jnp.concatenate(
        [jnp.zeros((SIDE - SHARE, LANES), BF16), gathered[ROW_SMALL:ROW_TOTAL]], axis=0
    )
    firsts = [jnp.concatenate([shares[0, k], side], axis=0)[None] for k in order]
    firsts = [
        jnp.concatenate(firsts[c + i : c + j]) for c in (0, PLANE) for i, j in FIRST_GROUPS
    ]
    rests = []
    for group in (order[:PLANE], order[PLANE:]):
        rests += [shares[1:, group[0]], jnp.concatenate([shares[1:, k] for k in group[1:]])]
    ids = jnp.array(order, jnp.int32)
    project, weights, attended, w_qkv, small, first = attend(ids, allowed, normed, firsts)
    middle, activated, grad_middle, grad_attended, w_down, rest, rest_send, first_grad = feed(
        ids, tokens, attended, cotangent, small, first, rests, F32
    )
    outputs = result(middle, activated, w_down, small)
    grad_project, first, first_send = attend_back(
        ids, project, weights, grad_attended, normed_turned, w_qkv, small, first_grad, F32
    )
    input_grad = input_gradient(tokens, grad_project, grad_middle, w_qkv, small)
    first = jnp.stack([first, first_send], axis=1)
    rest = jnp.stack([rest, rest_send]).reshape(2, PLANE, Z - 1, SHARE, LANES).transpose(2, 1, 0, 3, 4)
    flat = jnp.concatenate(
        [
            first[:, :, :SHARE].reshape(-1, LANES),
            rest.reshape(-1, LANES),
            jnp.zeros((total - ROW_TOTAL, LANES), F32),
        ],
        axis=0,
    )
    flat = flat.at[ROW_SMALL : ROW_SMALL + LATE_SMALL].add(
        first[PLANE - 1, 1, SIDE : SIDE + LATE_SMALL]
    )
    param_grad = lax.psum_scatter(flat, "fsdp", scatter_dimension=0, tiled=True)
    return outputs, input_grad, param_grad


def index_of(z, plane, core):
    return (z * PLANE + plane) * 2 + core


def move(values, step_z, step_plane, step_core):
    pairs = [
        (index_of(z, p, c), index_of((z + step_z) % Z, p ^ step_plane, c ^ step_core))
        for z in range(Z)
        for p in range(PLANE)
        for c in range(2)
    ]
    return lax.ppermute(values, "fsdp", pairs)


STEPS = (3, 1, 2)


def local_slice(tokens, params, segment_ids, cotangent):
    me = lax.axis_index("fsdp").astype(jnp.int32)
    z, plane, core = me // (2 * PLANE), (me // 2) % PLANE, me % 2
    where = z.reshape(1)
    ids = jnp.stack(
        [(plane ^ dp) * 2 + (core ^ dc) for dc in range(2) for dp in (0, *STEPS)]
    )

    normed, normed_turned, own, allowed = prepare(tokens, params, segment_ids)
    first, rest, both = call(
        sort_kernel, "sort_shares", where, [own] + [move(params, d, 0, 0) for d in range(1, Z)],
        [like(1, SIDE + SMALL_ROWS, LANES, kind=BF16), like(Z - 1, SHARE, LANES, kind=BF16), like(DIAGONAL_ROWS, LANES, kind=BF16)],
        [pltpu.VMEM((Z, SHARE, LANES), BF16), pltpu.VMEM((SIDE + SMALL_ROWS, LANES), F32)],
    )
    both = move(both, 0, STEPS[0], 0)
    firsts = [move(first, 0, d, 0) for d in STEPS[1:]]
    rests = [move(rest, 0, d, 0) for d in STEPS[1:]]
    firsts = [
        call(
            stack_first_kernel, "stack_first", None, [first, both],
            [like(2, SIDE + SMALL_ROWS, LANES, kind=BF16)], us=0.01,
        ),
        stack(firsts),
    ]
    firsts = firsts + [move(item, 0, 0, 1) for item in firsts]
    project, weights, attended, w_qkv, small, first = attend(ids, allowed, normed, firsts)
    *rests, attended = lax.optimization_barrier((*rests, attended))
    rests = call(
        stack_rest_kernel, "stack_rest", None, [both, *rests],
        [like((PLANE - 1) * (Z - 1), SHARE, LANES, kind=BF16)], us=0.01,
    )
    rests = [rest, rests, move(rest, 0, 0, 1), move(rests, 0, 0, 1)]
    middle, activated, grad_middle, grad_attended, w_down, rest, send, first_grad = feed(
        ids, tokens, attended, cotangent, small, first, rests, BF16
    )

    rest_in = move(send, 0, 0, 1)
    grad_project, first, send = attend_back(
        ids, project, weights, grad_attended, normed_turned, w_qkv, small, first_grad, BF16
    )
    first_in = move(send, 0, 0, 1)
    part = (Z, SHARE, LANES)
    kept, *sends = call(
        add_core_kernel, "add_core", None, [first, first_in, rest, rest_in],
        [like(*part)] + [like(*part, kind=BF16)] * (PLANE - 1), [pltpu.VMEM(part, F32)],
    )
    arrived = [move(item, 0, d, 0) for item, d in zip(sends, STEPS)]
    outputs = result(middle, activated, w_down, small)
    input_grad = input_gradient(tokens, grad_project, grad_middle, w_qkv, small)
    kept, *sends = call(
        add_plane_kernel, "add_plane", where, [kept] + arrived,
        [like(SHARE, LANES)] + [like(SHARE, LANES, kind=BF16)] * (Z - 1), [pltpu.VMEM(part, F32)],
    )
    arrived = [move(item, d + 1, 0, 0) for d, item in enumerate(sends)]
    param_grad = call(
        add_column_kernel, "add_column", None, [kept] + arrived, [like(SHARE, LANES)]
    )
    return outputs, input_grad, param_grad


def solution(mesh):
    n = mesh.shape["fsdp"]
    local = local_slice if n == 2 * PLANE * Z else functools.partial(local_any, n)
    in_specs = (P("fsdp", None), P("fsdp", None), P("fsdp"), P("fsdp", None))
    out_specs = (P("fsdp", None), P("fsdp", None), P("fsdp", None))
    return jax.shard_map(local, mesh=mesh, in_specs=in_specs, out_specs=out_specs, check_vma=False)
```

```python
import functools

import jax
import jax.numpy as jnp
from jax import lax
from jax.experimental import pallas as pl
from jax.experimental.pallas import tpu as pltpu
from jax.sharding import PartitionSpec as P

D = 256
HEADS = 4
HEAD_DIM = 64
FF = 1024
SEQ = 128
LANES = 128
GROUP = 4
WIDE = GROUP * SEQ
CHUNK = 256
STRIP = 64
EPSILON = 1e-05
SCALE = HEAD_DIM ** (-0.5)
VMEM_BYTES = 24 * 1024 * 1024

ROW_QKV = 0
ROW_OUT = 1536
ROW_UP = 2048
ROW_DOWN = 4096
ROW_SMALL = 6144
ROW_END = 6168
ROW_TOTAL = 6176
GAIN_ONE, SHIFT_ONE, BIAS_QUERY, BIAS_VALUE, BIAS_OUT = 0, 2, 4, 6, 8
GAIN_TWO, SHIFT_TWO, BIAS_UP, BIAS_DOWN = 10, 12, 14, 22
SMALL_ROWS = 32
LATE_SMALL = 8

SHARE = 193
Z, PLANE = 4, 4
FIRST_ROWS = 2 * PLANE * SHARE
HEAD_ROWS = FIRST_ROWS - ROW_OUT
SIDE, SIDE_ROWS = 208, 16
FIRST_GROUPS = ((0, 2), (2, 4))
SMALL_IN_SHARE = ROW_SMALL - (2 * PLANE * Z - 1) * SHARE

F32 = jnp.float32
BF16 = jnp.bfloat16


def dot(left, right):
    return jnp.dot(left, right, preferred_element_type=F32)


def dot_nt(left, right):
    return lax.dot_general(left, right, (((1,), (1,)), ((), ())), preferred_element_type=F32)


def dot_tn(left, right):
    return lax.dot_general(left, right, (((0,), (0,)), ((), ())), preferred_element_type=F32)


def small_vector(small, row, count):
    return jnp.concatenate([small[row + i : row + i + 1, :] for i in range(count)], axis=1)


def fold_rows(values):
    rows, columns = values.shape
    return jnp.sum(values.reshape(rows // 8, 8, columns), axis=0)


def normalize(values):
    center = values - jnp.mean(values, axis=-1, keepdims=True)
    rate = lax.rsqrt(jnp.mean(center * center, axis=-1, keepdims=True) + EPSILON)
    return center * rate, rate


def normalize_back(grad, gain, normed, rate):
    scaled = grad * gain
    return rate * (
        scaled
        - jnp.mean(scaled, axis=-1, keepdims=True)
        - normed * jnp.mean(scaled * normed, axis=-1, keepdims=True)
    )


def head_masks():
    lane = lax.broadcasted_iota(jnp.int32, (1, D), 1)
    return [(lane // HEAD_DIM == h).astype(F32).astype(BF16) for h in range(HEADS)]


def spread_heads(rows):
    return jnp.concatenate([rows * mask for mask in head_masks()], axis=0)


def matrix_from_flat(flat, start, rows, columns, out):
    per_row = columns // LANES
    for j in range(per_row):
        out[:, j * LANES : (j + 1) * LANES] = flat[
            pl.ds(start + j, rows, stride=per_row), :
        ].astype(BF16)


def matrix_to_flat(matrix, rows, columns, flat, start):
    per_row = columns // LANES
    for j in range(per_row):
        flat[pl.ds(start + j, rows, stride=per_row), :] = matrix[:, j * LANES : (j + 1) * LANES]


def prepare_kernel(tok, params, seg, normed_out, normed_turned, own, allowed):
    normed, _ = normalize(tok[...].astype(F32))
    normed_out[...] = normed
    normed_turned[...] = normed.astype(BF16).T
    own[...] = params[...]
    causal = lax.broadcasted_iota(jnp.int32, (SEQ, SEQ), 0) <= lax.broadcasted_iota(
        jnp.int32, (SEQ, SEQ), 1
    )
    for s in range(seg.shape[0]):
        across = jnp.broadcast_to(seg[s : s + 1, :].astype(F32), (SEQ, SEQ))
        allowed[s * SEQ : (s + 1) * SEQ, :] = (causal & (across == across.T)).astype(F32)


def sort_kernel(ids, *refs):
    received, (first, rest, stage, wide) = refs[:Z], refs[Z:]
    for d in range(Z):
        stage[lax.rem(ids[0] + Z - d, Z)] = received[d][...]
    rest[...] = stage[1:]
    wide[:SHARE, :] = stage[0].astype(F32)
    wide[SHARE:SIDE, :] = jnp.zeros((SIDE - SHARE, LANES), F32)
    last = stage[Z - 1].astype(F32)
    wide[SIDE:, :] = last[SMALL_IN_SHARE:, :]
    first[0] = wide[...].astype(BF16)


def attend_kernel(ids, allowed, normed, *refs):
    bufs = [ref.at[i] for ref in refs[:4] for i in range(ref.shape[0])]
    project_out, weights_out, attended_out, w_qkv, small, first_out, flat = refs[4:]
    for slot, buf in enumerate(bufs):
        wide = buf[...].astype(F32)
        flat[pl.ds(ids[slot] * SHARE, SHARE), :] = wide[:SHARE, :]

        @pl.when(ids[slot] == 2 * PLANE - 1)
        def _():
            small[...] = wide[SIDE:, :]

    matrix_from_flat(flat, ROW_QKV, D, 3 * D, w_qkv)
    first_out[...] = flat[ROW_OUT:FIRST_ROWS, :]

    gain = small_vector(small, GAIN_ONE, 2)
    shift = small_vector(small, SHIFT_ONE, 2)
    bias = jnp.concatenate(
        [
            small_vector(small, BIAS_QUERY, 2),
            jnp.zeros((1, D), F32),
            small_vector(small, BIAS_VALUE, 2),
        ],
        axis=1,
    )
    project_out[...] = (
        dot((normed[...] * gain + shift).astype(BF16), w_qkv[...]) + bias
    ).astype(BF16)
    for g in range(normed.shape[0] // WIDE):
        starts = range(g * WIDE, (g + 1) * WIDE, SEQ)
        scores = [
            dot_nt(
                spread_heads(project_out[r : r + SEQ, D : 2 * D]),
                project_out[r : r + SEQ, :D] * SCALE,
            )
            for r in starts
        ]
        weights = []
        for r, score in zip(starts, scores):
            open_pairs = allowed[r : r + SEQ, :] > 0.5
            turned = []
            for h in range(HEADS):
                mine = jnp.where(open_pairs, score[h * SEQ : (h + 1) * SEQ, :], -1e30)
                grown = jnp.exp(mine - jnp.max(mine, axis=0, keepdims=True))
                low = (grown * (1.0 / jnp.sum(grown, axis=0, keepdims=True))).astype(BF16)
                weights_out[r : r + SEQ, h * SEQ : (h + 1) * SEQ] = low
                turned.append(low.T)
            weights.append(jnp.concatenate(turned, axis=1))
        for r, weight in zip(starts, weights):
            value = spread_heads(project_out[r : r + SEQ, 2 * D :])
            attended_out[r : r + SEQ, :] = dot(weight, value).astype(BF16)


def feed_kernel(
    ids, tok, attended, cot, small, first_in, *refs,
):
    bufs = []
    for own, others in (refs[0:2], refs[2:4]):
        bufs.append(own)
        bufs += [others.at[pl.ds(p * (Z - 1), Z - 1)] for p in range(PLANE - 1)]
    (
        middle_out, activated_out, grad_middle_out, grad_attended_out, w_down, keep_out, send_out, first_out,
        w_out, w_up, grad_hidden, flat,
    ) = refs[4:]
    flat[:HEAD_ROWS, :] = first_in[...]
    for slot, buf in enumerate(bufs):
        for z in range(1, Z):
            share = ids[slot] + z * 2 * PLANE
            flat[pl.ds(share * SHARE - ROW_OUT, SHARE), :] = buf[z - 1].astype(F32)
    matrix_from_flat(flat, 0, D, D, w_out)
    matrix_from_flat(flat, ROW_UP - ROW_OUT, D, FF, w_up)
    matrix_from_flat(flat, ROW_DOWN - ROW_OUT, FF, D, w_down)

    gain = small_vector(small, GAIN_TWO, 2)
    middle = (
        tok[...].astype(F32) + dot(attended[...], w_out[...]) + small_vector(small, BIAS_OUT, 2)
    )
    middle_out[...] = middle
    normed, rate = normalize(middle)
    normed_low = (normed * gain + small_vector(small, SHIFT_TWO, 2)).astype(BF16)
    normed_turned = normed_low.T
    cotangent = cot[...]
    slope = 0.7978845608028654
    cubic = slope * 0.044715
    row_up, row_down = ROW_UP - ROW_OUT, ROW_DOWN - ROW_OUT

    def products(c):
        columns = slice(c, c + CHUNK)
        return dot(normed_low, w_up[:, columns]), dot_nt(cotangent, w_down[columns, :])

    def bend(c, hidden_all, grad_all):
        columns = slice(c, c + CHUNK)
        bias = small_vector(small, BIAS_UP + c // LANES, CHUNK // LANES)
        total = jnp.zeros((8, CHUNK), F32)
        for r in range(0, tok.shape[0], STRIP):
            rows = slice(r, r + STRIP)
            hidden = hidden_all[rows] + bias
            square = hidden * hidden
            half = 0.5 + 0.5 * jnp.tanh(hidden * (slope + cubic * square))
            activated = hidden * half
            derivative = half + activated * (1.0 - half) * (2 * slope + (6 * cubic) * square)
            low = (grad_all[rows] * derivative).astype(BF16)
            activated_out[rows, columns] = activated.astype(BF16)
            grad_hidden[rows, columns] = low
            total += fold_rows(low.astype(F32))
        return total

    def weight_gradients(c):
        columns = slice(c, c + CHUNK)
        if (c // CHUNK) % 2:
            start, rows = c - CHUNK, 2 * CHUNK
            turned = activated_out[:, start : start + rows].T
            matrix_to_flat(dot(turned, cotangent), rows, D, flat, row_down + start * D // LANES)
        grads = dot(normed_turned, grad_hidden[:, columns])
        for j in range(CHUNK // LANES):
            flat[pl.ds(row_up + c // LANES + j, D, stride=FF // LANES), :] = grads[
                :, j * LANES : (j + 1) * LANES
            ]

    ahead, totals = products(0), []
    for c in range(0, FF, CHUNK):
        now = ahead
        if c + CHUNK < FF:
            ahead = products(c + CHUNK)
        if c > 0:
            weight_gradients(c - CHUNK)
        totals.append(bend(c, *now))
    grad_normed = dot_nt(grad_hidden[...], w_up[...])
    weight_gradients(FF - CHUNK)
    grad_result = cotangent.astype(F32)
    grad_middle = grad_result + normalize_back(grad_normed, gain, normed, rate)
    grad_middle_out[...] = grad_middle
    grad_middle_low = grad_middle.astype(BF16)
    grad_attended_out[...] = dot_nt(grad_middle_low, w_out[...]).astype(BF16)
    matrix_to_flat(dot_tn(attended[...], grad_middle_low), D, D, flat, 0)
    sums = jnp.concatenate(
        [
            fold_rows(grad_middle_low.astype(F32)),
            fold_rows(grad_normed * normed),
            fold_rows(grad_normed),
            *totals,
            fold_rows(grad_result),
        ],
        axis=1,
    )
    sums = jnp.sum(sums, axis=0, keepdims=True)
    base = ROW_SMALL - ROW_OUT
    flat[base : base + LATE_SMALL, :] = jnp.zeros((LATE_SMALL, LANES), F32)
    for i in range(sums.shape[1] // LANES):
        row = base + LATE_SMALL + i
        flat[row : row + 1, :] = sums[:, i * LANES : (i + 1) * LANES]
    flat[ROW_END - ROW_OUT :, :] = jnp.zeros((ROW_TOTAL - ROW_END, LANES), F32)
    first_out[...] = flat[:HEAD_ROWS, :]
    for target, out in enumerate((keep_out, send_out)):
        for p in range(PLANE):
            for z in range(1, Z):
                share = ids[(2 + target) * PLANE + p] + z * 2 * PLANE
                rows = flat[pl.ds(share * SHARE - ROW_OUT, SHARE), :]
                out[p * (Z - 1) + z - 1] = rows.astype(out.dtype)


def result_kernel(middle, activated, w_down, small, result_out):
    result = middle[...] + dot(activated[...], w_down[...]) + small_vector(small, BIAS_DOWN, 2)
    result_out[...] = result.astype(BF16)


def attend_back_kernel(
    ids, project, weights, grad_attended, normed_turned, w_qkv, small, first_in,
    grad_project, keep_out, send_out, flat, wide,
):
    products, sums = 0.0, 0.0
    for g in range(project.shape[0] // WIDE):
        spans = [slice(r, r + SEQ) for r in range(g * WIDE, (g + 1) * WIDE, SEQ)]
        grad_weights = [
            dot_nt(spread_heads(project[span, 2 * D :]), grad_attended[span, :]) for span in spans
        ]
        scores_low, scores_turned = [], []
        for span, grads in zip(spans, grad_weights):
            low, turned = [], []
            for h in range(HEADS):
                mine = weights[span, h * SEQ : (h + 1) * SEQ].astype(F32)
                product = mine * grads[h * SEQ : (h + 1) * SEQ, :]
                grad_scores = (product - mine * jnp.sum(product, axis=0, keepdims=True)) * SCALE
                turned.append(grad_scores.astype(BF16))
                low.append(turned[-1].T)
            scores_low.append(jnp.concatenate(low, axis=1))
            scores_turned.append(jnp.concatenate(turned, axis=1))
        for s, span in enumerate(spans):
            key = spread_heads(project[span, D : 2 * D])
            grad_project[span, :D] = dot(scores_low[s], key).astype(BF16)
            query = spread_heads(project[span, :D])
            grad_project[span, D : 2 * D] = dot(scores_turned[s], query).astype(BF16)
            grad_value = dot(weights[span, :], spread_heads(grad_attended[span, :]))
            grad_project[span, 2 * D :] = grad_value.astype(BF16)
        span = slice(g * WIDE, (g + 1) * WIDE)
        products += dot(normed_turned[:, span], grad_project[span, :])
        sums += fold_rows(grad_project[span, :].astype(F32))
    sums = jnp.sum(sums, axis=0, keepdims=True)
    gain = jnp.broadcast_to(small_vector(small, GAIN_ONE, 2), (LANES, D)).T
    shift = jnp.broadcast_to(small_vector(small, SHIFT_ONE, 2), (LANES, D)).T
    grad_gain = jnp.zeros((D, LANES), F32)
    grad_shift = jnp.zeros((D, LANES), F32)
    per_row = 3 * D // LANES
    for j in range(per_row):
        columns = slice(j * LANES, (j + 1) * LANES)
        weight = w_qkv[:, columns].astype(F32)
        grad_gain += products[:, columns] * weight
        grad_shift += sums[:, columns] * weight
        flat[pl.ds(j, D, stride=per_row), :] = products[:, columns] * gain + sums[:, columns] * shift
    flat[ROW_OUT:, :] = first_in[...]
    grad_gain = jnp.sum(grad_gain.T, axis=0, keepdims=True)
    grad_shift = jnp.sum(grad_shift.T, axis=0, keepdims=True)
    late = jnp.concatenate([grad_gain, grad_shift, sums[:, :D], sums[:, 2 * D :]], axis=1)
    side = jnp.concatenate(
        [late[:, i * LANES : (i + 1) * LANES] for i in range(LATE_SMALL)]
        + [jnp.zeros((SIDE_ROWS - LATE_SMALL, LANES), F32)],
        axis=0,
    )
    wide[SHARE:SIDE, :] = jnp.zeros((SIDE - SHARE, LANES), F32)
    for target, out in enumerate((keep_out, send_out)):
        for p in range(PLANE):
            share = ids[target * PLANE + p]
            wide[:SHARE, :] = flat[pl.ds(share * SHARE, SHARE), :]
            wide[SIDE:, :] = jnp.where(share == 2 * PLANE - 1, side, 0.0)
            out[p] = wide[...].astype(out.dtype)


def input_grad_kernel(tok, grad_project, grad_middle, w_qkv, small, input_grad_out):
    gain = small_vector(small, GAIN_ONE, 2)

    def some(g, carry):
        span = pl.ds(pl.multiple_of(g * WIDE, WIDE), WIDE)
        normed, rate = normalize(tok[span, :].astype(F32))
        grad_normed = dot_nt(grad_project[span, :], w_qkv[...])
        input_grad_out[span, :] = grad_middle[span, :] + normalize_back(
            grad_normed, gain, normed, rate
        )
        return carry

    lax.fori_loop(0, tok.shape[0] // WIDE, some, 0)


def stack_kernel(*refs):
    row = 0
    for ref in refs[:-1]:
        refs[-1][row : row + ref.shape[0]] = ref[...]
        row += ref.shape[0]


def add_core_kernel(first, first_in, rest, rest_in, keep_out, *refs):
    sends, column = refs[:-1], refs[-1]
    end = SMALL_IN_SHARE + LATE_SMALL
    for p, out in enumerate((keep_out, *sends)):
        item = first[p] + first_in[p].astype(F32)
        span = slice(p * (Z - 1), (p + 1) * (Z - 1))
        column[0] = item[:SHARE, :]
        column[1:] = rest[span] + rest_in[span].astype(F32)
        column[Z - 1, SMALL_IN_SHARE:end, :] += item[SIDE : SIDE + LATE_SMALL, :]
        out[...] = column[...].astype(out.dtype)


def add_plane_kernel(ids, kept, *refs):
    arrived = refs[: PLANE - 1]
    keep_out, *sends, column = refs[PLANE - 1 :]
    column[...] = kept[...] + sum(item[...].astype(F32) for item in arrived)
    keep_out[...] = column[ids[0]]
    for d, out in enumerate(sends):
        out[...] = column[lax.rem(ids[0] + d + 1, Z)].astype(BF16)


def add_column_kernel(kept, *refs):
    refs[-1][...] = kept[...] + sum(item[...].astype(F32) for item in refs[:-1])


def like(*shape, kind=F32):
    return jax.ShapeDtypeStruct(shape, kind)


SMEM_SPEC = pl.BlockSpec(memory_space=pltpu.SMEM)
VMEM_SPEC = pl.BlockSpec(memory_space=pltpu.VMEM)

def cost(us):
    return pl.CostEstimate(flops=int(us * 1e9), bytes_accessed=1 << 20, transcendentals=0)


def call(kernel, name, ids, inputs, outs, scratch=(), us=1):
    with_ids = ids is not None
    results = pl.pallas_call(
        kernel,
        in_specs=[SMEM_SPEC] * with_ids + [VMEM_SPEC] * len(inputs),
        out_specs=[VMEM_SPEC] * len(outs),
        out_shape=list(outs),
        scratch_shapes=list(scratch),
        compiler_params=pltpu.CompilerParams(vmem_limit_bytes=VMEM_BYTES),
        cost_estimate=cost(us),
        name=name,
    )(*([ids] if with_ids else []), *inputs)
    return results if len(outs) > 1 else results[0]


def prepare(tokens, params, segment_ids):
    rows = tokens.shape[0]
    return call(
        prepare_kernel, "prepare", None, [tokens, params, segment_ids.reshape(-1, SEQ)],
        [
            like(rows, D),
            like(D, rows, kind=BF16),
            like(*params.shape, kind=BF16),
            like(rows, SEQ),
        ],
        us=2,
    )


def stack(items):
    shape = (sum(item.shape[0] for item in items),) + items[0].shape[1:]
    return call(stack_kernel, "stack", None, items, [like(*shape, kind=items[0].dtype)], us=0.01)


def attend(ids, allowed, normed, bufs):
    rows = normed.shape[0]
    shapes = [(rows, 3 * D), (rows, HEADS * SEQ), (rows, D), (D, 3 * D)]
    return call(
        attend_kernel, "attend", ids, [allowed, normed, *bufs],
        [like(*shape, kind=BF16) for shape in shapes]
        + [like(SMALL_ROWS, LANES), like(HEAD_ROWS, LANES)],
        [pltpu.VMEM((FIRST_ROWS, LANES), F32)], us=0.01,
    )


def feed(ids, tokens, attended, cotangent, small, first, bufs, send_kind):
    rows = tokens.shape[0]
    return call(
        feed_kernel, "feed", ids, [tokens, attended, cotangent, small, first, *bufs],
        [
            like(rows, D),
            like(rows, FF, kind=BF16),
            like(rows, D),
            like(rows, D, kind=BF16),
            like(FF, D, kind=BF16),
            like(PLANE * (Z - 1), SHARE, LANES),
            like(PLANE * (Z - 1), SHARE, LANES, kind=send_kind),
            like(HEAD_ROWS, LANES),
        ],
        [
            pltpu.VMEM((D, D), BF16),
            pltpu.VMEM((D, FF), BF16),
            pltpu.VMEM((rows, FF), BF16),
            pltpu.VMEM((ROW_TOTAL - ROW_OUT, LANES), F32),
        ],
        us=8,
    )


def result(middle, activated, w_down, small):
    return call(
        result_kernel, "result", None, [middle, activated, w_down, small],
        [like(*middle.shape, kind=BF16)], us=2,
    )


def attend_back(ids, project, weights, grad_attended, normed_turned, w_qkv, small, first, send_kind):
    shape = (PLANE, SIDE + SIDE_ROWS, LANES)
    return call(
        attend_back_kernel, "attend_back", ids,
        [project, weights, grad_attended, normed_turned, w_qkv, small, first],
        [like(*project.shape, kind=BF16), like(*shape), like(*shape, kind=send_kind)],
        [pltpu.VMEM((FIRST_ROWS, LANES), F32), pltpu.VMEM(shape[1:], F32)], us=4,
    )


def input_gradient(tokens, grad_project, grad_middle, w_qkv, small):
    return call(
        input_grad_kernel, "input_grad", None, [tokens, grad_project, grad_middle, w_qkv, small],
        [like(*tokens.shape)], us=2,
    )


def local_any(n, tokens, params, segment_ids, cotangent):
    total = n * params.shape[0]
    normed, normed_turned, _, allowed = prepare(tokens, params, segment_ids)
    gathered = lax.all_gather(params, "fsdp", axis=0).reshape(total, LANES)
    shares = gathered[:ROW_TOTAL].reshape(Z, 2 * PLANE, SHARE, LANES)
    order = [p * 2 + c for c in range(2) for p in range(PLANE)]
    side = jnp.concatenate(
        [jnp.zeros((SIDE - SHARE, LANES), BF16), gathered[ROW_SMALL:ROW_TOTAL]], axis=0
    )
    firsts = [jnp.concatenate([shares[0, k], side], axis=0)[None] for k in order]
    firsts = [
        jnp.concatenate(firsts[c + i : c + j]) for c in (0, PLANE) for i, j in FIRST_GROUPS
    ]
    rests = []
    for group in (order[:PLANE], order[PLANE:]):
        rests += [shares[1:, group[0]], jnp.concatenate([shares[1:, k] for k in group[1:]])]
    ids = jnp.array(order, jnp.int32)
    project, weights, attended, w_qkv, small, first = attend(ids, allowed, normed, firsts)
    middle, activated, grad_middle, grad_attended, w_down, rest, rest_send, first_grad = feed(
        jnp.concatenate([ids, ids]), tokens, attended, cotangent, small, first, rests, F32
    )
    outputs = result(middle, activated, w_down, small)
    grad_project, first, first_send = attend_back(
        ids, project, weights, grad_attended, normed_turned, w_qkv, small, first_grad, F32
    )
    input_grad = input_gradient(tokens, grad_project, grad_middle, w_qkv, small)
    first = jnp.stack([first, first_send], axis=1)
    rest = jnp.stack([rest, rest_send]).reshape(2, PLANE, Z - 1, SHARE, LANES).transpose(2, 1, 0, 3, 4)
    flat = jnp.concatenate(
        [
            first[:, :, :SHARE].reshape(-1, LANES),
            rest.reshape(-1, LANES),
            jnp.zeros((total - ROW_TOTAL, LANES), F32),
        ],
        axis=0,
    )
    flat = flat.at[ROW_SMALL : ROW_SMALL + LATE_SMALL].add(
        first[PLANE - 1, 1, SIDE : SIDE + LATE_SMALL]
    )
    param_grad = lax.psum_scatter(flat, "fsdp", scatter_dimension=0, tiled=True)
    return outputs, input_grad, param_grad


def index_of(z, plane, core):
    return (z * PLANE + plane) * 2 + core


def move(values, step_z, step_plane, step_core):
    pairs = [
        (index_of(z, p, c), index_of((z + step_z) % Z, p ^ step_plane, c ^ step_core))
        for z in range(Z)
        for p in range(PLANE)
        for c in range(2)
    ]
    return lax.ppermute(values, "fsdp", pairs)


STEPS = (3, 1, 2)
REST_STEPS = (1, 3, 2)


def local_slice(tokens, params, segment_ids, cotangent):
    me = lax.axis_index("fsdp").astype(jnp.int32)
    z, plane, core = me // (2 * PLANE), (me // 2) % PLANE, me % 2
    where = z.reshape(1)
    ids, rest_ids = (
        jnp.stack([(plane ^ dp) * 2 + (core ^ dc) for dc in range(2) for dp in (0, *steps)])
        for steps in (STEPS, REST_STEPS)
    )
    feed_ids = jnp.concatenate([rest_ids, ids])

    normed, normed_turned, own, allowed = prepare(tokens, params, segment_ids)
    first, rest = call(
        sort_kernel, "sort_shares", where, [own] + [move(params, d, 0, 0) for d in range(1, Z)],
        [like(1, SIDE + SMALL_ROWS, LANES, kind=BF16), like(Z - 1, SHARE, LANES, kind=BF16)],
        [pltpu.VMEM((Z, SHARE, LANES), BF16), pltpu.VMEM((SIDE + SMALL_ROWS, LANES), F32)],
    )
    firsts = [first] + [move(first, 0, d, 0) for d in STEPS]
    rests = [move(rest, 0, d, 0) for d in REST_STEPS]
    firsts = [stack(firsts[i:j]) if j > i + 1 else firsts[i] for i, j in FIRST_GROUPS]
    firsts = firsts + [move(item, 0, 0, 1) for item in firsts]
    project, weights, attended, w_qkv, small, first = attend(ids, allowed, normed, firsts)
    *rests, attended = lax.optimization_barrier((*rests, attended))
    rests = stack(rests)
    rests = [rest, rests, move(rest, 0, 0, 1), move(rests, 0, 0, 1)]
    middle, activated, grad_middle, grad_attended, w_down, rest, send, first_grad = feed(
        feed_ids, tokens, attended, cotangent, small, first, rests, BF16
    )

    rest_in = move(send, 0, 0, 1)
    grad_project, first, send = attend_back(
        ids, project, weights, grad_attended, normed_turned, w_qkv, small, first_grad, BF16
    )
    first_in = move(send, 0, 0, 1)
    part = (Z, SHARE, LANES)
    kept, *sends = call(
        add_core_kernel, "add_core", None, [first, first_in, rest, rest_in],
        [like(*part)] + [like(*part, kind=BF16)] * (PLANE - 1), [pltpu.VMEM(part, F32)],
    )
    arrived = [move(item, 0, d, 0) for item, d in zip(sends, STEPS)]
    outputs = result(middle, activated, w_down, small)
    input_grad = input_gradient(tokens, grad_project, grad_middle, w_qkv, small)
    kept, *sends = call(
        add_plane_kernel, "add_plane", where, [kept] + arrived,
        [like(SHARE, LANES)] + [like(SHARE, LANES, kind=BF16)] * (Z - 1), [pltpu.VMEM(part, F32)],
    )
    arrived = [move(item, d + 1, 0, 0) for d, item in enumerate(sends)]
    param_grad = call(
        add_column_kernel, "add_column", None, [kept] + arrived, [like(SHARE, LANES)]
    )
    return outputs, input_grad, param_grad


def solution(mesh):
    n = mesh.shape["fsdp"]
    local = local_slice if n == 2 * PLANE * Z else functools.partial(local_any, n)
    in_specs = (P("fsdp", None), P("fsdp", None), P("fsdp"), P("fsdp", None))
    out_specs = (P("fsdp", None), P("fsdp", None), P("fsdp", None))
    return jax.shard_map(local, mesh=mesh, in_specs=in_specs, out_specs=out_specs, check_vma=False)
```
